32 devices in a mesh: lon: 4 (over y, core), lat: 4 (over z), segment: 2 (over x).
Axes of the slice: x: 2, y: 2, z: 4, core: 2. Of those that a mesh axis runs over, the one named last changes fastest.
Arguments:
- inputs: bfloat16 [2, 64, 16, 512], P(None, 'lat', 'lon'), may hold values from -6 to 6
- cotangent: bfloat16 [2, 64, 16, 512], P(None, 'lat', 'lon'), may hold values from -6 to 6
- weights: bfloat16 [2, 3, 512, 512], P('segment'), may hold values from -0.15625 to 0.15625
- basis_values: float32 [64, 9, 3], replicated, may hold values from 0.05 to 0.5
- lat_step: int32 [64, 9], replicated, may hold values from -2 to 2, as said below
- lon_step: int32 [64, 9], replicated, may hold values from -2 to 2, as said below
Outputs:
- section_out: bfloat16 [2, 2, 64, 16, 512], P('segment', None, 'lat', 'lon')
- section_grad: bfloat16 [2, 2, 64, 16, 512], P('segment', None, 'lat', 'lon')
- weight_grad: float32 [2, 786432], P('segment', ('lon', 'lat'))
The draws below stay inside these ranges and needn't reach their ends.
Inputs may be any that keep to these rules, and one draw needn't show every extreme that they name: `lat_step`: row offsets of the support points; 2 and -2 each occur. `lon_step`: column offsets of the support points; 2 and -2 each occur.
All inputs are finite; a program needn't handle non-finite values.
Results may differ from the reference program's by a relative error of at most 0.017.
Values may be sent and summed in bfloat16 or wider, within the bound.
No kernel may reach another device: no remote copies, remote signals or barrier semaphores. Data moves between devices by JAX's collectives and lax.ppermute only.
A program may use at most 64 MiB of HBM per device.

```python
import math
import jax
import jax.numpy as jnp
from jax import lax

C = 512
BASIS = 3
TAPS = 9
REACH = 2
MEMBERS = 2
SEGMENTS = 2
NLAT = 64
NLON = 16


def offsets(key):
    base_key, row_key = jax.random.split(key)
    offset_table = jax.random.randint(base_key, (NLAT, TAPS), -REACH, REACH + 1)
    picked = jax.random.randint(row_key, (2,), 0, NLAT)
    offset_table = offset_table.at[picked[0], 1].set(REACH)
    offset_table = offset_table.at[picked[1], 2].set(-REACH)
    return offset_table.astype(jnp.int32)


def draw_lat_step(key, part):
    return offsets(jax.random.fold_in(key, 11))


def draw_lon_step(key, part):
    return offsets(jax.random.fold_in(key, 23))


def levels(stream_key, extent, pieces, low, largest):
    def one(axis_at, parts):
        draws = jax.random.uniform(jax.random.fold_in(jax.random.fold_in(stream_key, 6), axis_at), (parts,), jnp.float32, low / len(pieces), largest / len(pieces))
        return jnp.repeat(jnp.exp(draws), extent[axis_at] // parts).reshape((-1,) + (1,) * (len(extent) - axis_at - 1))

    factor_of = one(*pieces[0])
    for cut in pieces[1:]:
        factor_of = factor_of * one(*cut)
    return factor_of


def gaussian(own_key, extent, scale, most, cuts=(), kind=jnp.bfloat16):
    values = jax.random.normal(own_key, extent, jnp.float32) * scale
    if len(cuts) > 0:
        values = levels(own_key, extent, cuts, -0.22, 0.18) * values
    return jnp.clip(values, min=-most, max=most).astype(kind)


def setup_inputs(seed: int = 0) -> dict:
    arg_keys = jax.random.split(jax.random.key(seed), 7)
    return {
        "inputs": gaussian(arg_keys[0], (MEMBERS, NLAT, NLON, C), 1.0, 6.0, ((1, 4), (2, 4))),
        "cotangent": gaussian(arg_keys[1], (MEMBERS, NLAT, NLON, C), 1.0, 6.0, ((1, 4), (2, 4))),
        "weights": gaussian(arg_keys[2], (SEGMENTS, BASIS, C, C), (BASIS * C) ** -0.5, 0.15625, ((0, 2),)),
        "basis_values": jnp.clip(jnp.exp(jax.random.uniform(arg_keys[3], (NLAT, TAPS, BASIS), jnp.float32, math.log(0.05), math.log(0.5))), 0.05, 0.5),
        "lat_step": draw_lat_step(jax.random.fold_in(arg_keys[6], 71), 0),
        "lon_step": draw_lon_step(jax.random.fold_in(arg_keys[6], 71), 0),
    }


def spread_taps(features, basis_values, lat_step, lon_step):
    lat_total = features.shape[1]
    lon_total = features.shape[2]
    row_ids = jnp.arange(lat_total, dtype=jnp.int32)
    col_ids = jnp.arange(lon_total, dtype=jnp.int32)
    summed = jnp.zeros((BASIS,) + features.shape, features.dtype)
    for tap_num in range(TAPS):
        source = row_ids + lat_step[:, tap_num].astype(jnp.int32)
        inside = (source >= 0) & (source < lat_total)
        source = jnp.clip(source, 0, lat_total - 1).astype(jnp.int32)
        column = ((col_ids[None, :] + lon_step[:, tap_num].astype(jnp.int32)[:, None]) % lon_total).astype(jnp.int32)
        picked = features[:, source[:, None], column, :]
        picked = jnp.where(inside[None, :, None, None], picked, jnp.zeros_like(picked))
        factor = jnp.transpose(basis_values[:, tap_num, :]).astype(features.dtype)
        summed = summed + factor[:, None, :, None, None] * picked[None]
    return summed

def reference(inputs, cotangent, weights, basis_values, lat_step, lon_step):
    depth_total = weights.shape[0]
    channels = inputs.shape[3]
    grad_scale = 1.0 / math.sqrt(inputs.shape[0] * inputs.shape[1] * inputs.shape[2])
    current = inputs
    stored = []
    section_outs = []
    for segment_num in range(depth_total):
        widened = current.astype(jnp.float32)
        spread = spread_taps(widened, basis_values, lat_step, lon_step).astype(jnp.bfloat16)
        mixed = jnp.zeros((spread.shape[1] * spread.shape[2] * spread.shape[3], channels), jnp.float32)
        for basis_num in range(BASIS):
            mixed = mixed + jnp.dot(spread[basis_num].reshape(-1, channels), weights[segment_num, basis_num], preferred_element_type=jnp.float32)
        mixed = mixed.reshape(widened.shape)
        result = (widened + jax.nn.silu(mixed)).astype(jnp.bfloat16)
        stored.append((widened, spread, mixed))
        section_outs.append(result)
        current = result
    grad = cotangent
    section_grads = [None] * depth_total
    weight_grads = [None] * depth_total
    for segment_num in reversed(range(depth_total)):
        widened, spread, mixed = stored[segment_num]
        sigma = jax.nn.sigmoid(mixed)
        gate_grad = (grad.astype(jnp.float32) * sigma * (1.0 + mixed * (1.0 - sigma))).astype(jnp.bfloat16)
        flat_gate = gate_grad.reshape(-1, channels)
        feature_grad = jnp.stack([jnp.dot(flat_gate, jnp.transpose(weights[segment_num, basis_num]), preferred_element_type=jnp.float32) for basis_num in range(BASIS)]).astype(jnp.bfloat16)
        feature_grad = lax.optimization_barrier(feature_grad).astype(jnp.float32).reshape(spread.shape)
        _, pull_back = jax.vjp(lambda values_in: spread_taps(values_in, basis_values, lat_step, lon_step), widened)
        pulled = pull_back(feature_grad)[0]
        new_grad = (grad.astype(jnp.float32) + pulled).astype(jnp.bfloat16)
        weight_grads[segment_num] = jnp.stack([jnp.dot(jnp.transpose(spread[basis_num].reshape(-1, channels)), flat_gate, preferred_element_type=jnp.float32) for basis_num in range(BASIS)]).reshape(-1) * grad_scale
        section_grads[segment_num] = new_grad
        grad = new_grad
    return (jnp.stack(section_outs), jnp.stack(section_grads), jnp.stack(weight_grads))
```

```python
import functools
import math

import jax
import jax.numpy as jnp
from jax import lax
from jax.experimental import pallas as pl
from jax.experimental.pallas import tpu as pltpu
from jax.sharding import PartitionSpec as P

BASIS = 3
TAPS = 9
REACH = 2


def with_halo(array, sides, width):
    for axis, dim in sides:
        size, length = (lax.axis_size(axis), array.shape[dim])
        up = [(i, (i + 1) % size) for i in range(size)]
        down = [(j, i) for i, j in up]
        last = lax.slice_in_dim(array, length - width, length, axis=dim)
        first = lax.slice_in_dim(array, 0, width, axis=dim)
        before = lax.ppermute(last, axis, up)
        after = lax.ppermute(first, axis, down)
        array = jnp.concatenate([before, array, after], axis=dim)
    return array


def shifted(block, axis, distance):
    devices = range(lax.axis_size(axis))
    route = [(i - distance, i) for i in devices if i - distance in devices]
    return lax.ppermute(block, axis, route)


def widen(features):
    return with_halo(features, (("lon", 2), ("lat", 1)), REACH)


def pass_ahead(result):
    return shifted(result, "segment", 1)


def pass_behind(result):
    return shifted(result, "segment", -1)


def build_tables(basis_values, lat_step, lon_step, lat_rows, lon_cols, lat_index, lat_total):
    pad_rows = lat_rows + 2 * REACH
    pad_cols = lon_cols + 2 * REACH
    lat_padded = jnp.pad(lat_step, ((REACH, REACH), (0, 0)))
    lon_padded = jnp.pad(lon_step, ((REACH, REACH), (0, 0)))
    basis_padded = jnp.pad(basis_values, ((REACH, REACH), (0, 0), (0, 0)))
    row_start = lat_index * lat_rows
    lat_near = lax.dynamic_slice_in_dim(lat_padded, row_start, pad_rows, 0)
    lon_near = lax.dynamic_slice_in_dim(lon_padded, row_start, pad_rows, 0)
    basis_near = lax.dynamic_slice_in_dim(basis_padded, row_start, pad_rows, 0)
    lat_own = lat_near[REACH : REACH + lat_rows]
    lon_own = lon_near[REACH : REACH + lat_rows]
    basis_own = basis_near[REACH : REACH + lat_rows]
    own_rows = row_start + jnp.arange(lat_rows)
    inside = (own_rows[:, None] + lat_own >= 0) & (own_rows[:, None] + lat_own < lat_total)
    row_grid = jnp.arange(lat_rows)[:, None, None]
    col_grid = jnp.arange(lon_cols)[None, :, None]
    source = (row_grid + REACH + lat_own[:, None, :]) * pad_cols + (
        col_grid + REACH + lon_own[:, None, :]
    )
    tap_weight = jnp.where(inside[:, None, :, None], basis_own[:, None, :, :], 0.0)
    tap_weight = jnp.broadcast_to(tap_weight, (lat_rows, lon_cols, TAPS, BASIS))
    picker = (source[..., None] == jnp.arange(pad_rows * pad_cols)).astype(jnp.float32)
    forward_map = jnp.einsum("ijkb,ijks->bijs", tap_weight, picker, precision=lax.Precision.HIGHEST)
    forward_map = forward_map.reshape(BASIS, lat_rows * lon_cols, pad_rows * pad_cols)
    near_rows = row_start - REACH + jnp.arange(pad_rows)
    real_row = (near_rows >= 0) & (near_rows < lat_total)
    pad_row_grid = jnp.arange(pad_rows)[:, None, None]
    pad_col_grid = jnp.arange(pad_cols)[None, :, None]
    target_row = pad_row_grid - REACH + lat_near[:, None, :]
    target_col = pad_col_grid - REACH + lon_near[:, None, :]
    landed = (
        (target_row >= 0)
        & (target_row < lat_rows)
        & (target_col >= 0)
        & (target_col < lon_cols)
        & real_row[:, None, None]
    )
    target = target_row * lon_cols + target_col
    back_weight = jnp.where(landed[..., None], basis_near[:, None, :, :], 0.0)
    catcher = (target[..., None] == jnp.arange(lat_rows * lon_cols)).astype(jnp.float32)
    backward_map = jnp.einsum(
        "pqkb,pqkt->btpq", back_weight, catcher, precision=lax.Precision.HIGHEST
    )
    backward_map = backward_map.reshape(BASIS, lat_rows * lon_cols, pad_rows * pad_cols)
    return (forward_map, backward_map)


def per_device(inputs, cotangent, weights, basis_values, lat_step, lon_step):
    members, lat_rows, lon_cols, channels = inputs.shape
    pad_rows = lat_rows + 2 * REACH
    pad_cols = lon_cols + 2 * REACH
    cells = lat_rows * lon_cols
    lat_index = lax.axis_index("lat")
    lat_total = lat_rows * lax.axis_size("lat")
    segment_index = lax.axis_index("segment")
    depth = lax.axis_size("segment")
    grad_scale = 1.0 / math.sqrt(members * lat_total * lon_cols * lax.axis_size("lon"))
    forward_map, backward_map = build_tables(
        basis_values, lat_step, lon_step, lat_rows, lon_cols, lat_index, lat_total
    )
    kernel = weights[0]
    keep_spread = jnp.zeros((BASIS, members, cells, channels), jnp.bfloat16)
    keep_mixed = jnp.zeros((members, cells, channels), jnp.float32)
    keep_gate = jnp.zeros((members, cells, channels), jnp.bfloat16)
    section_out = jnp.zeros(inputs.shape, jnp.bfloat16)
    section_grad = jnp.zeros(inputs.shape, jnp.bfloat16)
    carry = inputs
    for tick_num in range(depth):
        layer_count = carry.shape[0]
        layer_padded = (
            widen(carry).reshape(layer_count, pad_rows * pad_cols, channels).astype(jnp.float32)
        )
        spread = jnp.einsum(
            "bts,msc->bmtc", forward_map, layer_padded, precision=lax.Precision.HIGHEST
        ).astype(jnp.bfloat16)
        layer_mixed = jnp.einsum(
            "bmtc,bcd->mtd", spread, kernel, preferred_element_type=jnp.float32
        )
        result = (
            carry.reshape(layer_count, cells, channels).astype(jnp.float32)
            + jax.nn.silu(layer_mixed)
        ).astype(jnp.bfloat16)
        spread, mixed, result = (spread, layer_mixed, result.reshape(carry.shape))
        here = segment_index == tick_num
        keep_spread = jnp.where(here, spread, keep_spread)
        keep_mixed = jnp.where(here, mixed, keep_mixed)
        section_out = jnp.where(here, result, section_out)
        if tick_num + 1 < depth:
            carry = pass_ahead(result)
    grad = cotangent
    for tick_num in range(depth):
        count = grad.shape[0]
        flat_grad = grad.reshape(count, cells, channels).astype(jnp.float32)
        sigma = jax.nn.sigmoid(keep_mixed)
        gate_grad = (flat_grad * sigma * (1.0 + keep_mixed * (1.0 - sigma))).astype(jnp.bfloat16)
        feature_grad = jnp.einsum(
            "mtd,bcd->bmtc", gate_grad, kernel, preferred_element_type=jnp.float32
        ).astype(jnp.bfloat16)
        padded = widen(feature_grad.reshape(BASIS * count, lat_rows, lon_cols, channels))
        padded = padded.reshape(BASIS, count, pad_rows * pad_cols, channels).astype(jnp.float32)
        pulled = jnp.einsum("bts,bmsc->mtc", backward_map, padded, precision=lax.Precision.HIGHEST)
        new_grad = (flat_grad + pulled).astype(jnp.bfloat16).reshape(grad.shape)
        gate_grad, new_grad = (gate_grad, new_grad)
        here = segment_index == depth - 1 - tick_num
        keep_gate = jnp.where(here, gate_grad, keep_gate)
        section_grad = jnp.where(here, new_grad, section_grad)
        if tick_num + 1 < depth:
            grad = pass_behind(new_grad)
    local_grad = (
        jnp.einsum("bmtc,mtd->bcd", keep_spread, keep_gate, preferred_element_type=jnp.float32)
        * grad_scale
    )
    owners = lax.axis_size("lon") * lax.axis_size("lat")
    grad_rows = local_grad.reshape(owners, -1)
    weight_grad = lax.psum_scatter(grad_rows, ("lon", "lat"), scatter_dimension=0, tiled=True)
    return (section_out[None], section_grad[None], weight_grad)


HALO = 8
BAND = 8


def swap(axis, bit):
    return [(i, i ^ bit) for i in range(lax.axis_size(axis))]


def window_plan(lat_rows):
    first = [(a, min(max(a - 4, -HALO), lat_rows + HALO - 16)) for a in range(-HALO, lat_rows + HALO, BAND)]
    second = [(a, a - 4) for a in range(-4, lat_rows + 4, BAND)]
    return first, second


def tap_tables(basis_values, lat_step, lon_step, lat_rows, lon_cols, blocks, lat_index, lon_index, lat_total):
    near = lat_rows + 2 * HALO
    base = lat_index * lat_rows
    steps = jnp.concatenate([lat_step, lon_step], axis=1)
    steps = lax.dynamic_slice_in_dim(jnp.pad(steps, ((HALO, HALO), (0, 0))), base, near, 0)
    basis = basis_values.reshape(basis_values.shape[0], TAPS * BASIS)
    basis = lax.dynamic_slice_in_dim(jnp.pad(basis, ((HALO, HALO), (0, 0))), base, near, 0)
    first, second = window_plan(lat_rows)
    plan = first + second
    rows = jnp.array([[a + r for r in range(BAND)] for a, _ in plan], jnp.int32)
    starts = jnp.array([w for _, w in plan], jnp.int32)
    pick = lambda table: jnp.stack([table[a + HALO : a + HALO + BAND] for a, _ in plan])
    step_rows = pick(steps)
    basis_rows = pick(basis)
    lat_near, lon_near = step_rows[..., :TAPS], step_rows[..., TAPS:]
    own = rows + base
    target = own[..., None] + lat_near
    inside = (own[..., None] >= 0) & (own[..., None] < lat_total) & (target >= 0) & (target < lat_total)
    local_row = rows[..., None] + lat_near - starts[:, None, None]
    shape = (len(plan), blocks, BAND, lon_cols, TAPS)
    block_ids = jnp.arange(blocks, dtype=jnp.int32) ^ lon_index
    column = block_ids[:, None, None, None] * lon_cols + jnp.arange(lon_cols, dtype=jnp.int32)[:, None]
    column = jnp.mod(column[None] + lon_near[:, None, :, None, :], blocks * lon_cols)
    place = ((column // lon_cols) ^ lon_index) * (16 * lon_cols) + local_row[:, None, :, None, :] * lon_cols + column % lon_cols
    place = jnp.where(inside[:, None, :, None, :], place, -1)
    spread_basis = jnp.broadcast_to(basis_rows[:, None, :, None, :], shape[:-1] + (TAPS * BASIS,))
    cells = len(plan) * blocks * BAND * lon_cols
    return place.reshape(cells, TAPS), spread_basis.reshape(cells, TAPS * BASIS)


def map_kernel(firsts, cells, window, place_ref, basis_ref, forward_ref, backward_ref):
    total = place_ref.shape[0] // cells
    lane = lax.broadcasted_iota(jnp.int32, (cells, window), 1)
    for g in range(total):
        span = slice(g * cells, (g + 1) * cells)
        hits = [place_ref[span, k : k + 1] == lane for k in range(TAPS)]
        for b in range(BASIS):
            table = jnp.zeros((cells, window), jnp.float32)
            for k in range(TAPS):
                at = k * BASIS + b
                table = table + jnp.where(hits[k], basis_ref[span, at : at + 1], 0.0)
            forward_ref[g, b * cells : (b + 1) * cells, :] = table.astype(jnp.bfloat16)
            if g >= firsts:
                backward_ref[g - firsts, :, b * cells : (b + 1) * cells] = table.T.astype(jnp.bfloat16)


def dot(a, b):
    return jnp.dot(a, b, preferred_element_type=jnp.float32)


def dot_nt(a, b):
    return lax.dot_general(a, b, (((1,), (1,)), ((), ())), preferred_element_type=jnp.float32)


def dot_tn(a, b):
    return lax.dot_general(a, b, (((0,), (0,)), ((), ())), preferred_element_type=jnp.float32)


def make_chain(lat_rows, lon_cols, blocks, members, channels, lat_devices):
    first, second = window_plan(lat_rows)
    nf, ns = len(first), len(second)
    band = BAND * lon_cols
    cells = blocks * band
    win = 16 * lon_cols
    own = lat_rows * lon_cols
    x_len = (lat_rows + 2 * HALO) * lon_cols
    c_len = (lat_rows + HALO) * lon_cols
    edge = HALO * lon_cols
    half_edge = edge // 2
    width = BASIS * channels
    lanes = 128
    pieces = channels // lanes

    def chain(idx, x0, x1, x2, x3, w_own, w_a, w_b, forward, backward, out_ref, grad_ref, gate_ref, own_ref, p1, p2, p3, w, s0, s1, slope, mid, gates, feat, pull, grads):
        blk = (x0, x1, x2, x3)
        seg, lon, lat = idx[0], idx[1], idx[2]
        half = w_a.shape[0]
        core = lon % 2
        w[pl.ds(pl.multiple_of(seg * width, width), width), :] = w_own[...]
        other = (1 - seg) * width
        w[pl.ds(pl.multiple_of(other + core * half, half), half), :] = w_a[...]
        w[pl.ds(pl.multiple_of(other + (1 - core) * half, half), half), :] = w_b[...]
        for m in range(members):
            for g, (a, start) in enumerate(first):
                o = (start + HALO) * lon_cols
                near = jnp.concatenate([r[m, o : o + win, :] for r in blk], axis=0)
                got = dot(forward[g], near).astype(jnp.bfloat16)
                at = (m * nf + g) * cells
                for b in range(BASIS):
                    s0[at : at + cells, b * channels : (b + 1) * channels] = got[b * cells : (b + 1) * cells]
        for m in range(members):
            for g in range(nf):
                at = (m * nf + g) * cells
                mixed = dot(s0[at : at + cells, :], w[0:width, :])
                sigma = jax.nn.sigmoid(mixed)
                here = jnp.concatenate([r[m, g * band : (g + 1) * band, :] for r in blk], axis=0)
                value = (here.astype(jnp.float32) + mixed * sigma).astype(jnp.bfloat16)
                mid[m, :, g * band : (g + 1) * band, :] = value.reshape(blocks, band, channels)
                tilt = sigma * (1.0 + mixed * (1.0 - sigma))
                slope[m, :, g * band : (g + 1) * band, :] = tilt.reshape(blocks, band, channels)
        for m in range(members):
            for g in range(ns):
                near = mid[m, :, g * band : g * band + win, :].reshape(blocks * win, channels)
                got = dot(forward[nf + g], near).astype(jnp.bfloat16)
                at = (m * ns + g) * cells
                for b in range(BASIS):
                    s1[at : at + cells, b * channels : (b + 1) * channels] = got[b * cells : (b + 1) * cells]
        for m in range(members):
            for g in range(ns):
                at = (m * ns + g) * cells
                mixed = dot(s1[at : at + cells, :], w[width : 2 * width, :])
                sigma = jax.nn.sigmoid(mixed)
                coming = jnp.concatenate(
                    [r[m, x_len + g * band : x_len + (g + 1) * band, :] for r in blk], axis=0
                ).astype(jnp.float32)
                gates[at : at + cells, :] = (coming * sigma * (1.0 + mixed * (1.0 - sigma))).astype(jnp.bfloat16)
                low, high = max(g * band, half_edge), min((g + 1) * band, half_edge + own)
                if low < high:
                    base = mid[m, 0, half_edge + low : half_edge + high, :].astype(jnp.float32)
                    local = slice(low - g * band, high - g * band)
                    last = (base + mixed[local] * sigma[local]).astype(jnp.bfloat16)
                    early = mid[m, 0, half_edge + low : half_edge + high, :]
                    out_ref[m, low - half_edge : high - half_edge, :] = jnp.where(seg == 0, early, last)
        for b in range(BASIS):
            got = dot_nt(gates[...], w[width + b * channels : width + (b + 1) * channels, :]).astype(jnp.bfloat16)
            for i in range(members * ns):
                feat[(i * BASIS + b) * cells : (i * BASIS + b + 1) * cells, :] = got[i * cells : (i + 1) * cells]
        pull[...] = jnp.zeros(pull.shape, jnp.float32)
        for m in range(members):
            for g in range(ns):
                at = (m * ns + g) * cells * BASIS
                got = dot(backward[g], feat[at : at + BASIS * cells, :])
                pull[m, :, g * band : g * band + win, :] += got.reshape(blocks, win, channels)
        for m in range(members):
            for q in range(blocks):
                coming = blk[q][m, x_len : x_len + c_len, :].astype(jnp.float32)
                value = (coming + pull[m, q, half_edge : half_edge + c_len, :]).astype(jnp.bfloat16)
                if q == 0:
                    grad_ref[m, :, :] = value[half_edge : half_edge + own]
                gate = value.astype(jnp.float32) * slope[m, q, half_edge : half_edge + c_len, :]
                gate_ref[m, q, :, :] = gate.astype(jnp.bfloat16)

        columns = pl.ds(pl.multiple_of(lon * (width // blocks), 128), width // blocks)

        @pl.when(seg == 0)
        def _():
            left, right = [], []
            for m in range(members):
                for g in range(1, nf - 1):
                    at = (m * nf + g) * cells
                    left.append(s0[at : at + cells, columns])
                    o = half_edge + (g - 1) * band
                    right.append(gate_ref[m, :, o : o + band, :].reshape(cells, channels))
            grads[...] = dot_tn(jnp.concatenate(left, axis=0), jnp.concatenate(right, axis=0))

        @pl.when(seg == 1)
        def _():
            left, right = [], []
            for m in range(members):
                for g in range(ns):
                    low, high = max(g * band, half_edge), min((g + 1) * band, half_edge + own)
                    for q in range(blocks):
                        at = (m * ns + g) * cells + q * band - g * band
                        left.append(s1[at + low : at + high, columns])
                        right.append(gates[at + low : at + high, :])
            grads[...] = dot_tn(jnp.concatenate(left, axis=0), jnp.concatenate(right, axis=0))

        share = width // blocks // lat_devices

        def rows_of(index):
            return grads[pl.ds(pl.multiple_of(index * share, share), share), :]

        own_ref[...] = rows_of(lat)
        for bit, ref in ((1, p1), (2, p2), (3, p3)):
            ref[...] = rows_of(lat ^ bit).astype(jnp.bfloat16)

    def finish(idx, w_own, backward, gate_ref, g1_ref, grad_ref, gates, feat, pull):
        seg = idx[0]

        @pl.when(seg == 1)
        def _():
            grad_ref[...] = g1_ref[...]

        @pl.when(seg == 0)
        def _():
            for m in range(members):
                for g in range(ns):
                    at = (m * ns + g) * cells
                    gates[at : at + cells, :] = gate_ref[m, :, g * band : (g + 1) * band, :].reshape(cells, channels)
            for b in range(BASIS):
                got = dot_nt(gates[...], w_own[b * channels : (b + 1) * channels, :]).astype(jnp.bfloat16)
                for i in range(members * ns):
                    feat[(i * BASIS + b) * cells : (i * BASIS + b + 1) * cells, :] = got[i * cells : (i + 1) * cells]
            pull[...] = jnp.zeros(pull.shape, jnp.float32)
            for m in range(members):
                for g in range(ns):
                    at = (m * ns + g) * cells * BASIS
                    got = dot(backward[g, 0:win, :], feat[at : at + BASIS * cells, :])
                    pull[m, g * band : g * band + win, :] += got
                total = g1_ref[m].astype(jnp.float32) + pull[m, edge : edge + own, :]
                grad_ref[m, :, :] = total.astype(jnp.bfloat16)

    return chain, finish


def whole_ring(inputs, cotangent, weights, basis_values, lat_step, lon_step):
    members, lat_rows, lon_cols, channels = inputs.shape
    blocks = lax.axis_size("lon")
    lat_devices = lax.axis_size("lat")
    lat_total = lat_rows * lat_devices
    lon_index = lax.axis_index("lon")
    lat_index = lax.axis_index("lat")
    segment_index = lax.axis_index("segment")
    grad_scale = 1.0 / math.sqrt(members * lat_total * lon_cols * blocks)
    own = lat_rows * lon_cols
    edge = HALO * lon_cols
    half_edge = edge // 2
    width = BASIS * channels
    state = inputs.reshape(members, own, channels)
    coming = cotangent.reshape(members, own, channels)
    kernel = weights.reshape(width, channels)
    up = [(i, i + 1) for i in range(lat_devices - 1)]
    down = [(i + 1, i) for i in range(lat_devices - 1)]
    tail = jnp.concatenate([state[:, own - edge :], coming[:, own - half_edge :]], axis=1)
    head = jnp.concatenate([state[:, :edge], coming[:, :half_edge]], axis=1)
    before = lax.ppermute(tail, "lat", up)
    after = lax.ppermute(head, "lat", down)
    half = lax.dynamic_slice_in_dim(kernel, (lon_index % 2) * (width // 2), width // 2, 0)
    near_half = lax.ppermute(half, "segment", swap("segment", 1))
    block = jnp.concatenate(
        [before[:, :edge], state, after[:, :edge], before[:, edge:], coming, after[:, edge:]], axis=1
    )
    far = lax.ppermute(block, "lon", swap("lon", 2))
    mate = lax.ppermute(block, "lon", swap("lon", 1))
    far_mate = lax.ppermute(far, "lon", swap("lon", 1))
    far_half = lax.ppermute(near_half, "lon", swap("lon", 1))

    place, basis = tap_tables(
        basis_values, lat_step, lon_step, lat_rows, lon_cols, blocks, lat_index, lon_index, lat_total
    )
    first, second = window_plan(lat_rows)
    nf, ns = len(first), len(second)
    band = BAND * lon_cols
    cells = blocks * band
    win = 16 * lon_cols
    vmem = pl.BlockSpec(memory_space=pltpu.VMEM)
    smem = pl.BlockSpec(memory_space=pltpu.SMEM)
    params = pltpu.CompilerParams(vmem_limit_bytes=48 * 1024 * 1024)
    half_type, full_type = jnp.bfloat16, jnp.float32
    forward, backward = pl.pallas_call(
        functools.partial(map_kernel, nf, cells, blocks * win),
        out_shape=(
            jax.ShapeDtypeStruct((nf + ns, BASIS * cells, blocks * win), half_type),
            jax.ShapeDtypeStruct((ns, blocks * win, BASIS * cells), half_type),
        ),
        in_specs=[vmem] * 2,
        out_specs=(vmem,) * 2,
        compiler_params=params,
        cost_estimate=pl.CostEstimate(flops=40_000_000, bytes_accessed=4_000_000, transcendentals=0),
        name="maps",
    )(place, basis)
    chain, finish = make_chain(lat_rows, lon_cols, blocks, members, channels, lat_devices)
    idx = jnp.stack([segment_index, lon_index, lat_index]).astype(jnp.int32)
    share = width // blocks // lat_devices
    shape = jax.ShapeDtypeStruct
    x_len = own + 2 * edge
    c_len = own + edge
    out, first_grad, gates, mine, *parts = pl.pallas_call(
        chain,
        out_shape=(
            shape((members, own, channels), half_type),
            shape((members, own, channels), half_type),
            shape((members, blocks, c_len, channels), half_type),
            shape((share, channels), full_type),
        )
        + (shape((share, channels), half_type),) * 3,
        in_specs=[smem] + [vmem] * 9,
        out_specs=(vmem,) * 7,
        scratch_shapes=[
            pltpu.VMEM((2 * width, channels), half_type),
            pltpu.VMEM((members * nf * cells, width), half_type),
            pltpu.VMEM((members * ns * cells, width), half_type),
            pltpu.VMEM((members, blocks, x_len, channels), full_type),
            pltpu.VMEM((members, blocks, x_len, channels), half_type),
            pltpu.VMEM((members * ns * cells, channels), half_type),
            pltpu.VMEM((members * ns * cells * BASIS, channels), half_type),
            pltpu.VMEM((members, blocks, x_len, channels), full_type),
            pltpu.VMEM((width // blocks, channels), full_type),
        ],
        compiler_params=params,
        cost_estimate=pl.CostEstimate(flops=6_000_000_000, bytes_accessed=10_000_000, transcendentals=2_000_000),
        name="chain",
    )(idx, block, mate, far, far_mate, kernel, near_half, far_half, forward, backward)
    got = [lax.ppermute(part, "lat", swap("lat", bit)) for bit, part in zip((1, 2, 3), parts)]
    grad = pl.pallas_call(
        finish,
        out_shape=shape((members, own, channels), half_type),
        in_specs=[smem] + [vmem] * 4,
        out_specs=vmem,
        scratch_shapes=[
            pltpu.VMEM((members * ns * cells, channels), half_type),
            pltpu.VMEM((members * ns * cells * BASIS, channels), half_type),
            pltpu.VMEM((members, x_len, channels), full_type),
        ],
        compiler_params=params,
        cost_estimate=pl.CostEstimate(flops=2_000_000_000, bytes_accessed=5_000_000, transcendentals=0),
        name="finish",
    )(idx, kernel, backward, gates, first_grad)
    total = mine
    for part in got:
        total = total + part.astype(full_type)
    weight_grad = (total * grad_scale).reshape(1, share * channels)
    return (out.reshape((1,) + inputs.shape), grad.reshape((1,) + inputs.shape), weight_grad)


def fits_ring(mesh, inputs):
    sizes = dict(mesh.shape)
    rows, cols = inputs.shape[1] // sizes["lat"], inputs.shape[2] // sizes["lon"]
    return sizes["segment"] == 2 and sizes["lon"] == 4 and sizes["lat"] == 4 and rows == 16 and cols == 4


def solution(mesh):
    def apply(*args):
        body = whole_ring if fits_ring(mesh, args[0]) else per_device
        return jax.shard_map(
            body,
            mesh=mesh,
            in_specs=(
                P(None, "lat", "lon", None),
                P(None, "lat", "lon", None),
                P("segment", None, None, None),
                P(),
                P(),
                P(),
            ),
            out_specs=(
                P("segment", None, "lat", "lon", None),
                P("segment", None, "lat", "lon", None),
                P("segment", ("lon", "lat")),
            ),
            check_vma=False,
        )(*args)

    return apply
```

```python
import functools
import math

import jax
import jax.numpy as jnp
from jax import lax
from jax.experimental import pallas as pl
from jax.experimental.pallas import tpu as pltpu
from jax.sharding import PartitionSpec as P

BASIS = 3
TAPS = 9
REACH = 2


def with_halo(array, sides, width):
    for axis, dim in sides:
        size, length = (lax.axis_size(axis), array.shape[dim])
        up = [(i, (i + 1) % size) for i in range(size)]
        down = [(j, i) for i, j in up]
        last = lax.slice_in_dim(array, length - width, length, axis=dim)
        first = lax.slice_in_dim(array, 0, width, axis=dim)
        before = lax.ppermute(last, axis, up)
        after = lax.ppermute(first, axis, down)
        array = jnp.concatenate([before, array, after], axis=dim)
    return array


def shifted(block, axis, distance):
    devices = range(lax.axis_size(axis))
    route = [(i - distance, i) for i in devices if i - distance in devices]
    return lax.ppermute(block, axis, route)


def widen(features):
    return with_halo(features, (("lon", 2), ("lat", 1)), REACH)


def pass_ahead(result):
    return shifted(result, "segment", 1)


def pass_behind(result):
    return shifted(result, "segment", -1)


def build_tables(basis_values, lat_step, lon_step, lat_rows, lon_cols, lat_index, lat_total):
    pad_rows = lat_rows + 2 * REACH
    pad_cols = lon_cols + 2 * REACH
    lat_padded = jnp.pad(lat_step, ((REACH, REACH), (0, 0)))
    lon_padded = jnp.pad(lon_step, ((REACH, REACH), (0, 0)))
    basis_padded = jnp.pad(basis_values, ((REACH, REACH), (0, 0), (0, 0)))
    row_start = lat_index * lat_rows
    lat_near = lax.dynamic_slice_in_dim(lat_padded, row_start, pad_rows, 0)
    lon_near = lax.dynamic_slice_in_dim(lon_padded, row_start, pad_rows, 0)
    basis_near = lax.dynamic_slice_in_dim(basis_padded, row_start, pad_rows, 0)
    lat_own = lat_near[REACH : REACH + lat_rows]
    lon_own = lon_near[REACH : REACH + lat_rows]
    basis_own = basis_near[REACH : REACH + lat_rows]
    own_rows = row_start + jnp.arange(lat_rows)
    inside = (own_rows[:, None] + lat_own >= 0) & (own_rows[:, None] + lat_own < lat_total)
    row_grid = jnp.arange(lat_rows)[:, None, None]
    col_grid = jnp.arange(lon_cols)[None, :, None]
    source = (row_grid + REACH + lat_own[:, None, :]) * pad_cols + (
        col_grid + REACH + lon_own[:, None, :]
    )
    tap_weight = jnp.where(inside[:, None, :, None], basis_own[:, None, :, :], 0.0)
    tap_weight = jnp.broadcast_to(tap_weight, (lat_rows, lon_cols, TAPS, BASIS))
    picker = (source[..., None] == jnp.arange(pad_rows * pad_cols)).astype(jnp.float32)
    forward_map = jnp.einsum("ijkb,ijks->bijs", tap_weight, picker, precision=lax.Precision.HIGHEST)
    forward_map = forward_map.reshape(BASIS, lat_rows * lon_cols, pad_rows * pad_cols)
    near_rows = row_start - REACH + jnp.arange(pad_rows)
    real_row = (near_rows >= 0) & (near_rows < lat_total)
    pad_row_grid = jnp.arange(pad_rows)[:, None, None]
    pad_col_grid = jnp.arange(pad_cols)[None, :, None]
    target_row = pad_row_grid - REACH + lat_near[:, None, :]
    target_col = pad_col_grid - REACH + lon_near[:, None, :]
    landed = (
        (target_row >= 0)
        & (target_row < lat_rows)
        & (target_col >= 0)
        & (target_col < lon_cols)
        & real_row[:, None, None]
    )
    target = target_row * lon_cols + target_col
    back_weight = jnp.where(landed[..., None], basis_near[:, None, :, :], 0.0)
    catcher = (target[..., None] == jnp.arange(lat_rows * lon_cols)).astype(jnp.float32)
    backward_map = jnp.einsum(
        "pqkb,pqkt->btpq", back_weight, catcher, precision=lax.Precision.HIGHEST
    )
    backward_map = backward_map.reshape(BASIS, lat_rows * lon_cols, pad_rows * pad_cols)
    return (forward_map, backward_map)


def per_device(inputs, cotangent, weights, basis_values, lat_step, lon_step):
    members, lat_rows, lon_cols, channels = inputs.shape
    pad_rows = lat_rows + 2 * REACH
    pad_cols = lon_cols + 2 * REACH
    cells = lat_rows * lon_cols
    lat_index = lax.axis_index("lat")
    lat_total = lat_rows * lax.axis_size("lat")
    segment_index = lax.axis_index("segment")
    depth = lax.axis_size("segment")
    grad_scale = 1.0 / math.sqrt(members * lat_total * lon_cols * lax.axis_size("lon"))
    forward_map, backward_map = build_tables(
        basis_values, lat_step, lon_step, lat_rows, lon_cols, lat_index, lat_total
    )
    kernel = weights[0]
    keep_spread = jnp.zeros((BASIS, members, cells, channels), jnp.bfloat16)
    keep_mixed = jnp.zeros((members, cells, channels), jnp.float32)
    keep_gate = jnp.zeros((members, cells, channels), jnp.bfloat16)
    section_out = jnp.zeros(inputs.shape, jnp.bfloat16)
    section_grad = jnp.zeros(inputs.shape, jnp.bfloat16)
    carry = inputs
    for tick_num in range(depth):
        layer_count = carry.shape[0]
        layer_padded = (
            widen(carry).reshape(layer_count, pad_rows * pad_cols, channels).astype(jnp.float32)
        )
        spread = jnp.einsum(
            "bts,msc->bmtc", forward_map, layer_padded, precision=lax.Precision.HIGHEST
        ).astype(jnp.bfloat16)
        layer_mixed = jnp.einsum(
            "bmtc,bcd->mtd", spread, kernel, preferred_element_type=jnp.float32
        )
        result = (
            carry.reshape(layer_count, cells, channels).astype(jnp.float32)
            + jax.nn.silu(layer_mixed)
        ).astype(jnp.bfloat16)
        spread, mixed, result = (spread, layer_mixed, result.reshape(carry.shape))
        here = segment_index == tick_num
        keep_spread = jnp.where(here, spread, keep_spread)
        keep_mixed = jnp.where(here, mixed, keep_mixed)
        section_out = jnp.where(here, result, section_out)
        if tick_num + 1 < depth:
            carry = pass_ahead(result)
    grad = cotangent
    for tick_num in range(depth):
        count = grad.shape[0]
        flat_grad = grad.reshape(count, cells, channels).astype(jnp.float32)
        sigma = jax.nn.sigmoid(keep_mixed)
        gate_grad = (flat_grad * sigma * (1.0 + keep_mixed * (1.0 - sigma))).astype(jnp.bfloat16)
        feature_grad = jnp.einsum(
            "mtd,bcd->bmtc", gate_grad, kernel, preferred_element_type=jnp.float32
        ).astype(jnp.bfloat16)
        padded = widen(feature_grad.reshape(BASIS * count, lat_rows, lon_cols, channels))
        padded = padded.reshape(BASIS, count, pad_rows * pad_cols, channels).astype(jnp.float32)
        pulled = jnp.einsum("bts,bmsc->mtc", backward_map, padded, precision=lax.Precision.HIGHEST)
        new_grad = (flat_grad + pulled).astype(jnp.bfloat16).reshape(grad.shape)
        gate_grad, new_grad = (gate_grad, new_grad)
        here = segment_index == depth - 1 - tick_num
        keep_gate = jnp.where(here, gate_grad, keep_gate)
        section_grad = jnp.where(here, new_grad, section_grad)
        if tick_num + 1 < depth:
            grad = pass_behind(new_grad)
    local_grad = (
        jnp.einsum("bmtc,mtd->bcd", keep_spread, keep_gate, preferred_element_type=jnp.float32)
        * grad_scale
    )
    owners = lax.axis_size("lon") * lax.axis_size("lat")
    grad_rows = local_grad.reshape(owners, -1)
    weight_grad = lax.psum_scatter(grad_rows, ("lon", "lat"), scatter_dimension=0, tiled=True)
    return (section_out[None], section_grad[None], weight_grad)


HALO = 8
BAND = 8


def swap(axis, bit):
    return [(i, i ^ bit) for i in range(lax.axis_size(axis))]


def window_plan(lat_rows):
    first = [(a, min(max(a - 4, -HALO), lat_rows + HALO - 16)) for a in range(-HALO, lat_rows + HALO, BAND)]
    second = [(a, a - 4) for a in range(-4, lat_rows + 4, BAND)]
    return first, second


def tap_tables(basis_values, lat_step, lon_step, lat_rows, lon_cols, blocks, lat_index, lon_index, lat_total):
    near = lat_rows + 2 * HALO
    base = lat_index * lat_rows
    steps = jnp.concatenate([lat_step, lon_step], axis=1)
    steps = lax.dynamic_slice_in_dim(jnp.pad(steps, ((HALO, HALO), (0, 0))), base, near, 0)
    basis = basis_values.reshape(basis_values.shape[0], TAPS * BASIS)
    basis = lax.dynamic_slice_in_dim(jnp.pad(basis, ((HALO, HALO), (0, 0))), base, near, 0)
    first, second = window_plan(lat_rows)
    plan = first + second
    rows = jnp.array([[a + r for r in range(BAND)] for a, _ in plan], jnp.int32)
    starts = jnp.array([w for _, w in plan], jnp.int32)
    pick = lambda table: jnp.stack([table[a + HALO : a + HALO + BAND] for a, _ in plan])
    step_rows = pick(steps)
    basis_rows = pick(basis)
    lat_near, lon_near = step_rows[..., :TAPS], step_rows[..., TAPS:]
    own = rows + base
    target = own[..., None] + lat_near
    inside = (own[..., None] >= 0) & (own[..., None] < lat_total) & (target >= 0) & (target < lat_total)
    local_row = rows[..., None] + lat_near - starts[:, None, None]
    shape = (len(plan), blocks, BAND, lon_cols, TAPS)
    block_ids = jnp.arange(blocks, dtype=jnp.int32) ^ lon_index
    column = block_ids[:, None, None, None] * lon_cols + jnp.arange(lon_cols, dtype=jnp.int32)[:, None]
    column = jnp.mod(column[None] + lon_near[:, None, :, None, :], blocks * lon_cols)
    place = ((column // lon_cols) ^ lon_index) * (16 * lon_cols) + local_row[:, None, :, None, :] * lon_cols + column % lon_cols
    place = jnp.where(inside[:, None, :, None, :], place, -1)
    spread_basis = jnp.broadcast_to(basis_rows[:, None, :, None, :], shape[:-1] + (TAPS * BASIS,))
    cells = len(plan) * blocks * BAND * lon_cols
    return place.reshape(cells, TAPS), spread_basis.reshape(cells, TAPS * BASIS)


def map_kernel(firsts, cells, window, place_ref, basis_ref, forward_ref, backward_ref):
    total = place_ref.shape[0] // cells
    piece = 32
    lane = lax.broadcasted_iota(jnp.int32, (piece, window), 1)

    def fill(i, carry):
        span = pl.ds(pl.multiple_of(i * piece, piece), piece)
        place, basis = place_ref[span, :], basis_ref[span, :]
        tables = [jnp.zeros((piece, window), jnp.float32) for _ in range(BASIS)]
        for k in range(TAPS):
            hit = place[:, k : k + 1] == lane
            for b in range(BASIS):
                at = k * BASIS + b
                tables[b] = tables[b] + jnp.where(hit, basis[:, at : at + 1], 0.0)
        g, row = i // (cells // piece), i % (cells // piece) * piece
        for b in range(BASIS):
            spot = pl.ds(pl.multiple_of(b * cells + row, piece), piece)
            forward_ref[g, spot, :] = tables[b].astype(jnp.bfloat16)
        return carry

    lax.fori_loop(0, total * cells // piece, fill, 0)
    for g in range(total - firsts):
        for b in range(BASIS):
            table = forward_ref[firsts + g, b * cells : (b + 1) * cells, :].astype(jnp.float32)
            backward_ref[g, :, b * cells : (b + 1) * cells] = table.T.astype(jnp.bfloat16)


def dot(a, b):
    return jnp.dot(a, b, preferred_element_type=jnp.float32)


def dot_nt(a, b):
    return lax.dot_general(a, b, (((1,), (1,)), ((), ())), preferred_element_type=jnp.float32)


def dot_tn(a, b):
    return lax.dot_general(a, b, (((0,), (0,)), ((), ())), preferred_element_type=jnp.float32)


def make_steps(lat_rows, lon_cols, blocks, members, channels, lat_devices):
    first, second = window_plan(lat_rows)
    nf, ns = len(first), len(second)
    band = BAND * lon_cols
    cells = blocks * band
    win = 16 * lon_cols
    own = lat_rows * lon_cols
    half_edge = HALO * lon_cols // 2
    width = BASIS * channels
    lanes = 128
    pieces = channels // lanes

    def put_spread(got, into, at):
        for b in range(BASIS):
            into[at : at + cells, b * channels : (b + 1) * channels] = got[b * cells : (b + 1) * cells]

    def first_section(blk, w, s0, s1, slope, mid, forward):
        for m in range(members):
            total = dot(s0[m * nf * cells : (m + 1) * nf * cells, :], w[...])
            for g in range(nf):
                mixed = total[g * cells : (g + 1) * cells]
                sigma = jax.nn.sigmoid(mixed)
                here = jnp.concatenate([r[m, g * band : (g + 1) * band, :] for r in blk], axis=0)
                value = (here.astype(jnp.float32) + mixed * sigma).astype(jnp.bfloat16)
                mid[m, :, g * band : (g + 1) * band, :] = value.reshape(blocks, band, channels)
                tilt = sigma * (1.0 + mixed * (1.0 - sigma))
                slope[m, :, g * band : (g + 1) * band, :] = tilt.reshape(blocks, band, channels)
            for g in range(ns):
                near = mid[m, :, g * band : g * band + win, :].reshape(blocks * win, channels)
                put_spread(dot(forward[nf + g], near).astype(jnp.bfloat16), s1, (m * ns + g) * cells)

    def spread(x0, x1, x2, x3, forward, s0):
        blk = (x0, x1, x2, x3)
        for m in range(members):
            for g, (a, start) in enumerate(first):
                o = (start + HALO) * lon_cols
                near = jnp.concatenate([r[m, o : o + win, :] for r in blk], axis=0)
                put_spread(dot(forward[g], near).astype(jnp.bfloat16), s0, (m * nf + g) * cells)

    def early(idx, x0, x1, x2, x3, w_own, forward, s0, s1, slope, mid):
        @pl.when(idx[0] == 0)
        def _():
            first_section((x0, x1, x2, x3), w_own, s0, s1, slope, mid, forward)

    def own_part(g):
        return max(g * band, half_edge), min((g + 1) * band, half_edge + own)

    def apply_back(w, gates, feat):
        for b in range(BASIS):
            got = dot_nt(gates[...], w[b * channels : (b + 1) * channels, :]).astype(jnp.bfloat16)
            for i in range(members * ns):
                feat[(i * BASIS + b) * cells : (i * BASIS + b + 1) * cells, :] = got[i * cells : (i + 1) * cells]

    def chain(idx, x0, x1, x2, x3, c0, c1, c2, c3, w_own, w_a, w_b, forward, backward, s0, s1_in, slope_in, mid_in,
              s1, slope, mid, out_ref, next_ref, gate_ref, own_ref, p1, p2, p3, w, gates, feat, pull, grads):
        coming_blocks = (c0, c1, c2, c3)
        seg, lon, lat = idx[0], idx[1], idx[2]
        half = w_a.shape[0]
        core = lon % 2
        w[pl.ds(pl.multiple_of(core * half, half), half), :] = w_a[...]
        w[pl.ds(pl.multiple_of((1 - core) * half, half), half), :] = w_b[...]
        columns = pl.ds(pl.multiple_of(lon * (width // blocks), 128), width // blocks)

        def coming_at(m, g):
            return jnp.concatenate([r[m, g * band : (g + 1) * band, :] for r in coming_blocks], axis=0).astype(jnp.float32)

        def second_section(weight, into, last):
            for m in range(members):
                total = dot(s1[m * ns * cells : (m + 1) * ns * cells, :], weight[...])
                for g in range(ns):
                    at = (m * ns + g) * cells
                    mixed = total[g * cells : (g + 1) * cells]
                    sigma = jax.nn.sigmoid(mixed)
                    into[at : at + cells, :] = (coming_at(m, g) * sigma * (1.0 + mixed * (1.0 - sigma))).astype(jnp.bfloat16)
                    low, high = own_part(g)
                    base = mid[m, 0, half_edge + low : half_edge + high, :]
                    if last:
                        local = slice(low - g * band, high - g * band)
                        base = (base.astype(jnp.float32) + mixed[local] * sigma[local]).astype(jnp.bfloat16)
                    out_ref[m, low - half_edge : high - half_edge, :] = base

        def store_grads(left, right):
            got = dot_tn(jnp.concatenate(left, axis=0), jnp.concatenate(right, axis=0))
            for c in range(pieces):
                grads[pl.ds(c, width // blocks, stride=pieces), :] = got[:, c * lanes : (c + 1) * lanes]

        @pl.when(seg == 0)
        def _():
            second_section(w, gates, False)
            apply_back(w, gates, feat)
            for m in range(members):
                for g in range(ns):
                    at = (m * ns + g) * cells * BASIS
                    got = dot(backward[g], feat[at : at + BASIS * cells, :]).reshape(blocks, win, channels)
                    if g == 0:
                        pull[m, :, :win, :] = got
                    else:
                        pull[m, :, g * band : (g + 1) * band, :] += got[:, :band]
                        pull[m, :, (g + 1) * band : g * band + win, :] = got[:, band:]
            left, right = [], []
            step = half_edge
            for m in range(members):
                for g in range(ns):
                    at = (m * ns + g) * cells
                    span = slice(half_edge + g * band, half_edge + (g + 1) * band)
                    value = (coming_at(m, g) + pull[m, :, span, :].reshape(cells, channels)).astype(jnp.bfloat16)
                    low, high = own_part(g)
                    next_ref[m, low - half_edge : high - half_edge, :] = value[low - g * band : high - g * band]
                    gate = value.astype(jnp.float32) * slope[m, :, span, :].reshape(cells, channels)
                    gate_ref[at : at + cells, :] = gate.astype(jnp.bfloat16)
                for g in range(1, nf - 1):
                    at = (m * nf + g) * cells
                    left.append(s0[at : at + cells, columns])
                    for q in range(blocks):
                        for o in range(0, band, step):
                            spot = half_edge + (g - 1) * band + o
                            turn, rest = spot // band, spot % band
                            at = (m * ns + turn) * cells + q * band + rest
                            right.append(gate_ref[at : at + step, :])
            store_grads(left, right)

        @pl.when(seg == 1)
        def _():
            first_section((x0, x1, x2, x3), w, s0, s1, slope, mid, forward)
            second_section(w_own, gate_ref, True)
            left, right = [], []
            for m in range(members):
                next_ref[m, :, :] = c0[m, half_edge : half_edge + own, :]
                for g in range(ns):
                    low, high = own_part(g)
                    for q in range(blocks):
                        at = (m * ns + g) * cells + q * band - g * band
                        left.append(s1[at + low : at + high, columns])
                        right.append(gate_ref[at + low : at + high, :])
            store_grads(left, right)

        share = width // blocks // lat_devices * pieces

        def rows_of(index):
            return grads[pl.ds(pl.multiple_of(index * share, share), share), :]

        own_ref[...] = rows_of(lat)
        for bit, ref in ((1, p1), (2, p2), (3, p3)):
            ref[...] = rows_of(lat ^ bit).astype(jnp.bfloat16)

    def finish(w_own, backward, gates, next_ref, last_ref, grad_ref, out_ref, feat, pull):
        apply_back(w_own, gates, feat)
        for m in range(members):
            for g in range(ns):
                at = (m * ns + g) * cells * BASIS
                got = dot(backward[g, 0:win, :], feat[at : at + BASIS * cells, :])
                if g == 0:
                    pull[m, :win, :] = got
                else:
                    pull[m, g * band : (g + 1) * band, :] += got[:band]
                    pull[m, (g + 1) * band : g * band + win, :] = got[band:]
            total = next_ref[m].astype(jnp.float32) + pull[m, 2 * half_edge : 2 * half_edge + own, :]
            grad_ref[m, :, :] = total.astype(jnp.bfloat16)
        out_ref[...] = last_ref[...]

    return spread, early, chain, finish


def whole_ring(inputs, cotangent, weights, basis_values, lat_step, lon_step):
    members, lat_rows, lon_cols, channels = inputs.shape
    blocks = lax.axis_size("lon")
    lat_devices = lax.axis_size("lat")
    lat_total = lat_rows * lat_devices
    lon_index = lax.axis_index("lon")
    lat_index = lax.axis_index("lat")
    segment_index = lax.axis_index("segment")
    grad_scale = 1.0 / math.sqrt(members * lat_total * lon_cols * blocks)
    own = lat_rows * lon_cols
    edge = HALO * lon_cols
    half_edge = edge // 2
    width = BASIS * channels
    kernel = weights.reshape(width, channels)
    half = lax.dynamic_slice_in_dim(kernel, (lon_index % 2) * (width // 2), width // 2, 0)
    near_half = lax.ppermute(half, "segment", swap("segment", 1))
    half, inputs, cotangent = lax.optimization_barrier((half, inputs, cotangent))
    state = inputs.reshape(members, own, channels)
    coming = cotangent.reshape(members, own, channels)
    up = [(i, i + 1) for i in range(lat_devices - 1)]
    down = [(i + 1, i) for i in range(lat_devices - 1)]
    cross = lambda steps: [(n * lat_devices + i, (n ^ 2) * lat_devices + j) for i, j in steps for n in range(blocks)]
    state_y = lax.ppermute(state, "lon", swap("lon", 2))
    tail, head = state[:, own - edge :], state[:, :edge]
    before_y = lax.ppermute(tail, ("lon", "lat"), cross(up))
    after_y = lax.ppermute(head, ("lon", "lat"), cross(down))
    before = lax.ppermute(jnp.concatenate([tail, coming[:, own - half_edge :]], axis=1), "lat", up)
    after = lax.ppermute(jnp.concatenate([head, coming[:, :half_edge]], axis=1), "lat", down)
    x0 = jnp.concatenate([before[:, :edge], state, after[:, :edge]], axis=1)
    c0 = jnp.concatenate([before[:, edge:], coming, after[:, edge:]], axis=1)
    x1 = lax.ppermute(x0, "lon", swap("lon", 1))
    x2 = jnp.concatenate([before_y, state_y, after_y], axis=1)
    place, basis = tap_tables(
        basis_values, lat_step, lon_step, lat_rows, lon_cols, blocks, lat_index, lon_index, lat_total
    )
    first, second = window_plan(lat_rows)
    nf, ns = len(first), len(second)
    band = BAND * lon_cols
    cells = blocks * band
    win = 16 * lon_cols
    vmem = pl.BlockSpec(memory_space=pltpu.VMEM)
    smem = pl.BlockSpec(memory_space=pltpu.SMEM)
    half_type, full_type = jnp.bfloat16, jnp.float32
    shape = jax.ShapeDtypeStruct
    x_len = own + 2 * edge

    def call(body, name, outs, ins, mib, gflops, scratch=(), aliases={}):
        return pl.pallas_call(
            body,
            out_shape=outs,
            in_specs=[smem if a.ndim == 1 else vmem for a in ins],
            out_specs=(vmem,) * len(outs),
            scratch_shapes=list(scratch),
            input_output_aliases=aliases,
            compiler_params=pltpu.CompilerParams(vmem_limit_bytes=mib * 1024 * 1024),
            cost_estimate=pl.CostEstimate(flops=int(gflops * 1e9), bytes_accessed=4_000_000, transcendentals=0),
            name=name,
        )(*ins)

    forward, backward = call(
        functools.partial(map_kernel, nf, cells, blocks * win),
        "maps",
        (shape((nf + ns, BASIS * cells, blocks * win), half_type), shape((ns, blocks * win, BASIS * cells), half_type)),
        (place, basis),
        6,
        4.0,
    )
    x2, forward, backward = lax.optimization_barrier((x2, forward, backward))
    x3 = lax.ppermute(x2, "lon", swap("lon", 1))
    c2 = lax.ppermute(c0, "lon", swap("lon", 2))
    c1 = lax.ppermute(c0, "lon", swap("lon", 1))
    x3, c2 = lax.optimization_barrier((x3, c2))
    c3 = lax.ppermute(c2, "lon", swap("lon", 1))
    spread, early, chain, finish = make_steps(lat_rows, lon_cols, blocks, members, channels, lat_devices)
    idx = jnp.stack([segment_index, lon_index, lat_index]).astype(jnp.int32)
    share = width // blocks // lat_devices
    lines = (share * channels // 128, 128)
    blocks_type = (members, blocks, x_len, channels)
    s1_type, slope_type, mid_type = (
        shape((members * ns * cells, width), half_type),
        shape(blocks_type, full_type),
        shape(blocks_type, half_type),
    )
    (s0,) = call(
        spread, "spread", (shape((members * nf * cells, width), half_type),), (x0, x1, x2, x3, forward), 8, 1.5
    )
    near_half, s0 = lax.optimization_barrier((near_half, s0))
    far_half = lax.ppermute(near_half, "lon", swap("lon", 1))
    s1, slope, mid = call(
        early, "early", (s1_type, slope_type, mid_type), (idx, x0, x1, x2, x3, kernel, forward, s0), 12, 3.0
    )
    _, _, _, out, follow, gates, mine, *parts = call(
        chain,
        "chain",
        (
            s1_type,
            slope_type,
            mid_type,
            shape((members, own, channels), half_type),
            shape((members, own, channels), half_type),
            shape((members * ns * cells, channels), half_type),
            shape(lines, full_type),
        )
        + (shape(lines, half_type),) * 3,
        (idx, x0, x1, x2, x3, c0, c1, c2, c3, kernel, near_half, far_half, forward, backward, s0, s1, slope, mid),
        20,
        6.0,
        (
            pltpu.VMEM((width, channels), half_type),
            pltpu.VMEM((members * ns * cells, channels), half_type),
            pltpu.VMEM((members * ns * cells * BASIS, channels), half_type),
            pltpu.VMEM(blocks_type, full_type),
            pltpu.VMEM((width // blocks * channels // 128, 128), full_type),
        ),
        {15: 0, 16: 1, 17: 2},
    )
    got = [lax.ppermute(part, "lat", swap("lat", bit)) for bit, part in zip((1, 2, 3), parts)]
    grad, out = call(
        finish,
        "finish",
        (shape((members, own, channels), half_type),) * 2,
        (kernel, backward, gates, follow, out),
        12,
        2.0,
        (
            pltpu.VMEM((members * ns * cells * BASIS, channels), half_type),
            pltpu.VMEM((members, x_len, channels), full_type),
        ),
    )
    total = mine
    for part in got:
        total = total + part.astype(full_type)
    weight_grad = (total * grad_scale).reshape(1, share * channels)
    return (out.reshape((1,) + inputs.shape), grad.reshape((1,) + inputs.shape), weight_grad)


def fits_ring(mesh, inputs):
    sizes = dict(mesh.shape)
    rows, cols = inputs.shape[1] // sizes["lat"], inputs.shape[2] // sizes["lon"]
    return sizes["segment"] == 2 and sizes["lon"] == 4 and sizes["lat"] == 4 and rows == 16 and cols == 4


def solution(mesh):
    def apply(*args):
        body = whole_ring if fits_ring(mesh, args[0]) else per_device
        return jax.shard_map(
            body,
            mesh=mesh,
            in_specs=(
                P(None, "lat", "lon", None),
                P(None, "lat", "lon", None),
                P("segment", None, None, None),
                P(),
                P(),
                P(),
            ),
            out_specs=(
                P("segment", None, "lat", "lon", None),
                P("segment", None, "lat", "lon", None),
                P("segment", ("lon", "lat")),
            ),
            check_vma=False,
        )(*args)

    return apply
```

```python
import functools
import math

import jax
import jax.numpy as jnp
from jax import lax
from jax.experimental import pallas as pl
from jax.experimental.pallas import tpu as pltpu
from jax.sharding import PartitionSpec as P

BASIS = 3
TAPS = 9
REACH = 2


def with_halo(array, sides, width):
    for axis, dim in sides:
        size, length = (lax.axis_size(axis), array.shape[dim])
        up = [(i, (i + 1) % size) for i in range(size)]
        down = [(j, i) for i, j in up]
        last = lax.slice_in_dim(array, length - width, length, axis=dim)
        first = lax.slice_in_dim(array, 0, width, axis=dim)
        before = lax.ppermute(last, axis, up)
        after = lax.ppermute(first, axis, down)
        array = jnp.concatenate([before, array, after], axis=dim)
    return array


def shifted(block, axis, distance):
    devices = range(lax.axis_size(axis))
    route = [(i - distance, i) for i in devices if i - distance in devices]
    return lax.ppermute(block, axis, route)


def widen(features):
    return with_halo(features, (("lon", 2), ("lat", 1)), REACH)


def pass_ahead(result):
    return shifted(result, "segment", 1)


def pass_behind(result):
    return shifted(result, "segment", -1)


def build_tables(basis_values, lat_step, lon_step, lat_rows, lon_cols, lat_index, lat_total):
    pad_rows = lat_rows + 2 * REACH
    pad_cols = lon_cols + 2 * REACH
    lat_padded = jnp.pad(lat_step, ((REACH, REACH), (0, 0)))
    lon_padded = jnp.pad(lon_step, ((REACH, REACH), (0, 0)))
    basis_padded = jnp.pad(basis_values, ((REACH, REACH), (0, 0), (0, 0)))
    row_start = lat_index * lat_rows
    lat_near = lax.dynamic_slice_in_dim(lat_padded, row_start, pad_rows, 0)
    lon_near = lax.dynamic_slice_in_dim(lon_padded, row_start, pad_rows, 0)
    basis_near = lax.dynamic_slice_in_dim(basis_padded, row_start, pad_rows, 0)
    lat_own = lat_near[REACH : REACH + lat_rows]
    lon_own = lon_near[REACH : REACH + lat_rows]
    basis_own = basis_near[REACH : REACH + lat_rows]
    own_rows = row_start + jnp.arange(lat_rows)
    inside = (own_rows[:, None] + lat_own >= 0) & (own_rows[:, None] + lat_own < lat_total)
    row_grid = jnp.arange(lat_rows)[:, None, None]
    col_grid = jnp.arange(lon_cols)[None, :, None]
    source = (row_grid + REACH + lat_own[:, None, :]) * pad_cols + (
        col_grid + REACH + lon_own[:, None, :]
    )
    tap_weight = jnp.where(inside[:, None, :, None], basis_own[:, None, :, :], 0.0)
    tap_weight = jnp.broadcast_to(tap_weight, (lat_rows, lon_cols, TAPS, BASIS))
    picker = (source[..., None] == jnp.arange(pad_rows * pad_cols)).astype(jnp.float32)
    forward_map = jnp.einsum("ijkb,ijks->bijs", tap_weight, picker, precision=lax.Precision.HIGHEST)
    forward_map = forward_map.reshape(BASIS, lat_rows * lon_cols, pad_rows * pad_cols)
    near_rows = row_start - REACH + jnp.arange(pad_rows)
    real_row = (near_rows >= 0) & (near_rows < lat_total)
    pad_row_grid = jnp.arange(pad_rows)[:, None, None]
    pad_col_grid = jnp.arange(pad_cols)[None, :, None]
    target_row = pad_row_grid - REACH + lat_near[:, None, :]
    target_col = pad_col_grid - REACH + lon_near[:, None, :]
    landed = (
        (target_row >= 0)
        & (target_row < lat_rows)
        & (target_col >= 0)
        & (target_col < lon_cols)
        & real_row[:, None, None]
    )
    target = target_row * lon_cols + target_col
    back_weight = jnp.where(landed[..., None], basis_near[:, None, :, :], 0.0)
    catcher = (target[..., None] == jnp.arange(lat_rows * lon_cols)).astype(jnp.float32)
    backward_map = jnp.einsum(
        "pqkb,pqkt->btpq", back_weight, catcher, precision=lax.Precision.HIGHEST
    )
    backward_map = backward_map.reshape(BASIS, lat_rows * lon_cols, pad_rows * pad_cols)
    return (forward_map, backward_map)


def per_device(inputs, cotangent, weights, basis_values, lat_step, lon_step):
    members, lat_rows, lon_cols, channels = inputs.shape
    pad_rows = lat_rows + 2 * REACH
    pad_cols = lon_cols + 2 * REACH
    cells = lat_rows * lon_cols
    lat_index = lax.axis_index("lat")
    lat_total = lat_rows * lax.axis_size("lat")
    segment_index = lax.axis_index("segment")
    depth = lax.axis_size("segment")
    grad_scale = 1.0 / math.sqrt(members * lat_total * lon_cols * lax.axis_size("lon"))
    forward_map, backward_map = build_tables(
        basis_values, lat_step, lon_step, lat_rows, lon_cols, lat_index, lat_total
    )
    kernel = weights[0]
    keep_spread = jnp.zeros((BASIS, members, cells, channels), jnp.bfloat16)
    keep_mixed = jnp.zeros((members, cells, channels), jnp.float32)
    keep_gate = jnp.zeros((members, cells, channels), jnp.bfloat16)
    section_out = jnp.zeros(inputs.shape, jnp.bfloat16)
    section_grad = jnp.zeros(inputs.shape, jnp.bfloat16)
    carry = inputs
    for tick_num in range(depth):
        layer_count = carry.shape[0]
        layer_padded = (
            widen(carry).reshape(layer_count, pad_rows * pad_cols, channels).astype(jnp.float32)
        )
        spread = jnp.einsum(
            "bts,msc->bmtc", forward_map, layer_padded, precision=lax.Precision.HIGHEST
        ).astype(jnp.bfloat16)
        layer_mixed = jnp.einsum(
            "bmtc,bcd->mtd", spread, kernel, preferred_element_type=jnp.float32
        )
        result = (
            carry.reshape(layer_count, cells, channels).astype(jnp.float32)
            + jax.nn.silu(layer_mixed)
        ).astype(jnp.bfloat16)
        spread, mixed, result = (spread, layer_mixed, result.reshape(carry.shape))
        here = segment_index == tick_num
        keep_spread = jnp.where(here, spread, keep_spread)
        keep_mixed = jnp.where(here, mixed, keep_mixed)
        section_out = jnp.where(here, result, section_out)
        if tick_num + 1 < depth:
            carry = pass_ahead(result)
    grad = cotangent
    for tick_num in range(depth):
        count = grad.shape[0]
        flat_grad = grad.reshape(count, cells, channels).astype(jnp.float32)
        sigma = jax.nn.sigmoid(keep_mixed)
        gate_grad = (flat_grad * sigma * (1.0 + keep_mixed * (1.0 - sigma))).astype(jnp.bfloat16)
        feature_grad = jnp.einsum(
            "mtd,bcd->bmtc", gate_grad, kernel, preferred_element_type=jnp.float32
        ).astype(jnp.bfloat16)
        padded = widen(feature_grad.reshape(BASIS * count, lat_rows, lon_cols, channels))
        padded = padded.reshape(BASIS, count, pad_rows * pad_cols, channels).astype(jnp.float32)
        pulled = jnp.einsum("bts,bmsc->mtc", backward_map, padded, precision=lax.Precision.HIGHEST)
        new_grad = (flat_grad + pulled).astype(jnp.bfloat16).reshape(grad.shape)
        gate_grad, new_grad = (gate_grad, new_grad)
        here = segment_index == depth - 1 - tick_num
        keep_gate = jnp.where(here, gate_grad, keep_gate)
        section_grad = jnp.where(here, new_grad, section_grad)
        if tick_num + 1 < depth:
            grad = pass_behind(new_grad)
    local_grad = (
        jnp.einsum("bmtc,mtd->bcd", keep_spread, keep_gate, preferred_element_type=jnp.float32)
        * grad_scale
    )
    owners = lax.axis_size("lon") * lax.axis_size("lat")
    grad_rows = local_grad.reshape(owners, -1)
    weight_grad = lax.psum_scatter(grad_rows, ("lon", "lat"), scatter_dimension=0, tiled=True)
    return (section_out[None], section_grad[None], weight_grad)


HALO = 8
BAND = 8


def swap(axis, bit):
    return [(i, i ^ bit) for i in range(lax.axis_size(axis))]


def window_plan(lat_rows):
    first = [(a, min(max(a - 4, -HALO), lat_rows + HALO - 16)) for a in range(-HALO, lat_rows + HALO, BAND)]
    second = [(a, a - 4) for a in range(-4, lat_rows + 4, BAND)]
    return first, second


def dot(a, b):
    return jnp.dot(a, b, preferred_element_type=jnp.float32)


def dot_nt(a, b):
    return lax.dot_general(a, b, (((1,), (1,)), ((), ())), preferred_element_type=jnp.float32)


def dot_tn(a, b):
    return lax.dot_general(a, b, (((0,), (0,)), ((), ())), preferred_element_type=jnp.float32)


def make_steps(lat_rows, lon_cols, blocks, members, channels, lat_devices):
    first, second = window_plan(lat_rows)
    nf, ns = len(first), len(second)
    lat_total = lat_rows * lat_devices
    ring = lon_cols * blocks
    band = BAND * lon_cols
    cells = blocks * band
    win = 16 * lon_cols
    own = lat_rows * lon_cols
    edge = HALO * lon_cols
    half_edge = edge // 2
    width = BASIS * channels
    lanes = 128
    pieces = channels // lanes
    halo = edge + half_edge
    state_parts = ((0, edge, 2 * own), (edge, own, 0), (edge + own, edge, 2 * own + halo))
    coming_parts = (
        (0, half_edge, 2 * own + edge),
        (half_edge, own, own),
        (half_edge + own, half_edge, 2 * own + halo + edge),
    )

    def take(blks, m, parts, low, high):
        found = []
        for r in blks:
            for start, size, at in parts:
                lo, hi = max(low, start), min(high, start + size)
                if lo < hi:
                    found.append(r[m, at + lo - start : at + hi - start, :])
        return jnp.concatenate(found, axis=0)

    def prep(idx, x, c, w, both, tail, head, half, sem):
        rows = half.shape[0]
        start = pl.multiple_of(idx[1] % 2 * rows, rows)
        copy = pltpu.make_async_copy(w.at[pl.ds(start, rows), :], half, sem)
        copy.start()
        for m in range(members):
            state = x[m].reshape(own, channels)
            coming = c[m].reshape(own, channels)
            both[m, :own, :] = state
            both[m, own:, :] = coming
            tail[m, :edge, :] = state[own - edge :]
            tail[m, edge:, :] = coming[own - half_edge :]
            head[m, :edge, :] = state[:edge]
            head[m, edge:, :] = coming[:half_edge]
        copy.wait()

    def maps(idx, lat_step, lon_step, basis, forward, again, backward, tab):
        lon, lat = idx[1], idx[2]
        base = lat * lat_rows
        tab[...] = jnp.zeros(tab.shape, jnp.float32)
        tab[0:TAPS, :] = lat_step[...].astype(jnp.float32)
        tab[TAPS : 2 * TAPS, :] = lon_step[...].astype(jnp.float32)
        for k in range(TAPS):
            tab[2 * TAPS + k * BASIS : 2 * TAPS + (k + 1) * BASIS, :] = basis[k]
        table = tab[...].astype(jnp.bfloat16)
        source = lax.broadcasted_iota(jnp.int32, (tab.shape[1], cells), 0)
        lane = lax.broadcasted_iota(jnp.int32, (1, cells), 1)
        block, rest = lane // band, lane % band
        row_in, col_in = rest // lon_cols, rest % lon_cols
        column_home = (block ^ lon) * lon_cols + col_in
        piece = 64
        spot = lax.broadcasted_iota(jnp.int32, (piece, cells), 0)
        for i, (a, start) in enumerate(first + second):
            row = row_in + (base + a)
            got = dot(table, (source == row).astype(jnp.bfloat16))
            step_lat = got[0:TAPS].astype(jnp.int32)
            step_lon = got[TAPS : 2 * TAPS].astype(jnp.int32)
            target = row + step_lat
            inside = (row >= 0) & (row < lat_total) & (target >= 0) & (target < lat_total)
            column = column_home + step_lon
            column = jnp.where(column < 0, column + ring, column)
            column = jnp.where(column >= ring, column - ring, column)
            local = target - (base + start)
            place = ((column // lon_cols) ^ lon) * win + local * lon_cols + column % lon_cols
            place = jnp.where(inside, place, -1)
            for p in range(0, blocks * win, piece):
                tables = [jnp.zeros((piece, cells), jnp.float32) for _ in range(BASIS)]
                for k in range(TAPS):
                    hit = spot == place[k : k + 1] - p
                    for b in range(BASIS):
                        at = 2 * TAPS + k * BASIS + b
                        tables[b] = tables[b] + jnp.where(hit, got[at : at + 1], 0.0)
                for b in range(BASIS):
                    span = slice(b * cells, (b + 1) * cells)
                    if i < nf:
                        forward[i, span, p : p + piece] = tables[b].T.astype(jnp.bfloat16)
                    else:
                        again[i - nf, span, p : p + piece] = tables[b].T.astype(jnp.bfloat16)
                        backward[i - nf, p : p + piece, span] = tables[b].astype(jnp.bfloat16)

    def put_spread(got, into, at):
        for b in range(BASIS):
            into[at : at + cells, b * channels : (b + 1) * channels] = got[b * cells : (b + 1) * cells]

    def spread(blk, forward, into):
        for m in range(members):
            for g, (a, start) in enumerate(first):
                o = (start + HALO) * lon_cols
                near = take(blk, m, state_parts, o, o + win)
                put_spread(dot(forward[g], near).astype(jnp.bfloat16), into, (m * nf + g) * cells)

    def first_section(blk, w, s0, s1, again, mid, slope):
        for m in range(members):
            total = dot(s0[m * nf * cells : (m + 1) * nf * cells, :], w[...])
            for g in range(nf):
                mixed = total[g * cells : (g + 1) * cells]
                sigma = jax.nn.sigmoid(mixed)
                here = take(blk, m, state_parts, g * band, (g + 1) * band)
                value = (here.astype(jnp.float32) + mixed * sigma).astype(jnp.bfloat16)
                mid[m, :, g * band : (g + 1) * band, :] = value.reshape(blocks, band, channels)
                if slope is not None:
                    tilt = (sigma * (1.0 + mixed * (1.0 - sigma))).astype(slope.dtype).reshape(blocks, band, channels)
                    low, high = max(g * band, half_edge), min((g + 1) * band, 3 * half_edge + own)
                    slope[m, :, low - half_edge : high - half_edge, :] = tilt[:, low - g * band : high - g * band]
            for g in range(ns):
                near = mid[m, :, g * band : g * band + win, :].reshape(blocks * win, channels)
                put_spread(dot(again[g], near).astype(jnp.bfloat16), s1, (m * ns + g) * cells)

    def columns_of(lon):
        return pl.ds(pl.multiple_of(lon * (width // blocks), 128), width // blocks)

    def early(idx, b0, b1, b2, b3, w_own, forward, again, s, left, slope, out, s0, mid):
        blk = (b0, b1, b2, b3)

        @pl.when(idx[0] == 0)
        def _():
            spread(blk, forward, s0)
            first_section(blk, w_own, s0, s, again, mid, slope)
            for m in range(members):
                size = (nf - 2) * cells
                left[m * size : (m + 1) * size, :] = s0[(m * nf + 1) * cells : (m * nf + nf - 1) * cells, columns_of(idx[1])]
                out[m, :, :] = mid[m, 0, edge : edge + own, :]

        @pl.when(idx[0] == 1)
        def _():
            spread(blk, forward, s)

    def own_part(g):
        return max(g * band, half_edge), min((g + 1) * band, half_edge + own)

    def apply_back(w, gates, feat):
        for b in range(BASIS):
            got = dot_nt(gates[...], w[b * channels : (b + 1) * channels, :]).astype(jnp.bfloat16)
            for i in range(members * ns):
                feat[(i * BASIS + b) * cells : (i * BASIS + b + 1) * cells, :] = got[i * cells : (i + 1) * cells]

    def chain(idx, b0, b1, b2, b3, w_own, w_a, w_b, again, backward, s, left0, slope, early_out,
              out_ref, next_ref, gate_ref, own_ref, p1, p2, p3, w, s1, mid, gates, feat, pull, grads):
        blk = (b0, b1, b2, b3)
        seg, lon, lat = idx[0], idx[1], idx[2]
        half = w_a.shape[0]
        core = lon % 2
        w[pl.ds(pl.multiple_of(core * half, half), half), :] = w_a[...]
        w[pl.ds(pl.multiple_of((1 - core) * half, half), half), :] = w_b[...]

        def coming_at(m, g):
            return take(blk, m, coming_parts, g * band, (g + 1) * band).astype(jnp.float32)

        def second_section(weight, spread_ref, into, last):
            for m in range(members):
                total = dot(spread_ref[m * ns * cells : (m + 1) * ns * cells, :], weight[...])
                for g in range(ns):
                    at = (m * ns + g) * cells
                    mixed = total[g * cells : (g + 1) * cells]
                    sigma = jax.nn.sigmoid(mixed)
                    into[at : at + cells, :] = (coming_at(m, g) * sigma * (1.0 + mixed * (1.0 - sigma))).astype(jnp.bfloat16)
                    if last:
                        low, high = own_part(g)
                        base = mid[m, 0, half_edge + low : half_edge + high, :]
                        local = slice(low - g * band, high - g * band)
                        base = (base.astype(jnp.float32) + mixed[local] * sigma[local]).astype(jnp.bfloat16)
                        out_ref[m, low - half_edge : high - half_edge, :] = base

        def store_grads(left, right):
            got = dot_tn(left, jnp.concatenate(right, axis=0))
            for c in range(pieces):
                grads[pl.ds(c, width // blocks, stride=pieces), :] = got[:, c * lanes : (c + 1) * lanes]

        @pl.when(seg == 0)
        def _():
            second_section(w, s, gates, False)
            out_ref[...] = early_out[...]
            apply_back(w, gates, feat)
            for m in range(members):
                for g in range(ns):
                    at = (m * ns + g) * cells * BASIS
                    got = dot(backward[g], feat[at : at + BASIS * cells, :]).reshape(blocks, win, channels)
                    if g == 0:
                        pull[m, :, :win, :] = got
                    else:
                        pull[m, :, g * band : (g + 1) * band, :] += got[:, :band]
                        pull[m, :, (g + 1) * band : g * band + win, :] = got[:, band:]
            right = []
            step = half_edge
            for m in range(members):
                for g in range(ns):
                    at = (m * ns + g) * cells
                    span = slice(half_edge + g * band, half_edge + (g + 1) * band)
                    value = (coming_at(m, g) + pull[m, :, span, :].reshape(cells, channels)).astype(jnp.bfloat16)
                    low, high = own_part(g)
                    next_ref[m, low - half_edge : high - half_edge, :] = value[low - g * band : high - g * band]
                    tilt = slope[m, :, g * band : (g + 1) * band, :].reshape(cells, channels)
                    gate_ref[at : at + cells, :] = (value.astype(jnp.float32) * tilt).astype(jnp.bfloat16)
                for g in range(1, nf - 1):
                    for q in range(blocks):
                        for o in range(0, band, step):
                            spot = half_edge + (g - 1) * band + o
                            turn, rest = spot // band, spot % band
                            at = (m * ns + turn) * cells + q * band + rest
                            right.append(gate_ref[at : at + step, :])
            store_grads(left0[...], right)

        @pl.when(seg == 1)
        def _():
            first_section(blk, w, s, s1, again, mid, None)
            second_section(w_own, s1, gate_ref, True)
            left, right = [], []
            for m in range(members):
                next_ref[m, :, :] = b0[m, own : 2 * own, :]
                for g in range(ns):
                    low, high = own_part(g)
                    for q in range(blocks):
                        at = (m * ns + g) * cells + q * band - g * band
                        left.append(s1[at + low : at + high, columns_of(lon)])
                        right.append(gate_ref[at + low : at + high, :])
            store_grads(jnp.concatenate(left, axis=0), right)

        share = width // blocks // lat_devices * pieces

        def rows_of(index):
            return grads[pl.ds(pl.multiple_of(index * share, share), share), :]

        own_ref[...] = rows_of(lat)
        for bit, ref in ((1, p1), (2, p2), (3, p3)):
            ref[...] = rows_of(lat ^ bit).astype(jnp.bfloat16)

    def finish(w_own, backward, gates, next_ref, last_ref, grad_ref, out_ref, feat, pull):
        apply_back(w_own, gates, feat)
        for m in range(members):
            for g in range(ns):
                at = (m * ns + g) * cells * BASIS
                got = dot(backward[g, 0:win, :], feat[at : at + BASIS * cells, :])
                if g == 0:
                    pull[m, :win, :] = got
                else:
                    pull[m, g * band : (g + 1) * band, :] += got[:band]
                    pull[m, (g + 1) * band : g * band + win, :] = got[band:]
            total = next_ref[m].astype(jnp.float32) + pull[m, edge : edge + own, :]
            grad_ref[m] = total.astype(jnp.bfloat16).reshape(lat_rows, lon_cols, channels)
            out_ref[m] = last_ref[m].reshape(lat_rows, lon_cols, channels)

    return prep, maps, early, chain, finish


def add_up(scale, mine, p1, p2, p3, out):
    out[...] = (mine[...] + p1[...].astype(jnp.float32) + p2[...].astype(jnp.float32) + p3[...].astype(jnp.float32)) * scale


def whole_ring(inputs, cotangent, weights, basis_values, lat_step, lon_step):
    members, lat_rows, lon_cols, channels = inputs.shape
    blocks = lax.axis_size("lon")
    lat_devices = lax.axis_size("lat")
    lat_total = lat_rows * lat_devices
    grad_scale = 1.0 / math.sqrt(members * lat_total * lon_cols * blocks)
    own = lat_rows * lon_cols
    edge = HALO * lon_cols
    half_edge = edge // 2
    halo = edge + half_edge
    width = BASIS * channels
    half_type, full_type = jnp.bfloat16, jnp.float32
    shape = jax.ShapeDtypeStruct
    first, second = window_plan(lat_rows)
    nf, ns = len(first), len(second)
    cells = blocks * BAND * lon_cols
    win = 16 * lon_cols
    vmem = pl.BlockSpec(memory_space=pltpu.VMEM)
    smem = pl.BlockSpec(memory_space=pltpu.SMEM)
    anywhere = pl.BlockSpec(memory_space=pltpu.HBM)

    def call(body, name, outs, ins, mib, gflops, scratch=(), far=()):
        return pl.pallas_call(
            body,
            out_shape=outs,
            in_specs=[smem if a.ndim == 1 else anywhere if i in far else vmem for i, a in enumerate(ins)],
            out_specs=(vmem,) * len(outs),
            scratch_shapes=list(scratch),
            compiler_params=pltpu.CompilerParams(vmem_limit_bytes=mib * 1024 * 1024),
            cost_estimate=pl.CostEstimate(flops=int(gflops * 1e9), bytes_accessed=4_000_000, transcendentals=0),
            name=name,
        )(*ins)

    prep, maps, early, chain, finish = make_steps(lat_rows, lon_cols, blocks, members, channels, lat_devices)
    idx = jnp.stack([lax.axis_index("segment"), lax.axis_index("lon"), lax.axis_index("lat")]).astype(jnp.int32)
    kernel = weights.reshape(width, channels)
    both, tail, head, half = call(
        prep,
        "prep",
        (
            shape((members, 2 * own, channels), half_type),
            shape((members, halo, channels), half_type),
            shape((members, halo, channels), half_type),
            shape((width // 2, channels), half_type),
        ),
        (idx, inputs, cotangent, kernel),
        4,
        0.5,
        (pltpu.SemaphoreType.DMA,),
        (3,),
    )
    up = [(i, i + 1) for i in range(lat_devices - 1)]
    down = [(i + 1, i) for i in range(lat_devices - 1)]
    near_half = lax.ppermute(half, "segment", swap("segment", 1))
    both_y = lax.ppermute(both, "lon", swap("lon", 2))
    before = lax.ppermute(tail, "lat", up)
    after = lax.ppermute(head, "lat", down)
    sides = jnp.concatenate([before, after], axis=1)
    sides_y = lax.ppermute(sides, "lon", swap("lon", 2))
    b0 = jnp.concatenate([both, sides], axis=1)
    b1 = lax.ppermute(b0, "lon", swap("lon", 1))
    forward, again, backward = call(
        maps,
        "maps",
        (
            shape((nf, BASIS * cells, blocks * win), half_type),
            shape((ns, BASIS * cells, blocks * win), half_type),
            shape((ns, blocks * win, BASIS * cells), half_type),
        ),
        (idx, lat_step.T, lon_step.T, jnp.transpose(basis_values, (1, 2, 0))),
        4,
        3.0,
        (pltpu.VMEM((48, lat_total), full_type),),
    )
    b2 = jnp.concatenate([both_y, sides_y], axis=1)
    b2, forward = lax.optimization_barrier((b2, forward))
    b3 = lax.ppermute(b2, "lon", swap("lon", 1))
    far_half = lax.ppermute(near_half, "lon", swap("lon", 1))
    s_type = (members * nf * cells, width)
    s, left, slope, early_out = call(
        early,
        "early",
        (
            shape(s_type, half_type),
            shape((members * (nf - 2) * cells, width // blocks), half_type),
            shape((members, blocks, own + edge, channels), half_type),
            shape((members, own, channels), half_type),
        ),
        (idx, b0, b1, b2, b3, kernel, forward, again),
        12,
        3.0,
        (pltpu.VMEM(s_type, half_type), pltpu.VMEM((members, blocks, own + 2 * edge, channels), half_type)),
    )
    lines = (width // blocks // lat_devices * channels // 128, 128)
    out, follow, gates, mine, *parts = call(
        chain,
        "chain",
        (
            shape((members, own, channels), half_type),
            shape((members, own, channels), half_type),
            shape((members * ns * cells, channels), half_type),
            shape(lines, full_type),
        )
        + (shape(lines, half_type),) * 3,
        (idx, b0, b1, b2, b3, kernel, near_half, far_half, again, backward, s, left, slope, early_out),
        18,
        6.0,
        (
            pltpu.VMEM((width, channels), half_type),
            pltpu.VMEM((members * ns * cells, width), half_type),
            pltpu.VMEM((members, blocks, own + 2 * edge, channels), half_type),
            pltpu.VMEM((members * ns * cells, channels), half_type),
            pltpu.VMEM((members * ns * cells * BASIS, channels), half_type),
            pltpu.VMEM((members, blocks, own + 2 * edge, channels), full_type),
            pltpu.VMEM((width // blocks * channels // 128, 128), full_type),
        ),
    )
    got = [lax.ppermute(part, "lat", swap("lat", bit)) for bit, part in zip((1, 2, 3), parts)]
    block = (members, lat_rows, lon_cols, channels)
    grad, out = call(
        finish,
        "finish",
        (shape(block, half_type),) * 2,
        (kernel, backward, gates, follow, out),
        10,
        2.0,
        (
            pltpu.VMEM((members * ns * cells * BASIS, channels), half_type),
            pltpu.VMEM((members, own + 2 * edge, channels), full_type),
        ),
    )
    (total,) = call(functools.partial(add_up, grad_scale), "add_up", (shape(lines, full_type),), (mine, *got), 2, 0.1)
    return (out[None], grad[None], total.reshape(1, lines[0] * lines[1]))


def fits_ring(mesh, inputs):
    sizes = dict(mesh.shape)
    rows, cols = inputs.shape[1] // sizes["lat"], inputs.shape[2] // sizes["lon"]
    return sizes["segment"] == 2 and sizes["lon"] == 4 and sizes["lat"] == 4 and rows == 16 and cols == 4


def solution(mesh):
    def apply(*args):
        body = whole_ring if fits_ring(mesh, args[0]) else per_device
        return jax.shard_map(
            body,
            mesh=mesh,
            in_specs=(
                P(None, "lat", "lon", None),
                P(None, "lat", "lon", None),
                P("segment", None, None, None),
                P(),
                P(),
                P(),
            ),
            out_specs=(
                P("segment", None, "lat", "lon", None),
                P("segment", None, "lat", "lon", None),
                P("segment", ("lon", "lat")),
            ),
            check_vma=False,
        )(*args)

    return apply
```

```python
import functools
import math

import jax
import jax.numpy as jnp
from jax import lax
from jax.experimental import pallas as pl
from jax.experimental.pallas import tpu as pltpu
from jax.sharding import PartitionSpec as P

BASIS = 3
TAPS = 9
REACH = 2


def with_halo(array, sides, width):
    for axis, dim in sides:
        size, length = (lax.axis_size(axis), array.shape[dim])
        up = [(i, (i + 1) % size) for i in range(size)]
        down = [(j, i) for i, j in up]
        last = lax.slice_in_dim(array, length - width, length, axis=dim)
        first = lax.slice_in_dim(array, 0, width, axis=dim)
        before = lax.ppermute(last, axis, up)
        after = lax.ppermute(first, axis, down)
        array = jnp.concatenate([before, array, after], axis=dim)
    return array


def shifted(block, axis, distance):
    devices = range(lax.axis_size(axis))
    route = [(i - distance, i) for i in devices if i - distance in devices]
    return lax.ppermute(block, axis, route)


def widen(features):
    return with_halo(features, (("lon", 2), ("lat", 1)), REACH)


def pass_ahead(result):
    return shifted(result, "segment", 1)


def pass_behind(result):
    return shifted(result, "segment", -1)


def build_tables(basis_values, lat_step, lon_step, lat_rows, lon_cols, lat_index, lat_total):
    pad_rows = lat_rows + 2 * REACH
    pad_cols = lon_cols + 2 * REACH
    lat_padded = jnp.pad(lat_step, ((REACH, REACH), (0, 0)))
    lon_padded = jnp.pad(lon_step, ((REACH, REACH), (0, 0)))
    basis_padded = jnp.pad(basis_values, ((REACH, REACH), (0, 0), (0, 0)))
    row_start = lat_index * lat_rows
    lat_near = lax.dynamic_slice_in_dim(lat_padded, row_start, pad_rows, 0)
    lon_near = lax.dynamic_slice_in_dim(lon_padded, row_start, pad_rows, 0)
    basis_near = lax.dynamic_slice_in_dim(basis_padded, row_start, pad_rows, 0)
    lat_own = lat_near[REACH : REACH + lat_rows]
    lon_own = lon_near[REACH : REACH + lat_rows]
    basis_own = basis_near[REACH : REACH + lat_rows]
    own_rows = row_start + jnp.arange(lat_rows)
    inside = (own_rows[:, None] + lat_own >= 0) & (own_rows[:, None] + lat_own < lat_total)
    row_grid = jnp.arange(lat_rows)[:, None, None]
    col_grid = jnp.arange(lon_cols)[None, :, None]
    source = (row_grid + REACH + lat_own[:, None, :]) * pad_cols + (
        col_grid + REACH + lon_own[:, None, :]
    )
    tap_weight = jnp.where(inside[:, None, :, None], basis_own[:, None, :, :], 0.0)
    tap_weight = jnp.broadcast_to(tap_weight, (lat_rows, lon_cols, TAPS, BASIS))
    picker = (source[..., None] == jnp.arange(pad_rows * pad_cols)).astype(jnp.float32)
    forward_map = jnp.einsum("ijkb,ijks->bijs", tap_weight, picker, precision=lax.Precision.HIGHEST)
    forward_map = forward_map.reshape(BASIS, lat_rows * lon_cols, pad_rows * pad_cols)
    near_rows = row_start - REACH + jnp.arange(pad_rows)
    real_row = (near_rows >= 0) & (near_rows < lat_total)
    pad_row_grid = jnp.arange(pad_rows)[:, None, None]
    pad_col_grid = jnp.arange(pad_cols)[None, :, None]
    target_row = pad_row_grid - REACH + lat_near[:, None, :]
    target_col = pad_col_grid - REACH + lon_near[:, None, :]
    landed = (
        (target_row >= 0)
        & (target_row < lat_rows)
        & (target_col >= 0)
        & (target_col < lon_cols)
        & real_row[:, None, None]
    )
    target = target_row * lon_cols + target_col
    back_weight = jnp.where(landed[..., None], basis_near[:, None, :, :], 0.0)
    catcher = (target[..., None] == jnp.arange(lat_rows * lon_cols)).astype(jnp.float32)
    backward_map = jnp.einsum(
        "pqkb,pqkt->btpq", back_weight, catcher, precision=lax.Precision.HIGHEST
    )
    backward_map = backward_map.reshape(BASIS, lat_rows * lon_cols, pad_rows * pad_cols)
    return (forward_map, backward_map)


def per_device(inputs, cotangent, weights, basis_values, lat_step, lon_step):
    members, lat_rows, lon_cols, channels = inputs.shape
    pad_rows = lat_rows + 2 * REACH
    pad_cols = lon_cols + 2 * REACH
    cells = lat_rows * lon_cols
    lat_index = lax.axis_index("lat")
    lat_total = lat_rows * lax.axis_size("lat")
    segment_index = lax.axis_index("segment")
    depth = lax.axis_size("segment")
    grad_scale = 1.0 / math.sqrt(members * lat_total * lon_cols * lax.axis_size("lon"))
    forward_map, backward_map = build_tables(
        basis_values, lat_step, lon_step, lat_rows, lon_cols, lat_index, lat_total
    )
    kernel = weights[0]
    keep_spread = jnp.zeros((BASIS, members, cells, channels), jnp.bfloat16)
    keep_mixed = jnp.zeros((members, cells, channels), jnp.float32)
    keep_gate = jnp.zeros((members, cells, channels), jnp.bfloat16)
    section_out = jnp.zeros(inputs.shape, jnp.bfloat16)
    section_grad = jnp.zeros(inputs.shape, jnp.bfloat16)
    carry = inputs
    for tick_num in range(depth):
        layer_count = carry.shape[0]
        layer_padded = (
            widen(carry).reshape(layer_count, pad_rows * pad_cols, channels).astype(jnp.float32)
        )
        spread = jnp.einsum(
            "bts,msc->bmtc", forward_map, layer_padded, precision=lax.Precision.HIGHEST
        ).astype(jnp.bfloat16)
        layer_mixed = jnp.einsum(
            "bmtc,bcd->mtd", spread, kernel, preferred_element_type=jnp.float32
        )
        result = (
            carry.reshape(layer_count, cells, channels).astype(jnp.float32)
            + jax.nn.silu(layer_mixed)
        ).astype(jnp.bfloat16)
        spread, mixed, result = (spread, layer_mixed, result.reshape(carry.shape))
        here = segment_index == tick_num
        keep_spread = jnp.where(here, spread, keep_spread)
        keep_mixed = jnp.where(here, mixed, keep_mixed)
        section_out = jnp.where(here, result, section_out)
        if tick_num + 1 < depth:
            carry = pass_ahead(result)
    grad = cotangent
    for tick_num in range(depth):
        count = grad.shape[0]
        flat_grad = grad.reshape(count, cells, channels).astype(jnp.float32)
        sigma = jax.nn.sigmoid(keep_mixed)
        gate_grad = (flat_grad * sigma * (1.0 + keep_mixed * (1.0 - sigma))).astype(jnp.bfloat16)
        feature_grad = jnp.einsum(
            "mtd,bcd->bmtc", gate_grad, kernel, preferred_element_type=jnp.float32
        ).astype(jnp.bfloat16)
        padded = widen(feature_grad.reshape(BASIS * count, lat_rows, lon_cols, channels))
        padded = padded.reshape(BASIS, count, pad_rows * pad_cols, channels).astype(jnp.float32)
        pulled = jnp.einsum("bts,bmsc->mtc", backward_map, padded, precision=lax.Precision.HIGHEST)
        new_grad = (flat_grad + pulled).astype(jnp.bfloat16).reshape(grad.shape)
        gate_grad, new_grad = (gate_grad, new_grad)
        here = segment_index == depth - 1 - tick_num
        keep_gate = jnp.where(here, gate_grad, keep_gate)
        section_grad = jnp.where(here, new_grad, section_grad)
        if tick_num + 1 < depth:
            grad = pass_behind(new_grad)
    local_grad = (
        jnp.einsum("bmtc,mtd->bcd", keep_spread, keep_gate, preferred_element_type=jnp.float32)
        * grad_scale
    )
    owners = lax.axis_size("lon") * lax.axis_size("lat")
    grad_rows = local_grad.reshape(owners, -1)
    weight_grad = lax.psum_scatter(grad_rows, ("lon", "lat"), scatter_dimension=0, tiled=True)
    return (section_out[None], section_grad[None], weight_grad)


HALO = 8
BAND = 8
PREP_MIB = 59.2


def swap(axis, bit):
    return [(i, i ^ bit) for i in range(lax.axis_size(axis))]


def window_plan(lat_rows):
    first = [(a, min(max(a - 4, -HALO), lat_rows + HALO - 16)) for a in range(-HALO, lat_rows + HALO, BAND)]
    second = [(a, a - 4) for a in range(-4, lat_rows + 4, BAND)]
    return first, second


def dot(a, b):
    return jnp.dot(a, b, preferred_element_type=jnp.float32)


def dot_nt(a, b):
    return lax.dot_general(a, b, (((1,), (1,)), ((), ())), preferred_element_type=jnp.float32)


def dot_tn(a, b):
    return lax.dot_general(a, b, (((0,), (0,)), ((), ())), preferred_element_type=jnp.float32)


def make_steps(lat_rows, lon_cols, blocks, members, channels, lat_devices):
    first, second = window_plan(lat_rows)
    nf, ns = len(first), len(second)
    lat_total = lat_rows * lat_devices
    ring = lon_cols * blocks
    band = BAND * lon_cols
    cells = blocks * band
    win = 16 * lon_cols
    own = lat_rows * lon_cols
    edge = HALO * lon_cols
    half_edge = edge // 2
    width = BASIS * channels
    lanes = 128
    pieces = channels // lanes
    halo = edge + half_edge
    state_parts = ((0, edge, 2 * own), (edge, own, 0), (edge + own, edge, 2 * own + halo))
    coming_parts = (
        (0, half_edge, 2 * own + edge),
        (half_edge, own, own),
        (half_edge + own, half_edge, 2 * own + halo + edge),
    )

    def take(blks, m, parts, low, high):
        found = []
        for r in blks:
            for start, size, at in parts:
                lo, hi = max(low, start), min(high, start + size)
                if lo < hi:
                    found.append(r[m, at + lo - start : at + hi - start, :])
        return jnp.concatenate(found, axis=0)

    def take_half(idx, w, half, sem):
        rows = half.shape[0]
        start = pl.multiple_of(idx[1] % 2 * rows, rows)
        move = pltpu.make_async_copy(w.at[pl.ds(start, rows), :], half, sem)
        move.start()
        move.wait()

    def prep(x_in, c_in, both, tail, head, x, c, sems):
        moves = [pltpu.make_async_copy(x_in, x, sems.at[0]), pltpu.make_async_copy(c_in, c, sems.at[1])]
        for move in moves:
            move.start()
        moves[0].wait()
        moves[1].wait()
        for m in range(members):
            state = x[m].reshape(own, channels)
            coming = c[m].reshape(own, channels)
            both[m, :own, :] = state
            both[m, own:, :] = coming
            tail[m, :edge, :] = state[own - edge :]
            tail[m, edge:, :] = coming[own - half_edge :]
            head[m, :edge, :] = state[:edge]
            head[m, edge:, :] = coming[:half_edge]

    def maps(idx, lat_step, lon_step, basis, forward, again, backward, tab):
        lon, lat = idx[1], idx[2]
        base = lat * lat_rows
        tab[...] = jnp.zeros(tab.shape, jnp.float32)
        tab[0:TAPS, :] = lat_step[...].astype(jnp.float32)
        tab[TAPS : 2 * TAPS, :] = lon_step[...].astype(jnp.float32)
        for k in range(TAPS):
            tab[2 * TAPS + k * BASIS : 2 * TAPS + (k + 1) * BASIS, :] = basis[k]
        table = tab[...].astype(jnp.bfloat16)
        source = lax.broadcasted_iota(jnp.int32, (tab.shape[1], cells), 0)
        lane = lax.broadcasted_iota(jnp.int32, (1, cells), 1)
        block, rest = lane // band, lane % band
        row_in, col_in = rest // lon_cols, rest % lon_cols
        column_home = (block ^ lon) * lon_cols + col_in
        piece = 64
        spot = lax.broadcasted_iota(jnp.int32, (piece, cells), 0)
        for i, (a, start) in enumerate(first + second):
            row = row_in + (base + a)
            got = dot(table, (source == row).astype(jnp.bfloat16))
            step_lat = got[0:TAPS].astype(jnp.int32)
            step_lon = got[TAPS : 2 * TAPS].astype(jnp.int32)
            target = row + step_lat
            inside = (row >= 0) & (row < lat_total) & (target >= 0) & (target < lat_total)
            column = column_home + step_lon
            column = jnp.where(column < 0, column + ring, column)
            column = jnp.where(column >= ring, column - ring, column)
            local = target - (base + start)
            place = ((column // lon_cols) ^ lon) * win + local * lon_cols + column % lon_cols
            place = jnp.where(inside, place, -1)
            for p in range(0, blocks * win, piece):
                tables = [jnp.zeros((piece, cells), jnp.float32) for _ in range(BASIS)]
                for k in range(TAPS):
                    hit = spot == place[k : k + 1] - p
                    for b in range(BASIS):
                        at = 2 * TAPS + k * BASIS + b
                        tables[b] = tables[b] + jnp.where(hit, got[at : at + 1], 0.0)
                for b in range(BASIS):
                    span = slice(b * cells, (b + 1) * cells)
                    if i < nf:
                        forward[i, span, p : p + piece] = tables[b].T.astype(jnp.bfloat16)
                    else:
                        again[i - nf, span, p : p + piece] = tables[b].T.astype(jnp.bfloat16)
                        backward[i - nf, p : p + piece, span] = tables[b].astype(jnp.bfloat16)

    def put_spread(got, into, at):
        for b in range(BASIS):
            into[at : at + cells, b * channels : (b + 1) * channels] = got[b * cells : (b + 1) * cells]

    def spread(blk, forward, into):
        for m in range(members):
            for g, (a, start) in enumerate(first):
                o = (start + HALO) * lon_cols
                near = take(blk, m, state_parts, o, o + win)
                put_spread(dot(forward[g], near).astype(jnp.bfloat16), into, (m * nf + g) * cells)

    def first_section(blk, w, s0, s1, again, mid, slope):
        for m in range(members):
            total = dot(s0[m * nf * cells : (m + 1) * nf * cells, :], w[...])
            for g in range(nf):
                mixed = total[g * cells : (g + 1) * cells]
                sigma = jax.nn.sigmoid(mixed)
                here = take(blk, m, state_parts, g * band, (g + 1) * band)
                value = (here.astype(jnp.float32) + mixed * sigma).astype(jnp.bfloat16)
                mid[m, :, g * band : (g + 1) * band, :] = value.reshape(blocks, band, channels)
                if slope is not None:
                    tilt = (sigma * (1.0 + mixed * (1.0 - sigma))).astype(slope.dtype).reshape(blocks, band, channels)
                    low, high = max(g * band, half_edge), min((g + 1) * band, 3 * half_edge + own)
                    slope[m, :, low - half_edge : high - half_edge, :] = tilt[:, low - g * band : high - g * band]
            for g in range(ns):
                near = mid[m, :, g * band : g * band + win, :].reshape(blocks * win, channels)
                put_spread(dot(again[g], near).astype(jnp.bfloat16), s1, (m * ns + g) * cells)

    def columns_of(lon):
        return pl.ds(pl.multiple_of(lon * (width // blocks), 128), width // blocks)

    def early(idx, b0, b1, b2, b3, w_own, forward, again, s, left, slope, out, s0, mid):
        blk = (b0, b1, b2, b3)

        @pl.when(idx[0] == 0)
        def _():
            spread(blk, forward, s0)
            first_section(blk, w_own, s0, s, again, mid, slope)
            for m in range(members):
                size = (nf - 2) * cells
                left[m * size : (m + 1) * size, :] = s0[(m * nf + 1) * cells : (m * nf + nf - 1) * cells, columns_of(idx[1])]
                out[m, :, :] = mid[m, 0, edge : edge + own, :]

        @pl.when(idx[0] == 1)
        def _():
            spread(blk, forward, s)

    def own_part(g):
        return max(g * band, half_edge), min((g + 1) * band, half_edge + own)

    def apply_back(w, gates, feat):
        for b in range(BASIS):
            got = dot_nt(gates[...], w[b * channels : (b + 1) * channels, :]).astype(jnp.bfloat16)
            for i in range(members * ns):
                feat[(i * BASIS + b) * cells : (i * BASIS + b + 1) * cells, :] = got[i * cells : (i + 1) * cells]

    def chain(idx, b0, b1, b2, b3, w_own, w_a, w_b, again, backward, s, left0, slope, early_out,
              out_ref, next_ref, gate_ref, own_ref, p1, p2, p3, w, s1, mid, gates, feat, pull, grads):
        blk = (b0, b1, b2, b3)
        seg, lon, lat = idx[0], idx[1], idx[2]
        half = w_a.shape[0]
        core = lon % 2
        w[pl.ds(pl.multiple_of(core * half, half), half), :] = w_a[...]
        w[pl.ds(pl.multiple_of((1 - core) * half, half), half), :] = w_b[...]

        def coming_at(m, g):
            return take(blk, m, coming_parts, g * band, (g + 1) * band).astype(jnp.float32)

        def second_section(weight, spread_ref, into, last):
            for m in range(members):
                total = dot(spread_ref[m * ns * cells : (m + 1) * ns * cells, :], weight[...])
                for g in range(ns):
                    at = (m * ns + g) * cells
                    mixed = total[g * cells : (g + 1) * cells]
                    sigma = jax.nn.sigmoid(mixed)
                    into[at : at + cells, :] = (coming_at(m, g) * sigma * (1.0 + mixed * (1.0 - sigma))).astype(jnp.bfloat16)
                    if last:
                        low, high = own_part(g)
                        base = mid[m, 0, half_edge + low : half_edge + high, :]
                        local = slice(low - g * band, high - g * band)
                        base = (base.astype(jnp.float32) + mixed[local] * sigma[local]).astype(jnp.bfloat16)
                        out_ref[m, low - half_edge : high - half_edge, :] = base

        def store_grads(left, right):
            got = dot_tn(left, jnp.concatenate(right, axis=0))
            for c in range(pieces):
                grads[pl.ds(c, width // blocks, stride=pieces), :] = got[:, c * lanes : (c + 1) * lanes]

        @pl.when(seg == 0)
        def _():
            second_section(w, s, gates, False)
            out_ref[...] = early_out[...]
            apply_back(w, gates, feat)
            for m in range(members):
                for g in range(ns):
                    at = (m * ns + g) * cells * BASIS
                    got = dot(backward[g], feat[at : at + BASIS * cells, :]).reshape(blocks, win, channels)
                    if g == 0:
                        pull[m, :, :win, :] = got
                    else:
                        pull[m, :, g * band : (g + 1) * band, :] += got[:, :band]
                        pull[m, :, (g + 1) * band : g * band + win, :] = got[:, band:]
            right = []
            step = half_edge
            for m in range(members):
                for g in range(ns):
                    at = (m * ns + g) * cells
                    span = slice(half_edge + g * band, half_edge + (g + 1) * band)
                    value = (coming_at(m, g) + pull[m, :, span, :].reshape(cells, channels)).astype(jnp.bfloat16)
                    low, high = own_part(g)
                    next_ref[m, low - half_edge : high - half_edge, :] = value[low - g * band : high - g * band]
                    tilt = slope[m, :, g * band : (g + 1) * band, :].reshape(cells, channels)
                    gate_ref[at : at + cells, :] = (value.astype(jnp.float32) * tilt).astype(jnp.bfloat16)
                for g in range(1, nf - 1):
                    for q in range(blocks):
                        for o in range(0, band, step):
                            spot = half_edge + (g - 1) * band + o
                            turn, rest = spot // band, spot % band
                            at = (m * ns + turn) * cells + q * band + rest
                            right.append(gate_ref[at : at + step, :])
            store_grads(left0[...], right)

        @pl.when(seg == 1)
        def _():
            first_section(blk, w, s, s1, again, mid, None)
            second_section(w_own, s1, gate_ref, True)
            left, right = [], []
            for m in range(members):
                next_ref[m, :, :] = b0[m, own : 2 * own, :]
                for g in range(ns):
                    low, high = own_part(g)
                    for q in range(blocks):
                        at = (m * ns + g) * cells + q * band - g * band
                        left.append(s1[at + low : at + high, columns_of(lon)])
                        right.append(gate_ref[at + low : at + high, :])
            store_grads(jnp.concatenate(left, axis=0), right)

        share = width // blocks // lat_devices * pieces

        def rows_of(index):
            return grads[pl.ds(pl.multiple_of(index * share, share), share), :]

        own_ref[...] = rows_of(lat)
        for bit, ref in ((1, p1), (2, p2), (3, p3)):
            ref[...] = rows_of(lat ^ bit).astype(jnp.bfloat16)

    def finish(w_own, backward, gates, next_ref, last_ref, grad_ref, out_ref, feat, pull):
        apply_back(w_own, gates, feat)
        for m in range(members):
            for g in range(ns):
                at = (m * ns + g) * cells * BASIS
                got = dot(backward[g, 0:win, :], feat[at : at + BASIS * cells, :])
                if g == 0:
                    pull[m, :win, :] = got
                else:
                    pull[m, g * band : (g + 1) * band, :] += got[:band]
                    pull[m, (g + 1) * band : g * band + win, :] = got[band:]
            total = next_ref[m].astype(jnp.float32) + pull[m, edge : edge + own, :]
            grad_ref[m] = total.astype(jnp.bfloat16).reshape(lat_rows, lon_cols, channels)
            out_ref[m] = last_ref[m].reshape(lat_rows, lon_cols, channels)

    return take_half, prep, maps, early, chain, finish


def add_up(scale, mine, p1, p2, p3, out):
    out[...] = (mine[...] + p1[...].astype(jnp.float32) + p2[...].astype(jnp.float32) + p3[...].astype(jnp.float32)) * scale


def whole_ring(inputs, cotangent, weights, basis_values, lat_step, lon_step):
    members, lat_rows, lon_cols, channels = inputs.shape
    blocks = lax.axis_size("lon")
    lat_devices = lax.axis_size("lat")
    lat_total = lat_rows * lat_devices
    grad_scale = 1.0 / math.sqrt(members * lat_total * lon_cols * blocks)
    own = lat_rows * lon_cols
    edge = HALO * lon_cols
    half_edge = edge // 2
    halo = edge + half_edge
    width = BASIS * channels
    half_type, full_type = jnp.bfloat16, jnp.float32
    shape = jax.ShapeDtypeStruct
    first, second = window_plan(lat_rows)
    nf, ns = len(first), len(second)
    cells = blocks * BAND * lon_cols
    win = 16 * lon_cols
    vmem = pl.BlockSpec(memory_space=pltpu.VMEM)
    smem = pl.BlockSpec(memory_space=pltpu.SMEM)
    anywhere = pl.BlockSpec(memory_space=pltpu.HBM)

    def call(body, name, outs, ins, mib, gflops, scratch=(), far=(), far_out=False):
        return pl.pallas_call(
            body,
            out_shape=outs,
            in_specs=[smem if a.ndim == 1 else anywhere if i in far else vmem for i, a in enumerate(ins)],
            out_specs=(anywhere if far_out else vmem,) * len(outs),
            scratch_shapes=list(scratch),
            compiler_params=pltpu.CompilerParams(vmem_limit_bytes=int(mib * 1024 * 1024)),
            cost_estimate=pl.CostEstimate(flops=int(gflops * 1e9), bytes_accessed=4_000_000, transcendentals=0),
            name=name,
        )(*ins)

    take_half, prep, maps, early, chain, finish = make_steps(lat_rows, lon_cols, blocks, members, channels, lat_devices)
    idx = jnp.stack([lax.axis_index("segment"), lax.axis_index("lon"), lax.axis_index("lat")]).astype(jnp.int32)
    kernel = weights.reshape(width, channels)
    (half,) = call(
        take_half,
        "take_half",
        (shape((width // 2, channels), half_type),),
        (idx, kernel),
        PREP_MIB,
        0.5,
        (pltpu.SemaphoreType.DMA,),
        (1,),
        True,
    )
    near_half = lax.ppermute(half, "segment", swap("segment", 1))
    half, inputs, cotangent = lax.optimization_barrier((half, inputs, cotangent))
    both, tail, head = call(
        prep,
        "prep",
        (
            shape((members, 2 * own, channels), half_type),
            shape((members, halo, channels), half_type),
            shape((members, halo, channels), half_type),
        ),
        (inputs, cotangent),
        PREP_MIB,
        0.5,
        (pltpu.VMEM(inputs.shape, half_type), pltpu.VMEM(inputs.shape, half_type), pltpu.SemaphoreType.DMA((2,))),
        (0, 1),
    )
    up = [(i, i + 1) for i in range(lat_devices - 1)]
    down = [(i + 1, i) for i in range(lat_devices - 1)]
    both_y = lax.ppermute(both, "lon", swap("lon", 2))
    before = lax.ppermute(tail, "lat", up)
    after = lax.ppermute(head, "lat", down)
    sides = jnp.concatenate([before, after], axis=1)
    sides_y = lax.ppermute(sides, "lon", swap("lon", 2))
    b0 = jnp.concatenate([both, sides], axis=1)
    b1 = lax.ppermute(b0, "lon", swap("lon", 1))
    b0, lat_step, lon_step, basis_values = lax.optimization_barrier((b0, lat_step, lon_step, basis_values))
    forward, again, backward = call(
        maps,
        "maps",
        (
            shape((nf, BASIS * cells, blocks * win), half_type),
            shape((ns, BASIS * cells, blocks * win), half_type),
            shape((ns, blocks * win, BASIS * cells), half_type),
        ),
        (idx, lat_step.T, lon_step.T, jnp.transpose(basis_values, (1, 2, 0))),
        4,
        3.0,
        (pltpu.VMEM((48, lat_total), full_type),),
    )
    b2 = jnp.concatenate([both_y, sides_y], axis=1)
    b2, forward = lax.optimization_barrier((b2, forward))
    b3 = lax.ppermute(b2, "lon", swap("lon", 1))
    s_type = (members * nf * cells, width)
    s, left, slope, early_out = call(
        early,
        "early",
        (
            shape(s_type, half_type),
            shape((members * (nf - 2) * cells, width // blocks), half_type),
            shape((members, blocks, own + edge, channels), half_type),
            shape((members, own, channels), half_type),
        ),
        (idx, b0, b1, b2, b3, kernel, forward, again),
        12,
        3.0,
        (pltpu.VMEM(s_type, half_type), pltpu.VMEM((members, blocks, own + 2 * edge, channels), half_type)),
    )
    near_half, s = lax.optimization_barrier((near_half, s))
    far_half = lax.ppermute(near_half, "lon", swap("lon", 1))
    lines = (width // blocks // lat_devices * channels // 128, 128)
    out, follow, gates, mine, *parts = call(
        chain,
        "chain",
        (
            shape((members, own, channels), half_type),
            shape((members, own, channels), half_type),
            shape((members * ns * cells, channels), half_type),
            shape(lines, full_type),
        )
        + (shape(lines, half_type),) * 3,
        (idx, b0, b1, b2, b3, kernel, near_half, far_half, again, backward, s, left, slope, early_out),
        18,
        6.0,
        (
            pltpu.VMEM((width, channels), half_type),
            pltpu.VMEM((members * ns * cells, width), half_type),
            pltpu.VMEM((members, blocks, own + 2 * edge, channels), half_type),
            pltpu.VMEM((members * ns * cells, channels), half_type),
            pltpu.VMEM((members * ns * cells * BASIS, channels), half_type),
            pltpu.VMEM((members, blocks, own + 2 * edge, channels), full_type),
            pltpu.VMEM((width // blocks * channels // 128, 128), full_type),
        ),
    )
    got = [lax.ppermute(part, "lat", swap("lat", bit)) for bit, part in reversed(list(zip((1, 2, 3), parts)))]
    block = (members, lat_rows, lon_cols, channels)
    grad, out = call(
        finish,
        "finish",
        (shape(block, half_type),) * 2,
        (kernel, backward, gates, follow, out),
        10,
        2.0,
        (
            pltpu.VMEM((members * ns * cells * BASIS, channels), half_type),
            pltpu.VMEM((members, own + 2 * edge, channels), full_type),
        ),
    )
    (total,) = call(functools.partial(add_up, grad_scale), "add_up", (shape(lines, full_type),), (mine, *got), 2, 0.1)
    return (out[None], grad[None], total.reshape(1, lines[0] * lines[1]))


def fits_ring(mesh, inputs):
    sizes = dict(mesh.shape)
    rows, cols = inputs.shape[1] // sizes["lat"], inputs.shape[2] // sizes["lon"]
    return sizes["segment"] == 2 and sizes["lon"] == 4 and sizes["lat"] == 4 and rows == 16 and cols == 4


def solution(mesh):
    def apply(*args):
        body = whole_ring if fits_ring(mesh, args[0]) else per_device
        return jax.shard_map(
            body,
            mesh=mesh,
            in_specs=(
                P(None, "lat", "lon", None),
                P(None, "lat", "lon", None),
                P("segment", None, None, None),
                P(),
                P(),
                P(),
            ),
            out_specs=(
                P("segment", None, "lat", "lon", None),
                P("segment", None, "lat", "lon", None),
                P("segment", ("lon", "lat")),
            ),
            check_vma=False,
        )(*args)

    return apply
```

```python
import functools
import math

import jax
import jax.numpy as jnp
from jax import lax
from jax.experimental import pallas as pl
from jax.experimental.pallas import tpu as pltpu
from jax.sharding import PartitionSpec as P

BASIS = 3
TAPS = 9
REACH = 2


def with_halo(array, sides, width):
    for axis, dim in sides:
        size, length = (lax.axis_size(axis), array.shape[dim])
        up = [(i, (i + 1) % size) for i in range(size)]
        down = [(j, i) for i, j in up]
        last = lax.slice_in_dim(array, length - width, length, axis=dim)
        first = lax.slice_in_dim(array, 0, width, axis=dim)
        before = lax.ppermute(last, axis, up)
        after = lax.ppermute(first, axis, down)
        array = jnp.concatenate([before, array, after], axis=dim)
    return array


def shifted(block, axis, distance):
    devices = range(lax.axis_size(axis))
    route = [(i - distance, i) for i in devices if i - distance in devices]
    return lax.ppermute(block, axis, route)


def widen(features):
    return with_halo(features, (("lon", 2), ("lat", 1)), REACH)


def pass_ahead(result):
    return shifted(result, "segment", 1)


def pass_behind(result):
    return shifted(result, "segment", -1)


def build_tables(basis_values, lat_step, lon_step, lat_rows, lon_cols, lat_index, lat_total):
    pad_rows = lat_rows + 2 * REACH
    pad_cols = lon_cols + 2 * REACH
    lat_padded = jnp.pad(lat_step, ((REACH, REACH), (0, 0)))
    lon_padded = jnp.pad(lon_step, ((REACH, REACH), (0, 0)))
    basis_padded = jnp.pad(basis_values, ((REACH, REACH), (0, 0), (0, 0)))
    row_start = lat_index * lat_rows
    lat_near = lax.dynamic_slice_in_dim(lat_padded, row_start, pad_rows, 0)
    lon_near = lax.dynamic_slice_in_dim(lon_padded, row_start, pad_rows, 0)
    basis_near = lax.dynamic_slice_in_dim(basis_padded, row_start, pad_rows, 0)
    lat_own = lat_near[REACH : REACH + lat_rows]
    lon_own = lon_near[REACH : REACH + lat_rows]
    basis_own = basis_near[REACH : REACH + lat_rows]
    own_rows = row_start + jnp.arange(lat_rows)
    inside = (own_rows[:, None] + lat_own >= 0) & (own_rows[:, None] + lat_own < lat_total)
    row_grid = jnp.arange(lat_rows)[:, None, None]
    col_grid = jnp.arange(lon_cols)[None, :, None]
    source = (row_grid + REACH + lat_own[:, None, :]) * pad_cols + (
        col_grid + REACH + lon_own[:, None, :]
    )
    tap_weight = jnp.where(inside[:, None, :, None], basis_own[:, None, :, :], 0.0)
    tap_weight = jnp.broadcast_to(tap_weight, (lat_rows, lon_cols, TAPS, BASIS))
    picker = (source[..., None] == jnp.arange(pad_rows * pad_cols)).astype(jnp.float32)
    forward_map = jnp.einsum("ijkb,ijks->bijs", tap_weight, picker, precision=lax.Precision.HIGHEST)
    forward_map = forward_map.reshape(BASIS, lat_rows * lon_cols, pad_rows * pad_cols)
    near_rows = row_start - REACH + jnp.arange(pad_rows)
    real_row = (near_rows >= 0) & (near_rows < lat_total)
    pad_row_grid = jnp.arange(pad_rows)[:, None, None]
    pad_col_grid = jnp.arange(pad_cols)[None, :, None]
    target_row = pad_row_grid - REACH + lat_near[:, None, :]
    target_col = pad_col_grid - REACH + lon_near[:, None, :]
    landed = (
        (target_row >= 0)
        & (target_row < lat_rows)
        & (target_col >= 0)
        & (target_col < lon_cols)
        & real_row[:, None, None]
    )
    target = target_row * lon_cols + target_col
    back_weight = jnp.where(landed[..., None], basis_near[:, None, :, :], 0.0)
    catcher = (target[..., None] == jnp.arange(lat_rows * lon_cols)).astype(jnp.float32)
    backward_map = jnp.einsum(
        "pqkb,pqkt->btpq", back_weight, catcher, precision=lax.Precision.HIGHEST
    )
    backward_map = backward_map.reshape(BASIS, lat_rows * lon_cols, pad_rows * pad_cols)
    return (forward_map, backward_map)


def per_device(inputs, cotangent, weights, basis_values, lat_step, lon_step):
    members, lat_rows, lon_cols, channels = inputs.shape
    pad_rows = lat_rows + 2 * REACH
    pad_cols = lon_cols + 2 * REACH
    cells = lat_rows * lon_cols
    lat_index = lax.axis_index("lat")
    lat_total = lat_rows * lax.axis_size("lat")
    segment_index = lax.axis_index("segment")
    depth = lax.axis_size("segment")
    grad_scale = 1.0 / math.sqrt(members * lat_total * lon_cols * lax.axis_size("lon"))
    forward_map, backward_map = build_tables(
        basis_values, lat_step, lon_step, lat_rows, lon_cols, lat_index, lat_total
    )
    kernel = weights[0]
    keep_spread = jnp.zeros((BASIS, members, cells, channels), jnp.bfloat16)
    keep_mixed = jnp.zeros((members, cells, channels), jnp.float32)
    keep_gate = jnp.zeros((members, cells, channels), jnp.bfloat16)
    section_out = jnp.zeros(inputs.shape, jnp.bfloat16)
    section_grad = jnp.zeros(inputs.shape, jnp.bfloat16)
    carry = inputs
    for tick_num in range(depth):
        layer_count = carry.shape[0]
        layer_padded = (
            widen(carry).reshape(layer_count, pad_rows * pad_cols, channels).astype(jnp.float32)
        )
        spread = jnp.einsum(
            "bts,msc->bmtc", forward_map, layer_padded, precision=lax.Precision.HIGHEST
        ).astype(jnp.bfloat16)
        layer_mixed = jnp.einsum(
            "bmtc,bcd->mtd", spread, kernel, preferred_element_type=jnp.float32
        )
        result = (
            carry.reshape(layer_count, cells, channels).astype(jnp.float32)
            + jax.nn.silu(layer_mixed)
        ).astype(jnp.bfloat16)
        spread, mixed, result = (spread, layer_mixed, result.reshape(carry.shape))
        here = segment_index == tick_num
        keep_spread = jnp.where(here, spread, keep_spread)
        keep_mixed = jnp.where(here, mixed, keep_mixed)
        section_out = jnp.where(here, result, section_out)
        if tick_num + 1 < depth:
            carry = pass_ahead(result)
    grad = cotangent
    for tick_num in range(depth):
        count = grad.shape[0]
        flat_grad = grad.reshape(count, cells, channels).astype(jnp.float32)
        sigma = jax.nn.sigmoid(keep_mixed)
        gate_grad = (flat_grad * sigma * (1.0 + keep_mixed * (1.0 - sigma))).astype(jnp.bfloat16)
        feature_grad = jnp.einsum(
            "mtd,bcd->bmtc", gate_grad, kernel, preferred_element_type=jnp.float32
        ).astype(jnp.bfloat16)
        padded = widen(feature_grad.reshape(BASIS * count, lat_rows, lon_cols, channels))
        padded = padded.reshape(BASIS, count, pad_rows * pad_cols, channels).astype(jnp.float32)
        pulled = jnp.einsum("bts,bmsc->mtc", backward_map, padded, precision=lax.Precision.HIGHEST)
        new_grad = (flat_grad + pulled).astype(jnp.bfloat16).reshape(grad.shape)
        gate_grad, new_grad = (gate_grad, new_grad)
        here = segment_index == depth - 1 - tick_num
        keep_gate = jnp.where(here, gate_grad, keep_gate)
        section_grad = jnp.where(here, new_grad, section_grad)
        if tick_num + 1 < depth:
            grad = pass_behind(new_grad)
    local_grad = (
        jnp.einsum("bmtc,mtd->bcd", keep_spread, keep_gate, preferred_element_type=jnp.float32)
        * grad_scale
    )
    owners = lax.axis_size("lon") * lax.axis_size("lat")
    grad_rows = local_grad.reshape(owners, -1)
    weight_grad = lax.psum_scatter(grad_rows, ("lon", "lat"), scatter_dimension=0, tiled=True)
    return (section_out[None], section_grad[None], weight_grad)


HALO = 8
BAND = 8


def swap(axis, bit):
    return [(i, i ^ bit) for i in range(lax.axis_size(axis))]


def window_plan(lat_rows):
    first = [(a, min(max(a - 4, -HALO), lat_rows + HALO - 16)) for a in range(-HALO, lat_rows + HALO, BAND)]
    second = [(a, a - 4) for a in range(-4, lat_rows + 4, BAND)]
    return first, second


def dot(a, b):
    return jnp.dot(a, b, preferred_element_type=jnp.float32)


def dot_nt(a, b):
    return lax.dot_general(a, b, (((1,), (1,)), ((), ())), preferred_element_type=jnp.float32)


def dot_tn(a, b):
    return lax.dot_general(a, b, (((0,), (0,)), ((), ())), preferred_element_type=jnp.float32)


def make_steps(lat_rows, lon_cols, blocks, members, channels, lat_devices):
    first, second = window_plan(lat_rows)
    nf, ns = len(first), len(second)
    lat_total = lat_rows * lat_devices
    ring = lon_cols * blocks
    band = BAND * lon_cols
    cells = blocks * band
    win = 16 * lon_cols
    own = lat_rows * lon_cols
    edge = HALO * lon_cols
    half_edge = edge // 2
    width = BASIS * channels
    lanes = 128
    pieces = channels // lanes
    halo = edge + half_edge
    state_parts = ((0, edge, 2 * own), (edge, own, 0), (edge + own, edge, 2 * own + halo))
    coming_parts = (
        (0, half_edge, 2 * own + edge),
        (half_edge, own, own),
        (half_edge + own, half_edge, 2 * own + halo + edge),
    )

    def take(blks, m, parts, low, high):
        found = []
        for r in blks:
            for start, size, at in parts:
                lo, hi = max(low, start), min(high, start + size)
                if lo < hi:
                    found.append(r[m, at + lo - start : at + hi - start, :])
        return jnp.concatenate(found, axis=0)

    def prep(x, c, both):
        for m in range(members):
            both[m, :own, :] = x[m].reshape(own, channels)
            both[m, own:, :] = c[m].reshape(own, channels)

    def edges(both, tail, head):
        for m in range(members):
            tail[m, :edge, :] = both[m, own - edge : own, :]
            tail[m, edge:, :] = both[m, 2 * own - half_edge :, :]
            head[m, :edge, :] = both[m, :edge, :]
            head[m, edge:, :] = both[m, own : own + half_edge, :]

    def maps(lat_step, lon_step, basis, forward, again, backward, tab):
        lon, lat = lax.axis_index("lon"), lax.axis_index("lat")
        base = lat * lat_rows
        tab[...] = jnp.zeros(tab.shape, jnp.float32)
        tab[0:TAPS, :] = lat_step[...].astype(jnp.float32)
        tab[TAPS : 2 * TAPS, :] = lon_step[...].astype(jnp.float32)
        for k in range(TAPS):
            tab[2 * TAPS + k * BASIS : 2 * TAPS + (k + 1) * BASIS, :] = basis[k]
        table = tab[...].astype(jnp.bfloat16)
        source = lax.broadcasted_iota(jnp.int32, (tab.shape[1], cells), 0)
        lane = lax.broadcasted_iota(jnp.int32, (1, cells), 1)
        block, rest = lane // band, lane % band
        row_in, col_in = rest // lon_cols, rest % lon_cols
        column_home = (block ^ lon) * lon_cols + col_in
        piece = 64
        spot = lax.broadcasted_iota(jnp.int32, (piece, cells), 0)
        for i, (a, start) in enumerate(first + second):
            row = row_in + (base + a)
            got = dot(table, (source == row).astype(jnp.bfloat16))
            step_lat = got[0:TAPS].astype(jnp.int32)
            step_lon = got[TAPS : 2 * TAPS].astype(jnp.int32)
            target = row + step_lat
            inside = (row >= 0) & (row < lat_total) & (target >= 0) & (target < lat_total)
            column = column_home + step_lon
            column = jnp.where(column < 0, column + ring, column)
            column = jnp.where(column >= ring, column - ring, column)
            local = target - (base + start)
            place = ((column // lon_cols) ^ lon) * win + local * lon_cols + column % lon_cols
            place = jnp.where(inside, place, -1)
            for p in range(0, blocks * win, piece):
                tables = [jnp.zeros((piece, cells), jnp.float32) for _ in range(BASIS)]
                for k in range(TAPS):
                    hit = spot == place[k : k + 1] - p
                    for b in range(BASIS):
                        at = 2 * TAPS + k * BASIS + b
                        tables[b] = tables[b] + jnp.where(hit, got[at : at + 1], 0.0)
                for b in range(BASIS):
                    span = slice(b * cells, (b + 1) * cells)
                    if i < nf:
                        forward[i, span, p : p + piece] = tables[b].T.astype(jnp.bfloat16)
                    else:
                        again[i - nf, span, p : p + piece] = tables[b].T.astype(jnp.bfloat16)
                        backward[i - nf, p : p + piece, span] = tables[b].astype(jnp.bfloat16)

    def put_spread(got, into, at):
        for b in range(BASIS):
            into[at : at + cells, b * channels : (b + 1) * channels] = got[b * cells : (b + 1) * cells]

    def spread(blk, forward, into):
        for m in range(members):
            for g, (a, start) in enumerate(first):
                o = (start + HALO) * lon_cols
                near = take(blk, m, state_parts, o, o + win)
                put_spread(dot(forward[g], near).astype(jnp.bfloat16), into, (m * nf + g) * cells)

    def first_section(blk, w, s0, s1, again, mid, slope):
        for m in range(members):
            total = dot(s0[m * nf * cells : (m + 1) * nf * cells, :], w[...])
            for g in range(nf):
                mixed = total[g * cells : (g + 1) * cells]
                sigma = jax.nn.sigmoid(mixed)
                here = take(blk, m, state_parts, g * band, (g + 1) * band)
                value = (here.astype(jnp.float32) + mixed * sigma).astype(jnp.bfloat16)
                mid[m, :, g * band : (g + 1) * band, :] = value.reshape(blocks, band, channels)
                if slope is not None:
                    tilt = (sigma * (1.0 + mixed * (1.0 - sigma))).astype(slope.dtype).reshape(blocks, band, channels)
                    low, high = max(g * band, half_edge), min((g + 1) * band, 3 * half_edge + own)
                    slope[m, :, low - half_edge : high - half_edge, :] = tilt[:, low - g * band : high - g * band]
            for g in range(ns):
                near = mid[m, :, g * band : g * band + win, :].reshape(blocks * win, channels)
                put_spread(dot(again[g], near).astype(jnp.bfloat16), s1, (m * ns + g) * cells)

    def columns_of(lon):
        return pl.ds(pl.multiple_of(lon * (width // blocks), 128), width // blocks)

    def early(b0, b1, b2, b3, w_own, forward, again, s, left, slope, out, s0, mid):
        blk = (b0, b1, b2, b3)

        @pl.when(lax.axis_index("segment") == 0)
        def _():
            spread(blk, forward, s0)
            first_section(blk, w_own, s0, s, again, mid, slope)
            for m in range(members):
                size = (nf - 2) * cells
                left[m * size : (m + 1) * size, :] = s0[(m * nf + 1) * cells : (m * nf + nf - 1) * cells, columns_of(lax.axis_index("lon"))]
                out[m, :, :] = mid[m, 0, edge : edge + own, :]

        @pl.when(lax.axis_index("segment") == 1)
        def _():
            spread(blk, forward, s)

    def own_part(g):
        return max(g * band, half_edge), min((g + 1) * band, half_edge + own)

    def apply_back(w, gates, feat):
        for b in range(BASIS):
            got = dot_nt(gates[...], w[b * channels : (b + 1) * channels, :]).astype(jnp.bfloat16)
            for i in range(members * ns):
                feat[(i * BASIS + b) * cells : (i * BASIS + b + 1) * cells, :] = got[i * cells : (i + 1) * cells]

    def chain(b0, b1, b2, b3, w_own, w_a, w_b, again, backward, s, left0, slope, early_out,
              out_ref, next_ref, gate_ref, own_ref, p1, p2, p3, w, s1, mid, gates, feat, pull, grads):
        blk = (b0, b1, b2, b3)
        seg, lon, lat = lax.axis_index("segment"), lax.axis_index("lon"), lax.axis_index("lat")
        half = w_a.shape[0]
        core = lon % 2
        w[pl.ds(pl.multiple_of(core * half, half), half), :] = w_a[...]
        w[pl.ds(pl.multiple_of((1 - core) * half, half), half), :] = w_b[...]

        def coming_at(m, g):
            return take(blk, m, coming_parts, g * band, (g + 1) * band).astype(jnp.float32)

        def second_section(weight, spread_ref, into, last):
            for m in range(members):
                total = dot(spread_ref[m * ns * cells : (m + 1) * ns * cells, :], weight[...])
                for g in range(ns):
                    at = (m * ns + g) * cells
                    mixed = total[g * cells : (g + 1) * cells]
                    sigma = jax.nn.sigmoid(mixed)
                    into[at : at + cells, :] = (coming_at(m, g) * sigma * (1.0 + mixed * (1.0 - sigma))).astype(jnp.bfloat16)
                    if last:
                        low, high = own_part(g)
                        base = mid[m, 0, half_edge + low : half_edge + high, :]
                        local = slice(low - g * band, high - g * band)
                        base = (base.astype(jnp.float32) + mixed[local] * sigma[local]).astype(jnp.bfloat16)
                        out_ref[m, low - half_edge : high - half_edge, :] = base

        def store_grads(left, right):
            got = dot_tn(left, jnp.concatenate(right, axis=0))
            for c in range(pieces):
                grads[pl.ds(c, width // blocks, stride=pieces), :] = got[:, c * lanes : (c + 1) * lanes]

        @pl.when(seg == 0)
        def _():
            second_section(w, s, gates, False)
            out_ref[...] = early_out[...]
            apply_back(w, gates, feat)
            for m in range(members):
                for g in range(ns):
                    at = (m * ns + g) * cells * BASIS
                    got = dot(backward[g], feat[at : at + BASIS * cells, :]).reshape(blocks, win, channels)
                    if g == 0:
                        pull[m, :, :win, :] = got
                    else:
                        pull[m, :, g * band : (g + 1) * band, :] += got[:, :band]
                        pull[m, :, (g + 1) * band : g * band + win, :] = got[:, band:]
            right = []
            step = half_edge
            for m in range(members):
                for g in range(ns):
                    at = (m * ns + g) * cells
                    span = slice(half_edge + g * band, half_edge + (g + 1) * band)
                    value = (coming_at(m, g) + pull[m, :, span, :].reshape(cells, channels)).astype(jnp.bfloat16)
                    low, high = own_part(g)
                    next_ref[m, low - half_edge : high - half_edge, :] = value[low - g * band : high - g * band]
                    tilt = slope[m, :, g * band : (g + 1) * band, :].reshape(cells, channels)
                    gate_ref[at : at + cells, :] = (value.astype(jnp.float32) * tilt).astype(jnp.bfloat16)
                for g in range(1, nf - 1):
                    for q in range(blocks):
                        for o in range(0, band, step):
                            spot = half_edge + (g - 1) * band + o
                            turn, rest = spot // band, spot % band
                            at = (m * ns + turn) * cells + q * band + rest
                            right.append(gate_ref[at : at + step, :])
            store_grads(left0[...], right)

        @pl.when(seg == 1)
        def _():
            first_section(blk, w, s, s1, again, mid, None)
            second_section(w_own, s1, gate_ref, True)
            left, right = [], []
            for m in range(members):
                next_ref[m, :, :] = b0[m, own : 2 * own, :]
                for g in range(ns):
                    low, high = own_part(g)
                    for q in range(blocks):
                        at = (m * ns + g) * cells + q * band - g * band
                        left.append(s1[at + low : at + high, columns_of(lon)])
                        right.append(gate_ref[at + low : at + high, :])
            store_grads(jnp.concatenate(left, axis=0), right)

        share = width // blocks // lat_devices * pieces

        def rows_of(index):
            return grads[pl.ds(pl.multiple_of(index * share, share), share), :]

        own_ref[...] = rows_of(lat)
        for bit, ref in ((1, p1), (2, p2), (3, p3)):
            ref[...] = rows_of(lat ^ bit).astype(jnp.bfloat16)

    def finish(w_own, backward, gates, next_ref, last_ref, grad_ref, out_ref, feat, pull):
        apply_back(w_own, gates, feat)
        for m in range(members):
            for g in range(ns):
                at = (m * ns + g) * cells * BASIS
                got = dot(backward[g, 0:win, :], feat[at : at + BASIS * cells, :])
                if g == 0:
                    pull[m, :win, :] = got
                else:
                    pull[m, g * band : (g + 1) * band, :] += got[:band]
                    pull[m, (g + 1) * band : g * band + win, :] = got[band:]
            total = next_ref[m].astype(jnp.float32) + pull[m, edge : edge + own, :]
            grad_ref[m] = total.astype(jnp.bfloat16).reshape(lat_rows, lon_cols, channels)
            out_ref[m] = last_ref[m].reshape(lat_rows, lon_cols, channels)

    return prep, edges, maps, early, chain, finish


def add_up(scale, mine, p1, p2, p3, out):
    out[...] = (mine[...] + p1[...].astype(jnp.float32) + p2[...].astype(jnp.float32) + p3[...].astype(jnp.float32)) * scale


def whole_ring(inputs, cotangent, weights, basis_values, lat_step, lon_step):
    members, lat_rows, lon_cols, channels = inputs.shape
    blocks = lax.axis_size("lon")
    lat_devices = lax.axis_size("lat")
    lat_total = lat_rows * lat_devices
    grad_scale = 1.0 / math.sqrt(members * lat_total * lon_cols * blocks)
    own = lat_rows * lon_cols
    edge = HALO * lon_cols
    half_edge = edge // 2
    halo = edge + half_edge
    width = BASIS * channels
    half_type, full_type = jnp.bfloat16, jnp.float32
    shape = jax.ShapeDtypeStruct
    first, second = window_plan(lat_rows)
    nf, ns = len(first), len(second)
    cells = blocks * BAND * lon_cols
    win = 16 * lon_cols
    vmem = pl.BlockSpec(memory_space=pltpu.VMEM)
    anywhere = pl.BlockSpec(memory_space=pltpu.HBM)

    def call(body, name, outs, ins, mib, gflops, scratch=(), far=()):
        return pl.pallas_call(
            body,
            out_shape=outs,
            in_specs=[anywhere if i in far else vmem for i, a in enumerate(ins)],
            out_specs=(vmem,) * len(outs),
            scratch_shapes=list(scratch),
            compiler_params=pltpu.CompilerParams(vmem_limit_bytes=int(mib * 1024 * 1024)),
            cost_estimate=pl.CostEstimate(flops=int(gflops * 1e9), bytes_accessed=4_000_000, transcendentals=0),
            name=name,
        )(*ins)

    prep, edges, maps, early, chain, finish = make_steps(lat_rows, lon_cols, blocks, members, channels, lat_devices)
    kernel = weights.reshape(width, channels)
    half = lax.dynamic_slice_in_dim(kernel, lax.axis_index("lon") % 2 * (width // 2), width // 2, 0)
    near_half = lax.ppermute(half, "segment", swap("segment", 1))
    half, inputs, cotangent = lax.optimization_barrier((half, inputs, cotangent))
    (both,) = call(prep, "prep", (shape((members, 2 * own, channels), half_type),), (inputs, cotangent), 4, 0.5)
    sides_type = shape((members, halo, channels), half_type)
    tail, head = call(edges, "edges", (sides_type, sides_type), (both,), 4, 0.2)
    up = [(i, i + 1) for i in range(lat_devices - 1)]
    down = [(i + 1, i) for i in range(lat_devices - 1)]
    both_y = lax.ppermute(both, "lon", swap("lon", 2))
    before = lax.ppermute(tail, "lat", up)
    after = lax.ppermute(head, "lat", down)
    sides = jnp.concatenate([before, after], axis=1)
    sides, both_y = lax.optimization_barrier((sides, both_y))
    sides_y = lax.ppermute(sides, "lon", swap("lon", 2))
    b0 = jnp.concatenate([both, sides], axis=1)
    b1 = lax.ppermute(b0, "lon", swap("lon", 1))
    b0, lat_step, lon_step, basis_values = lax.optimization_barrier((b0, lat_step, lon_step, basis_values))
    forward, again, backward = call(
        maps,
        "maps",
        (
            shape((nf, BASIS * cells, blocks * win), half_type),
            shape((ns, BASIS * cells, blocks * win), half_type),
            shape((ns, blocks * win, BASIS * cells), half_type),
        ),
        (lat_step.T, lon_step.T, jnp.transpose(basis_values, (1, 2, 0))),
        4,
        3.0,
        (pltpu.VMEM((48, lat_total), full_type),),
    )
    b2 = jnp.concatenate([both_y, sides_y], axis=1)
    b2, forward = lax.optimization_barrier((b2, forward))
    b3 = lax.ppermute(b2, "lon", swap("lon", 1))
    near_half, _ = lax.optimization_barrier((near_half, b2))
    far_half = lax.ppermute(near_half, "lon", swap("lon", 1))
    s_type = (members * nf * cells, width)
    s, left, slope, early_out = call(
        early,
        "early",
        (
            shape(s_type, half_type),
            shape((members * (nf - 2) * cells, width // blocks), half_type),
            shape((members, blocks, own + edge, channels), half_type),
            shape((members, own, channels), half_type),
        ),
        (b0, b1, b2, b3, kernel, forward, again),
        12,
        3.0,
        (pltpu.VMEM(s_type, half_type), pltpu.VMEM((members, blocks, own + 2 * edge, channels), half_type)),
    )
    lines = (width // blocks // lat_devices * channels // 128, 128)
    out, follow, gates, mine, *parts = call(
        chain,
        "chain",
        (
            shape((members, own, channels), half_type),
            shape((members, own, channels), half_type),
            shape((members * ns * cells, channels), half_type),
            shape(lines, full_type),
        )
        + (shape(lines, half_type),) * 3,
        (b0, b1, b2, b3, kernel, near_half, far_half, again, backward, s, left, slope, early_out),
        18,
        6.0,
        (
            pltpu.VMEM((width, channels), half_type),
            pltpu.VMEM((members * ns * cells, width), half_type),
            pltpu.VMEM((members, blocks, own + 2 * edge, channels), half_type),
            pltpu.VMEM((members * ns * cells, channels), half_type),
            pltpu.VMEM((members * ns * cells * BASIS, channels), half_type),
            pltpu.VMEM((members, blocks, own + 2 * edge, channels), full_type),
            pltpu.VMEM((width // blocks * channels // 128, 128), full_type),
        ),
    )
    got = [lax.ppermute(part, "lat", swap("lat", bit)) for bit, part in reversed(list(zip((1, 2, 3), parts)))]
    block = (members, lat_rows, lon_cols, channels)
    grad, out = call(
        finish,
        "finish",
        (shape(block, half_type),) * 2,
        (kernel, backward, gates, follow, out),
        10,
        2.0,
        (
            pltpu.VMEM((members * ns * cells * BASIS, channels), half_type),
            pltpu.VMEM((members, own + 2 * edge, channels), full_type),
        ),
    )
    (total,) = call(functools.partial(add_up, grad_scale), "add_up", (shape(lines, full_type),), (mine, *got), 2, 0.1)
    return (out[None], grad[None], total.reshape(1, lines[0] * lines[1]))


def fits_ring(mesh, inputs):
    sizes = dict(mesh.shape)
    rows, cols = inputs.shape[1] // sizes["lat"], inputs.shape[2] // sizes["lon"]
    return sizes["segment"] == 2 and sizes["lon"] == 4 and sizes["lat"] == 4 and rows == 16 and cols == 4


def solution(mesh):
    def apply(*args):
        body = whole_ring if fits_ring(mesh, args[0]) else per_device
        return jax.shard_map(
            body,
            mesh=mesh,
            in_specs=(
                P(None, "lat", "lon", None),
                P(None, "lat", "lon", None),
                P("segment", None, None, None),
                P(),
                P(),
                P(),
            ),
            out_specs=(
                P("segment", None, "lat", "lon", None),
                P("segment", None, "lat", "lon", None),
                P("segment", ("lon", "lat")),
            ),
            check_vma=False,
        )(*args)

    return apply
```

```python
import functools
import math

import jax
import jax.numpy as jnp
from jax import lax
from jax.experimental import pallas as pl
from jax.experimental.pallas import tpu as pltpu
from jax.sharding import PartitionSpec as P

BASIS = 3
TAPS = 9
REACH = 2


def with_halo(array, sides, width):
    for axis, dim in sides:
        size, length = (lax.axis_size(axis), array.shape[dim])
        up = [(i, (i + 1) % size) for i in range(size)]
        down = [(j, i) for i, j in up]
        last = lax.slice_in_dim(array, length - width, length, axis=dim)
        first = lax.slice_in_dim(array, 0, width, axis=dim)
        before = lax.ppermute(last, axis, up)
        after = lax.ppermute(first, axis, down)
        array = jnp.concatenate([before, array, after], axis=dim)
    return array


def shifted(block, axis, distance):
    devices = range(lax.axis_size(axis))
    route = [(i - distance, i) for i in devices if i - distance in devices]
    return lax.ppermute(block, axis, route)


def widen(features):
    return with_halo(features, (("lon", 2), ("lat", 1)), REACH)


def pass_ahead(result):
    return shifted(result, "segment", 1)


def pass_behind(result):
    return shifted(result, "segment", -1)


def build_tables(basis_values, lat_step, lon_step, lat_rows, lon_cols, lat_index, lat_total):
    pad_rows = lat_rows + 2 * REACH
    pad_cols = lon_cols + 2 * REACH
    lat_padded = jnp.pad(lat_step, ((REACH, REACH), (0, 0)))
    lon_padded = jnp.pad(lon_step, ((REACH, REACH), (0, 0)))
    basis_padded = jnp.pad(basis_values, ((REACH, REACH), (0, 0), (0, 0)))
    row_start = lat_index * lat_rows
    lat_near = lax.dynamic_slice_in_dim(lat_padded, row_start, pad_rows, 0)
    lon_near = lax.dynamic_slice_in_dim(lon_padded, row_start, pad_rows, 0)
    basis_near = lax.dynamic_slice_in_dim(basis_padded, row_start, pad_rows, 0)
    lat_own = lat_near[REACH : REACH + lat_rows]
    lon_own = lon_near[REACH : REACH + lat_rows]
    basis_own = basis_near[REACH : REACH + lat_rows]
    own_rows = row_start + jnp.arange(lat_rows)
    inside = (own_rows[:, None] + lat_own >= 0) & (own_rows[:, None] + lat_own < lat_total)
    row_grid = jnp.arange(lat_rows)[:, None, None]
    col_grid = jnp.arange(lon_cols)[None, :, None]
    source = (row_grid + REACH + lat_own[:, None, :]) * pad_cols + (
        col_grid + REACH + lon_own[:, None, :]
    )
    tap_weight = jnp.where(inside[:, None, :, None], basis_own[:, None, :, :], 0.0)
    tap_weight = jnp.broadcast_to(tap_weight, (lat_rows, lon_cols, TAPS, BASIS))
    picker = (source[..., None] == jnp.arange(pad_rows * pad_cols)).astype(jnp.float32)
    forward_map = jnp.einsum("ijkb,ijks->bijs", tap_weight, picker, precision=lax.Precision.HIGHEST)
    forward_map = forward_map.reshape(BASIS, lat_rows * lon_cols, pad_rows * pad_cols)
    near_rows = row_start - REACH + jnp.arange(pad_rows)
    real_row = (near_rows >= 0) & (near_rows < lat_total)
    pad_row_grid = jnp.arange(pad_rows)[:, None, None]
    pad_col_grid = jnp.arange(pad_cols)[None, :, None]
    target_row = pad_row_grid - REACH + lat_near[:, None, :]
    target_col = pad_col_grid - REACH + lon_near[:, None, :]
    landed = (
        (target_row >= 0)
        & (target_row < lat_rows)
        & (target_col >= 0)
        & (target_col < lon_cols)
        & real_row[:, None, None]
    )
    target = target_row * lon_cols + target_col
    back_weight = jnp.where(landed[..., None], basis_near[:, None, :, :], 0.0)
    catcher = (target[..., None] == jnp.arange(lat_rows * lon_cols)).astype(jnp.float32)
    backward_map = jnp.einsum(
        "pqkb,pqkt->btpq", back_weight, catcher, precision=lax.Precision.HIGHEST
    )
    backward_map = backward_map.reshape(BASIS, lat_rows * lon_cols, pad_rows * pad_cols)
    return (forward_map, backward_map)


def per_device(inputs, cotangent, weights, basis_values, lat_step, lon_step):
    members, lat_rows, lon_cols, channels = inputs.shape
    pad_rows = lat_rows + 2 * REACH
    pad_cols = lon_cols + 2 * REACH
    cells = lat_rows * lon_cols
    lat_index = lax.axis_index("lat")
    lat_total = lat_rows * lax.axis_size("lat")
    segment_index = lax.axis_index("segment")
    depth = lax.axis_size("segment")
    grad_scale = 1.0 / math.sqrt(members * lat_total * lon_cols * lax.axis_size("lon"))
    forward_map, backward_map = build_tables(
        basis_values, lat_step, lon_step, lat_rows, lon_cols, lat_index, lat_total
    )
    kernel = weights[0]
    keep_spread = jnp.zeros((BASIS, members, cells, channels), jnp.bfloat16)
    keep_mixed = jnp.zeros((members, cells, channels), jnp.float32)
    keep_gate = jnp.zeros((members, cells, channels), jnp.bfloat16)
    section_out = jnp.zeros(inputs.shape, jnp.bfloat16)
    section_grad = jnp.zeros(inputs.shape, jnp.bfloat16)
    carry = inputs
    for tick_num in range(depth):
        layer_count = carry.shape[0]
        layer_padded = (
            widen(carry).reshape(layer_count, pad_rows * pad_cols, channels).astype(jnp.float32)
        )
        spread = jnp.einsum(
            "bts,msc->bmtc", forward_map, layer_padded, precision=lax.Precision.HIGHEST
        ).astype(jnp.bfloat16)
        layer_mixed = jnp.einsum(
            "bmtc,bcd->mtd", spread, kernel, preferred_element_type=jnp.float32
        )
        result = (
            carry.reshape(layer_count, cells, channels).astype(jnp.float32)
            + jax.nn.silu(layer_mixed)
        ).astype(jnp.bfloat16)
        spread, mixed, result = (spread, layer_mixed, result.reshape(carry.shape))
        here = segment_index == tick_num
        keep_spread = jnp.where(here, spread, keep_spread)
        keep_mixed = jnp.where(here, mixed, keep_mixed)
        section_out = jnp.where(here, result, section_out)
        if tick_num + 1 < depth:
            carry = pass_ahead(result)
    grad = cotangent
    for tick_num in range(depth):
        count = grad.shape[0]
        flat_grad = grad.reshape(count, cells, channels).astype(jnp.float32)
        sigma = jax.nn.sigmoid(keep_mixed)
        gate_grad = (flat_grad * sigma * (1.0 + keep_mixed * (1.0 - sigma))).astype(jnp.bfloat16)
        feature_grad = jnp.einsum(
            "mtd,bcd->bmtc", gate_grad, kernel, preferred_element_type=jnp.float32
        ).astype(jnp.bfloat16)
        padded = widen(feature_grad.reshape(BASIS * count, lat_rows, lon_cols, channels))
        padded = padded.reshape(BASIS, count, pad_rows * pad_cols, channels).astype(jnp.float32)
        pulled = jnp.einsum("bts,bmsc->mtc", backward_map, padded, precision=lax.Precision.HIGHEST)
        new_grad = (flat_grad + pulled).astype(jnp.bfloat16).reshape(grad.shape)
        gate_grad, new_grad = (gate_grad, new_grad)
        here = segment_index == depth - 1 - tick_num
        keep_gate = jnp.where(here, gate_grad, keep_gate)
        section_grad = jnp.where(here, new_grad, section_grad)
        if tick_num + 1 < depth:
            grad = pass_behind(new_grad)
    local_grad = (
        jnp.einsum("bmtc,mtd->bcd", keep_spread, keep_gate, preferred_element_type=jnp.float32)
        * grad_scale
    )
    owners = lax.axis_size("lon") * lax.axis_size("lat")
    grad_rows = local_grad.reshape(owners, -1)
    weight_grad = lax.psum_scatter(grad_rows, ("lon", "lat"), scatter_dimension=0, tiled=True)
    return (section_out[None], section_grad[None], weight_grad)


HALO = 8
BAND = 8


def swap(axis, bit):
    return [(i, i ^ bit) for i in range(lax.axis_size(axis))]


def window_plan(lat_rows):
    first = [(a, min(max(a - 4, -HALO), lat_rows + HALO - 16)) for a in range(-HALO, lat_rows + HALO, BAND)]
    second = [(a, a - 4) for a in range(-4, lat_rows + 4, BAND)]
    return first, second


def dot(a, b):
    return jnp.dot(a, b, preferred_element_type=jnp.float32)


def dot_nt(a, b):
    return lax.dot_general(a, b, (((1,), (1,)), ((), ())), preferred_element_type=jnp.float32)


def dot_tn(a, b):
    return lax.dot_general(a, b, (((0,), (0,)), ((), ())), preferred_element_type=jnp.float32)


def make_steps(lat_rows, lon_cols, blocks, members, channels, lat_devices):
    first, second = window_plan(lat_rows)
    nf, ns = len(first), len(second)
    lat_total = lat_rows * lat_devices
    ring = lon_cols * blocks
    band = BAND * lon_cols
    cells = blocks * band
    win = 16 * lon_cols
    own = lat_rows * lon_cols
    edge = HALO * lon_cols
    half_edge = edge // 2
    width = BASIS * channels
    lanes = 128
    pieces = channels // lanes
    halo = edge + half_edge
    state_parts = ((0, edge, 2 * own), (edge, own, 0), (edge + own, edge, 2 * own + halo))
    coming_parts = (
        (0, half_edge, 2 * own + edge),
        (half_edge, own, own),
        (half_edge + own, half_edge, 2 * own + halo + edge),
    )

    def take(blks, m, parts, low, high):
        found = []
        for r in blks:
            for start, size, at in parts:
                lo, hi = max(low, start), min(high, start + size)
                if lo < hi:
                    found.append(r[m, at + lo - start : at + hi - start, :])
        return jnp.concatenate(found, axis=0)

    def prep(x, c, both):
        for m in range(members):
            both[m, :own, :] = x[m].reshape(own, channels)
            both[m, own:, :] = c[m].reshape(own, channels)

    def edges(both, tail, head):
        for m in range(members):
            tail[m, :edge, :] = both[m, own - edge : own, :]
            tail[m, edge:, :] = both[m, 2 * own - half_edge :, :]
            head[m, :edge, :] = both[m, :edge, :]
            head[m, edge:, :] = both[m, own : own + half_edge, :]

    def maps(lat_step, lon_step, basis, forward, again, backward, tab):
        lon, lat = lax.axis_index("lon"), lax.axis_index("lat")
        base = lat * lat_rows
        tab[...] = jnp.zeros(tab.shape, jnp.float32)
        tab[0:TAPS, :] = lat_step[...].astype(jnp.float32)
        tab[TAPS : 2 * TAPS, :] = lon_step[...].astype(jnp.float32)
        for k in range(TAPS):
            tab[2 * TAPS + k * BASIS : 2 * TAPS + (k + 1) * BASIS, :] = basis[k]
        table = tab[...].astype(jnp.bfloat16)
        source = lax.broadcasted_iota(jnp.int32, (tab.shape[1], cells), 0)
        lane = lax.broadcasted_iota(jnp.int32, (1, cells), 1)
        block, rest = lane // band, lane % band
        row_in, col_in = rest // lon_cols, rest % lon_cols
        column_home = (block ^ lon) * lon_cols + col_in
        piece = 64
        spot = lax.broadcasted_iota(jnp.int32, (piece, cells), 0)
        for i, (a, start) in enumerate(first + second):
            row = row_in + (base + a)
            got = dot(table, (source == row).astype(jnp.bfloat16))
            step_lat = got[0:TAPS].astype(jnp.int32)
            step_lon = got[TAPS : 2 * TAPS].astype(jnp.int32)
            target = row + step_lat
            inside = (row >= 0) & (row < lat_total) & (target >= 0) & (target < lat_total)
            column = column_home + step_lon
            column = jnp.where(column < 0, column + ring, column)
            column = jnp.where(column >= ring, column - ring, column)
            local = target - (base + start)
            place = ((column // lon_cols) ^ lon) * win + local * lon_cols + column % lon_cols
            place = jnp.where(inside, place, -1)
            for p in range(0, blocks * win, piece):
                tables = [jnp.zeros((piece, cells), jnp.float32) for _ in range(BASIS)]
                for k in range(TAPS):
                    hit = spot == place[k : k + 1] - p
                    for b in range(BASIS):
                        at = 2 * TAPS + k * BASIS + b
                        tables[b] = tables[b] + jnp.where(hit, got[at : at + 1], 0.0)
                for b in range(BASIS):
                    span = slice(b * cells, (b + 1) * cells)
                    if i < nf:
                        forward[i, span, p : p + piece] = tables[b].T.astype(jnp.bfloat16)
                    else:
                        again[i - nf, span, p : p + piece] = tables[b].T.astype(jnp.bfloat16)
                        backward[i - nf, p : p + piece, span] = tables[b].astype(jnp.bfloat16)

    def put_spread(got, into, at):
        for b in range(BASIS):
            into[at : at + cells, b * channels : (b + 1) * channels] = got[b * cells : (b + 1) * cells]

    def spread(blk, forward, into):
        for m in range(members):
            for g, (a, start) in enumerate(first):
                o = (start + HALO) * lon_cols
                near = take(blk, m, state_parts, o, o + win)
                put_spread(dot(forward[g], near).astype(jnp.bfloat16), into, (m * nf + g) * cells)

    def first_section(blk, w, s0, s1, again, mid, slope):
        for m in range(members):
            total = dot(s0[m * nf * cells : (m + 1) * nf * cells, :], w[...])
            for g in range(nf):
                mixed = total[g * cells : (g + 1) * cells]
                sigma = jax.nn.sigmoid(mixed)
                here = take(blk, m, state_parts, g * band, (g + 1) * band)
                value = (here.astype(jnp.float32) + mixed * sigma).astype(jnp.bfloat16)
                mid[m, :, g * band : (g + 1) * band, :] = value.reshape(blocks, band, channels)
                if slope is not None:
                    tilt = (sigma * (1.0 + mixed * (1.0 - sigma))).astype(slope.dtype).reshape(blocks, band, channels)
                    low, high = max(g * band, half_edge), min((g + 1) * band, 3 * half_edge + own)
                    slope[m, :, low - half_edge : high - half_edge, :] = tilt[:, low - g * band : high - g * band]
            for g in range(ns):
                near = mid[m, :, g * band : g * band + win, :].reshape(blocks * win, channels)
                put_spread(dot(again[g], near).astype(jnp.bfloat16), s1, (m * ns + g) * cells)

    def columns_of(lon):
        return pl.ds(pl.multiple_of(lon * (width // blocks), 128), width // blocks)

    def early(b0, b1, b2, b3, w_own, forward, again, s, left, slope, out, s0, mid):
        blk = (b0, b1, b2, b3)

        @pl.when(lax.axis_index("segment") == 0)
        def _():
            spread(blk, forward, s0)
            first_section(blk, w_own, s0, s, again, mid, slope)
            for m in range(members):
                size = (nf - 2) * cells
                left[m * size : (m + 1) * size, :] = s0[(m * nf + 1) * cells : (m * nf + nf - 1) * cells, columns_of(lax.axis_index("lon"))]
                out[m, :, :] = mid[m, 0, edge : edge + own, :]

        @pl.when(lax.axis_index("segment") == 1)
        def _():
            spread(blk, forward, s)

    def own_part(g):
        return max(g * band, half_edge), min((g + 1) * band, half_edge + own)

    def apply_back(w, gates, feat):
        for b in range(BASIS):
            got = dot_nt(gates[...], w[b * channels : (b + 1) * channels, :]).astype(jnp.bfloat16)
            for i in range(members * ns):
                feat[(i * BASIS + b) * cells : (i * BASIS + b + 1) * cells, :] = got[i * cells : (i + 1) * cells]

    def chain(b0, b1, b2, b3, w_own, near_half, far_half, ends, again, backward, s, left0, slope, early_out,
              out_ref, next_ref, gate_ref, own_ref, p1, p2, p3, w, s1, mid, gates, feat, pull, grads):
        blk = (b0, b1, b2, b3)
        seg, lon, lat = lax.axis_index("segment"), lax.axis_index("lon"), lax.axis_index("lat")
        here = lon % 2 * (width // 2)
        there = width // 2 - here
        rows, rest = near_half.shape[0], ends.shape[0] // 2
        for base, ref in ((here, near_half), (there, far_half)):
            w[pl.ds(pl.multiple_of(base, 32), rows), :] = ref[...]
        w[rows : rows + rest, :] = ends[:rest]
        w[width - rest :, :] = ends[rest:]

        def coming_at(m, g):
            return take(blk, m, coming_parts, g * band, (g + 1) * band).astype(jnp.float32)

        def second_section(weight, spread_ref, into, last):
            for m in range(members):
                total = dot(spread_ref[m * ns * cells : (m + 1) * ns * cells, :], weight[...])
                for g in range(ns):
                    at = (m * ns + g) * cells
                    mixed = total[g * cells : (g + 1) * cells]
                    sigma = jax.nn.sigmoid(mixed)
                    into[at : at + cells, :] = (coming_at(m, g) * sigma * (1.0 + mixed * (1.0 - sigma))).astype(jnp.bfloat16)
                    if last:
                        low, high = own_part(g)
                        base = mid[m, 0, half_edge + low : half_edge + high, :]
                        local = slice(low - g * band, high - g * band)
                        base = (base.astype(jnp.float32) + mixed[local] * sigma[local]).astype(jnp.bfloat16)
                        out_ref[m, low - half_edge : high - half_edge, :] = base

        def store_grads(left, right):
            got = dot_tn(left, jnp.concatenate(right, axis=0))
            for c in range(pieces):
                grads[pl.ds(c, width // blocks, stride=pieces), :] = got[:, c * lanes : (c + 1) * lanes]

        @pl.when(seg == 0)
        def _():
            second_section(w, s, gates, False)
            out_ref[...] = early_out[...]
            apply_back(w, gates, feat)
            for m in range(members):
                for g in range(ns):
                    at = (m * ns + g) * cells * BASIS
                    got = dot(backward[g], feat[at : at + BASIS * cells, :]).reshape(blocks, win, channels)
                    if g == 0:
                        pull[m, :, :win, :] = got
                    else:
                        pull[m, :, g * band : (g + 1) * band, :] += got[:, :band]
                        pull[m, :, (g + 1) * band : g * band + win, :] = got[:, band:]
            right = []
            step = half_edge
            for m in range(members):
                for g in range(ns):
                    at = (m * ns + g) * cells
                    span = slice(half_edge + g * band, half_edge + (g + 1) * band)
                    value = (coming_at(m, g) + pull[m, :, span, :].reshape(cells, channels)).astype(jnp.bfloat16)
                    low, high = own_part(g)
                    next_ref[m, low - half_edge : high - half_edge, :] = value[low - g * band : high - g * band]
                    tilt = slope[m, :, g * band : (g + 1) * band, :].reshape(cells, channels)
                    gate_ref[at : at + cells, :] = (value.astype(jnp.float32) * tilt).astype(jnp.bfloat16)
                for g in range(1, nf - 1):
                    for q in range(blocks):
                        for o in range(0, band, step):
                            spot = half_edge + (g - 1) * band + o
                            turn, rest = spot // band, spot % band
                            at = (m * ns + turn) * cells + q * band + rest
                            right.append(gate_ref[at : at + step, :])
            store_grads(left0[...], right)

        @pl.when(seg == 1)
        def _():
            first_section(blk, w, s, s1, again, mid, None)
            second_section(w_own, s1, gate_ref, True)
            left, right = [], []
            for m in range(members):
                next_ref[m, :, :] = b0[m, own : 2 * own, :]
                for g in range(ns):
                    low, high = own_part(g)
                    for q in range(blocks):
                        at = (m * ns + g) * cells + q * band - g * band
                        left.append(s1[at + low : at + high, columns_of(lon)])
                        right.append(gate_ref[at + low : at + high, :])
            store_grads(jnp.concatenate(left, axis=0), right)

        share = width // blocks // lat_devices * pieces

        def rows_of(index):
            return grads[pl.ds(pl.multiple_of(index * share, share), share), :]

        own_ref[...] = rows_of(lat)
        for bit, ref in ((1, p1), (2, p2), (3, p3)):
            ref[...] = rows_of(lat ^ bit).astype(jnp.bfloat16)

    def finish(w_own, backward, gates, next_ref, last_ref, grad_ref, out_ref, feat, pull):
        apply_back(w_own, gates, feat)
        for m in range(members):
            for g in range(ns):
                at = (m * ns + g) * cells * BASIS
                got = dot(backward[g, 0:win, :], feat[at : at + BASIS * cells, :])
                if g == 0:
                    pull[m, :win, :] = got
                else:
                    pull[m, g * band : (g + 1) * band, :] += got[:band]
                    pull[m, (g + 1) * band : g * band + win, :] = got[band:]
            total = next_ref[m].astype(jnp.float32) + pull[m, edge : edge + own, :]
            grad_ref[m] = total.astype(jnp.bfloat16).reshape(lat_rows, lon_cols, channels)
            out_ref[m] = last_ref[m].reshape(lat_rows, lon_cols, channels)

    return prep, edges, maps, early, chain, finish


def add_up(scale, mine, p1, p2, p3, out):
    out[...] = (mine[...] + p1[...].astype(jnp.float32) + p2[...].astype(jnp.float32) + p3[...].astype(jnp.float32)) * scale


def whole_ring(inputs, cotangent, weights, basis_values, lat_step, lon_step):
    members, lat_rows, lon_cols, channels = inputs.shape
    blocks = lax.axis_size("lon")
    lat_devices = lax.axis_size("lat")
    lat_total = lat_rows * lat_devices
    grad_scale = 1.0 / math.sqrt(members * lat_total * lon_cols * blocks)
    own = lat_rows * lon_cols
    edge = HALO * lon_cols
    half_edge = edge // 2
    halo = edge + half_edge
    width = BASIS * channels
    half_type, full_type = jnp.bfloat16, jnp.float32
    shape = jax.ShapeDtypeStruct
    first, second = window_plan(lat_rows)
    nf, ns = len(first), len(second)
    cells = blocks * BAND * lon_cols
    win = 16 * lon_cols
    vmem = pl.BlockSpec(memory_space=pltpu.VMEM)
    anywhere = pl.BlockSpec(memory_space=pltpu.HBM)

    def call(body, name, outs, ins, mib, gflops, scratch=(), far=()):
        return pl.pallas_call(
            body,
            out_shape=outs,
            in_specs=[anywhere if i in far else vmem for i, a in enumerate(ins)],
            out_specs=(vmem,) * len(outs),
            scratch_shapes=list(scratch),
            compiler_params=pltpu.CompilerParams(vmem_limit_bytes=int(mib * 1024 * 1024)),
            cost_estimate=pl.CostEstimate(flops=int(gflops * 1e9), bytes_accessed=int(gflops * 1e6), transcendentals=0),
            name=name,
        )(*ins)

    prep, edges, maps, early, chain, finish = make_steps(lat_rows, lon_cols, blocks, members, channels, lat_devices)
    kernel = weights.reshape(width, channels)
    rest = width // 2 // 12
    rows = width // 2 - rest
    half = lax.dynamic_slice_in_dim(kernel, lax.axis_index("lon") % 2 * (width // 2), rows, 0)
    ends = jnp.concatenate([kernel[rows : rows + rest], kernel[width - rest :]], axis=0)
    near_half = lax.ppermute(half, "segment", swap("segment", 1))
    near_ends = lax.ppermute(ends, "segment", swap("segment", 1))
    half, inputs, cotangent = lax.optimization_barrier((half, inputs, cotangent))
    (both,) = call(prep, "prep", (shape((members, 2 * own, channels), half_type),), (inputs, cotangent), 4, 0.0)
    sides_type = shape((members, halo, channels), half_type)
    tail, head = call(edges, "edges", (sides_type, sides_type), (both,), 4, 0.0)
    up = [(i, i + 1) for i in range(lat_devices - 1)]
    down = [(i + 1, i) for i in range(lat_devices - 1)]
    both_y = lax.ppermute(both, "lon", swap("lon", 2))
    before = lax.ppermute(tail, "lat", up)
    after = lax.ppermute(head, "lat", down)
    sides = jnp.concatenate([before, after], axis=1)
    sides, both_y = lax.optimization_barrier((sides, both_y))
    sides_y = lax.ppermute(sides, "lon", swap("lon", 2))
    b0 = jnp.concatenate([both, sides], axis=1)
    b1 = lax.ppermute(b0, "lon", swap("lon", 1))
    b0, lat_step, lon_step, basis_values = lax.optimization_barrier((b0, lat_step, lon_step, basis_values))
    forward, again, backward = call(
        maps,
        "maps",
        (
            shape((nf, BASIS * cells, blocks * win), half_type),
            shape((ns, BASIS * cells, blocks * win), half_type),
            shape((ns, blocks * win, BASIS * cells), half_type),
        ),
        (lat_step.T, lon_step.T, jnp.transpose(basis_values, (1, 2, 0))),
        4,
        0.0,
        (pltpu.VMEM((48, lat_total), full_type),),
    )
    b2 = jnp.concatenate([both_y, sides_y], axis=1)
    b2, forward, near_half = lax.optimization_barrier((b2, forward, near_half))
    b3 = lax.ppermute(b2, "lon", swap("lon", 1))
    far_half = lax.ppermute(near_half, "lon", swap("lon", 1))
    s_type = (members * nf * cells, width)
    s, left, slope, early_out = call(
        early,
        "early",
        (
            shape(s_type, half_type),
            shape((members * (nf - 2) * cells, width // blocks), half_type),
            shape((members, blocks, own + edge, channels), half_type),
            shape((members, own, channels), half_type),
        ),
        (b0, b1, b2, b3, kernel, forward, again),
        12,
        3.0,
        (pltpu.VMEM(s_type, half_type), pltpu.VMEM((members, blocks, own + 2 * edge, channels), half_type)),
    )
    near_ends, s = lax.optimization_barrier((near_ends, s))
    lines = (width // blocks // lat_devices * channels // 128, 128)
    out, follow, gates, mine, *parts = call(
        chain,
        "chain",
        (
            shape((members, own, channels), half_type),
            shape((members, own, channels), half_type),
            shape((members * ns * cells, channels), half_type),
            shape(lines, full_type),
        )
        + (shape(lines, half_type),) * 3,
        (b0, b1, b2, b3, kernel, near_half, far_half, near_ends, again, backward, s, left, slope, early_out),
        18,
        6.0,
        (
            pltpu.VMEM((width, channels), half_type),
            pltpu.VMEM((members * ns * cells, width), half_type),
            pltpu.VMEM((members, blocks, own + 2 * edge, channels), half_type),
            pltpu.VMEM((members * ns * cells, channels), half_type),
            pltpu.VMEM((members * ns * cells * BASIS, channels), half_type),
            pltpu.VMEM((members, blocks, own + 2 * edge, channels), full_type),
            pltpu.VMEM((width // blocks * channels // 128, 128), full_type),
        ),
    )
    got = [lax.ppermute(part, "lat", swap("lat", bit)) for bit, part in reversed(list(zip((1, 2, 3), parts)))]
    block = (members, lat_rows, lon_cols, channels)
    grad, out = call(
        finish,
        "finish",
        (shape(block, half_type),) * 2,
        (kernel, backward, gates, follow, out),
        10,
        2.0,
        (
            pltpu.VMEM((members * ns * cells * BASIS, channels), half_type),
            pltpu.VMEM((members, own + 2 * edge, channels), full_type),
        ),
    )
    (total,) = call(functools.partial(add_up, grad_scale), "add_up", (shape(lines, full_type),), (mine, *got), 2, 0.1)
    return (out[None], grad[None], total.reshape(1, lines[0] * lines[1]))


def fits_ring(mesh, inputs):
    sizes = dict(mesh.shape)
    rows, cols = inputs.shape[1] // sizes["lat"], inputs.shape[2] // sizes["lon"]
    return sizes["segment"] == 2 and sizes["lon"] == 4 and sizes["lat"] == 4 and rows == 16 and cols == 4


def solution(mesh):
    def apply(*args):
        body = whole_ring if fits_ring(mesh, args[0]) else per_device
        return jax.shard_map(
            body,
            mesh=mesh,
            in_specs=(
                P(None, "lat", "lon", None),
                P(None, "lat", "lon", None),
                P("segment", None, None, None),
                P(),
                P(),
                P(),
            ),
            out_specs=(
                P("segment", None, "lat", "lon", None),
                P("segment", None, "lat", "lon", None),
                P("segment", ("lon", "lat")),
            ),
            check_vma=False,
        )(*args)

    return apply
```

```python
import functools
import math

import jax
import jax.numpy as jnp
from jax import lax
from jax.experimental import pallas as pl
from jax.experimental.pallas import tpu as pltpu
from jax.sharding import PartitionSpec as P

BASIS = 3
TAPS = 9
REACH = 2


def with_halo(array, sides, width):
    for axis, dim in sides:
        size, length = (lax.axis_size(axis), array.shape[dim])
        up = [(i, (i + 1) % size) for i in range(size)]
        down = [(j, i) for i, j in up]
        last = lax.slice_in_dim(array, length - width, length, axis=dim)
        first = lax.slice_in_dim(array, 0, width, axis=dim)
        before = lax.ppermute(last, axis, up)
        after = lax.ppermute(first, axis, down)
        array = jnp.concatenate([before, array, after], axis=dim)
    return array


def shifted(block, axis, distance):
    devices = range(lax.axis_size(axis))
    route = [(i - distance, i) for i in devices if i - distance in devices]
    return lax.ppermute(block, axis, route)


def widen(features):
    return with_halo(features, (("lon", 2), ("lat", 1)), REACH)


def pass_ahead(result):
    return shifted(result, "segment", 1)


def pass_behind(result):
    return shifted(result, "segment", -1)


def build_tables(basis_values, lat_step, lon_step, lat_rows, lon_cols, lat_index, lat_total):
    pad_rows = lat_rows + 2 * REACH
    pad_cols = lon_cols + 2 * REACH
    lat_padded = jnp.pad(lat_step, ((REACH, REACH), (0, 0)))
    lon_padded = jnp.pad(lon_step, ((REACH, REACH), (0, 0)))
    basis_padded = jnp.pad(basis_values, ((REACH, REACH), (0, 0), (0, 0)))
    row_start = lat_index * lat_rows
    lat_near = lax.dynamic_slice_in_dim(lat_padded, row_start, pad_rows, 0)
    lon_near = lax.dynamic_slice_in_dim(lon_padded, row_start, pad_rows, 0)
    basis_near = lax.dynamic_slice_in_dim(basis_padded, row_start, pad_rows, 0)
    lat_own = lat_near[REACH : REACH + lat_rows]
    lon_own = lon_near[REACH : REACH + lat_rows]
    basis_own = basis_near[REACH : REACH + lat_rows]
    own_rows = row_start + jnp.arange(lat_rows)
    inside = (own_rows[:, None] + lat_own >= 0) & (own_rows[:, None] + lat_own < lat_total)
    row_grid = jnp.arange(lat_rows)[:, None, None]
    col_grid = jnp.arange(lon_cols)[None, :, None]
    source = (row_grid + REACH + lat_own[:, None, :]) * pad_cols + (
        col_grid + REACH + lon_own[:, None, :]
    )
    tap_weight = jnp.where(inside[:, None, :, None], basis_own[:, None, :, :], 0.0)
    tap_weight = jnp.broadcast_to(tap_weight, (lat_rows, lon_cols, TAPS, BASIS))
    picker = (source[..., None] == jnp.arange(pad_rows * pad_cols)).astype(jnp.float32)
    forward_map = jnp.einsum("ijkb,ijks->bijs", tap_weight, picker, precision=lax.Precision.HIGHEST)
    forward_map = forward_map.reshape(BASIS, lat_rows * lon_cols, pad_rows * pad_cols)
    near_rows = row_start - REACH + jnp.arange(pad_rows)
    real_row = (near_rows >= 0) & (near_rows < lat_total)
    pad_row_grid = jnp.arange(pad_rows)[:, None, None]
    pad_col_grid = jnp.arange(pad_cols)[None, :, None]
    target_row = pad_row_grid - REACH + lat_near[:, None, :]
    target_col = pad_col_grid - REACH + lon_near[:, None, :]
    landed = (
        (target_row >= 0)
        & (target_row < lat_rows)
        & (target_col >= 0)
        & (target_col < lon_cols)
        & real_row[:, None, None]
    )
    target = target_row * lon_cols + target_col
    back_weight = jnp.where(landed[..., None], basis_near[:, None, :, :], 0.0)
    catcher = (target[..., None] == jnp.arange(lat_rows * lon_cols)).astype(jnp.float32)
    backward_map = jnp.einsum(
        "pqkb,pqkt->btpq", back_weight, catcher, precision=lax.Precision.HIGHEST
    )
    backward_map = backward_map.reshape(BASIS, lat_rows * lon_cols, pad_rows * pad_cols)
    return (forward_map, backward_map)


def per_device(inputs, cotangent, weights, basis_values, lat_step, lon_step):
    members, lat_rows, lon_cols, channels = inputs.shape
    pad_rows = lat_rows + 2 * REACH
    pad_cols = lon_cols + 2 * REACH
    cells = lat_rows * lon_cols
    lat_index = lax.axis_index("lat")
    lat_total = lat_rows * lax.axis_size("lat")
    segment_index = lax.axis_index("segment")
    depth = lax.axis_size("segment")
    grad_scale = 1.0 / math.sqrt(members * lat_total * lon_cols * lax.axis_size("lon"))
    forward_map, backward_map = build_tables(
        basis_values, lat_step, lon_step, lat_rows, lon_cols, lat_index, lat_total
    )
    kernel = weights[0]
    keep_spread = jnp.zeros((BASIS, members, cells, channels), jnp.bfloat16)
    keep_mixed = jnp.zeros((members, cells, channels), jnp.float32)
    keep_gate = jnp.zeros((members, cells, channels), jnp.bfloat16)
    section_out = jnp.zeros(inputs.shape, jnp.bfloat16)
    section_grad = jnp.zeros(inputs.shape, jnp.bfloat16)
    carry = inputs
    for tick_num in range(depth):
        layer_count = carry.shape[0]
        layer_padded = (
            widen(carry).reshape(layer_count, pad_rows * pad_cols, channels).astype(jnp.float32)
        )
        spread = jnp.einsum(
            "bts,msc->bmtc", forward_map, layer_padded, precision=lax.Precision.HIGHEST
        ).astype(jnp.bfloat16)
        layer_mixed = jnp.einsum(
            "bmtc,bcd->mtd", spread, kernel, preferred_element_type=jnp.float32
        )
        result = (
            carry.reshape(layer_count, cells, channels).astype(jnp.float32)
            + jax.nn.silu(layer_mixed)
        ).astype(jnp.bfloat16)
        spread, mixed, result = (spread, layer_mixed, result.reshape(carry.shape))
        here = segment_index == tick_num
        keep_spread = jnp.where(here, spread, keep_spread)
        keep_mixed = jnp.where(here, mixed, keep_mixed)
        section_out = jnp.where(here, result, section_out)
        if tick_num + 1 < depth:
            carry = pass_ahead(result)
    grad = cotangent
    for tick_num in range(depth):
        count = grad.shape[0]
        flat_grad = grad.reshape(count, cells, channels).astype(jnp.float32)
        sigma = jax.nn.sigmoid(keep_mixed)
        gate_grad = (flat_grad * sigma * (1.0 + keep_mixed * (1.0 - sigma))).astype(jnp.bfloat16)
        feature_grad = jnp.einsum(
            "mtd,bcd->bmtc", gate_grad, kernel, preferred_element_type=jnp.float32
        ).astype(jnp.bfloat16)
        padded = widen(feature_grad.reshape(BASIS * count, lat_rows, lon_cols, channels))
        padded = padded.reshape(BASIS, count, pad_rows * pad_cols, channels).astype(jnp.float32)
        pulled = jnp.einsum("bts,bmsc->mtc", backward_map, padded, precision=lax.Precision.HIGHEST)
        new_grad = (flat_grad + pulled).astype(jnp.bfloat16).reshape(grad.shape)
        gate_grad, new_grad = (gate_grad, new_grad)
        here = segment_index == depth - 1 - tick_num
        keep_gate = jnp.where(here, gate_grad, keep_gate)
        section_grad = jnp.where(here, new_grad, section_grad)
        if tick_num + 1 < depth:
            grad = pass_behind(new_grad)
    local_grad = (
        jnp.einsum("bmtc,mtd->bcd", keep_spread, keep_gate, preferred_element_type=jnp.float32)
        * grad_scale
    )
    owners = lax.axis_size("lon") * lax.axis_size("lat")
    grad_rows = local_grad.reshape(owners, -1)
    weight_grad = lax.psum_scatter(grad_rows, ("lon", "lat"), scatter_dimension=0, tiled=True)
    return (section_out[None], section_grad[None], weight_grad)


HALO = 8
BAND = 8


def swap(axis, bit):
    return [(i, i ^ bit) for i in range(lax.axis_size(axis))]


def window_plan(lat_rows):
    first = [(a, min(max(a - 4, -HALO), lat_rows + HALO - 16)) for a in range(-HALO, lat_rows + HALO, BAND)]
    second = [(a, a - 4) for a in range(-4, lat_rows + 4, BAND)]
    return first, second


def dot(a, b):
    return jnp.dot(a, b, preferred_element_type=jnp.float32)


def dot_nt(a, b):
    return lax.dot_general(a, b, (((1,), (1,)), ((), ())), preferred_element_type=jnp.float32)


def dot_tn(a, b):
    return lax.dot_general(a, b, (((0,), (0,)), ((), ())), preferred_element_type=jnp.float32)


def make_steps(lat_rows, lon_cols, blocks, members, channels, lat_devices):
    first, second = window_plan(lat_rows)
    nf, ns = len(first), len(second)
    lat_total = lat_rows * lat_devices
    ring = lon_cols * blocks
    band = BAND * lon_cols
    cells = blocks * band
    win = 16 * lon_cols
    own = lat_rows * lon_cols
    edge = HALO * lon_cols
    half_edge = edge // 2
    width = BASIS * channels
    lanes = 128
    pieces = channels // lanes
    halo = edge + half_edge
    state_parts = ((0, edge, 2 * own), (edge, own, 0), (edge + own, edge, 2 * own + halo))
    coming_parts = (
        (0, half_edge, 2 * own + edge),
        (half_edge, own, own),
        (half_edge + own, half_edge, 2 * own + halo + edge),
    )

    def take(blks, m, parts, low, high):
        found = []
        for r in blks:
            for start, size, at in parts:
                lo, hi = max(low, start), min(high, start + size)
                if lo < hi:
                    found.append(r[m, at + lo - start : at + hi - start, :])
        return jnp.concatenate(found, axis=0)

    def prep(loaded, both):
        for m in range(members):
            both[m, :own, :] = loaded[m].reshape(own, channels)
            both[m, own:, :] = loaded[members + m].reshape(own, channels)

    def edges(both, tail, head):
        for m in range(members):
            tail[m, :edge, :] = both[m, own - edge : own, :]
            tail[m, edge:, :] = both[m, 2 * own - half_edge :, :]
            head[m, :edge, :] = both[m, :edge, :]
            head[m, edge:, :] = both[m, own : own + half_edge, :]

    def maps(plan, lat_step, lon_step, basis, *outs):
        forward, tab = outs[0], outs[-1]
        lon, lat = lax.axis_index("lon"), lax.axis_index("lat")
        base = lat * lat_rows
        tab[...] = jnp.zeros(tab.shape, jnp.float32)
        tab[0:TAPS, :] = lat_step[...].astype(jnp.float32)
        tab[TAPS : 2 * TAPS, :] = lon_step[...].astype(jnp.float32)
        for k in range(TAPS):
            tab[2 * TAPS + k * BASIS : 2 * TAPS + (k + 1) * BASIS, :] = basis[k]
        table = tab[...].astype(jnp.bfloat16)
        source = lax.broadcasted_iota(jnp.int32, (tab.shape[1], cells), 0)
        lane = lax.broadcasted_iota(jnp.int32, (1, cells), 1)
        block, rest = lane // band, lane % band
        row_in, col_in = rest // lon_cols, rest % lon_cols
        column_home = (block ^ lon) * lon_cols + col_in
        piece = 64
        spot = lax.broadcasted_iota(jnp.int32, (piece, cells), 0)
        for i, (a, start) in enumerate(plan):
            row = row_in + (base + a)
            got = dot(table, (source == row).astype(jnp.bfloat16))
            step_lat = got[0:TAPS].astype(jnp.int32)
            step_lon = got[TAPS : 2 * TAPS].astype(jnp.int32)
            target = row + step_lat
            inside = (row >= 0) & (row < lat_total) & (target >= 0) & (target < lat_total)
            column = column_home + step_lon
            column = jnp.where(column < 0, column + ring, column)
            column = jnp.where(column >= ring, column - ring, column)
            local = target - (base + start)
            place = ((column // lon_cols) ^ lon) * win + local * lon_cols + column % lon_cols
            place = jnp.where(inside, place, -1)
            for p in range(0, blocks * win, piece):
                tables = [jnp.zeros((piece, cells), jnp.float32) for _ in range(BASIS)]
                for k in range(TAPS):
                    hit = spot == place[k : k + 1] - p
                    for b in range(BASIS):
                        at = 2 * TAPS + k * BASIS + b
                        tables[b] = tables[b] + jnp.where(hit, got[at : at + 1], 0.0)
                for b in range(BASIS):
                    span = slice(b * cells, (b + 1) * cells)
                    forward[i, span, p : p + piece] = tables[b].T.astype(jnp.bfloat16)
                    if len(outs) == 3:
                        outs[1][i, p : p + piece, span] = tables[b].astype(jnp.bfloat16)

    def put_spread(got, into, at):
        for b in range(BASIS):
            into[at : at + cells, b * channels : (b + 1) * channels] = got[b * cells : (b + 1) * cells]

    def spread(blk, forward, into):
        for m in range(members):
            for g, (a, start) in enumerate(first):
                o = (start + HALO) * lon_cols
                near = take(blk, m, state_parts, o, o + win)
                put_spread(dot(forward[g], near).astype(jnp.bfloat16), into, (m * nf + g) * cells)

    def first_section(blk, w, s0, s1, again, mid, slope):
        for m in range(members):
            total = dot(s0[m * nf * cells : (m + 1) * nf * cells, :], w[...])
            for g in range(nf):
                mixed = total[g * cells : (g + 1) * cells]
                sigma = jax.nn.sigmoid(mixed)
                here = take(blk, m, state_parts, g * band, (g + 1) * band)
                value = (here.astype(jnp.float32) + mixed * sigma).astype(jnp.bfloat16)
                mid[m, :, g * band : (g + 1) * band, :] = value.reshape(blocks, band, channels)
                if slope is not None:
                    tilt = (sigma * (1.0 + mixed * (1.0 - sigma))).astype(slope.dtype).reshape(blocks, band, channels)
                    low, high = max(g * band, half_edge), min((g + 1) * band, 3 * half_edge + own)
                    slope[m, :, low - half_edge : high - half_edge, :] = tilt[:, low - g * band : high - g * band]
            for g in range(ns):
                near = mid[m, :, g * band : g * band + win, :].reshape(blocks * win, channels)
                put_spread(dot(again[g], near).astype(jnp.bfloat16), s1, (m * ns + g) * cells)

    def columns_of(lon):
        return pl.ds(pl.multiple_of(lon * (width // blocks), 128), width // blocks)

    def early(b0, b1, b2, b3, w_own, forward, again, s, left, slope, out, s0, mid):
        blk = (b0, b1, b2, b3)

        @pl.when(lax.axis_index("segment") == 0)
        def _():
            spread(blk, forward, s0)
            first_section(blk, w_own, s0, s, again, mid, slope)
            for m in range(members):
                size = (nf - 2) * cells
                left[m * size : (m + 1) * size, :] = s0[(m * nf + 1) * cells : (m * nf + nf - 1) * cells, columns_of(lax.axis_index("lon"))]
                out[m, :, :] = mid[m, 0, edge : edge + own, :]

        @pl.when(lax.axis_index("segment") == 1)
        def _():
            spread(blk, forward, s)

    def own_part(g):
        return max(g * band, half_edge), min((g + 1) * band, half_edge + own)

    def apply_back(w, gates, feat):
        for b in range(BASIS):
            got = dot_nt(gates[...], w[b * channels : (b + 1) * channels, :]).astype(jnp.bfloat16)
            for i in range(members * ns):
                feat[(i * BASIS + b) * cells : (i * BASIS + b + 1) * cells, :] = got[i * cells : (i + 1) * cells]

    def chain(b0, b1, b2, b3, w_own, near_half, far_half, ends, again, backward, s, left0, slope, early_out,
              out_ref, next_ref, gate_ref, own_ref, p1, p2, p3, w, s1, mid, gates, feat, pull, grads):
        blk = (b0, b1, b2, b3)
        seg, lon, lat = lax.axis_index("segment"), lax.axis_index("lon"), lax.axis_index("lat")
        here = lon % 2 * (width // 2)
        there = width // 2 - here
        rows, rest = near_half.shape[0], ends.shape[0] // 2
        for base, ref in ((here, near_half), (there, far_half)):
            w[pl.ds(pl.multiple_of(base, 32), rows), :] = ref[...]
        w[rows : rows + rest, :] = ends[:rest]
        w[width - rest :, :] = ends[rest:]

        def coming_at(m, g):
            return take(blk, m, coming_parts, g * band, (g + 1) * band).astype(jnp.float32)

        def second_section(weight, spread_ref, into, last):
            for m in range(members):
                total = dot(spread_ref[m * ns * cells : (m + 1) * ns * cells, :], weight[...])
                for g in range(ns):
                    at = (m * ns + g) * cells
                    mixed = total[g * cells : (g + 1) * cells]
                    sigma = jax.nn.sigmoid(mixed)
                    into[at : at + cells, :] = (coming_at(m, g) * sigma * (1.0 + mixed * (1.0 - sigma))).astype(jnp.bfloat16)
                    if last:
                        low, high = own_part(g)
                        base = mid[m, 0, half_edge + low : half_edge + high, :]
                        local = slice(low - g * band, high - g * band)
                        base = (base.astype(jnp.float32) + mixed[local] * sigma[local]).astype(jnp.bfloat16)
                        out_ref[m, low - half_edge : high - half_edge, :] = base

        def store_grads(left, right):
            got = dot_tn(left, jnp.concatenate(right, axis=0))
            for c in range(pieces):
                grads[pl.ds(c, width // blocks, stride=pieces), :] = got[:, c * lanes : (c + 1) * lanes]

        @pl.when(seg == 0)
        def _():
            second_section(w, s, gates, False)
            out_ref[...] = early_out[...]
            apply_back(w, gates, feat)
            for m in range(members):
                for g in range(ns):
                    at = (m * ns + g) * cells * BASIS
                    got = dot(backward[g], feat[at : at + BASIS * cells, :]).reshape(blocks, win, channels)
                    if g == 0:
                        pull[m, :, :win, :] = got
                    else:
                        pull[m, :, g * band : (g + 1) * band, :] += got[:, :band]
                        pull[m, :, (g + 1) * band : g * band + win, :] = got[:, band:]
            right = []
            step = half_edge
            for m in range(members):
                for g in range(ns):
                    at = (m * ns + g) * cells
                    span = slice(half_edge + g * band, half_edge + (g + 1) * band)
                    value = (coming_at(m, g) + pull[m, :, span, :].reshape(cells, channels)).astype(jnp.bfloat16)
                    low, high = own_part(g)
                    next_ref[m, low - half_edge : high - half_edge, :] = value[low - g * band : high - g * band]
                    tilt = slope[m, :, g * band : (g + 1) * band, :].reshape(cells, channels)
                    gate_ref[at : at + cells, :] = (value.astype(jnp.float32) * tilt).astype(jnp.bfloat16)
                for g in range(1, nf - 1):
                    for q in range(blocks):
                        for o in range(0, band, step):
                            spot = half_edge + (g - 1) * band + o
                            turn, rest = spot // band, spot % band
                            at = (m * ns + turn) * cells + q * band + rest
                            right.append(gate_ref[at : at + step, :])
            store_grads(left0[...], right)

        @pl.when(seg == 1)
        def _():
            first_section(blk, w, s, s1, again, mid, None)
            second_section(w_own, s1, gate_ref, True)
            left, right = [], []
            for m in range(members):
                next_ref[m, :, :] = b0[m, own : 2 * own, :]
                for g in range(ns):
                    low, high = own_part(g)
                    for q in range(blocks):
                        at = (m * ns + g) * cells + q * band - g * band
                        left.append(s1[at + low : at + high, columns_of(lon)])
                        right.append(gate_ref[at + low : at + high, :])
            store_grads(jnp.concatenate(left, axis=0), right)

        share = width // blocks // lat_devices * pieces

        def rows_of(index):
            return grads[pl.ds(pl.multiple_of(index * share, share), share), :]

        own_ref[...] = rows_of(lat)
        for bit, ref in ((1, p1), (2, p2), (3, p3)):
            ref[...] = rows_of(lat ^ bit).astype(jnp.bfloat16)

    def finish(w_own, backward, gates, next_ref, last_ref, grad_ref, out_ref, feat, pull):
        apply_back(w_own, gates, feat)
        for m in range(members):
            for g in range(ns):
                at = (m * ns + g) * cells * BASIS
                got = dot(backward[g, 0:win, :], feat[at : at + BASIS * cells, :])
                if g == 0:
                    pull[m, :win, :] = got
                else:
                    pull[m, g * band : (g + 1) * band, :] += got[:band]
                    pull[m, (g + 1) * band : g * band + win, :] = got[band:]
            total = next_ref[m].astype(jnp.float32) + pull[m, edge : edge + own, :]
            grad_ref[m] = total.astype(jnp.bfloat16).reshape(lat_rows, lon_cols, channels)
            out_ref[m] = last_ref[m].reshape(lat_rows, lon_cols, channels)

    return prep, edges, maps, early, chain, finish


def add_up(scale, mine, p1, p2, p3, out):
    out[...] = (mine[...] + p1[...].astype(jnp.float32) + p2[...].astype(jnp.float32) + p3[...].astype(jnp.float32)) * scale


def whole_ring(inputs, cotangent, weights, basis_values, lat_step, lon_step):
    members, lat_rows, lon_cols, channels = inputs.shape
    blocks = lax.axis_size("lon")
    lat_devices = lax.axis_size("lat")
    lat_total = lat_rows * lat_devices
    grad_scale = 1.0 / math.sqrt(members * lat_total * lon_cols * blocks)
    own = lat_rows * lon_cols
    edge = HALO * lon_cols
    half_edge = edge // 2
    halo = edge + half_edge
    width = BASIS * channels
    half_type, full_type = jnp.bfloat16, jnp.float32
    shape = jax.ShapeDtypeStruct
    first, second = window_plan(lat_rows)
    nf, ns = len(first), len(second)
    cells = blocks * BAND * lon_cols
    win = 16 * lon_cols
    vmem = pl.BlockSpec(memory_space=pltpu.VMEM)
    anywhere = pl.BlockSpec(memory_space=pltpu.HBM)

    def call(body, name, outs, ins, mib, gflops, scratch=(), far=()):
        return pl.pallas_call(
            body,
            out_shape=outs,
            in_specs=[anywhere if i in far else vmem for i, a in enumerate(ins)],
            out_specs=(vmem,) * len(outs),
            scratch_shapes=list(scratch),
            compiler_params=pltpu.CompilerParams(vmem_limit_bytes=int(mib * 1024 * 1024)),
            cost_estimate=pl.CostEstimate(flops=int(gflops * 1e9), bytes_accessed=int(gflops * 1e6), transcendentals=0),
            name=name,
        )(*ins)

    prep, edges, maps, early, chain, finish = make_steps(lat_rows, lon_cols, blocks, members, channels, lat_devices)
    kernel = weights.reshape(width, channels)
    rest = width // 2 // 12
    rows = width // 2 - rest
    half = lax.dynamic_slice_in_dim(kernel, lax.axis_index("lon") % 2 * (width // 2), rows, 0)
    ends = jnp.concatenate([kernel[rows : rows + rest], kernel[width - rest :]], axis=0)
    near_ends = lax.ppermute(ends, "segment", swap("segment", 1))
    half, inputs, cotangent = lax.optimization_barrier((half, inputs, cotangent))
    loaded = jnp.concatenate([inputs, cotangent], axis=0)
    (both,) = call(prep, "prep", (shape((members, 2 * own, channels), half_type),), (loaded,), 4, 0.0)
    half, both = lax.optimization_barrier((half, both))
    near_half = lax.ppermute(half, "segment", swap("segment", 1))
    sides_type = shape((members, halo, channels), half_type)
    tail, head = call(edges, "edges", (sides_type, sides_type), (both,), 4, 0.0)
    up = [(i, i + 1) for i in range(lat_devices - 1)]
    down = [(i + 1, i) for i in range(lat_devices - 1)]
    both_y = lax.ppermute(both, "lon", swap("lon", 2))
    before = lax.ppermute(tail, "lat", up)
    after = lax.ppermute(head, "lat", down)
    tables = (lat_step.T, lon_step.T, jnp.transpose(basis_values, (1, 2, 0)))
    _, _, *tables = lax.optimization_barrier((tail, head, *tables))
    (forward,) = call(
        functools.partial(maps, first),
        "maps_first",
        (shape((nf, BASIS * cells, blocks * win), half_type),),
        tables,
        4,
        0.0,
        (pltpu.VMEM((48, lat_total), full_type),),
    )
    before, after, forward = lax.optimization_barrier((before, after, forward))
    sides = jnp.concatenate([before, after], axis=1)
    sides, both_y = lax.optimization_barrier((sides, both_y))
    sides_y = lax.ppermute(sides, "lon", swap("lon", 2))
    b0 = jnp.concatenate([both, sides], axis=1)
    b1 = lax.ppermute(b0, "lon", swap("lon", 1))
    b0, *tables = lax.optimization_barrier((b0, *tables))
    again, backward = call(
        functools.partial(maps, second),
        "maps_again",
        (shape((ns, BASIS * cells, blocks * win), half_type), shape((ns, blocks * win, BASIS * cells), half_type)),
        tables,
        4,
        0.0,
        (pltpu.VMEM((48, lat_total), full_type),),
    )
    b2 = jnp.concatenate([both_y, sides_y], axis=1)
    b2, again, near_half = lax.optimization_barrier((b2, again, near_half))
    b3 = lax.ppermute(b2, "lon", swap("lon", 1))
    far_half = lax.ppermute(near_half, "lon", swap("lon", 1))
    s_type = (members * nf * cells, width)
    s, left, slope, early_out = call(
        early,
        "early",
        (
            shape(s_type, half_type),
            shape((members * (nf - 2) * cells, width // blocks), half_type),
            shape((members, blocks, own + edge, channels), half_type),
            shape((members, own, channels), half_type),
        ),
        (b0, b1, b2, b3, kernel, forward, again),
        12,
        3.0,
        (pltpu.VMEM(s_type, half_type), pltpu.VMEM((members, blocks, own + 2 * edge, channels), half_type)),
    )
    near_ends, s = lax.optimization_barrier((near_ends, s))
    lines = (width // blocks // lat_devices * channels // 128, 128)
    out, follow, gates, mine, *parts = call(
        chain,
        "chain",
        (
            shape((members, own, channels), half_type),
            shape((members, own, channels), half_type),
            shape((members * ns * cells, channels), half_type),
            shape(lines, full_type),
        )
        + (shape(lines, half_type),) * 3,
        (b0, b1, b2, b3, kernel, near_half, far_half, near_ends, again, backward, s, left, slope, early_out),
        18,
        6.0,
        (
            pltpu.VMEM((width, channels), half_type),
            pltpu.VMEM((members * ns * cells, width), half_type),
            pltpu.VMEM((members, blocks, own + 2 * edge, channels), half_type),
            pltpu.VMEM((members * ns * cells, channels), half_type),
            pltpu.VMEM((members * ns * cells * BASIS, channels), half_type),
            pltpu.VMEM((members, blocks, own + 2 * edge, channels), full_type),
            pltpu.VMEM((width // blocks * channels // 128, 128), full_type),
        ),
    )
    got = [lax.ppermute(part, "lat", swap("lat", bit)) for bit, part in reversed(list(zip((1, 2, 3), parts)))]
    block = (members, lat_rows, lon_cols, channels)
    grad, out = call(
        finish,
        "finish",
        (shape(block, half_type),) * 2,
        (kernel, backward, gates, follow, out),
        10,
        2.0,
        (
            pltpu.VMEM((members * ns * cells * BASIS, channels), half_type),
            pltpu.VMEM((members, own + 2 * edge, channels), full_type),
        ),
    )
    (total,) = call(functools.partial(add_up, grad_scale), "add_up", (shape(lines, full_type),), (mine, *got), 2, 0.1)
    return (out[None], grad[None], total.reshape(1, lines[0] * lines[1]))


def fits_ring(mesh, inputs):
    sizes = dict(mesh.shape)
    rows, cols = inputs.shape[1] // sizes["lat"], inputs.shape[2] // sizes["lon"]
    return sizes["segment"] == 2 and sizes["lon"] == 4 and sizes["lat"] == 4 and rows == 16 and cols == 4


def solution(mesh):
    def apply(*args):
        body = whole_ring if fits_ring(mesh, args[0]) else per_device
        return jax.shard_map(
            body,
            mesh=mesh,
            in_specs=(
                P(None, "lat", "lon", None),
                P(None, "lat", "lon", None),
                P("segment", None, None, None),
                P(),
                P(),
                P(),
            ),
            out_specs=(
                P("segment", None, "lat", "lon", None),
                P("segment", None, "lat", "lon", None),
                P("segment", ("lon", "lat")),
            ),
            check_vma=False,
        )(*args)

    return apply
```

```python
import functools
import math

import jax
import jax.numpy as jnp
from jax import lax
from jax.experimental import pallas as pl
from jax.experimental.pallas import tpu as pltpu
from jax.sharding import PartitionSpec as P

BASIS = 3
TAPS = 9
REACH = 2


def with_halo(array, sides, width):
    for axis, dim in sides:
        size, length = (lax.axis_size(axis), array.shape[dim])
        up = [(i, (i + 1) % size) for i in range(size)]
        down = [(j, i) for i, j in up]
        last = lax.slice_in_dim(array, length - width, length, axis=dim)
        first = lax.slice_in_dim(array, 0, width, axis=dim)
        before = lax.ppermute(last, axis, up)
        after = lax.ppermute(first, axis, down)
        array = jnp.concatenate([before, array, after], axis=dim)
    return array


def shifted(block, axis, distance):
    devices = range(lax.axis_size(axis))
    route = [(i - distance, i) for i in devices if i - distance in devices]
    return lax.ppermute(block, axis, route)


def widen(features):
    return with_halo(features, (("lon", 2), ("lat", 1)), REACH)


def pass_ahead(result):
    return shifted(result, "segment", 1)


def pass_behind(result):
    return shifted(result, "segment", -1)


def build_tables(basis_values, lat_step, lon_step, lat_rows, lon_cols, lat_index, lat_total):
    pad_rows = lat_rows + 2 * REACH
    pad_cols = lon_cols + 2 * REACH
    lat_padded = jnp.pad(lat_step, ((REACH, REACH), (0, 0)))
    lon_padded = jnp.pad(lon_step, ((REACH, REACH), (0, 0)))
    basis_padded = jnp.pad(basis_values, ((REACH, REACH), (0, 0), (0, 0)))
    row_start = lat_index * lat_rows
    lat_near = lax.dynamic_slice_in_dim(lat_padded, row_start, pad_rows, 0)
    lon_near = lax.dynamic_slice_in_dim(lon_padded, row_start, pad_rows, 0)
    basis_near = lax.dynamic_slice_in_dim(basis_padded, row_start, pad_rows, 0)
    lat_own = lat_near[REACH : REACH + lat_rows]
    lon_own = lon_near[REACH : REACH + lat_rows]
    basis_own = basis_near[REACH : REACH + lat_rows]
    own_rows = row_start + jnp.arange(lat_rows)
    inside = (own_rows[:, None] + lat_own >= 0) & (own_rows[:, None] + lat_own < lat_total)
    row_grid = jnp.arange(lat_rows)[:, None, None]
    col_grid = jnp.arange(lon_cols)[None, :, None]
    source = (row_grid + REACH + lat_own[:, None, :]) * pad_cols + (
        col_grid + REACH + lon_own[:, None, :]
    )
    tap_weight = jnp.where(inside[:, None, :, None], basis_own[:, None, :, :], 0.0)
    tap_weight = jnp.broadcast_to(tap_weight, (lat_rows, lon_cols, TAPS, BASIS))
    picker = (source[..., None] == jnp.arange(pad_rows * pad_cols)).astype(jnp.float32)
    forward_map = jnp.einsum("ijkb,ijks->bijs", tap_weight, picker, precision=lax.Precision.HIGHEST)
    forward_map = forward_map.reshape(BASIS, lat_rows * lon_cols, pad_rows * pad_cols)
    near_rows = row_start - REACH + jnp.arange(pad_rows)
    real_row = (near_rows >= 0) & (near_rows < lat_total)
    pad_row_grid = jnp.arange(pad_rows)[:, None, None]
    pad_col_grid = jnp.arange(pad_cols)[None, :, None]
    target_row = pad_row_grid - REACH + lat_near[:, None, :]
    target_col = pad_col_grid - REACH + lon_near[:, None, :]
    landed = (
        (target_row >= 0)
        & (target_row < lat_rows)
        & (target_col >= 0)
        & (target_col < lon_cols)
        & real_row[:, None, None]
    )
    target = target_row * lon_cols + target_col
    back_weight = jnp.where(landed[..., None], basis_near[:, None, :, :], 0.0)
    catcher = (target[..., None] == jnp.arange(lat_rows * lon_cols)).astype(jnp.float32)
    backward_map = jnp.einsum(
        "pqkb,pqkt->btpq", back_weight, catcher, precision=lax.Precision.HIGHEST
    )
    backward_map = backward_map.reshape(BASIS, lat_rows * lon_cols, pad_rows * pad_cols)
    return (forward_map, backward_map)


def per_device(inputs, cotangent, weights, basis_values, lat_step, lon_step):
    members, lat_rows, lon_cols, channels = inputs.shape
    pad_rows = lat_rows + 2 * REACH
    pad_cols = lon_cols + 2 * REACH
    cells = lat_rows * lon_cols
    lat_index = lax.axis_index("lat")
    lat_total = lat_rows * lax.axis_size("lat")
    segment_index = lax.axis_index("segment")
    depth = lax.axis_size("segment")
    grad_scale = 1.0 / math.sqrt(members * lat_total * lon_cols * lax.axis_size("lon"))
    forward_map, backward_map = build_tables(
        basis_values, lat_step, lon_step, lat_rows, lon_cols, lat_index, lat_total
    )
    kernel = weights[0]
    keep_spread = jnp.zeros((BASIS, members, cells, channels), jnp.bfloat16)
    keep_mixed = jnp.zeros((members, cells, channels), jnp.float32)
    keep_gate = jnp.zeros((members, cells, channels), jnp.bfloat16)
    section_out = jnp.zeros(inputs.shape, jnp.bfloat16)
    section_grad = jnp.zeros(inputs.shape, jnp.bfloat16)
    carry = inputs
    for tick_num in range(depth):
        layer_count = carry.shape[0]
        layer_padded = (
            widen(carry).reshape(layer_count, pad_rows * pad_cols, channels).astype(jnp.float32)
        )
        spread = jnp.einsum(
            "bts,msc->bmtc", forward_map, layer_padded, precision=lax.Precision.HIGHEST
        ).astype(jnp.bfloat16)
        layer_mixed = jnp.einsum(
            "bmtc,bcd->mtd", spread, kernel, preferred_element_type=jnp.float32
        )
        result = (
            carry.reshape(layer_count, cells, channels).astype(jnp.float32)
            + jax.nn.silu(layer_mixed)
        ).astype(jnp.bfloat16)
        spread, mixed, result = (spread, layer_mixed, result.reshape(carry.shape))
        here = segment_index == tick_num
        keep_spread = jnp.where(here, spread, keep_spread)
        keep_mixed = jnp.where(here, mixed, keep_mixed)
        section_out = jnp.where(here, result, section_out)
        if tick_num + 1 < depth:
            carry = pass_ahead(result)
    grad = cotangent
    for tick_num in range(depth):
        count = grad.shape[0]
        flat_grad = grad.reshape(count, cells, channels).astype(jnp.float32)
        sigma = jax.nn.sigmoid(keep_mixed)
        gate_grad = (flat_grad * sigma * (1.0 + keep_mixed * (1.0 - sigma))).astype(jnp.bfloat16)
        feature_grad = jnp.einsum(
            "mtd,bcd->bmtc", gate_grad, kernel, preferred_element_type=jnp.float32
        ).astype(jnp.bfloat16)
        padded = widen(feature_grad.reshape(BASIS * count, lat_rows, lon_cols, channels))
        padded = padded.reshape(BASIS, count, pad_rows * pad_cols, channels).astype(jnp.float32)
        pulled = jnp.einsum("bts,bmsc->mtc", backward_map, padded, precision=lax.Precision.HIGHEST)
        new_grad = (flat_grad + pulled).astype(jnp.bfloat16).reshape(grad.shape)
        gate_grad, new_grad = (gate_grad, new_grad)
        here = segment_index == depth - 1 - tick_num
        keep_gate = jnp.where(here, gate_grad, keep_gate)
        section_grad = jnp.where(here, new_grad, section_grad)
        if tick_num + 1 < depth:
            grad = pass_behind(new_grad)
    local_grad = (
        jnp.einsum("bmtc,mtd->bcd", keep_spread, keep_gate, preferred_element_type=jnp.float32)
        * grad_scale
    )
    owners = lax.axis_size("lon") * lax.axis_size("lat")
    grad_rows = local_grad.reshape(owners, -1)
    weight_grad = lax.psum_scatter(grad_rows, ("lon", "lat"), scatter_dimension=0, tiled=True)
    return (section_out[None], section_grad[None], weight_grad)


HALO = 8
BAND = 8


def swap(axis, bit):
    return [(i, i ^ bit) for i in range(lax.axis_size(axis))]


def window_plan(lat_rows):
    first = [(a, min(max(a - 4, -HALO), lat_rows + HALO - 16)) for a in range(-HALO, lat_rows + HALO, BAND)]
    second = [(a, a - 4) for a in range(-4, lat_rows + 4, BAND)]
    return first, second


def dot(a, b):
    return jnp.dot(a, b, preferred_element_type=jnp.float32)


def dot_nt(a, b):
    return lax.dot_general(a, b, (((1,), (1,)), ((), ())), preferred_element_type=jnp.float32)


def dot_tn(a, b):
    return lax.dot_general(a, b, (((0,), (0,)), ((), ())), preferred_element_type=jnp.float32)


def make_steps(lat_rows, lon_cols, blocks, members, channels, lat_devices):
    first, second = window_plan(lat_rows)
    nf, ns = len(first), len(second)
    lat_total = lat_rows * lat_devices
    ring = lon_cols * blocks
    band = BAND * lon_cols
    cells = blocks * band
    win = 16 * lon_cols
    own = lat_rows * lon_cols
    edge = HALO * lon_cols
    half_edge = edge // 2
    width = BASIS * channels
    lanes = 128
    pieces = channels // lanes
    halo = edge + half_edge
    state_parts = ((0, edge, 0, 0), (edge, own, 0, None), (edge + own, edge, 0, 1))
    coming_parts = ((0, half_edge, edge, 0), (half_edge, own, own, None), (half_edge + own, half_edge, edge, 1))

    def take(blks, m, parts, low, high):
        found = []
        odd = lax.axis_index("lat") % 2
        for r in blks:
            for start, size, at, side in parts:
                lo, hi = max(low, start), min(high, start + size)
                if lo >= hi:
                    continue
                if side is None:
                    found.append(r[m, at + lo - start : at + hi - start, :])
                else:
                    slot = odd if side else 1 - odd
                    first_row = pl.multiple_of(2 * own + at + lo - start + slot * halo, 16)
                    found.append(r[m, pl.ds(first_row, hi - lo), :])
        return jnp.concatenate(found, axis=0)

    def prep(loaded, both):
        for m in range(members):
            both[m, :own, :] = loaded[m].reshape(own, channels)
            both[m, own:, :] = loaded[members + m].reshape(own, channels)

    def edges(both, toward, away):
        tail = ((own - edge, own), (2 * own - half_edge, 2 * own))
        head = ((0, edge), (own, own + half_edge))

        def fill(spans, ref):
            for m in range(members):
                ref[m, :edge, :] = both[m, spans[0][0] : spans[0][1], :]
                ref[m, edge:, :] = both[m, spans[1][0] : spans[1][1], :]

        @pl.when(lax.axis_index("lat") % 2 == 0)
        def _():
            fill(tail, toward)
            fill(head, away)

        @pl.when(lax.axis_index("lat") % 2 == 1)
        def _():
            fill(head, toward)
            fill(tail, away)

    def maps(plan, lat_step, lon_step, basis, *outs):
        forward, tab = outs[0], outs[-1]
        lon, lat = lax.axis_index("lon"), lax.axis_index("lat")
        base = lat * lat_rows
        tab[...] = jnp.zeros(tab.shape, jnp.float32)
        tab[0:TAPS, :] = lat_step[...].astype(jnp.float32)
        tab[TAPS : 2 * TAPS, :] = lon_step[...].astype(jnp.float32)
        for k in range(TAPS):
            tab[2 * TAPS + k * BASIS : 2 * TAPS + (k + 1) * BASIS, :] = basis[k]
        table = tab[...].astype(jnp.bfloat16)
        source = lax.broadcasted_iota(jnp.int32, (tab.shape[1], cells), 0)
        lane = lax.broadcasted_iota(jnp.int32, (1, cells), 1)
        block, rest = lane // band, lane % band
        row_in, col_in = rest // lon_cols, rest % lon_cols
        column_home = (block ^ lon) * lon_cols + col_in
        piece = 64
        spot = lax.broadcasted_iota(jnp.int32, (piece, cells), 0)
        for i, (a, start) in enumerate(plan):
            row = row_in + (base + a)
            got = dot(table, (source == row).astype(jnp.bfloat16))
            step_lat = got[0:TAPS].astype(jnp.int32)
            step_lon = got[TAPS : 2 * TAPS].astype(jnp.int32)
            target = row + step_lat
            inside = (row >= 0) & (row < lat_total) & (target >= 0) & (target < lat_total)
            column = column_home + step_lon
            column = jnp.where(column < 0, column + ring, column)
            column = jnp.where(column >= ring, column - ring, column)
            local = target - (base + start)
            place = ((column // lon_cols) ^ lon) * win + local * lon_cols + column % lon_cols
            place = jnp.where(inside, place, -1)
            for p in range(0, blocks * win, piece):
                tables = [jnp.zeros((piece, cells), jnp.float32) for _ in range(BASIS)]
                for k in range(TAPS):
                    hit = spot == place[k : k + 1] - p
                    for b in range(BASIS):
                        at = 2 * TAPS + k * BASIS + b
                        tables[b] = tables[b] + jnp.where(hit, got[at : at + 1], 0.0)
                for b in range(BASIS):
                    span = slice(b * cells, (b + 1) * cells)
                    forward[i, span, p : p + piece] = tables[b].T.astype(jnp.bfloat16)
                    if len(outs) == 3:
                        outs[1][i, p : p + piece, span] = tables[b].astype(jnp.bfloat16)

    def put_spread(got, into, at):
        for b in range(BASIS):
            into[at : at + cells, b * channels : (b + 1) * channels] = got[b * cells : (b + 1) * cells]

    def spread(blk, forward, into):
        for m in range(members):
            for g, (a, start) in enumerate(first):
                o = (start + HALO) * lon_cols
                near = take(blk, m, state_parts, o, o + win)
                put_spread(dot(forward[g], near).astype(jnp.bfloat16), into, (m * nf + g) * cells)

    def first_section(blk, w, s0, s1, again, mid, slope):
        for m in range(members):
            total = dot(s0[m * nf * cells : (m + 1) * nf * cells, :], w[...])
            for g in range(nf):
                mixed = total[g * cells : (g + 1) * cells]
                sigma = 0.5 + 0.5 * jnp.tanh(0.5 * mixed)
                here = take(blk, m, state_parts, g * band, (g + 1) * band)
                value = (here.astype(jnp.float32) + mixed * sigma).astype(jnp.bfloat16)
                mid[m, :, g * band : (g + 1) * band, :] = value.reshape(blocks, band, channels)
                if slope is not None:
                    tilt = (sigma * (1.0 + mixed * (1.0 - sigma))).astype(slope.dtype).reshape(blocks, band, channels)
                    low, high = max(g * band, half_edge), min((g + 1) * band, 3 * half_edge + own)
                    slope[m, :, low - half_edge : high - half_edge, :] = tilt[:, low - g * band : high - g * band]
            for g in range(ns):
                near = mid[m, :, g * band : g * band + win, :].reshape(blocks * win, channels)
                put_spread(dot(again[g], near).astype(jnp.bfloat16), s1, (m * ns + g) * cells)

    def columns_of(lon):
        return pl.ds(pl.multiple_of(lon * (width // blocks), 128), width // blocks)

    def early(b0, b1, b2, b3, w_own, forward, again, s, left, slope, out, s0, mid):
        blk = (b0, b1, b2, b3)

        @pl.when(lax.axis_index("segment") == 0)
        def _():
            spread(blk, forward, s0)
            first_section(blk, w_own, s0, s, again, mid, slope)
            for m in range(members):
                size = (nf - 2) * cells
                left[m * size : (m + 1) * size, :] = s0[(m * nf + 1) * cells : (m * nf + nf - 1) * cells, columns_of(lax.axis_index("lon"))]
                out[m, :, :] = mid[m, 0, edge : edge + own, :]

        @pl.when(lax.axis_index("segment") == 1)
        def _():
            spread(blk, forward, s)

    def own_part(g):
        return max(g * band, half_edge), min((g + 1) * band, half_edge + own)

    def apply_back(w, gates, feat):
        for b in range(BASIS):
            got = dot_nt(gates[...], w[b * channels : (b + 1) * channels, :]).astype(jnp.bfloat16)
            for i in range(members * ns):
                feat[(i * BASIS + b) * cells : (i * BASIS + b + 1) * cells, :] = got[i * cells : (i + 1) * cells]

    def chain(b0, b1, b2, b3, w_own, near_half, far_half, ends, again, backward, s, left0, slope, early_out,
              out_ref, next_ref, gate_ref, own_ref, p1, p2, p3, w, s1, mid, gates, feat, pull, grads):
        blk = (b0, b1, b2, b3)
        seg, lon, lat = lax.axis_index("segment"), lax.axis_index("lon"), lax.axis_index("lat")
        here = lon % 2 * (width // 2)
        there = width // 2 - here
        rows, rest = near_half.shape[0], ends.shape[0] // 2
        for base, ref in ((here, near_half), (there, far_half)):
            w[pl.ds(pl.multiple_of(base, 32), rows), :] = ref[...]
        w[rows : rows + rest, :] = ends[:rest]
        w[width - rest :, :] = ends[rest:]

        def coming_at(m, g):
            return take(blk, m, coming_parts, g * band, (g + 1) * band).astype(jnp.float32)

        def second_section(weight, spread_ref, into, last):
            for m in range(members):
                total = dot(spread_ref[m * ns * cells : (m + 1) * ns * cells, :], weight[...])
                for g in range(ns):
                    at = (m * ns + g) * cells
                    mixed = total[g * cells : (g + 1) * cells]
                    sigma = 0.5 + 0.5 * jnp.tanh(0.5 * mixed)
                    into[at : at + cells, :] = (coming_at(m, g) * sigma * (1.0 + mixed * (1.0 - sigma))).astype(jnp.bfloat16)
                    if last:
                        low, high = own_part(g)
                        base = mid[m, 0, half_edge + low : half_edge + high, :]
                        local = slice(low - g * band, high - g * band)
                        base = (base.astype(jnp.float32) + mixed[local] * sigma[local]).astype(jnp.bfloat16)
                        out_ref[m, low - half_edge : high - half_edge, :] = base

        def store_grads(left, right):
            got = dot_tn(left, jnp.concatenate(right, axis=0))
            for c in range(pieces):
                grads[pl.ds(c, width // blocks, stride=pieces), :] = got[:, c * lanes : (c + 1) * lanes]

        @pl.when(seg == 0)
        def _():
            second_section(w, s, gates, False)
            out_ref[...] = early_out[...]
            apply_back(w, gates, feat)
            for m in range(members):
                for g in range(ns):
                    at = (m * ns + g) * cells * BASIS
                    got = dot(backward[g], feat[at : at + BASIS * cells, :]).reshape(blocks, win, channels)
                    if g == 0:
                        pull[m, :, :win, :] = got
                    else:
                        pull[m, :, g * band : (g + 1) * band, :] += got[:, :band]
                        pull[m, :, (g + 1) * band : g * band + win, :] = got[:, band:]
            right = []
            step = half_edge
            for m in range(members):
                for g in range(ns):
                    at = (m * ns + g) * cells
                    span = slice(half_edge + g * band, half_edge + (g + 1) * band)
                    value = (coming_at(m, g) + pull[m, :, span, :].reshape(cells, channels)).astype(jnp.bfloat16)
                    low, high = own_part(g)
                    next_ref[m, low - half_edge : high - half_edge, :] = value[low - g * band : high - g * band]
                    tilt = slope[m, :, g * band : (g + 1) * band, :].reshape(cells, channels)
                    gate_ref[at : at + cells, :] = (value.astype(jnp.float32) * tilt).astype(jnp.bfloat16)
                for g in range(1, nf - 1):
                    for q in range(blocks):
                        for o in range(0, band, step):
                            spot = half_edge + (g - 1) * band + o
                            turn, rest = spot // band, spot % band
                            at = (m * ns + turn) * cells + q * band + rest
                            right.append(gate_ref[at : at + step, :])
            store_grads(left0[...], right)

        @pl.when(seg == 1)
        def _():
            first_section(blk, w, s, s1, again, mid, None)
            second_section(w_own, s1, gate_ref, True)
            left, right = [], []
            for m in range(members):
                next_ref[m, :, :] = b0[m, own : 2 * own, :]
                for g in range(ns):
                    low, high = own_part(g)
                    for q in range(blocks):
                        at = (m * ns + g) * cells + q * band - g * band
                        left.append(s1[at + low : at + high, columns_of(lon)])
                        right.append(gate_ref[at + low : at + high, :])
            store_grads(jnp.concatenate(left, axis=0), right)

        share = width // blocks // lat_devices * pieces

        def rows_of(index):
            return grads[pl.ds(pl.multiple_of(index * share, share), share), :]

        own_ref[...] = rows_of(lat)
        for bit, ref in ((1, p1), (2, p2), (3, p3)):
            ref[...] = rows_of(lat ^ bit).astype(jnp.bfloat16)

    def finish(w_own, backward, gates, next_ref, last_ref, grad_ref, out_ref, feat, pull):
        apply_back(w_own, gates, feat)
        for m in range(members):
            for g in range(ns):
                at = (m * ns + g) * cells * BASIS
                got = dot(backward[g, 0:win, :], feat[at : at + BASIS * cells, :])
                if g == 0:
                    pull[m, :win, :] = got
                else:
                    pull[m, g * band : (g + 1) * band, :] += got[:band]
                    pull[m, (g + 1) * band : g * band + win, :] = got[band:]
            total = next_ref[m].astype(jnp.float32) + pull[m, edge : edge + own, :]
            grad_ref[m] = total.astype(jnp.bfloat16).reshape(lat_rows, lon_cols, channels)
            out_ref[m] = last_ref[m].reshape(lat_rows, lon_cols, channels)

    return prep, edges, maps, early, chain, finish


def add_up(scale, mine, p1, p2, p3, out):
    out[...] = (mine[...] + p1[...].astype(jnp.float32) + p2[...].astype(jnp.float32) + p3[...].astype(jnp.float32)) * scale


def whole_ring(inputs, cotangent, weights, basis_values, lat_step, lon_step):
    members, lat_rows, lon_cols, channels = inputs.shape
    blocks = lax.axis_size("lon")
    lat_devices = lax.axis_size("lat")
    lat_total = lat_rows * lat_devices
    grad_scale = 1.0 / math.sqrt(members * lat_total * lon_cols * blocks)
    own = lat_rows * lon_cols
    edge = HALO * lon_cols
    half_edge = edge // 2
    halo = edge + half_edge
    width = BASIS * channels
    half_type, full_type = jnp.bfloat16, jnp.float32
    shape = jax.ShapeDtypeStruct
    first, second = window_plan(lat_rows)
    nf, ns = len(first), len(second)
    cells = blocks * BAND * lon_cols
    win = 16 * lon_cols
    vmem = pl.BlockSpec(memory_space=pltpu.VMEM)
    anywhere = pl.BlockSpec(memory_space=pltpu.HBM)

    def call(body, name, outs, ins, mib, gflops, scratch=(), far=()):
        return pl.pallas_call(
            body,
            out_shape=outs,
            in_specs=[anywhere if i in far else vmem for i, a in enumerate(ins)],
            out_specs=(vmem,) * len(outs),
            scratch_shapes=list(scratch),
            compiler_params=pltpu.CompilerParams(vmem_limit_bytes=int(mib * 1024 * 1024)),
            cost_estimate=pl.CostEstimate(flops=int(gflops * 1e9), bytes_accessed=int(gflops * 1e6), transcendentals=0),
            name=name,
        )(*ins)

    prep, edges, maps, early, chain, finish = make_steps(lat_rows, lon_cols, blocks, members, channels, lat_devices)
    kernel = weights.reshape(width, channels)
    rest = width // 2 // 12
    rows = width // 2 - rest
    half = lax.dynamic_slice_in_dim(kernel, lax.axis_index("lon") % 2 * (width // 2), rows, 0)
    ends = jnp.concatenate([kernel[rows : rows + rest], kernel[width - rest :]], axis=0)
    near_ends = lax.ppermute(ends, "segment", swap("segment", 1))
    half, inputs, cotangent = lax.optimization_barrier((half, inputs, cotangent))
    loaded = jnp.concatenate([inputs, cotangent], axis=0)
    (both,) = call(prep, "prep", (shape((members, 2 * own, channels), half_type),), (loaded,), 4, 0.0)
    half, both = lax.optimization_barrier((half, both))
    near_half = lax.ppermute(half, "segment", swap("segment", 1))
    sides_type = shape((members, halo, channels), half_type)
    toward, away = call(edges, "edges", (sides_type, sides_type), (both,), 4, 0.0)
    both_y = lax.ppermute(both, "lon", swap("lon", 2))
    near_pairs = [(i, i ^ 1) for i in range(lat_devices)]
    far_pairs = [(i, j) for i in range(lat_devices) for j in [i + 1 if i % 2 else i - 1] if 0 <= j < lat_devices]
    from_near = lax.ppermute(toward, "lat", near_pairs)
    from_far = lax.ppermute(away, "lat", far_pairs)
    tables = (lat_step.T, lon_step.T, jnp.transpose(basis_values, (1, 2, 0)))
    _, _, *tables = lax.optimization_barrier((toward, away, *tables))
    (forward,) = call(
        functools.partial(maps, first),
        "maps_first",
        (shape((nf, BASIS * cells, blocks * win), half_type),),
        tables,
        4,
        0.0,
        (pltpu.VMEM((48, lat_total), full_type),),
    )
    from_near, from_far, forward = lax.optimization_barrier((from_near, from_far, forward))
    sides = jnp.concatenate([from_near, from_far], axis=1)
    sides, both_y = lax.optimization_barrier((sides, both_y))
    sides_y = lax.ppermute(sides, "lon", swap("lon", 2))
    b0 = jnp.concatenate([both, sides], axis=1)
    b1 = lax.ppermute(b0, "lon", swap("lon", 1))
    b0, *tables = lax.optimization_barrier((b0, *tables))
    again, backward = call(
        functools.partial(maps, second),
        "maps_again",
        (shape((ns, BASIS * cells, blocks * win), half_type), shape((ns, blocks * win, BASIS * cells), half_type)),
        tables,
        4,
        0.0,
        (pltpu.VMEM((48, lat_total), full_type),),
    )
    b2 = jnp.concatenate([both_y, sides_y], axis=1)
    b2, again, near_half = lax.optimization_barrier((b2, again, near_half))
    b3 = lax.ppermute(b2, "lon", swap("lon", 1))
    far_half = lax.ppermute(near_half, "lon", swap("lon", 1))
    s_type = (members * nf * cells, width)
    s, left, slope, early_out = call(
        early,
        "early",
        (
            shape(s_type, half_type),
            shape((members * (nf - 2) * cells, width // blocks), half_type),
            shape((members, blocks, own + edge, channels), half_type),
            shape((members, own, channels), half_type),
        ),
        (b0, b1, b2, b3, kernel, forward, again),
        12,
        3.0,
        (pltpu.VMEM(s_type, half_type), pltpu.VMEM((members, blocks, own + 2 * edge, channels), half_type)),
    )
    near_ends, s = lax.optimization_barrier((near_ends, s))
    lines = (width // blocks // lat_devices * channels // 128, 128)
    out, follow, gates, mine, *parts = call(
        chain,
        "chain",
        (
            shape((members, own, channels), half_type),
            shape((members, own, channels), half_type),
            shape((members * ns * cells, channels), half_type),
            shape(lines, full_type),
        )
        + (shape(lines, half_type),) * 3,
        (b0, b1, b2, b3, kernel, near_half, far_half, near_ends, again, backward, s, left, slope, early_out),
        18,
        6.0,
        (
            pltpu.VMEM((width, channels), half_type),
            pltpu.VMEM((members * ns * cells, width), half_type),
            pltpu.VMEM((members, blocks, own + 2 * edge, channels), half_type),
            pltpu.VMEM((members * ns * cells, channels), half_type),
            pltpu.VMEM((members * ns * cells * BASIS, channels), half_type),
            pltpu.VMEM((members, blocks, own + 2 * edge, channels), full_type),
            pltpu.VMEM((width // blocks * channels // 128, 128), full_type),
        ),
    )
    got = [lax.ppermute(part, "lat", swap("lat", bit)) for bit, part in reversed(list(zip((1, 2, 3), parts)))]
    block = (members, lat_rows, lon_cols, channels)
    grad, out = call(
        finish,
        "finish",
        (shape(block, half_type),) * 2,
        (kernel, backward, gates, follow, out),
        10,
        2.0,
        (
            pltpu.VMEM((members * ns * cells * BASIS, channels), half_type),
            pltpu.VMEM((members, own + 2 * edge, channels), full_type),
        ),
    )
    (total,) = call(functools.partial(add_up, grad_scale), "add_up", (shape(lines, full_type),), (mine, *got), 2, 0.1)
    return (out[None], grad[None], total.reshape(1, lines[0] * lines[1]))


def fits_ring(mesh, inputs):
    sizes = dict(mesh.shape)
    rows, cols = inputs.shape[1] // sizes["lat"], inputs.shape[2] // sizes["lon"]
    return sizes["segment"] == 2 and sizes["lon"] == 4 and sizes["lat"] == 4 and rows == 16 and cols == 4


def solution(mesh):
    def apply(*args):
        body = whole_ring if fits_ring(mesh, args[0]) else per_device
        return jax.shard_map(
            body,
            mesh=mesh,
            in_specs=(
                P(None, "lat", "lon", None),
                P(None, "lat", "lon", None),
                P("segment", None, None, None),
                P(),
                P(),
                P(),
            ),
            out_specs=(
                P("segment", None, "lat", "lon", None),
                P("segment", None, "lat", "lon", None),
                P("segment", ("lon", "lat")),
            ),
            check_vma=False,
        )(*args)

    return apply
```

```python
import functools
import math

import jax
import jax.numpy as jnp
from jax import lax
from jax.experimental import pallas as pl
from jax.experimental.pallas import tpu as pltpu
from jax.sharding import PartitionSpec as P

BASIS = 3
TAPS = 9
REACH = 2


def with_halo(array, sides, width):
    for axis, dim in sides:
        size, length = (lax.axis_size(axis), array.shape[dim])
        up = [(i, (i + 1) % size) for i in range(size)]
        down = [(j, i) for i, j in up]
        last = lax.slice_in_dim(array, length - width, length, axis=dim)
        first = lax.slice_in_dim(array, 0, width, axis=dim)
        before = lax.ppermute(last, axis, up)
        after = lax.ppermute(first, axis, down)
        array = jnp.concatenate([before, array, after], axis=dim)
    return array


def shifted(block, axis, distance):
    devices = range(lax.axis_size(axis))
    route = [(i - distance, i) for i in devices if i - distance in devices]
    return lax.ppermute(block, axis, route)


def widen(features):
    return with_halo(features, (("lon", 2), ("lat", 1)), REACH)


def pass_ahead(result):
    return shifted(result, "segment", 1)


def pass_behind(result):
    return shifted(result, "segment", -1)


def build_tables(basis_values, lat_step, lon_step, lat_rows, lon_cols, lat_index, lat_total):
    pad_rows = lat_rows + 2 * REACH
    pad_cols = lon_cols + 2 * REACH
    lat_padded = jnp.pad(lat_step, ((REACH, REACH), (0, 0)))
    lon_padded = jnp.pad(lon_step, ((REACH, REACH), (0, 0)))
    basis_padded = jnp.pad(basis_values, ((REACH, REACH), (0, 0), (0, 0)))
    row_start = lat_index * lat_rows
    lat_near = lax.dynamic_slice_in_dim(lat_padded, row_start, pad_rows, 0)
    lon_near = lax.dynamic_slice_in_dim(lon_padded, row_start, pad_rows, 0)
    basis_near = lax.dynamic_slice_in_dim(basis_padded, row_start, pad_rows, 0)
    lat_own = lat_near[REACH : REACH + lat_rows]
    lon_own = lon_near[REACH : REACH + lat_rows]
    basis_own = basis_near[REACH : REACH + lat_rows]
    own_rows = row_start + jnp.arange(lat_rows)
    inside = (own_rows[:, None] + lat_own >= 0) & (own_rows[:, None] + lat_own < lat_total)
    row_grid = jnp.arange(lat_rows)[:, None, None]
    col_grid = jnp.arange(lon_cols)[None, :, None]
    source = (row_grid + REACH + lat_own[:, None, :]) * pad_cols + (
        col_grid + REACH + lon_own[:, None, :]
    )
    tap_weight = jnp.where(inside[:, None, :, None], basis_own[:, None, :, :], 0.0)
    tap_weight = jnp.broadcast_to(tap_weight, (lat_rows, lon_cols, TAPS, BASIS))
    picker = (source[..., None] == jnp.arange(pad_rows * pad_cols)).astype(jnp.float32)
    forward_map = jnp.einsum("ijkb,ijks->bijs", tap_weight, picker, precision=lax.Precision.HIGHEST)
    forward_map = forward_map.reshape(BASIS, lat_rows * lon_cols, pad_rows * pad_cols)
    near_rows = row_start - REACH + jnp.arange(pad_rows)
    real_row = (near_rows >= 0) & (near_rows < lat_total)
    pad_row_grid = jnp.arange(pad_rows)[:, None, None]
    pad_col_grid = jnp.arange(pad_cols)[None, :, None]
    target_row = pad_row_grid - REACH + lat_near[:, None, :]
    target_col = pad_col_grid - REACH + lon_near[:, None, :]
    landed = (
        (target_row >= 0)
        & (target_row < lat_rows)
        & (target_col >= 0)
        & (target_col < lon_cols)
        & real_row[:, None, None]
    )
    target = target_row * lon_cols + target_col
    back_weight = jnp.where(landed[..., None], basis_near[:, None, :, :], 0.0)
    catcher = (target[..., None] == jnp.arange(lat_rows * lon_cols)).astype(jnp.float32)
    backward_map = jnp.einsum(
        "pqkb,pqkt->btpq", back_weight, catcher, precision=lax.Precision.HIGHEST
    )
    backward_map = backward_map.reshape(BASIS, lat_rows * lon_cols, pad_rows * pad_cols)
    return (forward_map, backward_map)


def per_device(inputs, cotangent, weights, basis_values, lat_step, lon_step):
    members, lat_rows, lon_cols, channels = inputs.shape
    pad_rows = lat_rows + 2 * REACH
    pad_cols = lon_cols + 2 * REACH
    cells = lat_rows * lon_cols
    lat_index = lax.axis_index("lat")
    lat_total = lat_rows * lax.axis_size("lat")
    segment_index = lax.axis_index("segment")
    depth = lax.axis_size("segment")
    grad_scale = 1.0 / math.sqrt(members * lat_total * lon_cols * lax.axis_size("lon"))
    forward_map, backward_map = build_tables(
        basis_values, lat_step, lon_step, lat_rows, lon_cols, lat_index, lat_total
    )
    kernel = weights[0]
    keep_spread = jnp.zeros((BASIS, members, cells, channels), jnp.bfloat16)
    keep_mixed = jnp.zeros((members, cells, channels), jnp.float32)
    keep_gate = jnp.zeros((members, cells, channels), jnp.bfloat16)
    section_out = jnp.zeros(inputs.shape, jnp.bfloat16)
    section_grad = jnp.zeros(inputs.shape, jnp.bfloat16)
    carry = inputs
    for tick_num in range(depth):
        layer_count = carry.shape[0]
        layer_padded = (
            widen(carry).reshape(layer_count, pad_rows * pad_cols, channels).astype(jnp.float32)
        )
        spread = jnp.einsum(
            "bts,msc->bmtc", forward_map, layer_padded, precision=lax.Precision.HIGHEST
        ).astype(jnp.bfloat16)
        layer_mixed = jnp.einsum(
            "bmtc,bcd->mtd", spread, kernel, preferred_element_type=jnp.float32
        )
        result = (
            carry.reshape(layer_count, cells, channels).astype(jnp.float32)
            + jax.nn.silu(layer_mixed)
        ).astype(jnp.bfloat16)
        spread, mixed, result = (spread, layer_mixed, result.reshape(carry.shape))
        here = segment_index == tick_num
        keep_spread = jnp.where(here, spread, keep_spread)
        keep_mixed = jnp.where(here, mixed, keep_mixed)
        section_out = jnp.where(here, result, section_out)
        if tick_num + 1 < depth:
            carry = pass_ahead(result)
    grad = cotangent
    for tick_num in range(depth):
        count = grad.shape[0]
        flat_grad = grad.reshape(count, cells, channels).astype(jnp.float32)
        sigma = jax.nn.sigmoid(keep_mixed)
        gate_grad = (flat_grad * sigma * (1.0 + keep_mixed * (1.0 - sigma))).astype(jnp.bfloat16)
        feature_grad = jnp.einsum(
            "mtd,bcd->bmtc", gate_grad, kernel, preferred_element_type=jnp.float32
        ).astype(jnp.bfloat16)
        padded = widen(feature_grad.reshape(BASIS * count, lat_rows, lon_cols, channels))
        padded = padded.reshape(BASIS, count, pad_rows * pad_cols, channels).astype(jnp.float32)
        pulled = jnp.einsum("bts,bmsc->mtc", backward_map, padded, precision=lax.Precision.HIGHEST)
        new_grad = (flat_grad + pulled).astype(jnp.bfloat16).reshape(grad.shape)
        gate_grad, new_grad = (gate_grad, new_grad)
        here = segment_index == depth - 1 - tick_num
        keep_gate = jnp.where(here, gate_grad, keep_gate)
        section_grad = jnp.where(here, new_grad, section_grad)
        if tick_num + 1 < depth:
            grad = pass_behind(new_grad)
    local_grad = (
        jnp.einsum("bmtc,mtd->bcd", keep_spread, keep_gate, preferred_element_type=jnp.float32)
        * grad_scale
    )
    owners = lax.axis_size("lon") * lax.axis_size("lat")
    grad_rows = local_grad.reshape(owners, -1)
    weight_grad = lax.psum_scatter(grad_rows, ("lon", "lat"), scatter_dimension=0, tiled=True)
    return (section_out[None], section_grad[None], weight_grad)


HALO = 8
BAND = 8


def swap(axis, bit):
    return [(i, i ^ bit) for i in range(lax.axis_size(axis))]


def window_plan(lat_rows):
    first = [(a, min(max(a - 4, -HALO), lat_rows + HALO - 16)) for a in range(-HALO, lat_rows + HALO, BAND)]
    second = [(a, a - 4) for a in range(-4, lat_rows + 4, BAND)]
    return first, second


def dot(a, b):
    return jnp.dot(a, b, preferred_element_type=jnp.float32)


def dot_nt(a, b):
    return lax.dot_general(a, b, (((1,), (1,)), ((), ())), preferred_element_type=jnp.float32)


def dot_tn(a, b):
    return lax.dot_general(a, b, (((0,), (0,)), ((), ())), preferred_element_type=jnp.float32)


def make_steps(lat_rows, lon_cols, blocks, members, channels, lat_devices):
    first, second = window_plan(lat_rows)
    nf, ns = len(first), len(second)
    lat_total = lat_rows * lat_devices
    ring = lon_cols * blocks
    band = BAND * lon_cols
    cells = blocks * band
    win = 16 * lon_cols
    own = lat_rows * lon_cols
    edge = HALO * lon_cols
    half_edge = edge // 2
    width = BASIS * channels
    lanes = 128
    pieces = channels // lanes
    halo = edge + half_edge
    state_parts = ((0, edge, 0, 0), (edge, own, 0, None), (edge + own, edge, 0, 1))
    coming_parts = ((0, half_edge, edge, 0), (half_edge, own, own, None), (half_edge + own, half_edge, edge, 1))

    def take(blks, m, parts, low, high):
        found = []
        odd = lax.axis_index("lat") % 2
        for r in blks:
            for start, size, at, side in parts:
                lo, hi = max(low, start), min(high, start + size)
                if lo >= hi:
                    continue
                if side is None:
                    found.append(r[m, at + lo - start : at + hi - start, :])
                else:
                    slot = odd if side else 1 - odd
                    first_row = pl.multiple_of(2 * own + at + lo - start + slot * halo, 16)
                    found.append(r[m, pl.ds(first_row, hi - lo), :])
        return jnp.concatenate(found, axis=0)

    def prep(loaded, both):
        for m in range(members):
            both[m, :own, :] = loaded[m].reshape(own, channels)
            both[m, own:, :] = loaded[members + m].reshape(own, channels)

    def edges(both, toward, away):
        tail = ((own - edge, own), (2 * own - half_edge, 2 * own))
        head = ((0, edge), (own, own + half_edge))

        def fill(spans, ref):
            for m in range(members):
                ref[m, :edge, :] = both[m, spans[0][0] : spans[0][1], :]
                ref[m, edge:, :] = both[m, spans[1][0] : spans[1][1], :]

        @pl.when(lax.axis_index("lat") % 2 == 0)
        def _():
            fill(tail, toward)
            fill(head, away)

        @pl.when(lax.axis_index("lat") % 2 == 1)
        def _():
            fill(head, toward)
            fill(tail, away)

    def maps(plan, lat_step, lon_step, basis, *outs):
        forward, tab = outs[0], outs[-1]
        lon, lat = lax.axis_index("lon"), lax.axis_index("lat")
        base = lat * lat_rows
        tab[...] = jnp.zeros(tab.shape, jnp.float32)
        tab[0:TAPS, :] = lat_step[...].astype(jnp.float32)
        tab[TAPS : 2 * TAPS, :] = lon_step[...].astype(jnp.float32)
        for k in range(TAPS):
            tab[2 * TAPS + k * BASIS : 2 * TAPS + (k + 1) * BASIS, :] = basis[k]
        table = tab[...].astype(jnp.bfloat16)
        source = lax.broadcasted_iota(jnp.int32, (tab.shape[1], cells), 0)
        lane = lax.broadcasted_iota(jnp.int32, (1, cells), 1)
        block, rest = lane // band, lane % band
        row_in, col_in = rest // lon_cols, rest % lon_cols
        column_home = (block ^ lon) * lon_cols + col_in
        piece = 64
        spot = lax.broadcasted_iota(jnp.int32, (piece, cells), 0)
        for i, (a, start) in enumerate(plan):
            row = row_in + (base + a)
            got = dot(table, (source == row).astype(jnp.bfloat16))
            step_lat = got[0:TAPS].astype(jnp.int32)
            step_lon = got[TAPS : 2 * TAPS].astype(jnp.int32)
            target = row + step_lat
            inside = (row >= 0) & (row < lat_total) & (target >= 0) & (target < lat_total)
            column = column_home + step_lon
            column = jnp.where(column < 0, column + ring, column)
            column = jnp.where(column >= ring, column - ring, column)
            local = target - (base + start)
            place = ((column // lon_cols) ^ lon) * win + local * lon_cols + column % lon_cols
            place = jnp.where(inside, place, -1)
            for p in range(0, blocks * win, piece):
                tables = [jnp.zeros((piece, cells), jnp.float32) for _ in range(BASIS)]
                for k in range(TAPS):
                    hit = spot == place[k : k + 1] - p
                    for b in range(BASIS):
                        at = 2 * TAPS + k * BASIS + b
                        tables[b] = tables[b] + jnp.where(hit, got[at : at + 1], 0.0)
                for b in range(BASIS):
                    span = slice(b * cells, (b + 1) * cells)
                    forward[i, span, p : p + piece] = tables[b].T.astype(jnp.bfloat16)
                    if len(outs) == 3:
                        outs[1][i, p : p + piece, span] = tables[b].astype(jnp.bfloat16)

    def put_spread(got, into, at):
        for b in range(BASIS):
            into[at : at + cells, b * channels : (b + 1) * channels] = got[b * cells : (b + 1) * cells]

    def spread(blk, forward, into):
        for m in range(members):
            for g, (a, start) in enumerate(first):
                o = (start + HALO) * lon_cols
                near = take(blk, m, state_parts, o, o + win)
                put_spread(dot(forward[g], near).astype(jnp.bfloat16), into, (m * nf + g) * cells)

    def first_section(blk, w, s0, s1, again, mid, slope):
        total = dot(s0[...], w[...])
        for m in range(members):
            for g in range(nf):
                mixed = total[(m * nf + g) * cells : (m * nf + g + 1) * cells]
                sigma = 0.5 + 0.5 * jnp.tanh(0.5 * mixed)
                here = take(blk, m, state_parts, g * band, (g + 1) * band)
                value = (here.astype(jnp.float32) + mixed * sigma).astype(jnp.bfloat16)
                mid[m, :, g * band : (g + 1) * band, :] = value.reshape(blocks, band, channels)
                if slope is not None:
                    tilt = (sigma * (1.0 + mixed * (1.0 - sigma))).astype(slope.dtype).reshape(blocks, band, channels)
                    low, high = max(g * band, half_edge), min((g + 1) * band, 3 * half_edge + own)
                    slope[m, :, low - half_edge : high - half_edge, :] = tilt[:, low - g * band : high - g * band]
            for g in range(ns):
                near = mid[m, :, g * band : g * band + win, :].reshape(blocks * win, channels)
                put_spread(dot(again[g], near).astype(jnp.bfloat16), s1, (m * ns + g) * cells)

    def columns_of(lon):
        return pl.ds(pl.multiple_of(lon * (width // blocks), 128), width // blocks)

    def early(b0, b1, b2, b3, w_own, forward, again, s, left, slope, out, s0, mid):
        blk = (b0, b1, b2, b3)

        @pl.when(lax.axis_index("segment") == 0)
        def _():
            spread(blk, forward, s0)
            first_section(blk, w_own, s0, s, again, mid, slope)
            for m in range(members):
                size = (nf - 2) * cells
                left[m * size : (m + 1) * size, :] = s0[(m * nf + 1) * cells : (m * nf + nf - 1) * cells, columns_of(lax.axis_index("lon"))]
                out[m, :, :] = mid[m, 0, edge : edge + own, :]

        @pl.when(lax.axis_index("segment") == 1)
        def _():
            spread(blk, forward, s)

    def own_part(g):
        return max(g * band, half_edge), min((g + 1) * band, half_edge + own)

    def apply_back(w, gates, feat):
        for b in range(BASIS):
            got = dot_nt(gates[...], w[b * channels : (b + 1) * channels, :]).astype(jnp.bfloat16)
            for i in range(members * ns):
                feat[(i * BASIS + b) * cells : (i * BASIS + b + 1) * cells, :] = got[i * cells : (i + 1) * cells]

    def chain(b0, b1, b2, b3, w_own, near_half, far_half, ends, again, backward, s, left0, slope, early_out,
              out_ref, next_ref, gate_ref, own_ref, p1, p2, p3, w, s1, mid, gates, feat, pull, grads):
        blk = (b0, b1, b2, b3)
        seg, lon, lat = lax.axis_index("segment"), lax.axis_index("lon"), lax.axis_index("lat")
        here = lon % 2 * (width // 2)
        there = width // 2 - here
        rows, rest = near_half.shape[0], ends.shape[0] // 2
        for base, ref in ((here, near_half), (there, far_half)):
            w[pl.ds(pl.multiple_of(base, 32), rows), :] = ref[...]
        w[rows : rows + rest, :] = ends[:rest]
        w[width - rest :, :] = ends[rest:]

        def coming_at(m, g):
            return take(blk, m, coming_parts, g * band, (g + 1) * band).astype(jnp.float32)

        def second_section(weight, spread_ref, into, last):
            total = dot(spread_ref[: members * ns * cells, :], weight[...])
            for m in range(members):
                for g in range(ns):
                    at = (m * ns + g) * cells
                    mixed = total[at : at + cells]
                    sigma = 0.5 + 0.5 * jnp.tanh(0.5 * mixed)
                    into[at : at + cells, :] = (coming_at(m, g) * sigma * (1.0 + mixed * (1.0 - sigma))).astype(jnp.bfloat16)
                    if last:
                        low, high = own_part(g)
                        base = mid[m, 0, half_edge + low : half_edge + high, :]
                        local = slice(low - g * band, high - g * band)
                        base = (base.astype(jnp.float32) + mixed[local] * sigma[local]).astype(jnp.bfloat16)
                        out_ref[m, low - half_edge : high - half_edge, :] = base

        def store_grads(left, right):
            got = dot_tn(left, jnp.concatenate(right, axis=0))
            for c in range(pieces):
                grads[pl.ds(c, width // blocks, stride=pieces), :] = got[:, c * lanes : (c + 1) * lanes]

        @pl.when(seg == 0)
        def _():
            second_section(w, s, gates, False)
            out_ref[...] = early_out[...]
            apply_back(w, gates, feat)
            for m in range(members):
                for g in range(ns):
                    at = (m * ns + g) * cells * BASIS
                    got = dot(backward[g], feat[at : at + BASIS * cells, :]).reshape(blocks, win, channels)
                    if g == 0:
                        pull[m, :, :win, :] = got
                    else:
                        pull[m, :, g * band : (g + 1) * band, :] += got[:, :band]
                        pull[m, :, (g + 1) * band : g * band + win, :] = got[:, band:]
            right = []
            step = half_edge
            for m in range(members):
                for g in range(ns):
                    at = (m * ns + g) * cells
                    span = slice(half_edge + g * band, half_edge + (g + 1) * band)
                    value = (coming_at(m, g) + pull[m, :, span, :].reshape(cells, channels)).astype(jnp.bfloat16)
                    low, high = own_part(g)
                    next_ref[m, low - half_edge : high - half_edge, :] = value[low - g * band : high - g * band]
                    tilt = slope[m, :, g * band : (g + 1) * band, :].reshape(cells, channels)
                    gate_ref[at : at + cells, :] = (value.astype(jnp.float32) * tilt).astype(jnp.bfloat16)
                for g in range(1, nf - 1):
                    for q in range(blocks):
                        for o in range(0, band, step):
                            spot = half_edge + (g - 1) * band + o
                            turn, rest = spot // band, spot % band
                            at = (m * ns + turn) * cells + q * band + rest
                            right.append(gate_ref[at : at + step, :])
            store_grads(left0[...], right)

        @pl.when(seg == 1)
        def _():
            first_section(blk, w, s, s1, again, mid, None)
            second_section(w_own, s1, gate_ref, True)
            left, right = [], []
            for m in range(members):
                next_ref[m, :, :] = b0[m, own : 2 * own, :]
                for g in range(ns):
                    low, high = own_part(g)
                    for q in range(blocks):
                        at = (m * ns + g) * cells + q * band - g * band
                        left.append(s1[at + low : at + high, columns_of(lon)])
                        right.append(gate_ref[at + low : at + high, :])
            store_grads(jnp.concatenate(left, axis=0), right)

        share = width // blocks // lat_devices * pieces

        def rows_of(index):
            return grads[pl.ds(pl.multiple_of(index * share, share), share), :]

        own_ref[...] = rows_of(lat)
        for bit, ref in ((1, p1), (2, p2), (3, p3)):
            ref[...] = rows_of(lat ^ bit).astype(jnp.bfloat16)

    def finish(w_own, backward, gates, next_ref, last_ref, grad_ref, out_ref, feat, pull):
        apply_back(w_own, gates, feat)
        for m in range(members):
            for g in range(ns):
                at = (m * ns + g) * cells * BASIS
                got = dot(backward[g, 0:win, :], feat[at : at + BASIS * cells, :])
                if g == 0:
                    pull[m, :win, :] = got
                else:
                    pull[m, g * band : (g + 1) * band, :] += got[:band]
                    pull[m, (g + 1) * band : g * band + win, :] = got[band:]
            total = next_ref[m].astype(jnp.float32) + pull[m, edge : edge + own, :]
            grad_ref[m] = total.astype(jnp.bfloat16).reshape(lat_rows, lon_cols, channels)
            out_ref[m] = last_ref[m].reshape(lat_rows, lon_cols, channels)

    return prep, edges, maps, early, chain, finish


def add_up(scale, mine, p1, p2, p3, out):
    out[...] = (mine[...] + p1[...].astype(jnp.float32) + p2[...].astype(jnp.float32) + p3[...].astype(jnp.float32)) * scale


def whole_ring(inputs, cotangent, weights, basis_values, lat_step, lon_step):
    members, lat_rows, lon_cols, channels = inputs.shape
    blocks = lax.axis_size("lon")
    lat_devices = lax.axis_size("lat")
    lat_total = lat_rows * lat_devices
    grad_scale = 1.0 / math.sqrt(members * lat_total * lon_cols * blocks)
    own = lat_rows * lon_cols
    edge = HALO * lon_cols
    half_edge = edge // 2
    halo = edge + half_edge
    width = BASIS * channels
    half_type, full_type = jnp.bfloat16, jnp.float32
    shape = jax.ShapeDtypeStruct
    first, second = window_plan(lat_rows)
    nf, ns = len(first), len(second)
    cells = blocks * BAND * lon_cols
    win = 16 * lon_cols
    vmem = pl.BlockSpec(memory_space=pltpu.VMEM)
    anywhere = pl.BlockSpec(memory_space=pltpu.HBM)

    def call(body, name, outs, ins, mib, gflops, scratch=(), far=()):
        return pl.pallas_call(
            body,
            out_shape=outs,
            in_specs=[anywhere if i in far else vmem for i, a in enumerate(ins)],
            out_specs=(vmem,) * len(outs),
            scratch_shapes=list(scratch),
            compiler_params=pltpu.CompilerParams(vmem_limit_bytes=int(mib * 1024 * 1024)),
            cost_estimate=pl.CostEstimate(flops=int(gflops * 1e9), bytes_accessed=int(gflops * 1e6), transcendentals=0),
            name=name,
        )(*ins)

    prep, edges, maps, early, chain, finish = make_steps(lat_rows, lon_cols, blocks, members, channels, lat_devices)
    kernel = weights.reshape(width, channels)
    rest = width // 2 * 7 // 48
    rows = width // 2 - rest
    half = lax.dynamic_slice_in_dim(kernel, lax.axis_index("lon") % 2 * (width // 2), rows, 0)
    ends = jnp.concatenate([kernel[rows : rows + rest], kernel[width - rest :]], axis=0)
    near_ends = lax.ppermute(ends, "segment", swap("segment", 1))
    near_half = lax.ppermute(half, "segment", swap("segment", 1))
    half, inputs, cotangent = lax.optimization_barrier((half, inputs, cotangent))
    loaded = jnp.concatenate([inputs, cotangent], axis=0)
    (both,) = call(prep, "prep", (shape((members, 2 * own, channels), half_type),), (loaded,), 4, 0.0)
    sides_type = shape((members, halo, channels), half_type)
    toward, away = call(edges, "edges", (sides_type, sides_type), (both,), 4, 0.0)
    both_y = lax.ppermute(both, "lon", swap("lon", 2))
    near_pairs = [(i, i ^ 1) for i in range(lat_devices)]
    far_pairs = [(i, j) for i in range(lat_devices) for j in [i + 1 if i % 2 else i - 1] if 0 <= j < lat_devices]
    from_near = lax.ppermute(toward, "lat", near_pairs)
    from_far = lax.ppermute(away, "lat", far_pairs)
    tables = (lat_step.T, lon_step.T, jnp.transpose(basis_values, (1, 2, 0)))
    _, _, *tables = lax.optimization_barrier((toward, away, *tables))
    (forward,) = call(
        functools.partial(maps, first),
        "maps_first",
        (shape((nf, BASIS * cells, blocks * win), half_type),),
        tables,
        4,
        0.0,
        (pltpu.VMEM((48, lat_total), full_type),),
    )
    from_near, from_far, forward = lax.optimization_barrier((from_near, from_far, forward))
    sides = jnp.concatenate([from_near, from_far], axis=1)
    sides, both_y = lax.optimization_barrier((sides, both_y))
    sides_y = lax.ppermute(sides, "lon", swap("lon", 2))
    b0 = jnp.concatenate([both, sides], axis=1)
    b1 = lax.ppermute(b0, "lon", swap("lon", 1))
    b0, *tables = lax.optimization_barrier((b0, *tables))
    again, backward = call(
        functools.partial(maps, second),
        "maps_again",
        (shape((ns, BASIS * cells, blocks * win), half_type), shape((ns, blocks * win, BASIS * cells), half_type)),
        tables,
        4,
        0.0,
        (pltpu.VMEM((48, lat_total), full_type),),
    )
    b2 = jnp.concatenate([both_y, sides_y], axis=1)
    b2, again, near_half = lax.optimization_barrier((b2, again, near_half))
    b3 = lax.ppermute(b2, "lon", swap("lon", 1))
    far_half = lax.ppermute(near_half, "lon", swap("lon", 1))
    s_type = (members * nf * cells, width)
    s, left, slope, early_out = call(
        early,
        "early",
        (
            shape(s_type, half_type),
            shape((members * (nf - 2) * cells, width // blocks), half_type),
            shape((members, blocks, own + edge, channels), half_type),
            shape((members, own, channels), half_type),
        ),
        (b0, b1, b2, b3, kernel, forward, again),
        12,
        3.0,
        (pltpu.VMEM(s_type, half_type), pltpu.VMEM((members, blocks, own + 2 * edge, channels), half_type)),
    )
    near_ends, s = lax.optimization_barrier((near_ends, s))
    lines = (width // blocks // lat_devices * channels // 128, 128)
    out, follow, gates, mine, *parts = call(
        chain,
        "chain",
        (
            shape((members, own, channels), half_type),
            shape((members, own, channels), half_type),
            shape((members * ns * cells, channels), half_type),
            shape(lines, full_type),
        )
        + (shape(lines, half_type),) * 3,
        (b0, b1, b2, b3, kernel, near_half, far_half, near_ends, again, backward, s, left, slope, early_out),
        18,
        6.0,
        (
            pltpu.VMEM((width, channels), half_type),
            pltpu.VMEM((members * ns * cells, width), half_type),
            pltpu.VMEM((members, blocks, own + 2 * edge, channels), half_type),
            pltpu.VMEM((members * ns * cells, channels), half_type),
            pltpu.VMEM((members * ns * cells * BASIS, channels), half_type),
            pltpu.VMEM((members, blocks, own + 2 * edge, channels), full_type),
            pltpu.VMEM((width // blocks * channels // 128, 128), full_type),
        ),
    )
    got = [lax.ppermute(part, "lat", swap("lat", bit)) for bit, part in reversed(list(zip((1, 2, 3), parts)))]
    block = (members, lat_rows, lon_cols, channels)
    grad, out = call(
        finish,
        "finish",
        (shape(block, half_type),) * 2,
        (kernel, backward, gates, follow, out),
        10,
        2.0,
        (
            pltpu.VMEM((members * ns * cells * BASIS, channels), half_type),
            pltpu.VMEM((members, own + 2 * edge, channels), full_type),
        ),
    )
    (total,) = call(functools.partial(add_up, grad_scale), "add_up", (shape(lines, full_type),), (mine, *got), 2, 0.1)
    return (out[None], grad[None], total.reshape(1, lines[0] * lines[1]))


def fits_ring(mesh, inputs):
    sizes = dict(mesh.shape)
    rows, cols = inputs.shape[1] // sizes["lat"], inputs.shape[2] // sizes["lon"]
    return sizes["segment"] == 2 and sizes["lon"] == 4 and sizes["lat"] == 4 and rows == 16 and cols == 4


def solution(mesh):
    def apply(*args):
        body = whole_ring if fits_ring(mesh, args[0]) else per_device
        return jax.shard_map(
            body,
            mesh=mesh,
            in_specs=(
                P(None, "lat", "lon", None),
                P(None, "lat", "lon", None),
                P("segment", None, None, None),
                P(),
                P(),
                P(),
            ),
            out_specs=(
                P("segment", None, "lat", "lon", None),
                P("segment", None, "lat", "lon", None),
                P("segment", ("lon", "lat")),
            ),
            check_vma=False,
        )(*args)

    return apply
```

```python
import functools
import math

import jax
import jax.numpy as jnp
from jax import lax
from jax.experimental import pallas as pl
from jax.experimental.pallas import tpu as pltpu
from jax.sharding import PartitionSpec as P

BASIS = 3
TAPS = 9
REACH = 2


def with_halo(array, sides, width):
    for axis, dim in sides:
        size, length = (lax.axis_size(axis), array.shape[dim])
        up = [(i, (i + 1) % size) for i in range(size)]
        down = [(j, i) for i, j in up]
        last = lax.slice_in_dim(array, length - width, length, axis=dim)
        first = lax.slice_in_dim(array, 0, width, axis=dim)
        before = lax.ppermute(last, axis, up)
        after = lax.ppermute(first, axis, down)
        array = jnp.concatenate([before, array, after], axis=dim)
    return array


def shifted(block, axis, distance):
    devices = range(lax.axis_size(axis))
    route = [(i - distance, i) for i in devices if i - distance in devices]
    return lax.ppermute(block, axis, route)


def widen(features):
    return with_halo(features, (("lon", 2), ("lat", 1)), REACH)


def pass_ahead(result):
    return shifted(result, "segment", 1)


def pass_behind(result):
    return shifted(result, "segment", -1)


def build_tables(basis_values, lat_step, lon_step, lat_rows, lon_cols, lat_index, lat_total):
    pad_rows = lat_rows + 2 * REACH
    pad_cols = lon_cols + 2 * REACH
    lat_padded = jnp.pad(lat_step, ((REACH, REACH), (0, 0)))
    lon_padded = jnp.pad(lon_step, ((REACH, REACH), (0, 0)))
    basis_padded = jnp.pad(basis_values, ((REACH, REACH), (0, 0), (0, 0)))
    row_start = lat_index * lat_rows
    lat_near = lax.dynamic_slice_in_dim(lat_padded, row_start, pad_rows, 0)
    lon_near = lax.dynamic_slice_in_dim(lon_padded, row_start, pad_rows, 0)
    basis_near = lax.dynamic_slice_in_dim(basis_padded, row_start, pad_rows, 0)
    lat_own = lat_near[REACH : REACH + lat_rows]
    lon_own = lon_near[REACH : REACH + lat_rows]
    basis_own = basis_near[REACH : REACH + lat_rows]
    own_rows = row_start + jnp.arange(lat_rows)
    inside = (own_rows[:, None] + lat_own >= 0) & (own_rows[:, None] + lat_own < lat_total)
    row_grid = jnp.arange(lat_rows)[:, None, None]
    col_grid = jnp.arange(lon_cols)[None, :, None]
    source = (row_grid + REACH + lat_own[:, None, :]) * pad_cols + (
        col_grid + REACH + lon_own[:, None, :]
    )
    tap_weight = jnp.where(inside[:, None, :, None], basis_own[:, None, :, :], 0.0)
    tap_weight = jnp.broadcast_to(tap_weight, (lat_rows, lon_cols, TAPS, BASIS))
    picker = (source[..., None] == jnp.arange(pad_rows * pad_cols)).astype(jnp.float32)
    forward_map = jnp.einsum("ijkb,ijks->bijs", tap_weight, picker, precision=lax.Precision.HIGHEST)
    forward_map = forward_map.reshape(BASIS, lat_rows * lon_cols, pad_rows * pad_cols)
    near_rows = row_start - REACH + jnp.arange(pad_rows)
    real_row = (near_rows >= 0) & (near_rows < lat_total)
    pad_row_grid = jnp.arange(pad_rows)[:, None, None]
    pad_col_grid = jnp.arange(pad_cols)[None, :, None]
    target_row = pad_row_grid - REACH + lat_near[:, None, :]
    target_col = pad_col_grid - REACH + lon_near[:, None, :]
    landed = (
        (target_row >= 0)
        & (target_row < lat_rows)
        & (target_col >= 0)
        & (target_col < lon_cols)
        & real_row[:, None, None]
    )
    target = target_row * lon_cols + target_col
    back_weight = jnp.where(landed[..., None], basis_near[:, None, :, :], 0.0)
    catcher = (target[..., None] == jnp.arange(lat_rows * lon_cols)).astype(jnp.float32)
    backward_map = jnp.einsum(
        "pqkb,pqkt->btpq", back_weight, catcher, precision=lax.Precision.HIGHEST
    )
    backward_map = backward_map.reshape(BASIS, lat_rows * lon_cols, pad_rows * pad_cols)
    return (forward_map, backward_map)


def per_device(inputs, cotangent, weights, basis_values, lat_step, lon_step):
    members, lat_rows, lon_cols, channels = inputs.shape
    pad_rows = lat_rows + 2 * REACH
    pad_cols = lon_cols + 2 * REACH
    cells = lat_rows * lon_cols
    lat_index = lax.axis_index("lat")
    lat_total = lat_rows * lax.axis_size("lat")
    segment_index = lax.axis_index("segment")
    depth = lax.axis_size("segment")
    grad_scale = 1.0 / math.sqrt(members * lat_total * lon_cols * lax.axis_size("lon"))
    forward_map, backward_map = build_tables(
        basis_values, lat_step, lon_step, lat_rows, lon_cols, lat_index, lat_total
    )
    kernel = weights[0]
    keep_spread = jnp.zeros((BASIS, members, cells, channels), jnp.bfloat16)
    keep_mixed = jnp.zeros((members, cells, channels), jnp.float32)
    keep_gate = jnp.zeros((members, cells, channels), jnp.bfloat16)
    section_out = jnp.zeros(inputs.shape, jnp.bfloat16)
    section_grad = jnp.zeros(inputs.shape, jnp.bfloat16)
    carry = inputs
    for tick_num in range(depth):
        layer_count = carry.shape[0]
        layer_padded = (
            widen(carry).reshape(layer_count, pad_rows * pad_cols, channels).astype(jnp.float32)
        )
        spread = jnp.einsum(
            "bts,msc->bmtc", forward_map, layer_padded, precision=lax.Precision.HIGHEST
        ).astype(jnp.bfloat16)
        layer_mixed = jnp.einsum(
            "bmtc,bcd->mtd", spread, kernel, preferred_element_type=jnp.float32
        )
        result = (
            carry.reshape(layer_count, cells, channels).astype(jnp.float32)
            + jax.nn.silu(layer_mixed)
        ).astype(jnp.bfloat16)
        spread, mixed, result = (spread, layer_mixed, result.reshape(carry.shape))
        here = segment_index == tick_num
        keep_spread = jnp.where(here, spread, keep_spread)
        keep_mixed = jnp.where(here, mixed, keep_mixed)
        section_out = jnp.where(here, result, section_out)
        if tick_num + 1 < depth:
            carry = pass_ahead(result)
    grad = cotangent
    for tick_num in range(depth):
        count = grad.shape[0]
        flat_grad = grad.reshape(count, cells, channels).astype(jnp.float32)
        sigma = jax.nn.sigmoid(keep_mixed)
        gate_grad = (flat_grad * sigma * (1.0 + keep_mixed * (1.0 - sigma))).astype(jnp.bfloat16)
        feature_grad = jnp.einsum(
            "mtd,bcd->bmtc", gate_grad, kernel, preferred_element_type=jnp.float32
        ).astype(jnp.bfloat16)
        padded = widen(feature_grad.reshape(BASIS * count, lat_rows, lon_cols, channels))
        padded = padded.reshape(BASIS, count, pad_rows * pad_cols, channels).astype(jnp.float32)
        pulled = jnp.einsum("bts,bmsc->mtc", backward_map, padded, precision=lax.Precision.HIGHEST)
        new_grad = (flat_grad + pulled).astype(jnp.bfloat16).reshape(grad.shape)
        gate_grad, new_grad = (gate_grad, new_grad)
        here = segment_index == depth - 1 - tick_num
        keep_gate = jnp.where(here, gate_grad, keep_gate)
        section_grad = jnp.where(here, new_grad, section_grad)
        if tick_num + 1 < depth:
            grad = pass_behind(new_grad)
    local_grad = (
        jnp.einsum("bmtc,mtd->bcd", keep_spread, keep_gate, preferred_element_type=jnp.float32)
        * grad_scale
    )
    owners = lax.axis_size("lon") * lax.axis_size("lat")
    grad_rows = local_grad.reshape(owners, -1)
    weight_grad = lax.psum_scatter(grad_rows, ("lon", "lat"), scatter_dimension=0, tiled=True)
    return (section_out[None], section_grad[None], weight_grad)


HALO = 8
BAND = 8


def swap(axis, bit):
    return [(i, i ^ bit) for i in range(lax.axis_size(axis))]


def window_plan(lat_rows):
    first = [(a, min(max(a - 4, -HALO), lat_rows + HALO - 16)) for a in range(-HALO, lat_rows + HALO, BAND)]
    second = [(a, a - 4) for a in range(-4, lat_rows + 4, BAND)]
    return first, second


def dot(a, b):
    return jnp.dot(a, b, preferred_element_type=jnp.float32)


def dot_nt(a, b):
    return lax.dot_general(a, b, (((1,), (1,)), ((), ())), preferred_element_type=jnp.float32)


def dot_tn(a, b):
    return lax.dot_general(a, b, (((0,), (0,)), ((), ())), preferred_element_type=jnp.float32)


def make_steps(lat_rows, lon_cols, blocks, members, channels, lat_devices):
    first, second = window_plan(lat_rows)
    nf, ns = len(first), len(second)
    lat_total = lat_rows * lat_devices
    ring = lon_cols * blocks
    band = BAND * lon_cols
    cells = blocks * band
    win = 16 * lon_cols
    own = lat_rows * lon_cols
    edge = HALO * lon_cols
    half_edge = edge // 2
    width = BASIS * channels
    lanes = 128
    pieces = channels // lanes
    halo = edge + half_edge
    state_parts = ((0, edge, 0, 0), (edge, own, 0, None), (edge + own, edge, 0, 1))
    coming_parts = ((0, half_edge, edge, 0), (half_edge, own, own, None), (half_edge + own, half_edge, edge, 1))

    def take(blks, m, parts, low, high):
        found = []
        odd = lax.axis_index("lat") % 2
        for r in blks:
            for start, size, at, side in parts:
                lo, hi = max(low, start), min(high, start + size)
                if lo >= hi:
                    continue
                if side is None:
                    found.append(r[m, at + lo - start : at + hi - start, :])
                else:
                    slot = odd if side else 1 - odd
                    first_row = pl.multiple_of(2 * own + at + lo - start + slot * halo, 16)
                    found.append(r[m, pl.ds(first_row, hi - lo), :])
        return jnp.concatenate(found, axis=0)

    def prep(loaded, both):
        for m in range(members):
            both[m, :own, :] = loaded[m].reshape(own, channels)
            both[m, own:, :] = loaded[members + m].reshape(own, channels)

    def edges(both, toward, away):
        tail = ((own - edge, own), (2 * own - half_edge, 2 * own))
        head = ((0, edge), (own, own + half_edge))

        def fill(spans, ref):
            for m in range(members):
                ref[m, :edge, :] = both[m, spans[0][0] : spans[0][1], :]
                ref[m, edge:, :] = both[m, spans[1][0] : spans[1][1], :]

        @pl.when(lax.axis_index("lat") % 2 == 0)
        def _():
            fill(tail, toward)
            fill(head, away)

        @pl.when(lax.axis_index("lat") % 2 == 1)
        def _():
            fill(head, toward)
            fill(tail, away)

    def maps(plan, lat_step, lon_step, basis, *outs):
        forward, tab = outs[0], outs[-1]
        lon, lat = lax.axis_index("lon"), lax.axis_index("lat")
        base = lat * lat_rows
        tab[...] = jnp.zeros(tab.shape, jnp.float32)
        tab[0:TAPS, :] = lat_step[...].astype(jnp.float32)
        tab[TAPS : 2 * TAPS, :] = lon_step[...].astype(jnp.float32)
        for k in range(TAPS):
            tab[2 * TAPS + k * BASIS : 2 * TAPS + (k + 1) * BASIS, :] = basis[k]
        table = tab[...].astype(jnp.bfloat16)
        source = lax.broadcasted_iota(jnp.int32, (tab.shape[1], cells), 0)
        lane = lax.broadcasted_iota(jnp.int32, (1, cells), 1)
        block, rest = lane // band, lane % band
        row_in, col_in = rest // lon_cols, rest % lon_cols
        column_home = (block ^ lon) * lon_cols + col_in
        piece = 64
        spot = lax.broadcasted_iota(jnp.int32, (piece, cells), 0)
        for i, (a, start) in enumerate(plan):
            row = row_in + (base + a)
            got = dot(table, (source == row).astype(jnp.bfloat16))
            step_lat = got[0:TAPS].astype(jnp.int32)
            step_lon = got[TAPS : 2 * TAPS].astype(jnp.int32)
            target = row + step_lat
            inside = (row >= 0) & (row < lat_total) & (target >= 0) & (target < lat_total)
            column = column_home + step_lon
            column = jnp.where(column < 0, column + ring, column)
            column = jnp.where(column >= ring, column - ring, column)
            local = target - (base + start)
            place = ((column // lon_cols) ^ lon) * win + local * lon_cols + column % lon_cols
            place = jnp.where(inside, place, -1)
            for p in range(0, blocks * win, piece):
                tables = [jnp.zeros((piece, cells), jnp.float32) for _ in range(BASIS)]
                for k in range(TAPS):
                    hit = spot == place[k : k + 1] - p
                    for b in range(BASIS):
                        at = 2 * TAPS + k * BASIS + b
                        tables[b] = tables[b] + jnp.where(hit, got[at : at + 1], 0.0)
                for b in range(BASIS):
                    span = slice(b * cells, (b + 1) * cells)
                    forward[i, span, p : p + piece] = tables[b].T.astype(jnp.bfloat16)
                    if len(outs) == 3:
                        outs[1][i, p : p + piece, span] = tables[b].astype(jnp.bfloat16)

    def put_spread(got, into, at):
        for b in range(BASIS):
            into[at : at + cells, b * channels : (b + 1) * channels] = got[b * cells : (b + 1) * cells]

    def spread(blk, forward, into):
        for m in range(members):
            for g, (a, start) in enumerate(first):
                o = (start + HALO) * lon_cols
                near = take(blk, m, state_parts, o, o + win)
                put_spread(dot(forward[g], near).astype(jnp.bfloat16), into, (m * nf + g) * cells)

    def first_section(blk, total, s1, again, mid, slope):
        for m in range(members):
            for g in range(nf):
                mixed = total[(m * nf + g) * cells : (m * nf + g + 1) * cells]
                sigma = 0.5 + 0.5 * jnp.tanh(0.5 * mixed)
                here = take(blk, m, state_parts, g * band, (g + 1) * band)
                value = (here.astype(jnp.float32) + mixed * sigma).astype(jnp.bfloat16)
                mid[m, :, g * band : (g + 1) * band, :] = value.reshape(blocks, band, channels)
                if slope is not None:
                    tilt = (sigma * (1.0 + mixed * (1.0 - sigma))).astype(slope.dtype).reshape(blocks, band, channels)
                    low, high = max(g * band, half_edge), min((g + 1) * band, 3 * half_edge + own)
                    slope[m, :, low - half_edge : high - half_edge, :] = tilt[:, low - g * band : high - g * band]
            for g in range(ns):
                near = mid[m, :, g * band : g * band + win, :].reshape(blocks * win, channels)
                put_spread(dot(again[g], near).astype(jnp.bfloat16), s1, (m * ns + g) * cells)

    def columns_of(lon):
        return pl.ds(pl.multiple_of(lon * (width // blocks), 128), width // blocks)

    def early(b0, b1, b2, b3, w_own, forward, again, s, left, slope, out, s0, mid):
        blk = (b0, b1, b2, b3)

        @pl.when(lax.axis_index("segment") == 0)
        def _():
            spread(blk, forward, s0)
            first_section(blk, dot(s0[...], w_own[...]), s, again, mid, slope)
            for m in range(members):
                size = (nf - 2) * cells
                left[m * size : (m + 1) * size, :] = s0[(m * nf + 1) * cells : (m * nf + nf - 1) * cells, columns_of(lax.axis_index("lon"))]
                out[m, :, :] = mid[m, 0, edge : edge + own, :]

        @pl.when(lax.axis_index("segment") == 1)
        def _():
            spread(blk, forward, s)

    def partial(s, near_half, far_half, w, part):
        rows = near_half.shape[0]
        here = lax.axis_index("lon") % 2 * (width // 2)
        for base, ref in ((here, near_half), (width // 2 - here, far_half)):
            w[pl.ds(pl.multiple_of(base, 32), rows), :] = ref[...]
        for i in range(2):
            late = slice(i * (width // 2) + rows, (i + 1) * (width // 2))
            w[late, :] = jnp.zeros((width // 2 - rows, channels), w.dtype)

        @pl.when(lax.axis_index("segment") == 0)
        def _():
            size = members * ns * cells
            part[:size, :] = dot(s[:size, :], w[...])

        @pl.when(lax.axis_index("segment") == 1)
        def _():
            part[...] = dot(s[...], w[...])

    def own_part(g):
        return max(g * band, half_edge), min((g + 1) * band, half_edge + own)

    def apply_back(w, gates, feat):
        for b in range(BASIS):
            got = dot_nt(gates[...], w[b * channels : (b + 1) * channels, :]).astype(jnp.bfloat16)
            for i in range(members * ns):
                feat[(i * BASIS + b) * cells : (i * BASIS + b + 1) * cells, :] = got[i * cells : (i + 1) * cells]

    def chain(b0, b1, b2, b3, w_own, w_in, part, ends, again, backward, s, left0, slope, early_out, w,
              out_ref, next_ref, gate_ref, own_ref, p1, p2, p3, late, s1, mid, gates, feat, pull, grads):
        blk = (b0, b1, b2, b3)
        seg, lon, lat = lax.axis_index("segment"), lax.axis_index("lon"), lax.axis_index("lat")
        rest = ends.shape[0] // 2
        rows = width // 2 - rest
        aligned = rows // lanes * lanes
        span = width // 2 - aligned
        for i in range(2):
            piece = ends[i * rest : (i + 1) * rest, :]
            w[i * (width // 2) + rows : (i + 1) * (width // 2), :] = piece
            late[i * span : (i + 1) * span - rest, :] = jnp.zeros((span - rest, channels), late.dtype)
            late[(i + 1) * span - rest : (i + 1) * span, :] = piece

        def complete(size):
            total = part[:size, :]
            for i in range(2):
                at = i * (width // 2) + aligned
                total = total + dot(s[:size, at : at + span], late[i * span : (i + 1) * span, :])
            return total

        def coming_at(m, g):
            return take(blk, m, coming_parts, g * band, (g + 1) * band).astype(jnp.float32)

        def second_section(total, into, last):
            for m in range(members):
                for g in range(ns):
                    at = (m * ns + g) * cells
                    mixed = total[at : at + cells]
                    sigma = 0.5 + 0.5 * jnp.tanh(0.5 * mixed)
                    into[at : at + cells, :] = (coming_at(m, g) * sigma * (1.0 + mixed * (1.0 - sigma))).astype(jnp.bfloat16)
                    if last:
                        low, high = own_part(g)
                        base = mid[m, 0, half_edge + low : half_edge + high, :]
                        local = slice(low - g * band, high - g * band)
                        base = (base.astype(jnp.float32) + mixed[local] * sigma[local]).astype(jnp.bfloat16)
                        out_ref[m, low - half_edge : high - half_edge, :] = base

        def store_grads(left, right):
            got = dot_tn(left, jnp.concatenate(right, axis=0))
            for c in range(pieces):
                grads[pl.ds(c, width // blocks, stride=pieces), :] = got[:, c * lanes : (c + 1) * lanes]

        @pl.when(seg == 0)
        def _():
            second_section(complete(members * ns * cells), gates, False)
            out_ref[...] = early_out[...]
            apply_back(w, gates, feat)
            for m in range(members):
                for g in range(ns):
                    at = (m * ns + g) * cells * BASIS
                    got = dot(backward[g], feat[at : at + BASIS * cells, :]).reshape(blocks, win, channels)
                    if g == 0:
                        pull[m, :, :win, :] = got
                    else:
                        pull[m, :, g * band : (g + 1) * band, :] += got[:, :band]
                        pull[m, :, (g + 1) * band : g * band + win, :] = got[:, band:]
            right = []
            step = half_edge
            for m in range(members):
                for g in range(ns):
                    at = (m * ns + g) * cells
                    span = slice(half_edge + g * band, half_edge + (g + 1) * band)
                    value = (coming_at(m, g) + pull[m, :, span, :].reshape(cells, channels)).astype(jnp.bfloat16)
                    low, high = own_part(g)
                    next_ref[m, low - half_edge : high - half_edge, :] = value[low - g * band : high - g * band]
                    tilt = slope[m, :, g * band : (g + 1) * band, :].reshape(cells, channels)
                    gate_ref[at : at + cells, :] = (value.astype(jnp.float32) * tilt).astype(jnp.bfloat16)
                for g in range(1, nf - 1):
                    for q in range(blocks):
                        for o in range(0, band, step):
                            spot = half_edge + (g - 1) * band + o
                            turn, rest = spot // band, spot % band
                            at = (m * ns + turn) * cells + q * band + rest
                            right.append(gate_ref[at : at + step, :])
            store_grads(left0[...], right)

        @pl.when(seg == 1)
        def _():
            first_section(blk, complete(members * nf * cells), s1, again, mid, None)
            second_section(dot(s1[...], w_own[...]), gate_ref, True)
            left, right = [], []
            for m in range(members):
                next_ref[m, :, :] = b0[m, own : 2 * own, :]
                for g in range(ns):
                    low, high = own_part(g)
                    for q in range(blocks):
                        at = (m * ns + g) * cells + q * band - g * band
                        left.append(s1[at + low : at + high, columns_of(lon)])
                        right.append(gate_ref[at + low : at + high, :])
            store_grads(jnp.concatenate(left, axis=0), right)

        share = width // blocks // lat_devices * pieces

        def rows_of(index):
            return grads[pl.ds(pl.multiple_of(index * share, share), share), :]

        own_ref[...] = rows_of(lat)
        for bit, ref in ((1, p1), (2, p2), (3, p3)):
            ref[...] = rows_of(lat ^ bit).astype(jnp.bfloat16)

    def finish(w_own, backward, gates, next_ref, last_ref, grad_ref, out_ref, feat, pull):
        apply_back(w_own, gates, feat)
        for m in range(members):
            for g in range(ns):
                at = (m * ns + g) * cells * BASIS
                got = dot(backward[g, 0:win, :], feat[at : at + BASIS * cells, :])
                if g == 0:
                    pull[m, :win, :] = got
                else:
                    pull[m, g * band : (g + 1) * band, :] += got[:band]
                    pull[m, (g + 1) * band : g * band + win, :] = got[band:]
            total = next_ref[m].astype(jnp.float32) + pull[m, edge : edge + own, :]
            grad_ref[m] = total.astype(jnp.bfloat16).reshape(lat_rows, lon_cols, channels)
            out_ref[m] = last_ref[m].reshape(lat_rows, lon_cols, channels)

    return prep, edges, maps, early, partial, chain, finish


def add_up(scale, mine, p1, p2, p3, out):
    out[...] = (mine[...] + p1[...].astype(jnp.float32) + p2[...].astype(jnp.float32) + p3[...].astype(jnp.float32)) * scale


def whole_ring(inputs, cotangent, weights, basis_values, lat_step, lon_step):
    members, lat_rows, lon_cols, channels = inputs.shape
    blocks = lax.axis_size("lon")
    lat_devices = lax.axis_size("lat")
    lat_total = lat_rows * lat_devices
    grad_scale = 1.0 / math.sqrt(members * lat_total * lon_cols * blocks)
    own = lat_rows * lon_cols
    edge = HALO * lon_cols
    half_edge = edge // 2
    halo = edge + half_edge
    width = BASIS * channels
    half_type, full_type = jnp.bfloat16, jnp.float32
    shape = jax.ShapeDtypeStruct
    first, second = window_plan(lat_rows)
    nf, ns = len(first), len(second)
    cells = blocks * BAND * lon_cols
    win = 16 * lon_cols
    vmem = pl.BlockSpec(memory_space=pltpu.VMEM)

    def call(body, name, outs, ins, mib, gflops, scratch=(), aliases={}):
        return pl.pallas_call(
            body,
            out_shape=outs,
            in_specs=[vmem] * len(ins),
            out_specs=(vmem,) * len(outs),
            scratch_shapes=list(scratch),
            input_output_aliases=aliases,
            compiler_params=pltpu.CompilerParams(vmem_limit_bytes=int(mib * 1024 * 1024)),
            cost_estimate=pl.CostEstimate(flops=int(gflops * 1e9), bytes_accessed=int(gflops * 1e6), transcendentals=0),
            name=name,
        )(*ins)

    prep, edges, maps, early, partial, chain, finish = make_steps(lat_rows, lon_cols, blocks, members, channels, lat_devices)
    kernel = weights.reshape(width, channels)
    rest = width // 2 * 5 // 48
    rows = width // 2 - rest
    half = lax.dynamic_slice_in_dim(kernel, lax.axis_index("lon") % 2 * (width // 2), rows, 0)
    ends = jnp.concatenate([kernel[rows : rows + rest], kernel[width - rest :]], axis=0)
    near_ends = lax.ppermute(ends, "segment", swap("segment", 1))
    near_half = lax.ppermute(half, "segment", swap("segment", 1))
    half, inputs, cotangent = lax.optimization_barrier((half, inputs, cotangent))
    loaded = jnp.concatenate([inputs, cotangent], axis=0)
    (both,) = call(prep, "prep", (shape((members, 2 * own, channels), half_type),), (loaded,), 4, 0.0)
    sides_type = shape((members, halo, channels), half_type)
    toward, away = call(edges, "edges", (sides_type, sides_type), (both,), 4, 0.0)
    both_y = lax.ppermute(both, "lon", swap("lon", 2))
    near_pairs = [(i, i ^ 1) for i in range(lat_devices)]
    far_pairs = [(i, j) for i in range(lat_devices) for j in [i + 1 if i % 2 else i - 1] if 0 <= j < lat_devices]
    from_near = lax.ppermute(toward, "lat", near_pairs)
    from_far = lax.ppermute(away, "lat", far_pairs)
    tables = (lat_step.T, lon_step.T, jnp.transpose(basis_values, (1, 2, 0)))
    _, _, *tables = lax.optimization_barrier((toward, away, *tables))
    (forward,) = call(
        functools.partial(maps, first),
        "maps_first",
        (shape((nf, BASIS * cells, blocks * win), half_type),),
        tables,
        4,
        0.0,
        (pltpu.VMEM((48, lat_total), full_type),),
    )
    from_near, from_far, forward = lax.optimization_barrier((from_near, from_far, forward))
    sides = jnp.concatenate([from_near, from_far], axis=1)
    sides, both_y = lax.optimization_barrier((sides, both_y))
    sides_y = lax.ppermute(sides, "lon", swap("lon", 2))
    b0 = jnp.concatenate([both, sides], axis=1)
    b1 = lax.ppermute(b0, "lon", swap("lon", 1))
    b0, *tables = lax.optimization_barrier((b0, *tables))
    again, backward = call(
        functools.partial(maps, second),
        "maps_again",
        (shape((ns, BASIS * cells, blocks * win), half_type), shape((ns, blocks * win, BASIS * cells), half_type)),
        tables,
        4,
        0.0,
        (pltpu.VMEM((48, lat_total), full_type),),
    )
    b2 = jnp.concatenate([both_y, sides_y], axis=1)
    b2, again, near_half = lax.optimization_barrier((b2, again, near_half))
    b3 = lax.ppermute(b2, "lon", swap("lon", 1))
    far_half = lax.ppermute(near_half, "lon", swap("lon", 1))
    s_type = (members * nf * cells, width)
    s, left, slope, early_out = call(
        early,
        "early",
        (
            shape(s_type, half_type),
            shape((members * (nf - 2) * cells, width // blocks), half_type),
            shape((members, blocks, own + edge, channels), half_type),
            shape((members, own, channels), half_type),
        ),
        (b0, b1, b2, b3, kernel, forward, again),
        12,
        3.0,
        (pltpu.VMEM(s_type, half_type), pltpu.VMEM((members, blocks, own + 2 * edge, channels), half_type)),
    )
    w_type = shape((width, channels), half_type)
    w, part = call(
        partial,
        "partial",
        (w_type, shape((s_type[0], channels), full_type)),
        (s, near_half, far_half),
        8,
        1.5,
    )
    near_ends, part = lax.optimization_barrier((near_ends, part))
    lines = (width // blocks // lat_devices * channels // 128, 128)
    _, out, follow, gates, mine, *parts = call(
        chain,
        "chain",
        (
            w_type,
            shape((members, own, channels), half_type),
            shape((members, own, channels), half_type),
            shape((members * ns * cells, channels), half_type),
            shape(lines, full_type),
        )
        + (shape(lines, half_type),) * 3,
        (b0, b1, b2, b3, kernel, w, part, near_ends, again, backward, s, left, slope, early_out),
        18,
        6.0,
        (
            pltpu.VMEM((2 * (width // 2 - (width // 2 - rest) // 128 * 128), channels), half_type),
            pltpu.VMEM((members * ns * cells, width), half_type),
            pltpu.VMEM((members, blocks, own + 2 * edge, channels), half_type),
            pltpu.VMEM((members * ns * cells, channels), half_type),
            pltpu.VMEM((members * ns * cells * BASIS, channels), half_type),
            pltpu.VMEM((members, blocks, own + 2 * edge, channels), full_type),
            pltpu.VMEM((width // blocks * channels // 128, 128), full_type),
        ),
        {5: 0},
    )
    got = [lax.ppermute(part, "lat", swap("lat", bit)) for bit, part in reversed(list(zip((1, 2, 3), parts)))]
    block = (members, lat_rows, lon_cols, channels)
    grad, out = call(
        finish,
        "finish",
        (shape(block, half_type),) * 2,
        (kernel, backward, gates, follow, out),
        10,
        2.0,
        (
            pltpu.VMEM((members * ns * cells * BASIS, channels), half_type),
            pltpu.VMEM((members, own + 2 * edge, channels), full_type),
        ),
    )
    (total,) = call(functools.partial(add_up, grad_scale), "add_up", (shape(lines, full_type),), (mine, *got), 2, 0.1)
    return (out[None], grad[None], total.reshape(1, lines[0] * lines[1]))


def fits_ring(mesh, inputs):
    sizes = dict(mesh.shape)
    rows, cols = inputs.shape[1] // sizes["lat"], inputs.shape[2] // sizes["lon"]
    return sizes["segment"] == 2 and sizes["lon"] == 4 and sizes["lat"] == 4 and rows == 16 and cols == 4


def solution(mesh):
    def apply(*args):
        body = whole_ring if fits_ring(mesh, args[0]) else per_device
        return jax.shard_map(
            body,
            mesh=mesh,
            in_specs=(
                P(None, "lat", "lon", None),
                P(None, "lat", "lon", None),
                P("segment", None, None, None),
                P(),
                P(),
                P(),
            ),
            out_specs=(
                P("segment", None, "lat", "lon", None),
                P("segment", None, "lat", "lon", None),
                P("segment", ("lon", "lat")),
            ),
            check_vma=False,
        )(*args)

    return apply
```

```python
import functools
import math

import jax
import jax.numpy as jnp
from jax import lax
from jax.experimental import pallas as pl
from jax.experimental.pallas import tpu as pltpu
from jax.sharding import PartitionSpec as P

BASIS = 3
TAPS = 9
REACH = 2


def with_halo(array, sides, width):
    for axis, dim in sides:
        size, length = (lax.axis_size(axis), array.shape[dim])
        up = [(i, (i + 1) % size) for i in range(size)]
        down = [(j, i) for i, j in up]
        last = lax.slice_in_dim(array, length - width, length, axis=dim)
        first = lax.slice_in_dim(array, 0, width, axis=dim)
        before = lax.ppermute(last, axis, up)
        after = lax.ppermute(first, axis, down)
        array = jnp.concatenate([before, array, after], axis=dim)
    return array


def shifted(block, axis, distance):
    devices = range(lax.axis_size(axis))
    route = [(i - distance, i) for i in devices if i - distance in devices]
    return lax.ppermute(block, axis, route)


def widen(features):
    return with_halo(features, (("lon", 2), ("lat", 1)), REACH)


def pass_ahead(result):
    return shifted(result, "segment", 1)


def pass_behind(result):
    return shifted(result, "segment", -1)


def build_tables(basis_values, lat_step, lon_step, lat_rows, lon_cols, lat_index, lat_total):
    pad_rows = lat_rows + 2 * REACH
    pad_cols = lon_cols + 2 * REACH
    lat_padded = jnp.pad(lat_step, ((REACH, REACH), (0, 0)))
    lon_padded = jnp.pad(lon_step, ((REACH, REACH), (0, 0)))
    basis_padded = jnp.pad(basis_values, ((REACH, REACH), (0, 0), (0, 0)))
    row_start = lat_index * lat_rows
    lat_near = lax.dynamic_slice_in_dim(lat_padded, row_start, pad_rows, 0)
    lon_near = lax.dynamic_slice_in_dim(lon_padded, row_start, pad_rows, 0)
    basis_near = lax.dynamic_slice_in_dim(basis_padded, row_start, pad_rows, 0)
    lat_own = lat_near[REACH : REACH + lat_rows]
    lon_own = lon_near[REACH : REACH + lat_rows]
    basis_own = basis_near[REACH : REACH + lat_rows]
    own_rows = row_start + jnp.arange(lat_rows)
    inside = (own_rows[:, None] + lat_own >= 0) & (own_rows[:, None] + lat_own < lat_total)
    row_grid = jnp.arange(lat_rows)[:, None, None]
    col_grid = jnp.arange(lon_cols)[None, :, None]
    source = (row_grid + REACH + lat_own[:, None, :]) * pad_cols + (
        col_grid + REACH + lon_own[:, None, :]
    )
    tap_weight = jnp.where(inside[:, None, :, None], basis_own[:, None, :, :], 0.0)
    tap_weight = jnp.broadcast_to(tap_weight, (lat_rows, lon_cols, TAPS, BASIS))
    picker = (source[..., None] == jnp.arange(pad_rows * pad_cols)).astype(jnp.float32)
    forward_map = jnp.einsum("ijkb,ijks->bijs", tap_weight, picker, precision=lax.Precision.HIGHEST)
    forward_map = forward_map.reshape(BASIS, lat_rows * lon_cols, pad_rows * pad_cols)
    near_rows = row_start - REACH + jnp.arange(pad_rows)
    real_row = (near_rows >= 0) & (near_rows < lat_total)
    pad_row_grid = jnp.arange(pad_rows)[:, None, None]
    pad_col_grid = jnp.arange(pad_cols)[None, :, None]
    target_row = pad_row_grid - REACH + lat_near[:, None, :]
    target_col = pad_col_grid - REACH + lon_near[:, None, :]
    landed = (
        (target_row >= 0)
        & (target_row < lat_rows)
        & (target_col >= 0)
        & (target_col < lon_cols)
        & real_row[:, None, None]
    )
    target = target_row * lon_cols + target_col
    back_weight = jnp.where(landed[..., None], basis_near[:, None, :, :], 0.0)
    catcher = (target[..., None] == jnp.arange(lat_rows * lon_cols)).astype(jnp.float32)
    backward_map = jnp.einsum(
        "pqkb,pqkt->btpq", back_weight, catcher, precision=lax.Precision.HIGHEST
    )
    backward_map = backward_map.reshape(BASIS, lat_rows * lon_cols, pad_rows * pad_cols)
    return (forward_map, backward_map)


def per_device(inputs, cotangent, weights, basis_values, lat_step, lon_step):
    members, lat_rows, lon_cols, channels = inputs.shape
    pad_rows = lat_rows + 2 * REACH
    pad_cols = lon_cols + 2 * REACH
    cells = lat_rows * lon_cols
    lat_index = lax.axis_index("lat")
    lat_total = lat_rows * lax.axis_size("lat")
    segment_index = lax.axis_index("segment")
    depth = lax.axis_size("segment")
    grad_scale = 1.0 / math.sqrt(members * lat_total * lon_cols * lax.axis_size("lon"))
    forward_map, backward_map = build_tables(
        basis_values, lat_step, lon_step, lat_rows, lon_cols, lat_index, lat_total
    )
    kernel = weights[0]
    keep_spread = jnp.zeros((BASIS, members, cells, channels), jnp.bfloat16)
    keep_mixed = jnp.zeros((members, cells, channels), jnp.float32)
    keep_gate = jnp.zeros((members, cells, channels), jnp.bfloat16)
    section_out = jnp.zeros(inputs.shape, jnp.bfloat16)
    section_grad = jnp.zeros(inputs.shape, jnp.bfloat16)
    carry = inputs
    for tick_num in range(depth):
        layer_count = carry.shape[0]
        layer_padded = (
            widen(carry).reshape(layer_count, pad_rows * pad_cols, channels).astype(jnp.float32)
        )
        spread = jnp.einsum(
            "bts,msc->bmtc", forward_map, layer_padded, precision=lax.Precision.HIGHEST
        ).astype(jnp.bfloat16)
        layer_mixed = jnp.einsum(
            "bmtc,bcd->mtd", spread, kernel, preferred_element_type=jnp.float32
        )
        result = (
            carry.reshape(layer_count, cells, channels).astype(jnp.float32)
            + jax.nn.silu(layer_mixed)
        ).astype(jnp.bfloat16)
        spread, mixed, result = (spread, layer_mixed, result.reshape(carry.shape))
        here = segment_index == tick_num
        keep_spread = jnp.where(here, spread, keep_spread)
        keep_mixed = jnp.where(here, mixed, keep_mixed)
        section_out = jnp.where(here, result, section_out)
        if tick_num + 1 < depth:
            carry = pass_ahead(result)
    grad = cotangent
    for tick_num in range(depth):
        count = grad.shape[0]
        flat_grad = grad.reshape(count, cells, channels).astype(jnp.float32)
        sigma = jax.nn.sigmoid(keep_mixed)
        gate_grad = (flat_grad * sigma * (1.0 + keep_mixed * (1.0 - sigma))).astype(jnp.bfloat16)
        feature_grad = jnp.einsum(
            "mtd,bcd->bmtc", gate_grad, kernel, preferred_element_type=jnp.float32
        ).astype(jnp.bfloat16)
        padded = widen(feature_grad.reshape(BASIS * count, lat_rows, lon_cols, channels))
        padded = padded.reshape(BASIS, count, pad_rows * pad_cols, channels).astype(jnp.float32)
        pulled = jnp.einsum("bts,bmsc->mtc", backward_map, padded, precision=lax.Precision.HIGHEST)
        new_grad = (flat_grad + pulled).astype(jnp.bfloat16).reshape(grad.shape)
        gate_grad, new_grad = (gate_grad, new_grad)
        here = segment_index == depth - 1 - tick_num
        keep_gate = jnp.where(here, gate_grad, keep_gate)
        section_grad = jnp.where(here, new_grad, section_grad)
        if tick_num + 1 < depth:
            grad = pass_behind(new_grad)
    local_grad = (
        jnp.einsum("bmtc,mtd->bcd", keep_spread, keep_gate, preferred_element_type=jnp.float32)
        * grad_scale
    )
    owners = lax.axis_size("lon") * lax.axis_size("lat")
    grad_rows = local_grad.reshape(owners, -1)
    weight_grad = lax.psum_scatter(grad_rows, ("lon", "lat"), scatter_dimension=0, tiled=True)
    return (section_out[None], section_grad[None], weight_grad)


HALO = 8
BAND = 8


def swap(axis, bit):
    return [(i, i ^ bit) for i in range(lax.axis_size(axis))]


def window_plan(lat_rows):
    first = [(a, min(max(a - 4, -HALO), lat_rows + HALO - 16)) for a in range(-HALO, lat_rows + HALO, BAND)]
    second = [(a, a - 4) for a in range(-4, lat_rows + 4, BAND)]
    return first, second


def dot(a, b):
    return jnp.dot(a, b, preferred_element_type=jnp.float32)


def dot_nt(a, b):
    return lax.dot_general(a, b, (((1,), (1,)), ((), ())), preferred_element_type=jnp.float32)


def dot_tn(a, b):
    return lax.dot_general(a, b, (((0,), (0,)), ((), ())), preferred_element_type=jnp.float32)


def make_steps(lat_rows, lon_cols, blocks, members, channels, lat_devices):
    first, second = window_plan(lat_rows)
    nf, ns = len(first), len(second)
    lat_total = lat_rows * lat_devices
    ring = lon_cols * blocks
    band = BAND * lon_cols
    cells = blocks * band
    win = 16 * lon_cols
    own = lat_rows * lon_cols
    edge = HALO * lon_cols
    half_edge = edge // 2
    width = BASIS * channels
    lanes = 128
    pieces = channels // lanes
    halo = edge + half_edge
    state_parts = ((0, edge, 0, 0), (edge, own, 0, None), (edge + own, edge, 0, 1))
    coming_parts = ((0, half_edge, edge, 0), (half_edge, own, own, None), (half_edge + own, half_edge, edge, 1))

    def take(blks, m, parts, low, high):
        found = []
        odd = lax.axis_index("lat") % 2
        for r in blks:
            for start, size, at, side in parts:
                lo, hi = max(low, start), min(high, start + size)
                if lo >= hi:
                    continue
                if side is None:
                    found.append(r[m, at + lo - start : at + hi - start, :])
                else:
                    slot = odd if side else 1 - odd
                    first_row = pl.multiple_of(2 * own + at + lo - start + slot * halo, 16)
                    found.append(r[m, pl.ds(first_row, hi - lo), :])
        return jnp.concatenate(found, axis=0)

    def prep(loaded, both):
        for m in range(members):
            both[m, :own, :] = loaded[m].reshape(own, channels)
            both[m, own:, :] = loaded[members + m].reshape(own, channels)

    def edges(both, toward, away):
        tail = ((own - edge, own), (2 * own - half_edge, 2 * own))
        head = ((0, edge), (own, own + half_edge))

        def fill(spans, ref):
            for m in range(members):
                ref[m, :edge, :] = both[m, spans[0][0] : spans[0][1], :]
                ref[m, edge:, :] = both[m, spans[1][0] : spans[1][1], :]

        @pl.when(lax.axis_index("lat") % 2 == 0)
        def _():
            fill(tail, toward)
            fill(head, away)

        @pl.when(lax.axis_index("lat") % 2 == 1)
        def _():
            fill(head, toward)
            fill(tail, away)

    def maps(plan, lat_step, lon_step, basis, *outs):
        forward, tab = outs[0], outs[-1]
        lon, lat = lax.axis_index("lon"), lax.axis_index("lat")
        base = lat * lat_rows
        tab[...] = jnp.zeros(tab.shape, jnp.float32)
        tab[0:TAPS, :] = lat_step[...].astype(jnp.float32)
        tab[TAPS : 2 * TAPS, :] = lon_step[...].astype(jnp.float32)
        for k in range(TAPS):
            tab[2 * TAPS + k * BASIS : 2 * TAPS + (k + 1) * BASIS, :] = basis[k]
        table = tab[...].astype(jnp.bfloat16)
        source = lax.broadcasted_iota(jnp.int32, (tab.shape[1], cells), 0)
        lane = lax.broadcasted_iota(jnp.int32, (1, cells), 1)
        block, rest = lane // band, lane % band
        row_in, col_in = rest // lon_cols, rest % lon_cols
        column_home = (block ^ lon) * lon_cols + col_in
        piece = 64
        spot = lax.broadcasted_iota(jnp.int32, (piece, cells), 0)
        for i, (a, start) in enumerate(plan):
            row = row_in + (base + a)
            got = dot(table, (source == row).astype(jnp.bfloat16))
            step_lat = got[0:TAPS].astype(jnp.int32)
            step_lon = got[TAPS : 2 * TAPS].astype(jnp.int32)
            target = row + step_lat
            inside = (row >= 0) & (row < lat_total) & (target >= 0) & (target < lat_total)
            column = column_home + step_lon
            column = jnp.where(column < 0, column + ring, column)
            column = jnp.where(column >= ring, column - ring, column)
            local = target - (base + start)
            place = ((column // lon_cols) ^ lon) * win + local * lon_cols + column % lon_cols
            place = jnp.where(inside, place, -1)
            for p in range(0, blocks * win, piece):
                tables = [jnp.zeros((piece, cells), jnp.float32) for _ in range(BASIS)]
                for k in range(TAPS):
                    hit = spot == place[k : k + 1] - p
                    for b in range(BASIS):
                        at = 2 * TAPS + k * BASIS + b
                        tables[b] = tables[b] + jnp.where(hit, got[at : at + 1], 0.0)
                for b in range(BASIS):
                    span = slice(b * cells, (b + 1) * cells)
                    forward[i, span, p : p + piece] = tables[b].T.astype(jnp.bfloat16)
                    if len(outs) == 3:
                        outs[1][i, p : p + piece, span] = tables[b].astype(jnp.bfloat16)

    def put_spread(got, into, at):
        for b in range(BASIS):
            into[at : at + cells, b * channels : (b + 1) * channels] = got[b * cells : (b + 1) * cells]

    def spread(blk, forward, into):
        for m in range(members):
            for g, (a, start) in enumerate(first):
                o = (start + HALO) * lon_cols
                near = take(blk, m, state_parts, o, o + win)
                put_spread(dot(forward[g], near).astype(jnp.bfloat16), into, (m * nf + g) * cells)

    def first_section(blk, total, s1, again, mid, slope):
        for m in range(members):
            for g in range(nf):
                mixed = total[(m * nf + g) * cells : (m * nf + g + 1) * cells]
                sigma = 0.5 + 0.5 * jnp.tanh(0.5 * mixed)
                here = take(blk, m, state_parts, g * band, (g + 1) * band)
                value = (here.astype(jnp.float32) + mixed * sigma).astype(jnp.bfloat16)
                mid[m, :, g * band : (g + 1) * band, :] = value.reshape(blocks, band, channels)
                if slope is not None:
                    tilt = (sigma * (1.0 + mixed * (1.0 - sigma))).astype(slope.dtype).reshape(blocks, band, channels)
                    low, high = max(g * band, half_edge), min((g + 1) * band, 3 * half_edge + own)
                    slope[m, :, low - half_edge : high - half_edge, :] = tilt[:, low - g * band : high - g * band]
            for g in range(ns):
                near = mid[m, :, g * band : g * band + win, :].reshape(blocks * win, channels)
                put_spread(dot(again[g], near).astype(jnp.bfloat16), s1, (m * ns + g) * cells)

    def columns_of(lon):
        return pl.ds(pl.multiple_of(lon * (width // blocks), 128), width // blocks)

    def early(b0, b1, b2, b3, w_own, forward, again, s, left, slope, out, s0, mid):
        blk = (b0, b1, b2, b3)

        @pl.when(lax.axis_index("segment") == 0)
        def _():
            spread(blk, forward, s0)
            first_section(blk, dot(s0[...], w_own[...]), s, again, mid, slope)
            for m in range(members):
                size = (nf - 2) * cells
                left[m * size : (m + 1) * size, :] = s0[(m * nf + 1) * cells : (m * nf + nf - 1) * cells, columns_of(lax.axis_index("lon"))]
                out[m, :, :] = mid[m, 0, edge : edge + own, :]

        @pl.when(lax.axis_index("segment") == 1)
        def _():
            spread(blk, forward, s)

    def partial(s, near_half, far_half, w, part):
        rows = near_half.shape[0]
        here = lax.axis_index("lon") % 2 * (width // 2)
        for base, ref in ((here, near_half), (width // 2 - here, far_half)):
            w[pl.ds(pl.multiple_of(base, 32), rows), :] = ref[...]
        for i in range(2):
            late = slice(i * (width // 2) + rows, (i + 1) * (width // 2))
            w[late, :] = jnp.zeros((width // 2 - rows, channels), w.dtype)

        @pl.when(lax.axis_index("segment") == 0)
        def _():
            size = members * ns * cells
            part[:size, :] = dot(s[:size, :], w[...])

        @pl.when(lax.axis_index("segment") == 1)
        def _():
            part[...] = dot(s[...], w[...])

    def own_part(g):
        return max(g * band, half_edge), min((g + 1) * band, half_edge + own)

    def apply_back(w, gates, feat):
        for b in range(BASIS):
            got = dot_nt(gates[...], w[b * channels : (b + 1) * channels, :]).astype(jnp.bfloat16)
            for i in range(members * ns):
                feat[(i * BASIS + b) * cells : (i * BASIS + b + 1) * cells, :] = got[i * cells : (i + 1) * cells]

    def chain(b0, b1, b2, b3, w_own, w_in, part, ends, again, backward, s, left0, slope, early_out, w,
              out_ref, next_ref, gate_ref, parts, late, s1, mid, gates, feat, pull, grads):
        blk = (b0, b1, b2, b3)
        seg, lon, lat = lax.axis_index("segment"), lax.axis_index("lon"), lax.axis_index("lat")
        rest = ends.shape[0] // 2
        rows = width // 2 - rest
        aligned = rows // lanes * lanes
        span = width // 2 - aligned
        for i in range(2):
            piece = ends[i * rest : (i + 1) * rest, :]
            w[i * (width // 2) + rows : (i + 1) * (width // 2), :] = piece
            late[i * span : (i + 1) * span - rest, :] = jnp.zeros((span - rest, channels), late.dtype)
            late[(i + 1) * span - rest : (i + 1) * span, :] = piece

        def complete(size):
            total = part[:size, :]
            for i in range(2):
                at = i * (width // 2) + aligned
                total = total + dot(s[:size, at : at + span], late[i * span : (i + 1) * span, :])
            return total

        def coming_at(m, g):
            return take(blk, m, coming_parts, g * band, (g + 1) * band).astype(jnp.float32)

        def second_section(total, into, last):
            for m in range(members):
                for g in range(ns):
                    at = (m * ns + g) * cells
                    mixed = total[at : at + cells]
                    sigma = 0.5 + 0.5 * jnp.tanh(0.5 * mixed)
                    into[at : at + cells, :] = (coming_at(m, g) * sigma * (1.0 + mixed * (1.0 - sigma))).astype(jnp.bfloat16)
                    if last:
                        low, high = own_part(g)
                        base = mid[m, 0, half_edge + low : half_edge + high, :]
                        local = slice(low - g * band, high - g * band)
                        base = (base.astype(jnp.float32) + mixed[local] * sigma[local]).astype(jnp.bfloat16)
                        out_ref[m, low - half_edge : high - half_edge, :] = base

        def store_grads(left, right):
            got = dot_tn(left, jnp.concatenate(right, axis=0))
            for c in range(pieces):
                grads[pl.ds(c, width // blocks, stride=pieces), :] = got[:, c * lanes : (c + 1) * lanes]

        @pl.when(seg == 0)
        def _():
            second_section(complete(members * ns * cells), gates, False)
            out_ref[...] = early_out[...]
            apply_back(w, gates, feat)
            for m in range(members):
                for g in range(ns):
                    at = (m * ns + g) * cells * BASIS
                    got = dot(backward[g], feat[at : at + BASIS * cells, :]).reshape(blocks, win, channels)
                    if g == 0:
                        pull[m, :, :win, :] = got
                    else:
                        pull[m, :, g * band : (g + 1) * band, :] += got[:, :band]
                        pull[m, :, (g + 1) * band : g * band + win, :] = got[:, band:]
            right = []
            step = half_edge
            for m in range(members):
                for g in range(ns):
                    at = (m * ns + g) * cells
                    span = slice(half_edge + g * band, half_edge + (g + 1) * band)
                    value = (coming_at(m, g) + pull[m, :, span, :].reshape(cells, channels)).astype(jnp.bfloat16)
                    low, high = own_part(g)
                    next_ref[m, low - half_edge : high - half_edge, :] = value[low - g * band : high - g * band]
                    tilt = slope[m, :, g * band : (g + 1) * band, :].reshape(cells, channels)
                    gate_ref[at : at + cells, :] = (value.astype(jnp.float32) * tilt).astype(jnp.bfloat16)
                for g in range(1, nf - 1):
                    for q in range(blocks):
                        for o in range(0, band, step):
                            spot = half_edge + (g - 1) * band + o
                            turn, rest = spot // band, spot % band
                            at = (m * ns + turn) * cells + q * band + rest
                            right.append(gate_ref[at : at + step, :])
            store_grads(left0[...], right)

        @pl.when(seg == 1)
        def _():
            first_section(blk, complete(members * nf * cells), s1, again, mid, None)
            second_section(dot(s1[...], w_own[...]), gate_ref, True)
            left, right = [], []
            for m in range(members):
                next_ref[m, :, :] = b0[m, own : 2 * own, :]
                for g in range(ns):
                    low, high = own_part(g)
                    for q in range(blocks):
                        at = (m * ns + g) * cells + q * band - g * band
                        left.append(s1[at + low : at + high, columns_of(lon)])
                        right.append(gate_ref[at + low : at + high, :])
            store_grads(jnp.concatenate(left, axis=0), right)

        share = width // blocks // lat_devices * pieces

        def rows_of(index):
            return grads[pl.ds(pl.multiple_of(index * share, share), share), :]

        for index in range(lat_devices):
            parts[index] = rows_of(index).astype(jnp.bfloat16)

    def finish(w_own, backward, gates, next_ref, last_ref, grad_ref, out_ref, feat, pull):
        apply_back(w_own, gates, feat)
        for m in range(members):
            for g in range(ns):
                at = (m * ns + g) * cells * BASIS
                got = dot(backward[g, 0:win, :], feat[at : at + BASIS * cells, :])
                if g == 0:
                    pull[m, :win, :] = got
                else:
                    pull[m, g * band : (g + 1) * band, :] += got[:band]
                    pull[m, (g + 1) * band : g * band + win, :] = got[band:]
            total = next_ref[m].astype(jnp.float32) + pull[m, edge : edge + own, :]
            grad_ref[m] = total.astype(jnp.bfloat16).reshape(lat_rows, lon_cols, channels)
            out_ref[m] = last_ref[m].reshape(lat_rows, lon_cols, channels)

    return prep, edges, maps, early, partial, chain, finish


def add_up(scale, parts, out):
    total = parts[0].astype(jnp.float32)
    for index in range(1, parts.shape[0]):
        total = total + parts[index].astype(jnp.float32)
    out[...] = total * scale


def whole_ring(inputs, cotangent, weights, basis_values, lat_step, lon_step):
    members, lat_rows, lon_cols, channels = inputs.shape
    blocks = lax.axis_size("lon")
    lat_devices = lax.axis_size("lat")
    lat_total = lat_rows * lat_devices
    grad_scale = 1.0 / math.sqrt(members * lat_total * lon_cols * blocks)
    own = lat_rows * lon_cols
    edge = HALO * lon_cols
    half_edge = edge // 2
    halo = edge + half_edge
    width = BASIS * channels
    half_type, full_type = jnp.bfloat16, jnp.float32
    shape = jax.ShapeDtypeStruct
    first, second = window_plan(lat_rows)
    nf, ns = len(first), len(second)
    cells = blocks * BAND * lon_cols
    win = 16 * lon_cols
    vmem = pl.BlockSpec(memory_space=pltpu.VMEM)

    def call(body, name, outs, ins, mib, gflops, scratch=(), aliases={}):
        return pl.pallas_call(
            body,
            out_shape=outs,
            in_specs=[vmem] * len(ins),
            out_specs=(vmem,) * len(outs),
            scratch_shapes=list(scratch),
            input_output_aliases=aliases,
            compiler_params=pltpu.CompilerParams(vmem_limit_bytes=int(mib * 1024 * 1024)),
            cost_estimate=pl.CostEstimate(flops=int(gflops * 1e9), bytes_accessed=int(gflops * 1e6), transcendentals=0),
            name=name,
        )(*ins)

    prep, edges, maps, early, partial, chain, finish = make_steps(lat_rows, lon_cols, blocks, members, channels, lat_devices)
    kernel = weights.reshape(width, channels)
    rest = width // 2 // 8
    rows = width // 2 - rest
    half = lax.dynamic_slice_in_dim(kernel, lax.axis_index("lon") % 2 * (width // 2), rows, 0)
    ends = jnp.concatenate([kernel[rows : rows + rest], kernel[width - rest :]], axis=0)
    near_ends = lax.ppermute(ends, "segment", swap("segment", 1))
    near_half = lax.ppermute(half, "segment", swap("segment", 1))
    half, inputs, cotangent = lax.optimization_barrier((half, inputs, cotangent))
    loaded = jnp.concatenate([inputs, cotangent], axis=0)
    (both,) = call(prep, "prep", (shape((members, 2 * own, channels), half_type),), (loaded,), 4, 0.0)
    sides_type = shape((members, halo, channels), half_type)
    toward, away = call(edges, "edges", (sides_type, sides_type), (both,), 4, 0.0)
    both_y = lax.ppermute(both, "lon", swap("lon", 2))
    near_pairs = [(i, i ^ 1) for i in range(lat_devices)]
    far_pairs = [(i, j) for i in range(lat_devices) for j in [i + 1 if i % 2 else i - 1] if 0 <= j < lat_devices]
    from_near = lax.ppermute(toward, "lat", near_pairs)
    from_far = lax.ppermute(away, "lat", far_pairs)
    tables = (lat_step.T, lon_step.T, jnp.transpose(basis_values, (1, 2, 0)))
    _, _, *tables = lax.optimization_barrier((toward, away, *tables))
    (forward,) = call(
        functools.partial(maps, first),
        "maps_first",
        (shape((nf, BASIS * cells, blocks * win), half_type),),
        tables,
        4,
        0.0,
        (pltpu.VMEM((48, lat_total), full_type),),
    )
    from_near, from_far, forward = lax.optimization_barrier((from_near, from_far, forward))
    sides = jnp.concatenate([from_near, from_far], axis=1)
    sides, both_y = lax.optimization_barrier((sides, both_y))
    sides_y = lax.ppermute(sides, "lon", swap("lon", 2))
    b0 = jnp.concatenate([both, sides], axis=1)
    b1 = lax.ppermute(b0, "lon", swap("lon", 1))
    b0, *tables = lax.optimization_barrier((b0, *tables))
    again, backward = call(
        functools.partial(maps, second),
        "maps_again",
        (shape((ns, BASIS * cells, blocks * win), half_type), shape((ns, blocks * win, BASIS * cells), half_type)),
        tables,
        4,
        0.0,
        (pltpu.VMEM((48, lat_total), full_type),),
    )
    b2 = jnp.concatenate([both_y, sides_y], axis=1)
    b2, again, near_half = lax.optimization_barrier((b2, again, near_half))
    b3 = lax.ppermute(b2, "lon", swap("lon", 1))
    far_half = lax.ppermute(near_half, "lon", swap("lon", 1))
    s_type = (members * nf * cells, width)
    s, left, slope, early_out = call(
        early,
        "early",
        (
            shape(s_type, half_type),
            shape((members * (nf - 2) * cells, width // blocks), half_type),
            shape((members, blocks, own + edge, channels), half_type),
            shape((members, own, channels), half_type),
        ),
        (b0, b1, b2, b3, kernel, forward, again),
        12,
        3.0,
        (pltpu.VMEM(s_type, half_type), pltpu.VMEM((members, blocks, own + 2 * edge, channels), half_type)),
    )
    w_type = shape((width, channels), half_type)
    w, part = call(
        partial,
        "partial",
        (w_type, shape((s_type[0], channels), full_type)),
        (s, near_half, far_half),
        8,
        1.5,
    )
    near_ends, part = lax.optimization_barrier((near_ends, part))
    lines = (width // blocks // lat_devices * channels // 128, 128)
    _, out, follow, gates, parts = call(
        chain,
        "chain",
        (
            w_type,
            shape((members, own, channels), half_type),
            shape((members, own, channels), half_type),
            shape((members * ns * cells, channels), half_type),
            shape((lat_devices,) + lines, half_type),
        ),
        (b0, b1, b2, b3, kernel, w, part, near_ends, again, backward, s, left, slope, early_out),
        18,
        6.0,
        (
            pltpu.VMEM((2 * (width // 2 - (width // 2 - rest) // 128 * 128), channels), half_type),
            pltpu.VMEM((members * ns * cells, width), half_type),
            pltpu.VMEM((members, blocks, own + 2 * edge, channels), half_type),
            pltpu.VMEM((members * ns * cells, channels), half_type),
            pltpu.VMEM((members * ns * cells * BASIS, channels), half_type),
            pltpu.VMEM((members, blocks, own + 2 * edge, channels), full_type),
            pltpu.VMEM((width // blocks * channels // 128, 128), full_type),
        ),
        {5: 0},
    )
    got = lax.all_to_all(parts, "lat", 0, 0, tiled=True)
    block = (members, lat_rows, lon_cols, channels)
    grad, out = call(
        finish,
        "finish",
        (shape(block, half_type),) * 2,
        (kernel, backward, gates, follow, out),
        10,
        2.0,
        (
            pltpu.VMEM((members * ns * cells * BASIS, channels), half_type),
            pltpu.VMEM((members, own + 2 * edge, channels), full_type),
        ),
    )
    (total,) = call(functools.partial(add_up, grad_scale), "add_up", (shape(lines, full_type),), (got,), 2, 0.1)
    return (out[None], grad[None], total.reshape(1, lines[0] * lines[1]))


def fits_ring(mesh, inputs):
    sizes = dict(mesh.shape)
    rows, cols = inputs.shape[1] // sizes["lat"], inputs.shape[2] // sizes["lon"]
    return sizes["segment"] == 2 and sizes["lon"] == 4 and sizes["lat"] == 4 and rows == 16 and cols == 4


def solution(mesh):
    def apply(*args):
        body = whole_ring if fits_ring(mesh, args[0]) else per_device
        return jax.shard_map(
            body,
            mesh=mesh,
            in_specs=(
                P(None, "lat", "lon", None),
                P(None, "lat", "lon", None),
                P("segment", None, None, None),
                P(),
                P(),
                P(),
            ),
            out_specs=(
                P("segment", None, "lat", "lon", None),
                P("segment", None, "lat", "lon", None),
                P("segment", ("lon", "lat")),
            ),
            check_vma=False,
        )(*args)

    return apply
```

```python
import functools
import math

import jax
import jax.numpy as jnp
from jax import lax
from jax.experimental import pallas as pl
from jax.experimental.pallas import tpu as pltpu
from jax.sharding import PartitionSpec as P

BASIS = 3
TAPS = 9
REACH = 2


def with_halo(array, sides, width):
    for axis, dim in sides:
        size, length = (lax.axis_size(axis), array.shape[dim])
        up = [(i, (i + 1) % size) for i in range(size)]
        down = [(j, i) for i, j in up]
        last = lax.slice_in_dim(array, length - width, length, axis=dim)
        first = lax.slice_in_dim(array, 0, width, axis=dim)
        before = lax.ppermute(last, axis, up)
        after = lax.ppermute(first, axis, down)
        array = jnp.concatenate([before, array, after], axis=dim)
    return array


def shifted(block, axis, distance):
    devices = range(lax.axis_size(axis))
    route = [(i - distance, i) for i in devices if i - distance in devices]
    return lax.ppermute(block, axis, route)


def widen(features):
    return with_halo(features, (("lon", 2), ("lat", 1)), REACH)


def pass_ahead(result):
    return shifted(result, "segment", 1)


def pass_behind(result):
    return shifted(result, "segment", -1)


def build_tables(basis_values, lat_step, lon_step, lat_rows, lon_cols, lat_index, lat_total):
    pad_rows = lat_rows + 2 * REACH
    pad_cols = lon_cols + 2 * REACH
    lat_padded = jnp.pad(lat_step, ((REACH, REACH), (0, 0)))
    lon_padded = jnp.pad(lon_step, ((REACH, REACH), (0, 0)))
    basis_padded = jnp.pad(basis_values, ((REACH, REACH), (0, 0), (0, 0)))
    row_start = lat_index * lat_rows
    lat_near = lax.dynamic_slice_in_dim(lat_padded, row_start, pad_rows, 0)
    lon_near = lax.dynamic_slice_in_dim(lon_padded, row_start, pad_rows, 0)
    basis_near = lax.dynamic_slice_in_dim(basis_padded, row_start, pad_rows, 0)
    lat_own = lat_near[REACH : REACH + lat_rows]
    lon_own = lon_near[REACH : REACH + lat_rows]
    basis_own = basis_near[REACH : REACH + lat_rows]
    own_rows = row_start + jnp.arange(lat_rows)
    inside = (own_rows[:, None] + lat_own >= 0) & (own_rows[:, None] + lat_own < lat_total)
    row_grid = jnp.arange(lat_rows)[:, None, None]
    col_grid = jnp.arange(lon_cols)[None, :, None]
    source = (row_grid + REACH + lat_own[:, None, :]) * pad_cols + (
        col_grid + REACH + lon_own[:, None, :]
    )
    tap_weight = jnp.where(inside[:, None, :, None], basis_own[:, None, :, :], 0.0)
    tap_weight = jnp.broadcast_to(tap_weight, (lat_rows, lon_cols, TAPS, BASIS))
    picker = (source[..., None] == jnp.arange(pad_rows * pad_cols)).astype(jnp.float32)
    forward_map = jnp.einsum("ijkb,ijks->bijs", tap_weight, picker, precision=lax.Precision.HIGHEST)
    forward_map = forward_map.reshape(BASIS, lat_rows * lon_cols, pad_rows * pad_cols)
    near_rows = row_start - REACH + jnp.arange(pad_rows)
    real_row = (near_rows >= 0) & (near_rows < lat_total)
    pad_row_grid = jnp.arange(pad_rows)[:, None, None]
    pad_col_grid = jnp.arange(pad_cols)[None, :, None]
    target_row = pad_row_grid - REACH + lat_near[:, None, :]
    target_col = pad_col_grid - REACH + lon_near[:, None, :]
    landed = (
        (target_row >= 0)
        & (target_row < lat_rows)
        & (target_col >= 0)
        & (target_col < lon_cols)
        & real_row[:, None, None]
    )
    target = target_row * lon_cols + target_col
    back_weight = jnp.where(landed[..., None], basis_near[:, None, :, :], 0.0)
    catcher = (target[..., None] == jnp.arange(lat_rows * lon_cols)).astype(jnp.float32)
    backward_map = jnp.einsum(
        "pqkb,pqkt->btpq", back_weight, catcher, precision=lax.Precision.HIGHEST
    )
    backward_map = backward_map.reshape(BASIS, lat_rows * lon_cols, pad_rows * pad_cols)
    return (forward_map, backward_map)


def per_device(inputs, cotangent, weights, basis_values, lat_step, lon_step):
    members, lat_rows, lon_cols, channels = inputs.shape
    pad_rows = lat_rows + 2 * REACH
    pad_cols = lon_cols + 2 * REACH
    cells = lat_rows * lon_cols
    lat_index = lax.axis_index("lat")
    lat_total = lat_rows * lax.axis_size("lat")
    segment_index = lax.axis_index("segment")
    depth = lax.axis_size("segment")
    grad_scale = 1.0 / math.sqrt(members * lat_total * lon_cols * lax.axis_size("lon"))
    forward_map, backward_map = build_tables(
        basis_values, lat_step, lon_step, lat_rows, lon_cols, lat_index, lat_total
    )
    kernel = weights[0]
    keep_spread = jnp.zeros((BASIS, members, cells, channels), jnp.bfloat16)
    keep_mixed = jnp.zeros((members, cells, channels), jnp.float32)
    keep_gate = jnp.zeros((members, cells, channels), jnp.bfloat16)
    section_out = jnp.zeros(inputs.shape, jnp.bfloat16)
    section_grad = jnp.zeros(inputs.shape, jnp.bfloat16)
    carry = inputs
    for tick_num in range(depth):
        layer_count = carry.shape[0]
        layer_padded = (
            widen(carry).reshape(layer_count, pad_rows * pad_cols, channels).astype(jnp.float32)
        )
        spread = jnp.einsum(
            "bts,msc->bmtc", forward_map, layer_padded, precision=lax.Precision.HIGHEST
        ).astype(jnp.bfloat16)
        layer_mixed = jnp.einsum(
            "bmtc,bcd->mtd", spread, kernel, preferred_element_type=jnp.float32
        )
        result = (
            carry.reshape(layer_count, cells, channels).astype(jnp.float32)
            + jax.nn.silu(layer_mixed)
        ).astype(jnp.bfloat16)
        spread, mixed, result = (spread, layer_mixed, result.reshape(carry.shape))
        here = segment_index == tick_num
        keep_spread = jnp.where(here, spread, keep_spread)
        keep_mixed = jnp.where(here, mixed, keep_mixed)
        section_out = jnp.where(here, result, section_out)
        if tick_num + 1 < depth:
            carry = pass_ahead(result)
    grad = cotangent
    for tick_num in range(depth):
        count = grad.shape[0]
        flat_grad = grad.reshape(count, cells, channels).astype(jnp.float32)
        sigma = jax.nn.sigmoid(keep_mixed)
        gate_grad = (flat_grad * sigma * (1.0 + keep_mixed * (1.0 - sigma))).astype(jnp.bfloat16)
        feature_grad = jnp.einsum(
            "mtd,bcd->bmtc", gate_grad, kernel, preferred_element_type=jnp.float32
        ).astype(jnp.bfloat16)
        padded = widen(feature_grad.reshape(BASIS * count, lat_rows, lon_cols, channels))
        padded = padded.reshape(BASIS, count, pad_rows * pad_cols, channels).astype(jnp.float32)
        pulled = jnp.einsum("bts,bmsc->mtc", backward_map, padded, precision=lax.Precision.HIGHEST)
        new_grad = (flat_grad + pulled).astype(jnp.bfloat16).reshape(grad.shape)
        gate_grad, new_grad = (gate_grad, new_grad)
        here = segment_index == depth - 1 - tick_num
        keep_gate = jnp.where(here, gate_grad, keep_gate)
        section_grad = jnp.where(here, new_grad, section_grad)
        if tick_num + 1 < depth:
            grad = pass_behind(new_grad)
    local_grad = (
        jnp.einsum("bmtc,mtd->bcd", keep_spread, keep_gate, preferred_element_type=jnp.float32)
        * grad_scale
    )
    owners = lax.axis_size("lon") * lax.axis_size("lat")
    grad_rows = local_grad.reshape(owners, -1)
    weight_grad = lax.psum_scatter(grad_rows, ("lon", "lat"), scatter_dimension=0, tiled=True)
    return (section_out[None], section_grad[None], weight_grad)


HALO = 8
BAND = 8


def swap(axis, bit):
    return [(i, i ^ bit) for i in range(lax.axis_size(axis))]


def window_plan(lat_rows):
    first = [(a, min(max(a - 4, -HALO), lat_rows + HALO - 16)) for a in range(-HALO, lat_rows + HALO, BAND)]
    second = [(a, a - 4) for a in range(-4, lat_rows + 4, BAND)]
    return first, second


def dot(a, b):
    return jnp.dot(a, b, preferred_element_type=jnp.float32)


def dot_nt(a, b):
    return lax.dot_general(a, b, (((1,), (1,)), ((), ())), preferred_element_type=jnp.float32)


def dot_tn(a, b):
    return lax.dot_general(a, b, (((0,), (0,)), ((), ())), preferred_element_type=jnp.float32)


def make_steps(lat_rows, lon_cols, blocks, members, channels, lat_devices):
    first, second = window_plan(lat_rows)
    nf, ns = len(first), len(second)
    lat_total = lat_rows * lat_devices
    ring = lon_cols * blocks
    band = BAND * lon_cols
    cells = blocks * band
    win = 16 * lon_cols
    own = lat_rows * lon_cols
    edge = HALO * lon_cols
    half_edge = edge // 2
    width = BASIS * channels
    lanes = 128
    pieces = channels // lanes
    halo = edge + half_edge
    state_parts = ((0, edge, 0, 0), (edge, own, 0, None), (edge + own, edge, 0, 1))
    coming_parts = ((0, half_edge, edge, 0), (half_edge, own, own, None), (half_edge + own, half_edge, edge, 1))

    def take(blks, m, parts, low, high):
        found = []
        odd = lax.axis_index("lat") % 2
        for r in blks:
            for start, size, at, side in parts:
                lo, hi = max(low, start), min(high, start + size)
                if lo >= hi:
                    continue
                if side is None:
                    found.append(r[m, at + lo - start : at + hi - start, :])
                else:
                    slot = odd if side else 1 - odd
                    first_row = pl.multiple_of(2 * own + at + lo - start + slot * halo, 16)
                    found.append(r[m, pl.ds(first_row, hi - lo), :])
        return jnp.concatenate(found, axis=0)

    def prep(loaded, both):
        for m in range(members):
            both[m, :own, :] = loaded[m].reshape(own, channels)
            both[m, own:, :] = loaded[members + m].reshape(own, channels)

    def edges(both, toward, away):
        tail = ((own - edge, own), (2 * own - half_edge, 2 * own))
        head = ((0, edge), (own, own + half_edge))

        def fill(spans, ref):
            for m in range(members):
                ref[m, :edge, :] = both[m, spans[0][0] : spans[0][1], :]
                ref[m, edge:, :] = both[m, spans[1][0] : spans[1][1], :]

        @pl.when(lax.axis_index("lat") % 2 == 0)
        def _():
            fill(tail, toward)
            fill(head, away)

        @pl.when(lax.axis_index("lat") % 2 == 1)
        def _():
            fill(head, toward)
            fill(tail, away)

    def maps(plan, lat_step, lon_step, basis, *outs):
        forward, tab = outs[0], outs[-1]
        lon, lat = lax.axis_index("lon"), lax.axis_index("lat")
        base = lat * lat_rows
        tab[...] = jnp.zeros(tab.shape, jnp.float32)
        tab[0:TAPS, :] = lat_step[...].astype(jnp.float32)
        tab[TAPS : 2 * TAPS, :] = lon_step[...].astype(jnp.float32)
        for k in range(TAPS):
            tab[2 * TAPS + k * BASIS : 2 * TAPS + (k + 1) * BASIS, :] = basis[k]
        table = tab[...].astype(jnp.bfloat16)
        source = lax.broadcasted_iota(jnp.int32, (tab.shape[1], cells), 0)
        lane = lax.broadcasted_iota(jnp.int32, (1, cells), 1)
        block, rest = lane // band, lane % band
        row_in, col_in = rest // lon_cols, rest % lon_cols
        column_home = (block ^ lon) * lon_cols + col_in
        piece = 64
        spot = lax.broadcasted_iota(jnp.int32, (piece, cells), 0)
        for i, (a, start) in enumerate(plan):
            row = row_in + (base + a)
            got = dot(table, (source == row).astype(jnp.bfloat16))
            step_lat = got[0:TAPS].astype(jnp.int32)
            step_lon = got[TAPS : 2 * TAPS].astype(jnp.int32)
            target = row + step_lat
            inside = (row >= 0) & (row < lat_total) & (target >= 0) & (target < lat_total)
            column = column_home + step_lon
            column = jnp.where(column < 0, column + ring, column)
            column = jnp.where(column >= ring, column - ring, column)
            local = target - (base + start)
            place = ((column // lon_cols) ^ lon) * win + local * lon_cols + column % lon_cols
            place = jnp.where(inside, place, -1)
            for p in range(0, blocks * win, piece):
                tables = [jnp.zeros((piece, cells), jnp.float32) for _ in range(BASIS)]
                for k in range(TAPS):
                    hit = spot == place[k : k + 1] - p
                    for b in range(BASIS):
                        at = 2 * TAPS + k * BASIS + b
                        tables[b] = tables[b] + jnp.where(hit, got[at : at + 1], 0.0)
                for b in range(BASIS):
                    span = slice(b * cells, (b + 1) * cells)
                    forward[i, span, p : p + piece] = tables[b].T.astype(jnp.bfloat16)
                    if len(outs) == 3:
                        outs[1][i, p : p + piece, span] = tables[b].astype(jnp.bfloat16)

    def put_spread(got, into, at):
        for b in range(BASIS):
            into[at : at + cells, b * channels : (b + 1) * channels] = got[b * cells : (b + 1) * cells]

    def spread(blk, forward, into):
        for m in range(members):
            for g, (a, start) in enumerate(first):
                o = (start + HALO) * lon_cols
                near = take(blk, m, state_parts, o, o + win)
                put_spread(dot(forward[g], near).astype(jnp.bfloat16), into, (m * nf + g) * cells)

    def first_section(blk, total, s1, again, mid, slope):
        for m in range(members):
            for g in range(nf):
                mixed = total[(m * nf + g) * cells : (m * nf + g + 1) * cells]
                sigma = 0.5 + 0.5 * jnp.tanh(0.5 * mixed)
                here = take(blk, m, state_parts, g * band, (g + 1) * band)
                value = (here.astype(jnp.float32) + mixed * sigma).astype(jnp.bfloat16)
                mid[m, :, g * band : (g + 1) * band, :] = value.reshape(blocks, band, channels)
                if slope is not None:
                    tilt = (sigma * (1.0 + mixed * (1.0 - sigma))).astype(slope.dtype).reshape(blocks, band, channels)
                    low, high = max(g * band, half_edge), min((g + 1) * band, 3 * half_edge + own)
                    slope[m, :, low - half_edge : high - half_edge, :] = tilt[:, low - g * band : high - g * band]
            for g in range(ns):
                near = mid[m, :, g * band : g * band + win, :].reshape(blocks * win, channels)
                put_spread(dot(again[g], near).astype(jnp.bfloat16), s1, (m * ns + g) * cells)

    def columns_of(lon):
        return pl.ds(pl.multiple_of(lon * (width // blocks), 128), width // blocks)

    def early(b0, b1, b2, b3, w_own, forward, again, s, left, slope, out, s0, mid):
        blk = (b0, b1, b2, b3)

        @pl.when(lax.axis_index("segment") == 0)
        def _():
            spread(blk, forward, s0)
            first_section(blk, dot(s0[...], w_own[...]), s, again, mid, slope)
            for m in range(members):
                size = (nf - 2) * cells
                left[m * size : (m + 1) * size, :] = s0[(m * nf + 1) * cells : (m * nf + nf - 1) * cells, columns_of(lax.axis_index("lon"))]
                out[m, :, :] = mid[m, 0, edge : edge + own, :]

        @pl.when(lax.axis_index("segment") == 1)
        def _():
            spread(blk, forward, s)

    def partial(s, near_half, far_half, w, part):
        rows = near_half.shape[0]
        here = lax.axis_index("lon") % 2 * (width // 2)
        for base, ref in ((here, near_half), (width // 2 - here, far_half)):
            w[pl.ds(pl.multiple_of(base, 32), rows), :] = ref[...]
        for i in range(2):
            late = slice(i * (width // 2) + rows, (i + 1) * (width // 2))
            w[late, :] = jnp.zeros((width // 2 - rows, channels), w.dtype)

        @pl.when(lax.axis_index("segment") == 1)
        def _():
            part[...] = dot(s[...], w[...])

    def own_part(g):
        return max(g * band, half_edge), min((g + 1) * band, half_edge + own)

    def apply_back(w, gates, feat):
        for b in range(BASIS):
            got = dot_nt(gates[...], w[b * channels : (b + 1) * channels, :]).astype(jnp.bfloat16)
            for i in range(members * ns):
                feat[(i * BASIS + b) * cells : (i * BASIS + b + 1) * cells, :] = got[i * cells : (i + 1) * cells]

    def chain(b0, b1, b2, b3, w_own, w_in, part, ends, again, backward, s, left0, slope, early_out, w,
              out_ref, next_ref, gate_ref, own_ref, p1, p2, p3, late, s1, mid, gates, feat, pull, grads):
        blk = (b0, b1, b2, b3)
        seg, lon, lat = lax.axis_index("segment"), lax.axis_index("lon"), lax.axis_index("lat")
        rest = ends.shape[0] // 2
        rows = width // 2 - rest
        aligned = rows // lanes * lanes
        span = width // 2 - aligned
        for i in range(2):
            piece = ends[i * rest : (i + 1) * rest, :]
            w[i * (width // 2) + rows : (i + 1) * (width // 2), :] = piece
            late[i * span : (i + 1) * span - rest, :] = jnp.zeros((span - rest, channels), late.dtype)
            late[(i + 1) * span - rest : (i + 1) * span, :] = piece

        def complete():
            total = part[...]
            for i in range(2):
                at = i * (width // 2) + aligned
                total = total + dot(s[:, at : at + span], late[i * span : (i + 1) * span, :])
            return total

        def coming_at(m, g):
            return take(blk, m, coming_parts, g * band, (g + 1) * band).astype(jnp.float32)

        def second_section(total, into, last):
            for m in range(members):
                for g in range(ns):
                    at = (m * ns + g) * cells
                    mixed = total[at : at + cells]
                    sigma = 0.5 + 0.5 * jnp.tanh(0.5 * mixed)
                    into[at : at + cells, :] = (coming_at(m, g) * sigma * (1.0 + mixed * (1.0 - sigma))).astype(jnp.bfloat16)
                    if last:
                        low, high = own_part(g)
                        base = mid[m, 0, half_edge + low : half_edge + high, :]
                        local = slice(low - g * band, high - g * band)
                        base = (base.astype(jnp.float32) + mixed[local] * sigma[local]).astype(jnp.bfloat16)
                        out_ref[m, low - half_edge : high - half_edge, :] = base

        def store_grads(left, right):
            got = dot_tn(left, jnp.concatenate(right, axis=0))
            for c in range(pieces):
                grads[pl.ds(c, width // blocks, stride=pieces), :] = got[:, c * lanes : (c + 1) * lanes]

        @pl.when(seg == 0)
        def _():
            second_section(dot(s[: members * ns * cells, :], w[...]), gates, False)
            out_ref[...] = early_out[...]
            apply_back(w, gates, feat)
            for m in range(members):
                for g in range(ns):
                    at = (m * ns + g) * cells * BASIS
                    low = max(g * band, half_edge)
                    high = min(g * band + win, 3 * half_edge + own)
                    local = range(0, blocks * win, win)
                    rows = [backward[g, q + low - g * band : q + high - g * band, :] for q in local]
                    got = dot(jnp.concatenate(rows, axis=0), feat[at : at + BASIS * cells, :])
                    got = got.reshape(blocks, high - low, channels)
                    turn = low if g == 0 else (g + 1) * band
                    if g > 0:
                        pull[m, :, low:turn, :] += got[:, : turn - low]
                    pull[m, :, turn:high, :] = got[:, turn - low :]
            right = []
            step = half_edge
            for m in range(members):
                for g in range(ns):
                    at = (m * ns + g) * cells
                    span = slice(half_edge + g * band, half_edge + (g + 1) * band)
                    value = (coming_at(m, g) + pull[m, :, span, :].reshape(cells, channels)).astype(jnp.bfloat16)
                    low, high = own_part(g)
                    next_ref[m, low - half_edge : high - half_edge, :] = value[low - g * band : high - g * band]
                    tilt = slope[m, :, g * band : (g + 1) * band, :].reshape(cells, channels)
                    gate_ref[at : at + cells, :] = (value.astype(jnp.float32) * tilt).astype(jnp.bfloat16)
                for g in range(1, nf - 1):
                    for q in range(blocks):
                        for o in range(0, band, step):
                            spot = half_edge + (g - 1) * band + o
                            turn, rest = spot // band, spot % band
                            at = (m * ns + turn) * cells + q * band + rest
                            right.append(gate_ref[at : at + step, :])
            store_grads(left0[...], right)

        @pl.when(seg == 1)
        def _():
            first_section(blk, complete(), s1, again, mid, None)
            second_section(dot(s1[...], w_own[...]), gate_ref, True)
            left, right = [], []
            for m in range(members):
                next_ref[m, :, :] = b0[m, own : 2 * own, :]
                for g in range(ns):
                    low, high = own_part(g)
                    for q in range(blocks):
                        at = (m * ns + g) * cells + q * band - g * band
                        left.append(s1[at + low : at + high, columns_of(lon)])
                        right.append(gate_ref[at + low : at + high, :])
            store_grads(jnp.concatenate(left, axis=0), right)

        share = width // blocks // lat_devices * pieces

        def rows_of(index):
            return grads[pl.ds(pl.multiple_of(index * share, share), share), :]

        own_ref[...] = rows_of(lat)
        for bit, ref in ((1, p1), (2, p2), (3, p3)):
            ref[...] = rows_of(lat ^ bit).astype(jnp.bfloat16)

    def finish(w_own, backward, gates, next_ref, last_ref, grad_ref, out_ref, feat, pull):
        apply_back(w_own, gates, feat)
        for m in range(members):
            for g in range(ns):
                at = (m * ns + g) * cells * BASIS
                got = dot(backward[g, 0:win, :], feat[at : at + BASIS * cells, :])
                if g == 0:
                    pull[m, :win, :] = got
                else:
                    pull[m, g * band : (g + 1) * band, :] += got[:band]
                    pull[m, (g + 1) * band : g * band + win, :] = got[band:]
            total = next_ref[m].astype(jnp.float32) + pull[m, edge : edge + own, :]
            grad_ref[m] = total.astype(jnp.bfloat16).reshape(lat_rows, lon_cols, channels)
            out_ref[m] = last_ref[m].reshape(lat_rows, lon_cols, channels)

    return prep, edges, maps, early, partial, chain, finish


def add_up(scale, mine, p1, p2, p3, out):
    out[...] = (mine[...] + p1[...].astype(jnp.float32) + p2[...].astype(jnp.float32) + p3[...].astype(jnp.float32)) * scale


def whole_ring(inputs, cotangent, weights, basis_values, lat_step, lon_step):
    members, lat_rows, lon_cols, channels = inputs.shape
    blocks = lax.axis_size("lon")
    lat_devices = lax.axis_size("lat")
    lat_total = lat_rows * lat_devices
    grad_scale = 1.0 / math.sqrt(members * lat_total * lon_cols * blocks)
    own = lat_rows * lon_cols
    edge = HALO * lon_cols
    half_edge = edge // 2
    halo = edge + half_edge
    width = BASIS * channels
    half_type, full_type = jnp.bfloat16, jnp.float32
    shape = jax.ShapeDtypeStruct
    first, second = window_plan(lat_rows)
    nf, ns = len(first), len(second)
    cells = blocks * BAND * lon_cols
    win = 16 * lon_cols
    vmem = pl.BlockSpec(memory_space=pltpu.VMEM)

    def call(body, name, outs, ins, mib, gflops, scratch=(), aliases={}):
        return pl.pallas_call(
            body,
            out_shape=outs,
            in_specs=[vmem] * len(ins),
            out_specs=(vmem,) * len(outs),
            scratch_shapes=list(scratch),
            input_output_aliases=aliases,
            compiler_params=pltpu.CompilerParams(vmem_limit_bytes=int(mib * 1024 * 1024)),
            cost_estimate=pl.CostEstimate(flops=int(gflops * 1e9), bytes_accessed=int(gflops * 1e6), transcendentals=0),
            name=name,
        )(*ins)

    prep, edges, maps, early, partial, chain, finish = make_steps(lat_rows, lon_cols, blocks, members, channels, lat_devices)
    kernel = weights.reshape(width, channels)
    rest = width // 2 * 5 // 48
    rows = width // 2 - rest
    half = lax.dynamic_slice_in_dim(kernel, lax.axis_index("lon") % 2 * (width // 2), rows, 0)
    ends = jnp.concatenate([kernel[rows : rows + rest], kernel[width - rest :]], axis=0)
    near_ends = lax.ppermute(ends, "segment", swap("segment", 1))
    near_half = lax.ppermute(half, "segment", swap("segment", 1))
    half, inputs, cotangent = lax.optimization_barrier((half, inputs, cotangent))
    loaded = jnp.concatenate([inputs, cotangent], axis=0)
    (both,) = call(prep, "prep", (shape((members, 2 * own, channels), half_type),), (loaded,), 4, 0.0)
    sides_type = shape((members, halo, channels), half_type)
    toward, away = call(edges, "edges", (sides_type, sides_type), (both,), 4, 0.0)
    both_y = lax.ppermute(both, "lon", swap("lon", 2))
    near_pairs = [(i, i ^ 1) for i in range(lat_devices)]
    far_pairs = [(i, j) for i in range(lat_devices) for j in [i + 1 if i % 2 else i - 1] if 0 <= j < lat_devices]
    from_near = lax.ppermute(toward, "lat", near_pairs)
    from_far = lax.ppermute(away, "lat", far_pairs)
    tables = (lat_step.T, lon_step.T, jnp.transpose(basis_values, (1, 2, 0)))
    _, _, *tables = lax.optimization_barrier((toward, away, *tables))
    (forward,) = call(
        functools.partial(maps, first),
        "maps_first",
        (shape((nf, BASIS * cells, blocks * win), half_type),),
        tables,
        4,
        0.0,
        (pltpu.VMEM((48, lat_total), full_type),),
    )
    from_near, from_far, forward = lax.optimization_barrier((from_near, from_far, forward))
    sides = jnp.concatenate([from_near, from_far], axis=1)
    sides, both_y = lax.optimization_barrier((sides, both_y))
    sides_y = lax.ppermute(sides, "lon", swap("lon", 2))
    b0 = jnp.concatenate([both, sides], axis=1)
    b1 = lax.ppermute(b0, "lon", swap("lon", 1))
    b0, *tables = lax.optimization_barrier((b0, *tables))
    again, backward = call(
        functools.partial(maps, second),
        "maps_again",
        (shape((ns, BASIS * cells, blocks * win), half_type), shape((ns, blocks * win, BASIS * cells), half_type)),
        tables,
        4,
        0.0,
        (pltpu.VMEM((48, lat_total), full_type),),
    )
    b2 = jnp.concatenate([both_y, sides_y], axis=1)
    b2, again, near_half = lax.optimization_barrier((b2, again, near_half))
    b3 = lax.ppermute(b2, "lon", swap("lon", 1))
    far_half = lax.ppermute(near_half, "lon", swap("lon", 1))
    s_type = (members * nf * cells, width)
    s, left, slope, early_out = call(
        early,
        "early",
        (
            shape(s_type, half_type),
            shape((members * (nf - 2) * cells, width // blocks), half_type),
            shape((members, blocks, own + edge, channels), half_type),
            shape((members, own, channels), half_type),
        ),
        (b0, b1, b2, b3, kernel, forward, again),
        12,
        3.0,
        (pltpu.VMEM(s_type, half_type), pltpu.VMEM((members, blocks, own + 2 * edge, channels), half_type)),
    )
    w_type = shape((width, channels), half_type)
    w, part = call(
        partial,
        "partial",
        (w_type, shape((s_type[0], channels), full_type)),
        (s, near_half, far_half),
        8,
        1.5,
    )
    near_ends, part = lax.optimization_barrier((near_ends, part))
    lines = (width // blocks // lat_devices * channels // 128, 128)
    _, out, follow, gates, mine, *parts = call(
        chain,
        "chain",
        (
            w_type,
            shape((members, own, channels), half_type),
            shape((members, own, channels), half_type),
            shape((members * ns * cells, channels), half_type),
            shape(lines, full_type),
        )
        + (shape(lines, half_type),) * 3,
        (b0, b1, b2, b3, kernel, w, part, near_ends, again, backward, s, left, slope, early_out),
        18,
        6.0,
        (
            pltpu.VMEM((2 * (width // 2 - (width // 2 - rest) // 128 * 128), channels), half_type),
            pltpu.VMEM((members * ns * cells, width), half_type),
            pltpu.VMEM((members, blocks, own + 2 * edge, channels), half_type),
            pltpu.VMEM((members * ns * cells, channels), half_type),
            pltpu.VMEM((members * ns * cells * BASIS, channels), half_type),
            pltpu.VMEM((members, blocks, own + 2 * edge, channels), full_type),
            pltpu.VMEM((width // blocks * channels // 128, 128), full_type),
        ),
        {5: 0},
    )
    got = [lax.ppermute(part, "lat", swap("lat", bit)) for bit, part in reversed(list(zip((1, 2, 3), parts)))]
    block = (members, lat_rows, lon_cols, channels)
    grad, out = call(
        finish,
        "finish",
        (shape(block, half_type),) * 2,
        (kernel, backward, gates, follow, out),
        10,
        2.0,
        (
            pltpu.VMEM((members * ns * cells * BASIS, channels), half_type),
            pltpu.VMEM((members, own + 2 * edge, channels), full_type),
        ),
    )
    (total,) = call(functools.partial(add_up, grad_scale), "add_up", (shape(lines, full_type),), (mine, *got), 2, 0.1)
    return (out[None], grad[None], total.reshape(1, lines[0] * lines[1]))


def fits_ring(mesh, inputs):
    sizes = dict(mesh.shape)
    rows, cols = inputs.shape[1] // sizes["lat"], inputs.shape[2] // sizes["lon"]
    return sizes["segment"] == 2 and sizes["lon"] == 4 and sizes["lat"] == 4 and rows == 16 and cols == 4


def solution(mesh):
    def apply(*args):
        body = whole_ring if fits_ring(mesh, args[0]) else per_device
        return jax.shard_map(
            body,
            mesh=mesh,
            in_specs=(
                P(None, "lat", "lon", None),
                P(None, "lat", "lon", None),
                P("segment", None, None, None),
                P(),
                P(),
                P(),
            ),
            out_specs=(
                P("segment", None, "lat", "lon", None),
                P("segment", None, "lat", "lon", None),
                P("segment", ("lon", "lat")),
            ),
            check_vma=False,
        )(*args)

    return apply
```

```python
import functools
import math

import jax
import jax.numpy as jnp
from jax import lax
from jax.experimental import pallas as pl
from jax.experimental.pallas import tpu as pltpu
from jax.sharding import PartitionSpec as P

BASIS = 3
TAPS = 9
REACH = 2


def with_halo(array, sides, width):
    for axis, dim in sides:
        size, length = (lax.axis_size(axis), array.shape[dim])
        up = [(i, (i + 1) % size) for i in range(size)]
        down = [(j, i) for i, j in up]
        last = lax.slice_in_dim(array, length - width, length, axis=dim)
        first = lax.slice_in_dim(array, 0, width, axis=dim)
        before = lax.ppermute(last, axis, up)
        after = lax.ppermute(first, axis, down)
        array = jnp.concatenate([before, array, after], axis=dim)
    return array


def shifted(block, axis, distance):
    devices = range(lax.axis_size(axis))
    route = [(i - distance, i) for i in devices if i - distance in devices]
    return lax.ppermute(block, axis, route)


def widen(features):
    return with_halo(features, (("lon", 2), ("lat", 1)), REACH)


def pass_ahead(result):
    return shifted(result, "segment", 1)


def pass_behind(result):
    return shifted(result, "segment", -1)


def build_tables(basis_values, lat_step, lon_step, lat_rows, lon_cols, lat_index, lat_total):
    pad_rows = lat_rows + 2 * REACH
    pad_cols = lon_cols + 2 * REACH
    lat_padded = jnp.pad(lat_step, ((REACH, REACH), (0, 0)))
    lon_padded = jnp.pad(lon_step, ((REACH, REACH), (0, 0)))
    basis_padded = jnp.pad(basis_values, ((REACH, REACH), (0, 0), (0, 0)))
    row_start = lat_index * lat_rows
    lat_near = lax.dynamic_slice_in_dim(lat_padded, row_start, pad_rows, 0)
    lon_near = lax.dynamic_slice_in_dim(lon_padded, row_start, pad_rows, 0)
    basis_near = lax.dynamic_slice_in_dim(basis_padded, row_start, pad_rows, 0)
    lat_own = lat_near[REACH : REACH + lat_rows]
    lon_own = lon_near[REACH : REACH + lat_rows]
    basis_own = basis_near[REACH : REACH + lat_rows]
    own_rows = row_start + jnp.arange(lat_rows)
    inside = (own_rows[:, None] + lat_own >= 0) & (own_rows[:, None] + lat_own < lat_total)
    row_grid = jnp.arange(lat_rows)[:, None, None]
    col_grid = jnp.arange(lon_cols)[None, :, None]
    source = (row_grid + REACH + lat_own[:, None, :]) * pad_cols + (
        col_grid + REACH + lon_own[:, None, :]
    )
    tap_weight = jnp.where(inside[:, None, :, None], basis_own[:, None, :, :], 0.0)
    tap_weight = jnp.broadcast_to(tap_weight, (lat_rows, lon_cols, TAPS, BASIS))
    picker = (source[..., None] == jnp.arange(pad_rows * pad_cols)).astype(jnp.float32)
    forward_map = jnp.einsum("ijkb,ijks->bijs", tap_weight, picker, precision=lax.Precision.HIGHEST)
    forward_map = forward_map.reshape(BASIS, lat_rows * lon_cols, pad_rows * pad_cols)
    near_rows = row_start - REACH + jnp.arange(pad_rows)
    real_row = (near_rows >= 0) & (near_rows < lat_total)
    pad_row_grid = jnp.arange(pad_rows)[:, None, None]
    pad_col_grid = jnp.arange(pad_cols)[None, :, None]
    target_row = pad_row_grid - REACH + lat_near[:, None, :]
    target_col = pad_col_grid - REACH + lon_near[:, None, :]
    landed = (
        (target_row >= 0)
        & (target_row < lat_rows)
        & (target_col >= 0)
        & (target_col < lon_cols)
        & real_row[:, None, None]
    )
    target = target_row * lon_cols + target_col
    back_weight = jnp.where(landed[..., None], basis_near[:, None, :, :], 0.0)
    catcher = (target[..., None] == jnp.arange(lat_rows * lon_cols)).astype(jnp.float32)
    backward_map = jnp.einsum(
        "pqkb,pqkt->btpq", back_weight, catcher, precision=lax.Precision.HIGHEST
    )
    backward_map = backward_map.reshape(BASIS, lat_rows * lon_cols, pad_rows * pad_cols)
    return (forward_map, backward_map)


def per_device(inputs, cotangent, weights, basis_values, lat_step, lon_step):
    members, lat_rows, lon_cols, channels = inputs.shape
    pad_rows = lat_rows + 2 * REACH
    pad_cols = lon_cols + 2 * REACH
    cells = lat_rows * lon_cols
    lat_index = lax.axis_index("lat")
    lat_total = lat_rows * lax.axis_size("lat")
    segment_index = lax.axis_index("segment")
    depth = lax.axis_size("segment")
    grad_scale = 1.0 / math.sqrt(members * lat_total * lon_cols * lax.axis_size("lon"))
    forward_map, backward_map = build_tables(
        basis_values, lat_step, lon_step, lat_rows, lon_cols, lat_index, lat_total
    )
    kernel = weights[0]
    keep_spread = jnp.zeros((BASIS, members, cells, channels), jnp.bfloat16)
    keep_mixed = jnp.zeros((members, cells, channels), jnp.float32)
    keep_gate = jnp.zeros((members, cells, channels), jnp.bfloat16)
    section_out = jnp.zeros(inputs.shape, jnp.bfloat16)
    section_grad = jnp.zeros(inputs.shape, jnp.bfloat16)
    carry = inputs
    for tick_num in range(depth):
        layer_count = carry.shape[0]
        layer_padded = (
            widen(carry).reshape(layer_count, pad_rows * pad_cols, channels).astype(jnp.float32)
        )
        spread = jnp.einsum(
            "bts,msc->bmtc", forward_map, layer_padded, precision=lax.Precision.HIGHEST
        ).astype(jnp.bfloat16)
        layer_mixed = jnp.einsum(
            "bmtc,bcd->mtd", spread, kernel, preferred_element_type=jnp.float32
        )
        result = (
            carry.reshape(layer_count, cells, channels).astype(jnp.float32)
            + jax.nn.silu(layer_mixed)
        ).astype(jnp.bfloat16)
        spread, mixed, result = (spread, layer_mixed, result.reshape(carry.shape))
        here = segment_index == tick_num
        keep_spread = jnp.where(here, spread, keep_spread)
        keep_mixed = jnp.where(here, mixed, keep_mixed)
        section_out = jnp.where(here, result, section_out)
        if tick_num + 1 < depth:
            carry = pass_ahead(result)
    grad = cotangent
    for tick_num in range(depth):
        count = grad.shape[0]
        flat_grad = grad.reshape(count, cells, channels).astype(jnp.float32)
        sigma = jax.nn.sigmoid(keep_mixed)
        gate_grad = (flat_grad * sigma * (1.0 + keep_mixed * (1.0 - sigma))).astype(jnp.bfloat16)
        feature_grad = jnp.einsum(
            "mtd,bcd->bmtc", gate_grad, kernel, preferred_element_type=jnp.float32
        ).astype(jnp.bfloat16)
        padded = widen(feature_grad.reshape(BASIS * count, lat_rows, lon_cols, channels))
        padded = padded.reshape(BASIS, count, pad_rows * pad_cols, channels).astype(jnp.float32)
        pulled = jnp.einsum("bts,bmsc->mtc", backward_map, padded, precision=lax.Precision.HIGHEST)
        new_grad = (flat_grad + pulled).astype(jnp.bfloat16).reshape(grad.shape)
        gate_grad, new_grad = (gate_grad, new_grad)
        here = segment_index == depth - 1 - tick_num
        keep_gate = jnp.where(here, gate_grad, keep_gate)
        section_grad = jnp.where(here, new_grad, section_grad)
        if tick_num + 1 < depth:
            grad = pass_behind(new_grad)
    local_grad = (
        jnp.einsum("bmtc,mtd->bcd", keep_spread, keep_gate, preferred_element_type=jnp.float32)
        * grad_scale
    )
    owners = lax.axis_size("lon") * lax.axis_size("lat")
    grad_rows = local_grad.reshape(owners, -1)
    weight_grad = lax.psum_scatter(grad_rows, ("lon", "lat"), scatter_dimension=0, tiled=True)
    return (section_out[None], section_grad[None], weight_grad)


HALO = 8
BAND = 8


def swap(axis, bit):
    return [(i, i ^ bit) for i in range(lax.axis_size(axis))]


def window_plan(lat_rows):
    first = [(a, min(max(a - 4, -HALO), lat_rows + HALO - 16)) for a in range(-HALO, lat_rows + HALO, BAND)]
    second = [(a, a - 4) for a in range(-4, lat_rows + 4, BAND)]
    return first, second


def dot(a, b):
    return jnp.dot(a, b, preferred_element_type=jnp.float32)


def dot_nt(a, b):
    return lax.dot_general(a, b, (((1,), (1,)), ((), ())), preferred_element_type=jnp.float32)


def dot_tn(a, b):
    return lax.dot_general(a, b, (((0,), (0,)), ((), ())), preferred_element_type=jnp.float32)


def make_steps(lat_rows, lon_cols, blocks, members, channels, lat_devices):
    first, second = window_plan(lat_rows)
    nf, ns = len(first), len(second)
    lat_total = lat_rows * lat_devices
    ring = lon_cols * blocks
    band = BAND * lon_cols
    cells = blocks * band
    win = 16 * lon_cols
    own = lat_rows * lon_cols
    edge = HALO * lon_cols
    half_edge = edge // 2
    width = BASIS * channels
    lanes = 128
    pieces = channels // lanes
    halo = edge + half_edge
    state_parts = ((0, edge, 0, 0), (edge, own, 0, None), (edge + own, edge, 0, 1))
    coming_parts = ((0, half_edge, edge, 0), (half_edge, own, own, None), (half_edge + own, half_edge, edge, 1))

    def take(blks, m, parts, low, high):
        found = []
        odd = lax.axis_index("lat") % 2
        for r in blks:
            for start, size, at, side in parts:
                lo, hi = max(low, start), min(high, start + size)
                if lo >= hi:
                    continue
                if side is None:
                    found.append(r[m, at + lo - start : at + hi - start, :])
                else:
                    slot = odd if side else 1 - odd
                    first_row = pl.multiple_of(2 * own + at + lo - start + slot * halo, 16)
                    found.append(r[m, pl.ds(first_row, hi - lo), :])
        return jnp.concatenate(found, axis=0)

    def prep(loaded, both):
        for m in range(members):
            both[m, :own, :] = loaded[m].reshape(own, channels)
            both[m, own:, :] = loaded[members + m].reshape(own, channels)

    def edges(both, toward, away):
        tail = ((own - edge, own), (2 * own - half_edge, 2 * own))
        head = ((0, edge), (own, own + half_edge))

        def fill(spans, ref):
            for m in range(members):
                ref[m, :edge, :] = both[m, spans[0][0] : spans[0][1], :]
                ref[m, edge:, :] = both[m, spans[1][0] : spans[1][1], :]

        @pl.when(lax.axis_index("lat") % 2 == 0)
        def _():
            fill(tail, toward)
            fill(head, away)

        @pl.when(lax.axis_index("lat") % 2 == 1)
        def _():
            fill(head, toward)
            fill(tail, away)

    def maps(plan, lat_step, lon_step, basis, *outs):
        forward, tab = outs[0], outs[-1]
        lon, lat = lax.axis_index("lon"), lax.axis_index("lat")
        base = lat * lat_rows
        tab[...] = jnp.zeros(tab.shape, jnp.float32)
        tab[0:TAPS, :] = lat_step[...].astype(jnp.float32)
        tab[TAPS : 2 * TAPS, :] = lon_step[...].astype(jnp.float32)
        for k in range(TAPS):
            tab[2 * TAPS + k * BASIS : 2 * TAPS + (k + 1) * BASIS, :] = basis[k]
        table = tab[...].astype(jnp.bfloat16)
        source = lax.broadcasted_iota(jnp.int32, (tab.shape[1], cells), 0)
        lane = lax.broadcasted_iota(jnp.int32, (1, cells), 1)
        block, rest = lane // band, lane % band
        row_in, col_in = rest // lon_cols, rest % lon_cols
        column_home = (block ^ lon) * lon_cols + col_in
        piece = 64
        spot = lax.broadcasted_iota(jnp.int32, (piece, cells), 0)
        for i, (a, start) in enumerate(plan):
            row = row_in + (base + a)
            got = dot(table, (source == row).astype(jnp.bfloat16))
            step_lat = got[0:TAPS].astype(jnp.int32)
            step_lon = got[TAPS : 2 * TAPS].astype(jnp.int32)
            target = row + step_lat
            inside = (row >= 0) & (row < lat_total) & (target >= 0) & (target < lat_total)
            column = column_home + step_lon
            column = jnp.where(column < 0, column + ring, column)
            column = jnp.where(column >= ring, column - ring, column)
            local = target - (base + start)
            place = ((column // lon_cols) ^ lon) * win + local * lon_cols + column % lon_cols
            place = jnp.where(inside, place, -1)
            for p in range(0, blocks * win, piece):
                tables = [jnp.zeros((piece, cells), jnp.float32) for _ in range(BASIS)]
                for k in range(TAPS):
                    hit = spot == place[k : k + 1] - p
                    for b in range(BASIS):
                        at = 2 * TAPS + k * BASIS + b
                        tables[b] = tables[b] + jnp.where(hit, got[at : at + 1], 0.0)
                for b in range(BASIS):
                    span = slice(b * cells, (b + 1) * cells)
                    forward[i, span, p : p + piece] = tables[b].T.astype(jnp.bfloat16)
                    if len(outs) == 3:
                        outs[1][i, p : p + piece, span] = tables[b].astype(jnp.bfloat16)

    def put_spread(got, into, at):
        for b in range(BASIS):
            into[at : at + cells, b * channels : (b + 1) * channels] = got[b * cells : (b + 1) * cells]

    def spread(blk, forward, into):
        for m in range(members):
            for g, (a, start) in enumerate(first):
                o = (start + HALO) * lon_cols
                near = take(blk, m, state_parts, o, o + win)
                put_spread(dot(forward[g], near).astype(jnp.bfloat16), into, (m * nf + g) * cells)

    def first_section(blk, total, s1, again, mid, slope):
        for m in range(members):
            for g in range(nf):
                mixed = total[(m * nf + g) * cells : (m * nf + g + 1) * cells]
                sigma = 0.5 + 0.5 * jnp.tanh(0.5 * mixed)
                here = take(blk, m, state_parts, g * band, (g + 1) * band)
                value = (here.astype(jnp.float32) + mixed * sigma).astype(jnp.bfloat16)
                mid[m, :, g * band : (g + 1) * band, :] = value.reshape(blocks, band, channels)
                if slope is not None:
                    tilt = (sigma * (1.0 + mixed * (1.0 - sigma))).astype(slope.dtype).reshape(blocks, band, channels)
                    low, high = max(g * band, half_edge), min((g + 1) * band, 3 * half_edge + own)
                    slope[m, :, low - half_edge : high - half_edge, :] = tilt[:, low - g * band : high - g * band]
            for g in range(ns):
                near = mid[m, :, g * band : g * band + win, :].reshape(blocks * win, channels)
                put_spread(dot(again[g], near).astype(jnp.bfloat16), s1, (m * ns + g) * cells)

    def columns_of(lon):
        return pl.ds(pl.multiple_of(lon * (width // blocks), 128), width // blocks)

    def early(b0, b1, b2, b3, w_own, forward, again, s, left, slope, out, s0, mid):
        blk = (b0, b1, b2, b3)

        @pl.when(lax.axis_index("segment") == 0)
        def _():
            spread(blk, forward, s0)
            first_section(blk, dot(s0[...], w_own[...]), s, again, mid, slope)
            for m in range(members):
                size = (nf - 2) * cells
                left[m * size : (m + 1) * size, :] = s0[(m * nf + 1) * cells : (m * nf + nf - 1) * cells, columns_of(lax.axis_index("lon"))]
                out[m, :, :] = mid[m, 0, edge : edge + own, :]

        @pl.when(lax.axis_index("segment") == 1)
        def _():
            spread(blk, forward, s)

    def partial(s, near_half, far_half, w, part):
        rows = near_half.shape[0]
        here = lax.axis_index("lon") % 2 * (width // 2)
        for base, ref in ((here, near_half), (width // 2 - here, far_half)):
            w[pl.ds(pl.multiple_of(base, 32), rows), :] = ref[...]
        for i in range(2):
            late = slice(i * (width // 2) + rows, (i + 1) * (width // 2))
            w[late, :] = jnp.zeros((width // 2 - rows, channels), w.dtype)

        @pl.when(lax.axis_index("segment") == 1)
        def _():
            part[...] = dot(s[...], w[...])

    def own_part(g):
        return max(g * band, half_edge), min((g + 1) * band, half_edge + own)

    def apply_back(w, gates, feat):
        for b in range(BASIS):
            got = dot_nt(gates[...], w[b * channels : (b + 1) * channels, :]).astype(jnp.bfloat16)
            for i in range(members * ns):
                feat[(i * BASIS + b) * cells : (i * BASIS + b + 1) * cells, :] = got[i * cells : (i + 1) * cells]

    def chain(b0, b1, b2, b3, w_own, w_in, part, ends, again, backward, s, left0, slope, early_out, w,
              out_ref, next_ref, gate_ref, own_ref, p1, p2, p3, late, s1, mid, gates, feat, pull, grads):
        blk = (b0, b1, b2, b3)
        seg, lon, lat = lax.axis_index("segment"), lax.axis_index("lon"), lax.axis_index("lat")
        rest = ends.shape[0] // 2
        rows = width // 2 - rest
        aligned = rows // lanes * lanes
        span = width // 2 - aligned
        for i in range(2):
            piece = ends[i * rest : (i + 1) * rest, :]
            w[i * (width // 2) + rows : (i + 1) * (width // 2), :] = piece
            late[i * span : (i + 1) * span - rest, :] = jnp.zeros((span - rest, channels), late.dtype)
            late[(i + 1) * span - rest : (i + 1) * span, :] = piece

        def complete():
            total = part[...]
            for i in range(2):
                at = i * (width // 2) + aligned
                total = total + dot(s[:, at : at + span], late[i * span : (i + 1) * span, :])
            return total

        def coming_at(m, g):
            return take(blk, m, coming_parts, g * band, (g + 1) * band).astype(jnp.float32)

        def second_section(total, into, last):
            for m in range(members):
                for g in range(ns):
                    at = (m * ns + g) * cells
                    mixed = total[at : at + cells]
                    sigma = 0.5 + 0.5 * jnp.tanh(0.5 * mixed)
                    into[at : at + cells, :] = (coming_at(m, g) * sigma * (1.0 + mixed * (1.0 - sigma))).astype(jnp.bfloat16)
                    if last:
                        low, high = own_part(g)
                        base = mid[m, 0, half_edge + low : half_edge + high, :]
                        local = slice(low - g * band, high - g * band)
                        base = (base.astype(jnp.float32) + mixed[local] * sigma[local]).astype(jnp.bfloat16)
                        out_ref[m, low - half_edge : high - half_edge, :] = base

        def store_grads(left, right):
            got = dot_tn(left, jnp.concatenate(right, axis=0))
            for c in range(pieces):
                grads[pl.ds(c, width // blocks, stride=pieces), :] = got[:, c * lanes : (c + 1) * lanes]

        @pl.when(seg == 0)
        def _():
            second_section(dot(s[: members * ns * cells, :], w[...]), gates, False)
            out_ref[...] = early_out[...]
            apply_back(w, gates, feat)
            for m in range(members):
                for g in range(ns):
                    at = (m * ns + g) * cells * BASIS
                    low = max(g * band, half_edge)
                    high = min(g * band + win, 3 * half_edge + own)
                    local = range(0, blocks * win, win)
                    rows = [backward[g, q + low - g * band : q + high - g * band, :] for q in local]
                    got = dot(jnp.concatenate(rows, axis=0), feat[at : at + BASIS * cells, :])
                    got = got.reshape(blocks, high - low, channels)
                    turn = low if g == 0 else (g + 1) * band
                    if g > 0:
                        pull[m, :, low:turn, :] += got[:, : turn - low]
                    pull[m, :, turn:high, :] = got[:, turn - low :]
            right = []
            step = half_edge
            for m in range(members):
                for g in range(ns):
                    at = (m * ns + g) * cells
                    span = slice(half_edge + g * band, half_edge + (g + 1) * band)
                    value = (coming_at(m, g) + pull[m, :, span, :].reshape(cells, channels)).astype(jnp.bfloat16)
                    low, high = own_part(g)
                    next_ref[m, low - half_edge : high - half_edge, :] = value[low - g * band : high - g * band]
                    tilt = slope[m, :, g * band : (g + 1) * band, :].reshape(cells, channels)
                    gate_ref[at : at + cells, :] = (value.astype(jnp.float32) * tilt).astype(jnp.bfloat16)
                for g in range(1, nf - 1):
                    for q in range(blocks):
                        for o in range(0, band, step):
                            spot = half_edge + (g - 1) * band + o
                            turn, rest = spot // band, spot % band
                            at = (m * ns + turn) * cells + q * band + rest
                            right.append(gate_ref[at : at + step, :])
            store_grads(left0[...], right)

        @pl.when(seg == 1)
        def _():
            first_section(blk, complete(), s1, again, mid, None)
            second_section(dot(s1[...], w_own[...]), gate_ref, True)
            left, right = [], []
            for m in range(members):
                next_ref[m, :, :] = b0[m, own : 2 * own, :]
                for g in range(ns):
                    low, high = own_part(g)
                    for q in range(blocks):
                        at = (m * ns + g) * cells + q * band - g * band
                        left.append(s1[at + low : at + high, columns_of(lon)])
                        right.append(gate_ref[at + low : at + high, :])
            store_grads(jnp.concatenate(left, axis=0), right)

        share = width // blocks // lat_devices * pieces

        def rows_of(index):
            return grads[pl.ds(pl.multiple_of(index * share, share), share), :]

        own_ref[...] = rows_of(lat)
        for bit, ref in ((1, p1), (2, p2), (3, p3)):
            ref[...] = rows_of(lat ^ bit).astype(jnp.bfloat16)

    def finish(w_own, backward, gates, next_ref, last_ref, grad_ref, out_ref, feat, pull):
        apply_back(w_own, gates, feat)
        for m in range(members):
            for g in range(ns):
                at = (m * ns + g) * cells * BASIS
                got = dot(backward[g, 0:win, :], feat[at : at + BASIS * cells, :])
                if g == 0:
                    pull[m, :win, :] = got
                else:
                    pull[m, g * band : (g + 1) * band, :] += got[:band]
                    pull[m, (g + 1) * band : g * band + win, :] = got[band:]
            total = next_ref[m].astype(jnp.float32) + pull[m, edge : edge + own, :]
            grad_ref[m] = total.astype(jnp.bfloat16).reshape(lat_rows, lon_cols, channels)
            out_ref[m] = last_ref[m].reshape(lat_rows, lon_cols, channels)

    return prep, edges, maps, early, partial, chain, finish


def add_up(scale, mine, p1, p2, p3, out):
    out[...] = (mine[...] + p1[...].astype(jnp.float32) + p2[...].astype(jnp.float32) + p3[...].astype(jnp.float32)) * scale


def whole_ring(inputs, cotangent, weights, basis_values, lat_step, lon_step):
    members, lat_rows, lon_cols, channels = inputs.shape
    blocks = lax.axis_size("lon")
    lat_devices = lax.axis_size("lat")
    lat_total = lat_rows * lat_devices
    grad_scale = 1.0 / math.sqrt(members * lat_total * lon_cols * blocks)
    own = lat_rows * lon_cols
    edge = HALO * lon_cols
    half_edge = edge // 2
    halo = edge + half_edge
    width = BASIS * channels
    half_type, full_type = jnp.bfloat16, jnp.float32
    shape = jax.ShapeDtypeStruct
    first, second = window_plan(lat_rows)
    nf, ns = len(first), len(second)
    cells = blocks * BAND * lon_cols
    win = 16 * lon_cols
    vmem = pl.BlockSpec(memory_space=pltpu.VMEM)

    def call(body, name, outs, ins, mib, gflops, scratch=(), aliases={}):
        return pl.pallas_call(
            body,
            out_shape=outs,
            in_specs=[vmem] * len(ins),
            out_specs=(vmem,) * len(outs),
            scratch_shapes=list(scratch),
            input_output_aliases=aliases,
            compiler_params=pltpu.CompilerParams(vmem_limit_bytes=int(mib * 1024 * 1024)),
            cost_estimate=pl.CostEstimate(flops=int(gflops * 1e9), bytes_accessed=int(gflops * 1e6), transcendentals=0),
            name=name,
        )(*ins)

    prep, edges, maps, early, partial, chain, finish = make_steps(lat_rows, lon_cols, blocks, members, channels, lat_devices)
    kernel = weights.reshape(width, channels)
    rest = width // 2 // 12
    rows = width // 2 - rest
    half = lax.dynamic_slice_in_dim(kernel, lax.axis_index("lon") % 2 * (width // 2), rows, 0)
    ends = jnp.concatenate([kernel[rows : rows + rest], kernel[width - rest :]], axis=0)
    near_ends = lax.ppermute(ends, "segment", swap("segment", 1))
    near_half = lax.ppermute(half, "segment", swap("segment", 1))
    half, inputs, cotangent = lax.optimization_barrier((half, inputs, cotangent))
    loaded = jnp.concatenate([inputs, cotangent], axis=0)
    (both,) = call(prep, "prep", (shape((members, 2 * own, channels), half_type),), (loaded,), 4, 0.0)
    sides_type = shape((members, halo, channels), half_type)
    toward, away = call(edges, "edges", (sides_type, sides_type), (both,), 4, 0.0)
    both_y = lax.ppermute(both, "lon", swap("lon", 2))
    near_pairs = [(i, i ^ 1) for i in range(lat_devices)]
    far_pairs = [(i, j) for i in range(lat_devices) for j in [i + 1 if i % 2 else i - 1] if 0 <= j < lat_devices]
    from_near = lax.ppermute(toward, "lat", near_pairs)
    from_far = lax.ppermute(away, "lat", far_pairs)
    tables = (lat_step.T, lon_step.T, jnp.transpose(basis_values, (1, 2, 0)))
    _, _, *tables = lax.optimization_barrier((toward, away, *tables))
    (forward,) = call(
        functools.partial(maps, first),
        "maps_first",
        (shape((nf, BASIS * cells, blocks * win), half_type),),
        tables,
        4,
        0.0,
        (pltpu.VMEM((48, lat_total), full_type),),
    )
    from_near, from_far, forward = lax.optimization_barrier((from_near, from_far, forward))
    sides = jnp.concatenate([from_near, from_far], axis=1)
    sides, both_y = lax.optimization_barrier((sides, both_y))
    sides_y = lax.ppermute(sides, "lon", swap("lon", 2))
    b0 = jnp.concatenate([both, sides], axis=1)
    b1 = lax.ppermute(b0, "lon", swap("lon", 1))
    b0, *tables = lax.optimization_barrier((b0, *tables))
    again, backward = call(
        functools.partial(maps, second),
        "maps_again",
        (shape((ns, BASIS * cells, blocks * win), half_type), shape((ns, blocks * win, BASIS * cells), half_type)),
        tables,
        4,
        0.0,
        (pltpu.VMEM((48, lat_total), full_type),),
    )
    b2 = jnp.concatenate([both_y, sides_y], axis=1)
    b2, again, near_half = lax.optimization_barrier((b2, again, near_half))
    b3 = lax.ppermute(b2, "lon", swap("lon", 1))
    far_half = lax.ppermute(near_half, "lon", swap("lon", 1))
    s_type = (members * nf * cells, width)
    s, left, slope, early_out = call(
        early,
        "early",
        (
            shape(s_type, half_type),
            shape((members * (nf - 2) * cells, width // blocks), half_type),
            shape((members, blocks, own + edge, channels), half_type),
            shape((members, own, channels), half_type),
        ),
        (b0, b1, b2, b3, kernel, forward, again),
        12,
        3.0,
        (pltpu.VMEM(s_type, half_type), pltpu.VMEM((members, blocks, own + 2 * edge, channels), half_type)),
    )
    w_type = shape((width, channels), half_type)
    w, part = call(
        partial,
        "partial",
        (w_type, shape((s_type[0], channels), full_type)),
        (s, near_half, far_half),
        8,
        1.5,
    )
    near_ends, part = lax.optimization_barrier((near_ends, part))
    lines = (width // blocks // lat_devices * channels // 128, 128)
    _, out, follow, gates, mine, *parts = call(
        chain,
        "chain",
        (
            w_type,
            shape((members, own, channels), half_type),
            shape((members, own, channels), half_type),
            shape((members * ns * cells, channels), half_type),
            shape(lines, full_type),
        )
        + (shape(lines, half_type),) * 3,
        (b0, b1, b2, b3, kernel, w, part, near_ends, again, backward, s, left, slope, early_out),
        18,
        6.0,
        (
            pltpu.VMEM((2 * (width // 2 - (width // 2 - rest) // 128 * 128), channels), half_type),
            pltpu.VMEM((members * ns * cells, width), half_type),
            pltpu.VMEM((members, blocks, own + 2 * edge, channels), half_type),
            pltpu.VMEM((members * ns * cells, channels), half_type),
            pltpu.VMEM((members * ns * cells * BASIS, channels), half_type),
            pltpu.VMEM((members, blocks, own + 2 * edge, channels), full_type),
            pltpu.VMEM((width // blocks * channels // 128, 128), full_type),
        ),
        {5: 0},
    )
    got = [lax.ppermute(part, "lat", swap("lat", bit)) for bit, part in reversed(list(zip((1, 2, 3), parts)))]
    block = (members, lat_rows, lon_cols, channels)
    grad, out = call(
        finish,
        "finish",
        (shape(block, half_type),) * 2,
        (kernel, backward, gates, follow, out),
        10,
        2.0,
        (
            pltpu.VMEM((members * ns * cells * BASIS, channels), half_type),
            pltpu.VMEM((members, own + 2 * edge, channels), full_type),
        ),
    )
    (total,) = call(functools.partial(add_up, grad_scale), "add_up", (shape(lines, full_type),), (mine, *got), 2, 0.1)
    return (out[None], grad[None], total.reshape(1, lines[0] * lines[1]))


def fits_ring(mesh, inputs):
    sizes = dict(mesh.shape)
    rows, cols = inputs.shape[1] // sizes["lat"], inputs.shape[2] // sizes["lon"]
    return sizes["segment"] == 2 and sizes["lon"] == 4 and sizes["lat"] == 4 and rows == 16 and cols == 4


def solution(mesh):
    def apply(*args):
        body = whole_ring if fits_ring(mesh, args[0]) else per_device
        return jax.shard_map(
            body,
            mesh=mesh,
            in_specs=(
                P(None, "lat", "lon", None),
                P(None, "lat", "lon", None),
                P("segment", None, None, None),
                P(),
                P(),
                P(),
            ),
            out_specs=(
                P("segment", None, "lat", "lon", None),
                P("segment", None, "lat", "lon", None),
                P("segment", ("lon", "lat")),
            ),
            check_vma=False,
        )(*args)

    return apply
```

```python
import functools
import math

import jax
import jax.numpy as jnp
from jax import lax
from jax.experimental import pallas as pl
from jax.experimental.pallas import tpu as pltpu
from jax.sharding import PartitionSpec as P

BASIS = 3
TAPS = 9
REACH = 2


def with_halo(array, sides, width):
    for axis, dim in sides:
        size, length = (lax.axis_size(axis), array.shape[dim])
        up = [(i, (i + 1) % size) for i in range(size)]
        down = [(j, i) for i, j in up]
        last = lax.slice_in_dim(array, length - width, length, axis=dim)
        first = lax.slice_in_dim(array, 0, width, axis=dim)
        before = lax.ppermute(last, axis, up)
        after = lax.ppermute(first, axis, down)
        array = jnp.concatenate([before, array, after], axis=dim)
    return array


def shifted(block, axis, distance):
    devices = range(lax.axis_size(axis))
    route = [(i - distance, i) for i in devices if i - distance in devices]
    return lax.ppermute(block, axis, route)


def widen(features):
    return with_halo(features, (("lon", 2), ("lat", 1)), REACH)


def pass_ahead(result):
    return shifted(result, "segment", 1)


def pass_behind(result):
    return shifted(result, "segment", -1)


def build_tables(basis_values, lat_step, lon_step, lat_rows, lon_cols, lat_index, lat_total):
    pad_rows = lat_rows + 2 * REACH
    pad_cols = lon_cols + 2 * REACH
    lat_padded = jnp.pad(lat_step, ((REACH, REACH), (0, 0)))
    lon_padded = jnp.pad(lon_step, ((REACH, REACH), (0, 0)))
    basis_padded = jnp.pad(basis_values, ((REACH, REACH), (0, 0), (0, 0)))
    row_start = lat_index * lat_rows
    lat_near = lax.dynamic_slice_in_dim(lat_padded, row_start, pad_rows, 0)
    lon_near = lax.dynamic_slice_in_dim(lon_padded, row_start, pad_rows, 0)
    basis_near = lax.dynamic_slice_in_dim(basis_padded, row_start, pad_rows, 0)
    lat_own = lat_near[REACH : REACH + lat_rows]
    lon_own = lon_near[REACH : REACH + lat_rows]
    basis_own = basis_near[REACH : REACH + lat_rows]
    own_rows = row_start + jnp.arange(lat_rows)
    inside = (own_rows[:, None] + lat_own >= 0) & (own_rows[:, None] + lat_own < lat_total)
    row_grid = jnp.arange(lat_rows)[:, None, None]
    col_grid = jnp.arange(lon_cols)[None, :, None]
    source = (row_grid + REACH + lat_own[:, None, :]) * pad_cols + (
        col_grid + REACH + lon_own[:, None, :]
    )
    tap_weight = jnp.where(inside[:, None, :, None], basis_own[:, None, :, :], 0.0)
    tap_weight = jnp.broadcast_to(tap_weight, (lat_rows, lon_cols, TAPS, BASIS))
    picker = (source[..., None] == jnp.arange(pad_rows * pad_cols)).astype(jnp.float32)
    forward_map = jnp.einsum("ijkb,ijks->bijs", tap_weight, picker, precision=lax.Precision.HIGHEST)
    forward_map = forward_map.reshape(BASIS, lat_rows * lon_cols, pad_rows * pad_cols)
    near_rows = row_start - REACH + jnp.arange(pad_rows)
    real_row = (near_rows >= 0) & (near_rows < lat_total)
    pad_row_grid = jnp.arange(pad_rows)[:, None, None]
    pad_col_grid = jnp.arange(pad_cols)[None, :, None]
    target_row = pad_row_grid - REACH + lat_near[:, None, :]
    target_col = pad_col_grid - REACH + lon_near[:, None, :]
    landed = (
        (target_row >= 0)
        & (target_row < lat_rows)
        & (target_col >= 0)
        & (target_col < lon_cols)
        & real_row[:, None, None]
    )
    target = target_row * lon_cols + target_col
    back_weight = jnp.where(landed[..., None], basis_near[:, None, :, :], 0.0)
    catcher = (target[..., None] == jnp.arange(lat_rows * lon_cols)).astype(jnp.float32)
    backward_map = jnp.einsum(
        "pqkb,pqkt->btpq", back_weight, catcher, precision=lax.Precision.HIGHEST
    )
    backward_map = backward_map.reshape(BASIS, lat_rows * lon_cols, pad_rows * pad_cols)
    return (forward_map, backward_map)


def per_device(inputs, cotangent, weights, basis_values, lat_step, lon_step):
    members, lat_rows, lon_cols, channels = inputs.shape
    pad_rows = lat_rows + 2 * REACH
    pad_cols = lon_cols + 2 * REACH
    cells = lat_rows * lon_cols
    lat_index = lax.axis_index("lat")
    lat_total = lat_rows * lax.axis_size("lat")
    segment_index = lax.axis_index("segment")
    depth = lax.axis_size("segment")
    grad_scale = 1.0 / math.sqrt(members * lat_total * lon_cols * lax.axis_size("lon"))
    forward_map, backward_map = build_tables(
        basis_values, lat_step, lon_step, lat_rows, lon_cols, lat_index, lat_total
    )
    kernel = weights[0]
    keep_spread = jnp.zeros((BASIS, members, cells, channels), jnp.bfloat16)
    keep_mixed = jnp.zeros((members, cells, channels), jnp.float32)
    keep_gate = jnp.zeros((members, cells, channels), jnp.bfloat16)
    section_out = jnp.zeros(inputs.shape, jnp.bfloat16)
    section_grad = jnp.zeros(inputs.shape, jnp.bfloat16)
    carry = inputs
    for tick_num in range(depth):
        layer_count = carry.shape[0]
        layer_padded = (
            widen(carry).reshape(layer_count, pad_rows * pad_cols, channels).astype(jnp.float32)
        )
        spread = jnp.einsum(
            "bts,msc->bmtc", forward_map, layer_padded, precision=lax.Precision.HIGHEST
        ).astype(jnp.bfloat16)
        layer_mixed = jnp.einsum(
            "bmtc,bcd->mtd", spread, kernel, preferred_element_type=jnp.float32
        )
        result = (
            carry.reshape(layer_count, cells, channels).astype(jnp.float32)
            + jax.nn.silu(layer_mixed)
        ).astype(jnp.bfloat16)
        spread, mixed, result = (spread, layer_mixed, result.reshape(carry.shape))
        here = segment_index == tick_num
        keep_spread = jnp.where(here, spread, keep_spread)
        keep_mixed = jnp.where(here, mixed, keep_mixed)
        section_out = jnp.where(here, result, section_out)
        if tick_num + 1 < depth:
            carry = pass_ahead(result)
    grad = cotangent
    for tick_num in range(depth):
        count = grad.shape[0]
        flat_grad = grad.reshape(count, cells, channels).astype(jnp.float32)
        sigma = jax.nn.sigmoid(keep_mixed)
        gate_grad = (flat_grad * sigma * (1.0 + keep_mixed * (1.0 - sigma))).astype(jnp.bfloat16)
        feature_grad = jnp.einsum(
            "mtd,bcd->bmtc", gate_grad, kernel, preferred_element_type=jnp.float32
        ).astype(jnp.bfloat16)
        padded = widen(feature_grad.reshape(BASIS * count, lat_rows, lon_cols, channels))
        padded = padded.reshape(BASIS, count, pad_rows * pad_cols, channels).astype(jnp.float32)
        pulled = jnp.einsum("bts,bmsc->mtc", backward_map, padded, precision=lax.Precision.HIGHEST)
        new_grad = (flat_grad + pulled).astype(jnp.bfloat16).reshape(grad.shape)
        gate_grad, new_grad = (gate_grad, new_grad)
        here = segment_index == depth - 1 - tick_num
        keep_gate = jnp.where(here, gate_grad, keep_gate)
        section_grad = jnp.where(here, new_grad, section_grad)
        if tick_num + 1 < depth:
            grad = pass_behind(new_grad)
    local_grad = (
        jnp.einsum("bmtc,mtd->bcd", keep_spread, keep_gate, preferred_element_type=jnp.float32)
        * grad_scale
    )
    owners = lax.axis_size("lon") * lax.axis_size("lat")
    grad_rows = local_grad.reshape(owners, -1)
    weight_grad = lax.psum_scatter(grad_rows, ("lon", "lat"), scatter_dimension=0, tiled=True)
    return (section_out[None], section_grad[None], weight_grad)


HALO = 8
BAND = 8


def swap(axis, bit):
    return [(i, i ^ bit) for i in range(lax.axis_size(axis))]


def window_plan(lat_rows):
    first = [(a, min(max(a - 4, -HALO), lat_rows + HALO - 16)) for a in range(-HALO, lat_rows + HALO, BAND)]
    second = [(a, a - 4) for a in range(-4, lat_rows + 4, BAND)]
    return first, second


def dot(a, b):
    return jnp.dot(a, b, preferred_element_type=jnp.float32)


def dot_nt(a, b):
    return lax.dot_general(a, b, (((1,), (1,)), ((), ())), preferred_element_type=jnp.float32)


def dot_tn(a, b):
    return lax.dot_general(a, b, (((0,), (0,)), ((), ())), preferred_element_type=jnp.float32)


def make_steps(lat_rows, lon_cols, blocks, members, channels, lat_devices):
    first, second = window_plan(lat_rows)
    nf, ns = len(first), len(second)
    lat_total = lat_rows * lat_devices
    ring = lon_cols * blocks
    band = BAND * lon_cols
    cells = blocks * band
    win = 16 * lon_cols
    own = lat_rows * lon_cols
    edge = HALO * lon_cols
    half_edge = edge // 2
    width = BASIS * channels
    lanes = 128
    pieces = channels // lanes
    halo = edge + half_edge
    state_parts = ((0, edge, 0, 0), (edge, own, 0, None), (edge + own, edge, 0, 1))
    coming_parts = ((0, half_edge, edge, 0), (half_edge, own, own, None), (half_edge + own, half_edge, edge, 1))

    def take(blks, m, parts, low, high):
        found = []
        odd = lax.axis_index("lat") % 2
        for r in blks:
            for start, size, at, side in parts:
                lo, hi = max(low, start), min(high, start + size)
                if lo >= hi:
                    continue
                if side is None:
                    found.append(r[m, at + lo - start : at + hi - start, :])
                else:
                    slot = odd if side else 1 - odd
                    first_row = pl.multiple_of(2 * own + at + lo - start + slot * halo, 16)
                    found.append(r[m, pl.ds(first_row, hi - lo), :])
        return jnp.concatenate(found, axis=0)

    def prep(loaded, both):
        for m in range(members):
            both[m, :own, :] = loaded[m].reshape(own, channels)
            both[m, own:, :] = loaded[members + m].reshape(own, channels)

    def edges(both, toward, away):
        tail = ((own - edge, own), (2 * own - half_edge, 2 * own))
        head = ((0, edge), (own, own + half_edge))

        def fill(spans, ref):
            for m in range(members):
                ref[m, :edge, :] = both[m, spans[0][0] : spans[0][1], :]
                ref[m, edge:, :] = both[m, spans[1][0] : spans[1][1], :]

        @pl.when(lax.axis_index("lat") % 2 == 0)
        def _():
            fill(tail, toward)
            fill(head, away)

        @pl.when(lax.axis_index("lat") % 2 == 1)
        def _():
            fill(head, toward)
            fill(tail, away)

    def maps(plan, lat_step, lon_step, basis, *outs):
        forward, tab = outs[0], outs[-1]
        lon, lat = lax.axis_index("lon"), lax.axis_index("lat")
        base = lat * lat_rows
        tab[...] = jnp.zeros(tab.shape, jnp.float32)
        tab[0:TAPS, :] = lat_step[...].astype(jnp.float32)
        tab[TAPS : 2 * TAPS, :] = lon_step[...].astype(jnp.float32)
        for k in range(TAPS):
            tab[2 * TAPS + k * BASIS : 2 * TAPS + (k + 1) * BASIS, :] = basis[k]
        table = tab[...].astype(jnp.bfloat16)
        source = lax.broadcasted_iota(jnp.int32, (tab.shape[1], cells), 0)
        lane = lax.broadcasted_iota(jnp.int32, (1, cells), 1)
        block, rest = lane // band, lane % band
        row_in, col_in = rest // lon_cols, rest % lon_cols
        column_home = (block ^ lon) * lon_cols + col_in
        piece = 64
        spot = lax.broadcasted_iota(jnp.int32, (piece, cells), 0)
        for i, (a, start) in enumerate(plan):
            row = row_in + (base + a)
            got = dot(table, (source == row).astype(jnp.bfloat16))
            step_lat = got[0:TAPS].astype(jnp.int32)
            step_lon = got[TAPS : 2 * TAPS].astype(jnp.int32)
            target = row + step_lat
            inside = (row >= 0) & (row < lat_total) & (target >= 0) & (target < lat_total)
            column = column_home + step_lon
            column = jnp.where(column < 0, column + ring, column)
            column = jnp.where(column >= ring, column - ring, column)
            local = target - (base + start)
            place = ((column // lon_cols) ^ lon) * win + local * lon_cols + column % lon_cols
            place = jnp.where(inside, place, -1)
            for p in range(0, blocks * win, piece):
                tables = [jnp.zeros((piece, cells), jnp.float32) for _ in range(BASIS)]
                for k in range(TAPS):
                    hit = spot == place[k : k + 1] - p
                    for b in range(BASIS):
                        at = 2 * TAPS + k * BASIS + b
                        tables[b] = tables[b] + jnp.where(hit, got[at : at + 1], 0.0)
                for b in range(BASIS):
                    span = slice(b * cells, (b + 1) * cells)
                    forward[i, span, p : p + piece] = tables[b].T.astype(jnp.bfloat16)
                    if len(outs) == 3:
                        outs[1][i, p : p + piece, span] = tables[b].astype(jnp.bfloat16)

    def put_spread(got, into, at):
        for b in range(BASIS):
            into[at : at + cells, b * channels : (b + 1) * channels] = got[b * cells : (b + 1) * cells]

    def spread(blk, forward, into):
        for m in range(members):
            for g, (a, start) in enumerate(first):
                o = (start + HALO) * lon_cols
                near = take(blk, m, state_parts, o, o + win)
                put_spread(dot(forward[g], near).astype(jnp.bfloat16), into, (m * nf + g) * cells)

    def first_section(blk, total, s1, again, mid, slope):
        for m in range(members):
            for g in range(nf):
                mixed = total[(m * nf + g) * cells : (m * nf + g + 1) * cells]
                sigma = 0.5 + 0.5 * jnp.tanh(0.5 * mixed)
                here = take(blk, m, state_parts, g * band, (g + 1) * band)
                value = (here.astype(jnp.float32) + mixed * sigma).astype(jnp.bfloat16)
                mid[m, :, g * band : (g + 1) * band, :] = value.reshape(blocks, band, channels)
                if slope is not None:
                    tilt = (sigma * (1.0 + mixed * (1.0 - sigma))).astype(slope.dtype).reshape(blocks, band, channels)
                    low, high = max(g * band, half_edge), min((g + 1) * band, 3 * half_edge + own)
                    slope[m, :, low - half_edge : high - half_edge, :] = tilt[:, low - g * band : high - g * band]
            for g in range(ns):
                near = mid[m, :, g * band : g * band + win, :].reshape(blocks * win, channels)
                put_spread(dot(again[g], near).astype(jnp.bfloat16), s1, (m * ns + g) * cells)

    def columns_of(lon):
        return pl.ds(pl.multiple_of(lon * (width // blocks), 128), width // blocks)

    def early(b0, b1, b2, b3, w_own, forward, again, s, left, slope, out, s0, mid):
        blk = (b0, b1, b2, b3)

        @pl.when(lax.axis_index("segment") == 0)
        def _():
            spread(blk, forward, s0)
            first_section(blk, dot(s0[...], w_own[...]), s, again, mid, slope)
            for m in range(members):
                size = (nf - 2) * cells
                left[m * size : (m + 1) * size, :] = s0[(m * nf + 1) * cells : (m * nf + nf - 1) * cells, columns_of(lax.axis_index("lon"))]
                out[m, :, :] = mid[m, 0, edge : edge + own, :]

        @pl.when(lax.axis_index("segment") == 1)
        def _():
            spread(blk, forward, s)

    def partial(s, near_half, far_half, w, part):
        rows = near_half.shape[0]
        here = lax.axis_index("lon") % 2 * (width // 2)
        for base, ref in ((here, near_half), (width // 2 - here, far_half)):
            w[pl.ds(pl.multiple_of(base, 32), rows), :] = ref[...]
        for i in range(2):
            late = slice(i * (width // 2) + rows, (i + 1) * (width // 2))
            w[late, :] = jnp.zeros((width // 2 - rows, channels), w.dtype)

        @pl.when(lax.axis_index("segment") == 1)
        def _():
            part[...] = dot(s[...], w[...])

    def own_part(g):
        return max(g * band, half_edge), min((g + 1) * band, half_edge + own)

    def apply_back(w, gates, feat):
        for b in range(BASIS):
            got = dot_nt(gates[...], w[b * channels : (b + 1) * channels, :]).astype(jnp.bfloat16)
            for i in range(members * ns):
                feat[(i * BASIS + b) * cells : (i * BASIS + b + 1) * cells, :] = got[i * cells : (i + 1) * cells]

    def chain(b0, b1, b2, b3, w_own, w_in, part, ends, again, backward, s, left0, slope, early_out, w,
              out_ref, next_ref, gate_ref, own_ref, p1, p2, p3, late, s1, mid, gates, feat, pull, grads):
        blk = (b0, b1, b2, b3)
        seg, lon, lat = lax.axis_index("segment"), lax.axis_index("lon"), lax.axis_index("lat")
        rest = ends.shape[0] // 2
        rows = width // 2 - rest
        aligned = rows // lanes * lanes
        span = width // 2 - aligned
        for i in range(2):
            piece = ends[i * rest : (i + 1) * rest, :]
            w[i * (width // 2) + rows : (i + 1) * (width // 2), :] = piece
            late[i * span : (i + 1) * span - rest, :] = jnp.zeros((span - rest, channels), late.dtype)
            late[(i + 1) * span - rest : (i + 1) * span, :] = piece

        def complete():
            total = part[...]
            for i in range(2):
                at = i * (width // 2) + aligned
                total = total + dot(s[:, at : at + span], late[i * span : (i + 1) * span, :])
            return total

        def coming_at(m, g):
            return take(blk, m, coming_parts, g * band, (g + 1) * band).astype(jnp.float32)

        def second_section(total, into, last):
            for m in range(members):
                for g in range(ns):
                    at = (m * ns + g) * cells
                    mixed = total[at : at + cells]
                    sigma = 0.5 + 0.5 * jnp.tanh(0.5 * mixed)
                    into[at : at + cells, :] = (coming_at(m, g) * sigma * (1.0 + mixed * (1.0 - sigma))).astype(jnp.bfloat16)
                    if last:
                        low, high = own_part(g)
                        base = mid[m, 0, half_edge + low : half_edge + high, :]
                        local = slice(low - g * band, high - g * band)
                        base = (base.astype(jnp.float32) + mixed[local] * sigma[local]).astype(jnp.bfloat16)
                        out_ref[m, low - half_edge : high - half_edge, :] = base

        def store_grads(left, right):
            got = dot_tn(left, jnp.concatenate(right, axis=0))
            for c in range(pieces):
                grads[pl.ds(c, width // blocks, stride=pieces), :] = got[:, c * lanes : (c + 1) * lanes]

        @pl.when(seg == 0)
        def _():
            second_section(dot(s[: members * ns * cells, :], w[...]), gates, False)
            out_ref[...] = early_out[...]
            apply_back(w, gates, feat)
            for m in range(members):
                for g in range(ns):
                    at = (m * ns + g) * cells * BASIS
                    low = max(g * band, half_edge)
                    high = min(g * band + win, 3 * half_edge + own)
                    local = range(0, blocks * win, win)
                    rows = [backward[g, q + low - g * band : q + high - g * band, :] for q in local]
                    got = dot(jnp.concatenate(rows, axis=0), feat[at : at + BASIS * cells, :])
                    got = got.reshape(blocks, high - low, channels)
                    turn = low if g == 0 else (g + 1) * band
                    if g > 0:
                        pull[m, :, low:turn, :] += got[:, : turn - low]
                    pull[m, :, turn:high, :] = got[:, turn - low :]
            right = []
            step = half_edge
            for m in range(members):
                for g in range(ns):
                    at = (m * ns + g) * cells
                    span = slice(half_edge + g * band, half_edge + (g + 1) * band)
                    value = (coming_at(m, g) + pull[m, :, span, :].reshape(cells, channels)).astype(jnp.bfloat16)
                    low, high = own_part(g)
                    next_ref[m, low - half_edge : high - half_edge, :] = value[low - g * band : high - g * band]
                    tilt = slope[m, :, g * band : (g + 1) * band, :].reshape(cells, channels)
                    gate_ref[at : at + cells, :] = (value.astype(jnp.float32) * tilt).astype(jnp.bfloat16)
                for g in range(1, nf - 1):
                    for q in range(blocks):
                        for o in range(0, band, step):
                            spot = half_edge + (g - 1) * band + o
                            turn, rest = spot // band, spot % band
                            at = (m * ns + turn) * cells + q * band + rest
                            right.append(gate_ref[at : at + step, :])
            store_grads(left0[...], right)

        @pl.when(seg == 1)
        def _():
            first_section(blk, complete(), s1, again, mid, None)
            second_section(dot(s1[...], w_own[...]), gate_ref, True)
            left, right = [], []
            for m in range(members):
                next_ref[m, :, :] = b0[m, own : 2 * own, :]
                for g in range(ns):
                    low, high = own_part(g)
                    for q in range(blocks):
                        at = (m * ns + g) * cells + q * band - g * band
                        left.append(s1[at + low : at + high, columns_of(lon)])
                        right.append(gate_ref[at + low : at + high, :])
            store_grads(jnp.concatenate(left, axis=0), right)

        share = width // blocks // lat_devices * pieces

        def rows_of(index):
            return grads[pl.ds(pl.multiple_of(index * share, share), share), :]

        own_ref[...] = rows_of(lat)
        for bit, ref in ((1, p1), (2, p2), (3, p3)):
            ref[...] = rows_of(lat ^ bit).astype(jnp.bfloat16)

    def finish(w_own, backward, gates, next_ref, last_ref, grad_ref, out_ref, feat, pull):
        apply_back(w_own, gates, feat)
        for m in range(members):
            for g in range(ns):
                at = (m * ns + g) * cells * BASIS
                got = dot(backward[g, 0:win, :], feat[at : at + BASIS * cells, :])
                if g == 0:
                    pull[m, :win, :] = got
                else:
                    pull[m, g * band : (g + 1) * band, :] += got[:band]
                    pull[m, (g + 1) * band : g * band + win, :] = got[band:]
            total = next_ref[m].astype(jnp.float32) + pull[m, edge : edge + own, :]
            grad_ref[m] = total.astype(jnp.bfloat16).reshape(lat_rows, lon_cols, channels)
            out_ref[m] = last_ref[m].reshape(lat_rows, lon_cols, channels)

    return prep, edges, maps, early, partial, chain, finish


def add_up(scale, mine, p1, p2, p3, out):
    out[...] = (mine[...] + p1[...].astype(jnp.float32) + p2[...].astype(jnp.float32) + p3[...].astype(jnp.float32)) * scale


def whole_ring(inputs, cotangent, weights, basis_values, lat_step, lon_step):
    members, lat_rows, lon_cols, channels = inputs.shape
    blocks = lax.axis_size("lon")
    lat_devices = lax.axis_size("lat")
    lat_total = lat_rows * lat_devices
    grad_scale = 1.0 / math.sqrt(members * lat_total * lon_cols * blocks)
    own = lat_rows * lon_cols
    edge = HALO * lon_cols
    half_edge = edge // 2
    halo = edge + half_edge
    width = BASIS * channels
    half_type, full_type = jnp.bfloat16, jnp.float32
    shape = jax.ShapeDtypeStruct
    first, second = window_plan(lat_rows)
    nf, ns = len(first), len(second)
    cells = blocks * BAND * lon_cols
    win = 16 * lon_cols
    vmem = pl.BlockSpec(memory_space=pltpu.VMEM)

    def call(body, name, outs, ins, mib, gflops, scratch=(), aliases={}):
        return pl.pallas_call(
            body,
            out_shape=outs,
            in_specs=[vmem] * len(ins),
            out_specs=(vmem,) * len(outs),
            scratch_shapes=list(scratch),
            input_output_aliases=aliases,
            compiler_params=pltpu.CompilerParams(vmem_limit_bytes=int(mib * 1024 * 1024)),
            cost_estimate=pl.CostEstimate(flops=int(gflops * 1e9), bytes_accessed=int(gflops * 1e6), transcendentals=0),
            name=name,
        )(*ins)

    prep, edges, maps, early, partial, chain, finish = make_steps(lat_rows, lon_cols, blocks, members, channels, lat_devices)
    kernel = weights.reshape(width, channels)
    rest = width // 2 * 5 // 48
    rows = width // 2 - rest
    half = lax.dynamic_slice_in_dim(kernel, lax.axis_index("lon") % 2 * (width // 2), rows, 0)
    ends = jnp.concatenate([kernel[rows : rows + rest], kernel[width - rest :]], axis=0)
    near_ends = lax.ppermute(ends, "segment", swap("segment", 1))
    near_half = lax.ppermute(half, "segment", swap("segment", 1))
    half, inputs, cotangent = lax.optimization_barrier((half, inputs, cotangent))
    loaded = jnp.concatenate([inputs, cotangent], axis=0)
    (both,) = call(prep, "prep", (shape((members, 2 * own, channels), half_type),), (loaded,), 4, 0.0)
    sides_type = shape((members, halo, channels), half_type)
    toward, away = call(edges, "edges", (sides_type, sides_type), (both,), 4, 0.0)
    both_y = lax.ppermute(both, "lon", swap("lon", 2))
    near_pairs = [(i, i ^ 1) for i in range(lat_devices)]
    far_pairs = [(i, j) for i in range(lat_devices) for j in [i + 1 if i % 2 else i - 1] if 0 <= j < lat_devices]
    from_near = lax.ppermute(toward, "lat", near_pairs)
    from_far = lax.ppermute(away, "lat", far_pairs)
    tables = (lat_step.T, lon_step.T, jnp.transpose(basis_values, (1, 2, 0)))
    _, _, *tables = lax.optimization_barrier((toward, away, *tables))
    (forward,) = call(
        functools.partial(maps, first),
        "maps_first",
        (shape((nf, BASIS * cells, blocks * win), half_type),),
        tables,
        4,
        0.0,
        (pltpu.VMEM((48, lat_total), full_type),),
    )
    from_near, from_far, forward = lax.optimization_barrier((from_near, from_far, forward))
    sides = jnp.concatenate([from_near, from_far], axis=1)
    sides, both_y = lax.optimization_barrier((sides, both_y))
    sides_y = lax.ppermute(sides, "lon", swap("lon", 2))
    b0 = jnp.concatenate([both, sides], axis=1)
    b1 = lax.ppermute(b0, "lon", swap("lon", 1))
    b0, *tables = lax.optimization_barrier((b0, *tables))
    again, backward = call(
        functools.partial(maps, second),
        "maps_again",
        (shape((ns, BASIS * cells, blocks * win), half_type), shape((ns, blocks * win, BASIS * cells), half_type)),
        tables,
        4,
        0.0,
        (pltpu.VMEM((48, lat_total), full_type),),
    )
    b2 = jnp.concatenate([both_y, sides_y], axis=1)
    b2, again, near_half = lax.optimization_barrier((b2, again, near_half))
    b3 = lax.ppermute(b2, "lon", swap("lon", 1))
    far_half = lax.ppermute(near_half, "lon", swap("lon", 1))
    s_type = (members * nf * cells, width)
    s, left, slope, early_out = call(
        early,
        "early",
        (
            shape(s_type, half_type),
            shape((members * (nf - 2) * cells, width // blocks), half_type),
            shape((members, blocks, own + edge, channels), half_type),
            shape((members, own, channels), half_type),
        ),
        (b0, b1, b2, b3, kernel, forward, again),
        12,
        3.0,
        (pltpu.VMEM(s_type, half_type), pltpu.VMEM((members, blocks, own + 2 * edge, channels), half_type)),
    )
    w_type = shape((width, channels), half_type)
    w, part = call(
        partial,
        "partial",
        (w_type, shape((s_type[0], channels), full_type)),
        (s, near_half, far_half),
        8,
        1.5,
    )
    near_ends, part = lax.optimization_barrier((near_ends, part))
    lines = (width // blocks // lat_devices * channels // 128, 128)
    _, out, follow, gates, mine, *parts = call(
        chain,
        "chain",
        (
            w_type,
            shape((members, own, channels), half_type),
            shape((members, own, channels), half_type),
            shape((members * ns * cells, channels), half_type),
            shape(lines, full_type),
        )
        + (shape(lines, half_type),) * 3,
        (b0, b1, b2, b3, kernel, w, part, near_ends, again, backward, s, left, slope, early_out),
        18,
        6.0,
        (
            pltpu.VMEM((2 * (width // 2 - (width // 2 - rest) // 128 * 128), channels), half_type),
            pltpu.VMEM((members * ns * cells, width), half_type),
            pltpu.VMEM((members, blocks, own + 2 * edge, channels), half_type),
            pltpu.VMEM((members * ns * cells, channels), half_type),
            pltpu.VMEM((members * ns * cells * BASIS, channels), half_type),
            pltpu.VMEM((members, blocks, own + 2 * edge, channels), full_type),
            pltpu.VMEM((width // blocks * channels // 128, 128), full_type),
        ),
        {5: 0},
    )
    got = [lax.ppermute(parts[bit - 1], "lat", swap("lat", bit)) for bit in (2, 3, 1)]
    block = (members, lat_rows, lon_cols, channels)
    grad, out = call(
        finish,
        "finish",
        (shape(block, half_type),) * 2,
        (kernel, backward, gates, follow, out),
        10,
        2.0,
        (
            pltpu.VMEM((members * ns * cells * BASIS, channels), half_type),
            pltpu.VMEM((members, own + 2 * edge, channels), full_type),
        ),
    )
    (total,) = call(functools.partial(add_up, grad_scale), "add_up", (shape(lines, full_type),), (mine, *got), 2, 0.1)
    return (out[None], grad[None], total.reshape(1, lines[0] * lines[1]))


def fits_ring(mesh, inputs):
    sizes = dict(mesh.shape)
    rows, cols = inputs.shape[1] // sizes["lat"], inputs.shape[2] // sizes["lon"]
    return sizes["segment"] == 2 and sizes["lon"] == 4 and sizes["lat"] == 4 and rows == 16 and cols == 4


def solution(mesh):
    def apply(*args):
        body = whole_ring if fits_ring(mesh, args[0]) else per_device
        return jax.shard_map(
            body,
            mesh=mesh,
            in_specs=(
                P(None, "lat", "lon", None),
                P(None, "lat", "lon", None),
                P("segment", None, None, None),
                P(),
                P(),
                P(),
            ),
            out_specs=(
                P("segment", None, "lat", "lon", None),
                P("segment", None, "lat", "lon", None),
                P("segment", ("lon", "lat")),
            ),
            check_vma=False,
        )(*args)

    return apply
```

```python
import functools
import math

import jax
import jax.numpy as jnp
from jax import lax
from jax.experimental import pallas as pl
from jax.experimental.pallas import tpu as pltpu
from jax.sharding import PartitionSpec as P

BASIS = 3
TAPS = 9
REACH = 2


def with_halo(array, sides, width):
    for axis, dim in sides:
        size, length = (lax.axis_size(axis), array.shape[dim])
        up = [(i, (i + 1) % size) for i in range(size)]
        down = [(j, i) for i, j in up]
        last = lax.slice_in_dim(array, length - width, length, axis=dim)
        first = lax.slice_in_dim(array, 0, width, axis=dim)
        before = lax.ppermute(last, axis, up)
        after = lax.ppermute(first, axis, down)
        array = jnp.concatenate([before, array, after], axis=dim)
    return array


def shifted(block, axis, distance):
    devices = range(lax.axis_size(axis))
    route = [(i - distance, i) for i in devices if i - distance in devices]
    return lax.ppermute(block, axis, route)


def widen(features):
    return with_halo(features, (("lon", 2), ("lat", 1)), REACH)


def pass_ahead(result):
    return shifted(result, "segment", 1)


def pass_behind(result):
    return shifted(result, "segment", -1)


def build_tables(basis_values, lat_step, lon_step, lat_rows, lon_cols, lat_index, lat_total):
    pad_rows = lat_rows + 2 * REACH
    pad_cols = lon_cols + 2 * REACH
    lat_padded = jnp.pad(lat_step, ((REACH, REACH), (0, 0)))
    lon_padded = jnp.pad(lon_step, ((REACH, REACH), (0, 0)))
    basis_padded = jnp.pad(basis_values, ((REACH, REACH), (0, 0), (0, 0)))
    row_start = lat_index * lat_rows
    lat_near = lax.dynamic_slice_in_dim(lat_padded, row_start, pad_rows, 0)
    lon_near = lax.dynamic_slice_in_dim(lon_padded, row_start, pad_rows, 0)
    basis_near = lax.dynamic_slice_in_dim(basis_padded, row_start, pad_rows, 0)
    lat_own = lat_near[REACH : REACH + lat_rows]
    lon_own = lon_near[REACH : REACH + lat_rows]
    basis_own = basis_near[REACH : REACH + lat_rows]
    own_rows = row_start + jnp.arange(lat_rows)
    inside = (own_rows[:, None] + lat_own >= 0) & (own_rows[:, None] + lat_own < lat_total)
    row_grid = jnp.arange(lat_rows)[:, None, None]
    col_grid = jnp.arange(lon_cols)[None, :, None]
    source = (row_grid + REACH + lat_own[:, None, :]) * pad_cols + (
        col_grid + REACH + lon_own[:, None, :]
    )
    tap_weight = jnp.where(inside[:, None, :, None], basis_own[:, None, :, :], 0.0)
    tap_weight = jnp.broadcast_to(tap_weight, (lat_rows, lon_cols, TAPS, BASIS))
    picker = (source[..., None] == jnp.arange(pad_rows * pad_cols)).astype(jnp.float32)
    forward_map = jnp.einsum("ijkb,ijks->bijs", tap_weight, picker, precision=lax.Precision.HIGHEST)
    forward_map = forward_map.reshape(BASIS, lat_rows * lon_cols, pad_rows * pad_cols)
    near_rows = row_start - REACH + jnp.arange(pad_rows)
    real_row = (near_rows >= 0) & (near_rows < lat_total)
    pad_row_grid = jnp.arange(pad_rows)[:, None, None]
    pad_col_grid = jnp.arange(pad_cols)[None, :, None]
    target_row = pad_row_grid - REACH + lat_near[:, None, :]
    target_col = pad_col_grid - REACH + lon_near[:, None, :]
    landed = (
        (target_row >= 0)
        & (target_row < lat_rows)
        & (target_col >= 0)
        & (target_col < lon_cols)
        & real_row[:, None, None]
    )
    target = target_row * lon_cols + target_col
    back_weight = jnp.where(landed[..., None], basis_near[:, None, :, :], 0.0)
    catcher = (target[..., None] == jnp.arange(lat_rows * lon_cols)).astype(jnp.float32)
    backward_map = jnp.einsum(
        "pqkb,pqkt->btpq", back_weight, catcher, precision=lax.Precision.HIGHEST
    )
    backward_map = backward_map.reshape(BASIS, lat_rows * lon_cols, pad_rows * pad_cols)
    return (forward_map, backward_map)


def per_device(inputs, cotangent, weights, basis_values, lat_step, lon_step):
    members, lat_rows, lon_cols, channels = inputs.shape
    pad_rows = lat_rows + 2 * REACH
    pad_cols = lon_cols + 2 * REACH
    cells = lat_rows * lon_cols
    lat_index = lax.axis_index("lat")
    lat_total = lat_rows * lax.axis_size("lat")
    segment_index = lax.axis_index("segment")
    depth = lax.axis_size("segment")
    grad_scale = 1.0 / math.sqrt(members * lat_total * lon_cols * lax.axis_size("lon"))
    forward_map, backward_map = build_tables(
        basis_values, lat_step, lon_step, lat_rows, lon_cols, lat_index, lat_total
    )
    kernel = weights[0]
    keep_spread = jnp.zeros((BASIS, members, cells, channels), jnp.bfloat16)
    keep_mixed = jnp.zeros((members, cells, channels), jnp.float32)
    keep_gate = jnp.zeros((members, cells, channels), jnp.bfloat16)
    section_out = jnp.zeros(inputs.shape, jnp.bfloat16)
    section_grad = jnp.zeros(inputs.shape, jnp.bfloat16)
    carry = inputs
    for tick_num in range(depth):
        layer_count = carry.shape[0]
        layer_padded = (
            widen(carry).reshape(layer_count, pad_rows * pad_cols, channels).astype(jnp.float32)
        )
        spread = jnp.einsum(
            "bts,msc->bmtc", forward_map, layer_padded, precision=lax.Precision.HIGHEST
        ).astype(jnp.bfloat16)
        layer_mixed = jnp.einsum(
            "bmtc,bcd->mtd", spread, kernel, preferred_element_type=jnp.float32
        )
        result = (
            carry.reshape(layer_count, cells, channels).astype(jnp.float32)
            + jax.nn.silu(layer_mixed)
        ).astype(jnp.bfloat16)
        spread, mixed, result = (spread, layer_mixed, result.reshape(carry.shape))
        here = segment_index == tick_num
        keep_spread = jnp.where(here, spread, keep_spread)
        keep_mixed = jnp.where(here, mixed, keep_mixed)
        section_out = jnp.where(here, result, section_out)
        if tick_num + 1 < depth:
            carry = pass_ahead(result)
    grad = cotangent
    for tick_num in range(depth):
        count = grad.shape[0]
        flat_grad = grad.reshape(count, cells, channels).astype(jnp.float32)
        sigma = jax.nn.sigmoid(keep_mixed)
        gate_grad = (flat_grad * sigma * (1.0 + keep_mixed * (1.0 - sigma))).astype(jnp.bfloat16)
        feature_grad = jnp.einsum(
            "mtd,bcd->bmtc", gate_grad, kernel, preferred_element_type=jnp.float32
        ).astype(jnp.bfloat16)
        padded = widen(feature_grad.reshape(BASIS * count, lat_rows, lon_cols, channels))
        padded = padded.reshape(BASIS, count, pad_rows * pad_cols, channels).astype(jnp.float32)
        pulled = jnp.einsum("bts,bmsc->mtc", backward_map, padded, precision=lax.Precision.HIGHEST)
        new_grad = (flat_grad + pulled).astype(jnp.bfloat16).reshape(grad.shape)
        gate_grad, new_grad = (gate_grad, new_grad)
        here = segment_index == depth - 1 - tick_num
        keep_gate = jnp.where(here, gate_grad, keep_gate)
        section_grad = jnp.where(here, new_grad, section_grad)
        if tick_num + 1 < depth:
            grad = pass_behind(new_grad)
    local_grad = (
        jnp.einsum("bmtc,mtd->bcd", keep_spread, keep_gate, preferred_element_type=jnp.float32)
        * grad_scale
    )
    owners = lax.axis_size("lon") * lax.axis_size("lat")
    grad_rows = local_grad.reshape(owners, -1)
    weight_grad = lax.psum_scatter(grad_rows, ("lon", "lat"), scatter_dimension=0, tiled=True)
    return (section_out[None], section_grad[None], weight_grad)


HALO = 8
BAND = 8


def swap(axis, bit):
    return [(i, i ^ bit) for i in range(lax.axis_size(axis))]


def window_plan(lat_rows):
    first = [(a, min(max(a - 4, -HALO), lat_rows + HALO - 16)) for a in range(-HALO, lat_rows + HALO, BAND)]
    second = [(a, a - 4) for a in range(-4, lat_rows + 4, BAND)]
    return first, second


def dot(a, b):
    return jnp.dot(a, b, preferred_element_type=jnp.float32)


def dot_nt(a, b):
    return lax.dot_general(a, b, (((1,), (1,)), ((), ())), preferred_element_type=jnp.float32)


def dot_tn(a, b):
    return lax.dot_general(a, b, (((0,), (0,)), ((), ())), preferred_element_type=jnp.float32)


def make_steps(lat_rows, lon_cols, blocks, members, channels, lat_devices):
    first, second = window_plan(lat_rows)
    nf, ns = len(first), len(second)
    lat_total = lat_rows * lat_devices
    ring = lon_cols * blocks
    band = BAND * lon_cols
    cells = blocks * band
    win = 16 * lon_cols
    own = lat_rows * lon_cols
    edge = HALO * lon_cols
    half_edge = edge // 2
    width = BASIS * channels
    lanes = 128
    pieces = channels // lanes
    halo = edge + half_edge
    state_parts = ((0, edge, 0, 0), (edge, own, 0, None), (edge + own, edge, 0, 1))
    coming_parts = ((0, half_edge, edge, 0), (half_edge, own, own, None), (half_edge + own, half_edge, edge, 1))

    def take(blks, m, parts, low, high):
        found = []
        odd = lax.axis_index("lat") % 2
        for r in blks:
            for start, size, at, side in parts:
                lo, hi = max(low, start), min(high, start + size)
                if lo >= hi:
                    continue
                if side is None:
                    found.append(r[m, at + lo - start : at + hi - start, :])
                else:
                    slot = odd if side else 1 - odd
                    first_row = pl.multiple_of(2 * own + at + lo - start + slot * halo, 16)
                    found.append(r[m, pl.ds(first_row, hi - lo), :])
        return jnp.concatenate(found, axis=0)

    def prep(loaded, both):
        for m in range(members):
            both[m, :own, :] = loaded[m].reshape(own, channels)
            both[m, own:, :] = loaded[members + m].reshape(own, channels)

    def edges(both, toward, away):
        tail = ((own - edge, own), (2 * own - half_edge, 2 * own))
        head = ((0, edge), (own, own + half_edge))

        def fill(spans, ref):
            for m in range(members):
                ref[m, :edge, :] = both[m, spans[0][0] : spans[0][1], :]
                ref[m, edge:, :] = both[m, spans[1][0] : spans[1][1], :]

        @pl.when(lax.axis_index("lat") % 2 == 0)
        def _():
            fill(tail, toward)
            fill(head, away)

        @pl.when(lax.axis_index("lat") % 2 == 1)
        def _():
            fill(head, toward)
            fill(tail, away)

    def maps(plan, lat_step, lon_step, basis, *outs):
        forward, tab = outs[0], outs[-1]
        lon, lat = lax.axis_index("lon"), lax.axis_index("lat")
        base = lat * lat_rows
        tab[...] = jnp.zeros(tab.shape, jnp.float32)
        tab[0:TAPS, :] = lat_step[...].astype(jnp.float32)
        tab[TAPS : 2 * TAPS, :] = lon_step[...].astype(jnp.float32)
        for k in range(TAPS):
            tab[2 * TAPS + k * BASIS : 2 * TAPS + (k + 1) * BASIS, :] = basis[k]
        table = tab[...].astype(jnp.bfloat16)
        source = lax.broadcasted_iota(jnp.int32, (tab.shape[1], cells), 0)
        lane = lax.broadcasted_iota(jnp.int32, (1, cells), 1)
        block, rest = lane // band, lane % band
        row_in, col_in = rest // lon_cols, rest % lon_cols
        column_home = (block ^ lon) * lon_cols + col_in
        piece = 64
        spot = lax.broadcasted_iota(jnp.int32, (piece, cells), 0)
        for i, (a, start) in enumerate(plan):
            row = row_in + (base + a)
            got = dot(table, (source == row).astype(jnp.bfloat16))
            step_lat = got[0:TAPS].astype(jnp.int32)
            step_lon = got[TAPS : 2 * TAPS].astype(jnp.int32)
            target = row + step_lat
            inside = (row >= 0) & (row < lat_total) & (target >= 0) & (target < lat_total)
            column = column_home + step_lon
            column = jnp.where(column < 0, column + ring, column)
            column = jnp.where(column >= ring, column - ring, column)
            local = target - (base + start)
            place = ((column // lon_cols) ^ lon) * win + local * lon_cols + column % lon_cols
            place = jnp.where(inside, place, -1)
            for p in range(0, blocks * win, piece):
                tables = [jnp.zeros((piece, cells), jnp.float32) for _ in range(BASIS)]
                for k in range(TAPS):
                    hit = spot == place[k : k + 1] - p
                    for b in range(BASIS):
                        at = 2 * TAPS + k * BASIS + b
                        tables[b] = tables[b] + jnp.where(hit, got[at : at + 1], 0.0)
                for b in range(BASIS):
                    span = slice(b * cells, (b + 1) * cells)
                    forward[i, span, p : p + piece] = tables[b].T.astype(jnp.bfloat16)
                    if len(outs) == 3:
                        outs[1][i, p : p + piece, span] = tables[b].astype(jnp.bfloat16)

    def put_spread(got, into, at):
        for b in range(BASIS):
            into[at : at + cells, b * channels : (b + 1) * channels] = got[b * cells : (b + 1) * cells]

    def spread(blk, forward, into):
        for m in range(members):
            for g, (a, start) in enumerate(first):
                o = (start + HALO) * lon_cols
                near = take(blk, m, state_parts, o, o + win)
                put_spread(dot(forward[g], near).astype(jnp.bfloat16), into, (m * nf + g) * cells)

    def first_section(blk, total, s1, again, mid, slope):
        for m in range(members):
            for g in range(nf):
                mixed = total[(m * nf + g) * cells : (m * nf + g + 1) * cells]
                sigma = 0.5 + 0.5 * jnp.tanh(0.5 * mixed)
                here = take(blk, m, state_parts, g * band, (g + 1) * band)
                value = (here.astype(jnp.float32) + mixed * sigma).astype(jnp.bfloat16)
                mid[m, :, g * band : (g + 1) * band, :] = value.reshape(blocks, band, channels)
                if slope is not None:
                    tilt = (sigma * (1.0 + mixed * (1.0 - sigma))).astype(slope.dtype).reshape(blocks, band, channels)
                    low, high = max(g * band, half_edge), min((g + 1) * band, 3 * half_edge + own)
                    slope[m, :, low - half_edge : high - half_edge, :] = tilt[:, low - g * band : high - g * band]
            for g in range(ns):
                near = mid[m, :, g * band : g * band + win, :].reshape(blocks * win, channels)
                put_spread(dot(again[g], near).astype(jnp.bfloat16), s1, (m * ns + g) * cells)

    def columns_of(lon):
        return pl.ds(pl.multiple_of(lon * (width // blocks), 128), width // blocks)

    def early(b0, b1, b2, b3, w_own, forward, again, s, left, slope, out, s0, mid):
        blk = (b0, b1, b2, b3)

        @pl.when(lax.axis_index("segment") == 0)
        def _():
            spread(blk, forward, s0)
            first_section(blk, dot(s0[...], w_own[...]), s, again, mid, slope)
            for m in range(members):
                size = (nf - 2) * cells
                left[m * size : (m + 1) * size, :] = s0[(m * nf + 1) * cells : (m * nf + nf - 1) * cells, columns_of(lax.axis_index("lon"))]
                out[m, :, :] = mid[m, 0, edge : edge + own, :]

        @pl.when(lax.axis_index("segment") == 1)
        def _():
            spread(blk, forward, s)

    def partial(s, near_half, far_half, w, part):
        rows = near_half.shape[0]
        here = lax.axis_index("lon") % 2 * (width // 2)
        for base, ref in ((here, near_half), (width // 2 - here, far_half)):
            w[pl.ds(pl.multiple_of(base, 32), rows), :] = ref[...]
        for i in range(2):
            late = slice(i * (width // 2) + rows, (i + 1) * (width // 2))
            w[late, :] = jnp.zeros((width // 2 - rows, channels), w.dtype)

        @pl.when(lax.axis_index("segment") == 1)
        def _():
            part[...] = dot(s[...], w[...])

    def own_part(g):
        return max(g * band, half_edge), min((g + 1) * band, half_edge + own)

    def apply_back(w, gates, feat):
        for b in range(BASIS):
            got = dot_nt(gates[...], w[b * channels : (b + 1) * channels, :]).astype(jnp.bfloat16)
            for i in range(members * ns):
                feat[(i * BASIS + b) * cells : (i * BASIS + b + 1) * cells, :] = got[i * cells : (i + 1) * cells]

    def chain(b0, b1, b2, b3, w_own, w_in, part, ends, again, backward, s, left0, slope, early_out, w,
              out_ref, next_ref, gate_ref, own_ref, p1, p2, p3, late, s1, mid, gates, feat, pull, grads):
        blk = (b0, b1, b2, b3)
        seg, lon, lat = lax.axis_index("segment"), lax.axis_index("lon"), lax.axis_index("lat")
        rest = ends.shape[0] // 2
        rows = width // 2 - rest
        aligned = rows // lanes * lanes
        span = width // 2 - aligned
        for i in range(2):
            piece = ends[i * rest : (i + 1) * rest, :]
            w[i * (width // 2) + rows : (i + 1) * (width // 2), :] = piece
            late[i * span : (i + 1) * span - rest, :] = jnp.zeros((span - rest, channels), late.dtype)
            late[(i + 1) * span - rest : (i + 1) * span, :] = piece

        def complete():
            total = part[...]
            for i in range(2):
                at = i * (width // 2) + aligned
                total = total + dot(s[:, at : at + span], late[i * span : (i + 1) * span, :])
            return total

        def coming_at(m, g):
            return take(blk, m, coming_parts, g * band, (g + 1) * band).astype(jnp.float32)

        def second_section(total, into, last):
            for m in range(members):
                for g in range(ns):
                    at = (m * ns + g) * cells
                    mixed = total[at : at + cells]
                    sigma = 0.5 + 0.5 * jnp.tanh(0.5 * mixed)
                    into[at : at + cells, :] = (coming_at(m, g) * sigma * (1.0 + mixed * (1.0 - sigma))).astype(jnp.bfloat16)
                    if last:
                        low, high = own_part(g)
                        base = mid[m, 0, half_edge + low : half_edge + high, :]
                        local = slice(low - g * band, high - g * band)
                        base = (base.astype(jnp.float32) + mixed[local] * sigma[local]).astype(jnp.bfloat16)
                        out_ref[m, low - half_edge : high - half_edge, :] = base

        def store_grads(left, right):
            got = dot_tn(left, jnp.concatenate(right, axis=0))
            for c in range(pieces):
                grads[pl.ds(c, width // blocks, stride=pieces), :] = got[:, c * lanes : (c + 1) * lanes]

        @pl.when(seg == 0)
        def _():
            second_section(dot(s[: members * ns * cells, :], w[...]), gates, False)
            out_ref[...] = early_out[...]
            apply_back(w, gates, feat)
            for m in range(members):
                for g in range(ns):
                    at = (m * ns + g) * cells * BASIS
                    low = max(g * band, half_edge)
                    high = min(g * band + win, 3 * half_edge + own)
                    local = range(0, blocks * win, win)
                    rows = [backward[g, q + low - g * band : q + high - g * band, :] for q in local]
                    got = dot(jnp.concatenate(rows, axis=0), feat[at : at + BASIS * cells, :])
                    got = got.reshape(blocks, high - low, channels)
                    turn = low if g == 0 else (g + 1) * band
                    if g > 0:
                        pull[m, :, low:turn, :] += got[:, : turn - low]
                    pull[m, :, turn:high, :] = got[:, turn - low :]
            right = []
            step = half_edge
            for m in range(members):
                for g in range(ns):
                    at = (m * ns + g) * cells
                    span = slice(half_edge + g * band, half_edge + (g + 1) * band)
                    value = (coming_at(m, g) + pull[m, :, span, :].reshape(cells, channels)).astype(jnp.bfloat16)
                    low, high = own_part(g)
                    next_ref[m, low - half_edge : high - half_edge, :] = value[low - g * band : high - g * band]
                    tilt = slope[m, :, g * band : (g + 1) * band, :].reshape(cells, channels)
                    gate_ref[at : at + cells, :] = (value.astype(jnp.float32) * tilt).astype(jnp.bfloat16)
                for g in range(1, nf - 1):
                    for q in range(blocks):
                        for o in range(0, band, step):
                            spot = half_edge + (g - 1) * band + o
                            turn, rest = spot // band, spot % band
                            at = (m * ns + turn) * cells + q * band + rest
                            right.append(gate_ref[at : at + step, :])
            store_grads(left0[...], right)

        @pl.when(seg == 1)
        def _():
            first_section(blk, complete(), s1, again, mid, None)
            second_section(dot(s1[...], w_own[...]), gate_ref, True)
            left, right = [], []
            for m in range(members):
                next_ref[m, :, :] = b0[m, own : 2 * own, :]
                for g in range(ns):
                    low, high = own_part(g)
                    for q in range(blocks):
                        at = (m * ns + g) * cells + q * band - g * band
                        left.append(s1[at + low : at + high, columns_of(lon)])
                        right.append(gate_ref[at + low : at + high, :])
            store_grads(jnp.concatenate(left, axis=0), right)

        share = width // blocks // lat_devices * pieces

        def rows_of(index):
            return grads[pl.ds(pl.multiple_of(index * share, share), share), :]

        own_ref[...] = rows_of(lat)
        for bit, ref in ((1, p1), (2, p2), (3, p3)):
            ref[...] = rows_of(lat ^ bit).astype(jnp.bfloat16)

    def finish(w_own, backward, gates, next_ref, last_ref, grad_ref, out_ref, feat, pull):
        apply_back(w_own, gates, feat)
        for m in range(members):
            for g in range(ns):
                at = (m * ns + g) * cells * BASIS
                got = dot(backward[g, 0:win, :], feat[at : at + BASIS * cells, :])
                if g == 0:
                    pull[m, :win, :] = got
                else:
                    pull[m, g * band : (g + 1) * band, :] += got[:band]
                    pull[m, (g + 1) * band : g * band + win, :] = got[band:]
            total = next_ref[m].astype(jnp.float32) + pull[m, edge : edge + own, :]
            grad_ref[m] = total.astype(jnp.bfloat16).reshape(lat_rows, lon_cols, channels)
            out_ref[m] = last_ref[m].reshape(lat_rows, lon_cols, channels)

    return prep, edges, maps, early, partial, chain, finish


def add_up(scale, mine, p1, p2, p3, out):
    out[...] = (mine[...] + p1[...].astype(jnp.float32) + p2[...].astype(jnp.float32) + p3[...].astype(jnp.float32)) * scale


def whole_ring(inputs, cotangent, weights, basis_values, lat_step, lon_step):
    members, lat_rows, lon_cols, channels = inputs.shape
    blocks = lax.axis_size("lon")
    lat_devices = lax.axis_size("lat")
    lat_total = lat_rows * lat_devices
    grad_scale = 1.0 / math.sqrt(members * lat_total * lon_cols * blocks)
    own = lat_rows * lon_cols
    edge = HALO * lon_cols
    half_edge = edge // 2
    halo = edge + half_edge
    width = BASIS * channels
    half_type, full_type = jnp.bfloat16, jnp.float32
    shape = jax.ShapeDtypeStruct
    first, second = window_plan(lat_rows)
    nf, ns = len(first), len(second)
    cells = blocks * BAND * lon_cols
    win = 16 * lon_cols
    vmem = pl.BlockSpec(memory_space=pltpu.VMEM)

    def call(body, name, outs, ins, mib, gflops, scratch=(), aliases={}):
        return pl.pallas_call(
            body,
            out_shape=outs,
            in_specs=[vmem] * len(ins),
            out_specs=(vmem,) * len(outs),
            scratch_shapes=list(scratch),
            input_output_aliases=aliases,
            compiler_params=pltpu.CompilerParams(vmem_limit_bytes=int(mib * 1024 * 1024)),
            cost_estimate=pl.CostEstimate(flops=int(gflops * 1e9), bytes_accessed=int(gflops * 1e6), transcendentals=0),
            name=name,
        )(*ins)

    prep, edges, maps, early, partial, chain, finish = make_steps(lat_rows, lon_cols, blocks, members, channels, lat_devices)
    kernel = weights.reshape(width, channels)
    rest = width // 2 * 5 // 48
    rows = width // 2 - rest
    half = lax.dynamic_slice_in_dim(kernel, lax.axis_index("lon") % 2 * (width // 2), rows, 0)
    ends = jnp.concatenate([kernel[rows : rows + rest], kernel[width - rest :]], axis=0)
    near_ends = lax.ppermute(ends, "segment", swap("segment", 1))
    near_half = lax.ppermute(half, "segment", swap("segment", 1))
    half, inputs, cotangent = lax.optimization_barrier((half, inputs, cotangent))
    loaded = jnp.concatenate([inputs, cotangent], axis=0)
    (both,) = call(prep, "prep", (shape((members, 2 * own, channels), half_type),), (loaded,), 4, 0.0)
    sides_type = shape((members, halo, channels), half_type)
    toward, away = call(edges, "edges", (sides_type, sides_type), (both,), 4, 0.0)
    both_y = lax.ppermute(both, "lon", swap("lon", 2))
    near_pairs = [(i, i ^ 1) for i in range(lat_devices)]
    far_pairs = [(i, j) for i in range(lat_devices) for j in [i + 1 if i % 2 else i - 1] if 0 <= j < lat_devices]
    from_near = lax.ppermute(toward, "lat", near_pairs)
    from_far = lax.ppermute(away, "lat", far_pairs)
    tables = (lat_step.T, lon_step.T, jnp.transpose(basis_values, (1, 2, 0)))
    _, _, *tables = lax.optimization_barrier((toward, away, *tables))
    (forward,) = call(
        functools.partial(maps, first),
        "maps_first",
        (shape((nf, BASIS * cells, blocks * win), half_type),),
        tables,
        4,
        0.0,
        (pltpu.VMEM((48, lat_total), full_type),),
    )
    from_near, from_far, forward = lax.optimization_barrier((from_near, from_far, forward))
    sides = jnp.concatenate([from_near, from_far], axis=1)
    sides, both_y = lax.optimization_barrier((sides, both_y))
    sides_y = lax.ppermute(sides, "lon", swap("lon", 2))
    b0 = jnp.concatenate([both, sides], axis=1)
    b1 = lax.ppermute(b0, "lon", swap("lon", 1))
    b0, *tables = lax.optimization_barrier((b0, *tables))
    again, backward = call(
        functools.partial(maps, second),
        "maps_again",
        (shape((ns, BASIS * cells, blocks * win), half_type), shape((ns, blocks * win, BASIS * cells), half_type)),
        tables,
        4,
        0.0,
        (pltpu.VMEM((48, lat_total), full_type),),
    )
    b2 = jnp.concatenate([both_y, sides_y], axis=1)
    b2, again, near_half = lax.optimization_barrier((b2, again, near_half))
    b3 = lax.ppermute(b2, "lon", swap("lon", 1))
    far_half = lax.ppermute(near_half, "lon", swap("lon", 1))
    s_type = (members * nf * cells, width)
    s, left, slope, early_out = call(
        early,
        "early",
        (
            shape(s_type, half_type),
            shape((members * (nf - 2) * cells, width // blocks), half_type),
            shape((members, blocks, own + edge, channels), half_type),
            shape((members, own, channels), half_type),
        ),
        (b0, b1, b2, b3, kernel, forward, again),
        12,
        3.0,
        (pltpu.VMEM(s_type, half_type), pltpu.VMEM((members, blocks, own + 2 * edge, channels), half_type)),
    )
    w_type = shape((width, channels), half_type)
    w, part = call(
        partial,
        "partial",
        (w_type, shape((s_type[0], channels), full_type)),
        (s, near_half, far_half),
        8,
        1.5,
    )
    near_ends, part = lax.optimization_barrier((near_ends, part))
    lines = (width // blocks // lat_devices * channels // 128, 128)
    _, out, follow, gates, mine, *parts = call(
        chain,
        "chain",
        (
            w_type,
            shape((members, own, channels), half_type),
            shape((members, own, channels), half_type),
            shape((members * ns * cells, channels), half_type),
            shape(lines, full_type),
        )
        + (shape(lines, half_type),) * 3,
        (b0, b1, b2, b3, kernel, w, part, near_ends, again, backward, s, left, slope, early_out),
        18,
        6.0,
        (
            pltpu.VMEM((2 * (width // 2 - (width // 2 - rest) // 128 * 128), channels), half_type),
            pltpu.VMEM((members * ns * cells, width), half_type),
            pltpu.VMEM((members, blocks, own + 2 * edge, channels), half_type),
            pltpu.VMEM((members * ns * cells, channels), half_type),
            pltpu.VMEM((members * ns * cells * BASIS, channels), half_type),
            pltpu.VMEM((members, blocks, own + 2 * edge, channels), full_type),
            pltpu.VMEM((width // blocks * channels // 128, 128), full_type),
        ),
        {5: 0},
    )
    got = [lax.ppermute(parts[bit - 1], "lat", swap("lat", bit)) for bit in (2, 1, 3)]
    block = (members, lat_rows, lon_cols, channels)
    grad, out = call(
        finish,
        "finish",
        (shape(block, half_type),) * 2,
        (kernel, backward, gates, follow, out),
        10,
        2.0,
        (
            pltpu.VMEM((members * ns * cells * BASIS, channels), half_type),
            pltpu.VMEM((members, own + 2 * edge, channels), full_type),
        ),
    )
    (total,) = call(functools.partial(add_up, grad_scale), "add_up", (shape(lines, full_type),), (mine, *got), 2, 0.1)
    return (out[None], grad[None], total.reshape(1, lines[0] * lines[1]))


def fits_ring(mesh, inputs):
    sizes = dict(mesh.shape)
    rows, cols = inputs.shape[1] // sizes["lat"], inputs.shape[2] // sizes["lon"]
    return sizes["segment"] == 2 and sizes["lon"] == 4 and sizes["lat"] == 4 and rows == 16 and cols == 4


def solution(mesh):
    def apply(*args):
        body = whole_ring if fits_ring(mesh, args[0]) else per_device
        return jax.shard_map(
            body,
            mesh=mesh,
            in_specs=(
                P(None, "lat", "lon", None),
                P(None, "lat", "lon", None),
                P("segment", None, None, None),
                P(),
                P(),
                P(),
            ),
            out_specs=(
                P("segment", None, "lat", "lon", None),
                P("segment", None, "lat", "lon", None),
                P("segment", ("lon", "lat")),
            ),
            check_vma=False,
        )(*args)

    return apply
```

```python
import functools
import math

import jax
import jax.numpy as jnp
from jax import lax
from jax.experimental import pallas as pl
from jax.experimental.pallas import tpu as pltpu
from jax.sharding import PartitionSpec as P

BASIS = 3
TAPS = 9
REACH = 2


def with_halo(array, sides, width):
    for axis, dim in sides:
        size, length = (lax.axis_size(axis), array.shape[dim])
        up = [(i, (i + 1) % size) for i in range(size)]
        down = [(j, i) for i, j in up]
        last = lax.slice_in_dim(array, length - width, length, axis=dim)
        first = lax.slice_in_dim(array, 0, width, axis=dim)
        before = lax.ppermute(last, axis, up)
        after = lax.ppermute(first, axis, down)
        array = jnp.concatenate([before, array, after], axis=dim)
    return array


def shifted(block, axis, distance):
    devices = range(lax.axis_size(axis))
    route = [(i - distance, i) for i in devices if i - distance in devices]
    return lax.ppermute(block, axis, route)


def widen(features):
    return with_halo(features, (("lon", 2), ("lat", 1)), REACH)


def pass_ahead(result):
    return shifted(result, "segment", 1)


def pass_behind(result):
    return shifted(result, "segment", -1)


def build_tables(basis_values, lat_step, lon_step, lat_rows, lon_cols, lat_index, lat_total):
    pad_rows = lat_rows + 2 * REACH
    pad_cols = lon_cols + 2 * REACH
    lat_padded = jnp.pad(lat_step, ((REACH, REACH), (0, 0)))
    lon_padded = jnp.pad(lon_step, ((REACH, REACH), (0, 0)))
    basis_padded = jnp.pad(basis_values, ((REACH, REACH), (0, 0), (0, 0)))
    row_start = lat_index * lat_rows
    lat_near = lax.dynamic_slice_in_dim(lat_padded, row_start, pad_rows, 0)
    lon_near = lax.dynamic_slice_in_dim(lon_padded, row_start, pad_rows, 0)
    basis_near = lax.dynamic_slice_in_dim(basis_padded, row_start, pad_rows, 0)
    lat_own = lat_near[REACH : REACH + lat_rows]
    lon_own = lon_near[REACH : REACH + lat_rows]
    basis_own = basis_near[REACH : REACH + lat_rows]
    own_rows = row_start + jnp.arange(lat_rows)
    inside = (own_rows[:, None] + lat_own >= 0) & (own_rows[:, None] + lat_own < lat_total)
    row_grid = jnp.arange(lat_rows)[:, None, None]
    col_grid = jnp.arange(lon_cols)[None, :, None]
    source = (row_grid + REACH + lat_own[:, None, :]) * pad_cols + (
        col_grid + REACH + lon_own[:, None, :]
    )
    tap_weight = jnp.where(inside[:, None, :, None], basis_own[:, None, :, :], 0.0)
    tap_weight = jnp.broadcast_to(tap_weight, (lat_rows, lon_cols, TAPS, BASIS))
    picker = (source[..., None] == jnp.arange(pad_rows * pad_cols)).astype(jnp.float32)
    forward_map = jnp.einsum("ijkb,ijks->bijs", tap_weight, picker, precision=lax.Precision.HIGHEST)
    forward_map = forward_map.reshape(BASIS, lat_rows * lon_cols, pad_rows * pad_cols)
    near_rows = row_start - REACH + jnp.arange(pad_rows)
    real_row = (near_rows >= 0) & (near_rows < lat_total)
    pad_row_grid = jnp.arange(pad_rows)[:, None, None]
    pad_col_grid = jnp.arange(pad_cols)[None, :, None]
    target_row = pad_row_grid - REACH + lat_near[:, None, :]
    target_col = pad_col_grid - REACH + lon_near[:, None, :]
    landed = (
        (target_row >= 0)
        & (target_row < lat_rows)
        & (target_col >= 0)
        & (target_col < lon_cols)
        & real_row[:, None, None]
    )
    target = target_row * lon_cols + target_col
    back_weight = jnp.where(landed[..., None], basis_near[:, None, :, :], 0.0)
    catcher = (target[..., None] == jnp.arange(lat_rows * lon_cols)).astype(jnp.float32)
    backward_map = jnp.einsum(
        "pqkb,pqkt->btpq", back_weight, catcher, precision=lax.Precision.HIGHEST
    )
    backward_map = backward_map.reshape(BASIS, lat_rows * lon_cols, pad_rows * pad_cols)
    return (forward_map, backward_map)


def per_device(inputs, cotangent, weights, basis_values, lat_step, lon_step):
    members, lat_rows, lon_cols, channels = inputs.shape
    pad_rows = lat_rows + 2 * REACH
    pad_cols = lon_cols + 2 * REACH
    cells = lat_rows * lon_cols
    lat_index = lax.axis_index("lat")
    lat_total = lat_rows * lax.axis_size("lat")
    segment_index = lax.axis_index("segment")
    depth = lax.axis_size("segment")
    grad_scale = 1.0 / math.sqrt(members * lat_total * lon_cols * lax.axis_size("lon"))
    forward_map, backward_map = build_tables(
        basis_values, lat_step, lon_step, lat_rows, lon_cols, lat_index, lat_total
    )
    kernel = weights[0]
    keep_spread = jnp.zeros((BASIS, members, cells, channels), jnp.bfloat16)
    keep_mixed = jnp.zeros((members, cells, channels), jnp.float32)
    keep_gate = jnp.zeros((members, cells, channels), jnp.bfloat16)
    section_out = jnp.zeros(inputs.shape, jnp.bfloat16)
    section_grad = jnp.zeros(inputs.shape, jnp.bfloat16)
    carry = inputs
    for tick_num in range(depth):
        layer_count = carry.shape[0]
        layer_padded = (
            widen(carry).reshape(layer_count, pad_rows * pad_cols, channels).astype(jnp.float32)
        )
        spread = jnp.einsum(
            "bts,msc->bmtc", forward_map, layer_padded, precision=lax.Precision.HIGHEST
        ).astype(jnp.bfloat16)
        layer_mixed = jnp.einsum(
            "bmtc,bcd->mtd", spread, kernel, preferred_element_type=jnp.float32
        )
        result = (
            carry.reshape(layer_count, cells, channels).astype(jnp.float32)
            + jax.nn.silu(layer_mixed)
        ).astype(jnp.bfloat16)
        spread, mixed, result = (spread, layer_mixed, result.reshape(carry.shape))
        here = segment_index == tick_num
        keep_spread = jnp.where(here, spread, keep_spread)
        keep_mixed = jnp.where(here, mixed, keep_mixed)
        section_out = jnp.where(here, result, section_out)
        if tick_num + 1 < depth:
            carry = pass_ahead(result)
    grad = cotangent
    for tick_num in range(depth):
        count = grad.shape[0]
        flat_grad = grad.reshape(count, cells, channels).astype(jnp.float32)
        sigma = jax.nn.sigmoid(keep_mixed)
        gate_grad = (flat_grad * sigma * (1.0 + keep_mixed * (1.0 - sigma))).astype(jnp.bfloat16)
        feature_grad = jnp.einsum(
            "mtd,bcd->bmtc", gate_grad, kernel, preferred_element_type=jnp.float32
        ).astype(jnp.bfloat16)
        padded = widen(feature_grad.reshape(BASIS * count, lat_rows, lon_cols, channels))
        padded = padded.reshape(BASIS, count, pad_rows * pad_cols, channels).astype(jnp.float32)
        pulled = jnp.einsum("bts,bmsc->mtc", backward_map, padded, precision=lax.Precision.HIGHEST)
        new_grad = (flat_grad + pulled).astype(jnp.bfloat16).reshape(grad.shape)
        gate_grad, new_grad = (gate_grad, new_grad)
        here = segment_index == depth - 1 - tick_num
        keep_gate = jnp.where(here, gate_grad, keep_gate)
        section_grad = jnp.where(here, new_grad, section_grad)
        if tick_num + 1 < depth:
            grad = pass_behind(new_grad)
    local_grad = (
        jnp.einsum("bmtc,mtd->bcd", keep_spread, keep_gate, preferred_element_type=jnp.float32)
        * grad_scale
    )
    owners = lax.axis_size("lon") * lax.axis_size("lat")
    grad_rows = local_grad.reshape(owners, -1)
    weight_grad = lax.psum_scatter(grad_rows, ("lon", "lat"), scatter_dimension=0, tiled=True)
    return (section_out[None], section_grad[None], weight_grad)


HALO = 8
BAND = 8


def swap(axis, bit):
    return [(i, i ^ bit) for i in range(lax.axis_size(axis))]


def window_plan(lat_rows):
    first = [(a, min(max(a - 4, -HALO), lat_rows + HALO - 16)) for a in range(-HALO, lat_rows + HALO, BAND)]
    second = [(a, a - 4) for a in range(-4, lat_rows + 4, BAND)]
    return first, second


def dot(a, b):
    return jnp.dot(a, b, preferred_element_type=jnp.float32)


def dot_nt(a, b):
    return lax.dot_general(a, b, (((1,), (1,)), ((), ())), preferred_element_type=jnp.float32)


def dot_tn(a, b):
    return lax.dot_general(a, b, (((0,), (0,)), ((), ())), preferred_element_type=jnp.float32)


def make_steps(lat_rows, lon_cols, blocks, members, channels, lat_devices):
    first, second = window_plan(lat_rows)
    nf, ns = len(first), len(second)
    lat_total = lat_rows * lat_devices
    ring = lon_cols * blocks
    band = BAND * lon_cols
    cells = blocks * band
    win = 16 * lon_cols
    own = lat_rows * lon_cols
    edge = HALO * lon_cols
    half_edge = edge // 2
    width = BASIS * channels
    lanes = 128
    pieces = channels // lanes
    halo = edge + half_edge
    state_parts = ((0, edge, 0, 0), (edge, own, 0, None), (edge + own, edge, 0, 1))
    coming_parts = ((0, half_edge, edge, 0), (half_edge, own, own, None), (half_edge + own, half_edge, edge, 1))

    def take(blks, m, parts, low, high):
        found = []
        odd = lax.axis_index("lat") % 2
        for r in blks:
            for start, size, at, side in parts:
                lo, hi = max(low, start), min(high, start + size)
                if lo >= hi:
                    continue
                if side is None:
                    found.append(r[m, at + lo - start : at + hi - start, :])
                else:
                    slot = odd if side else 1 - odd
                    first_row = pl.multiple_of(2 * own + at + lo - start + slot * halo, 16)
                    found.append(r[m, pl.ds(first_row, hi - lo), :])
        return jnp.concatenate(found, axis=0)

    def prep(loaded, both):
        for m in range(members):
            both[m, :own, :] = loaded[m].reshape(own, channels)
            both[m, own:, :] = loaded[members + m].reshape(own, channels)

    def edges(both, toward, away):
        tail = ((own - edge, own), (2 * own - half_edge, 2 * own))
        head = ((0, edge), (own, own + half_edge))

        def fill(spans, ref):
            for m in range(members):
                ref[m, :edge, :] = both[m, spans[0][0] : spans[0][1], :]
                ref[m, edge:, :] = both[m, spans[1][0] : spans[1][1], :]

        @pl.when(lax.axis_index("lat") % 2 == 0)
        def _():
            fill(tail, toward)
            fill(head, away)

        @pl.when(lax.axis_index("lat") % 2 == 1)
        def _():
            fill(head, toward)
            fill(tail, away)

    def maps(plan, lat_step, lon_step, basis, *outs):
        forward, tab = outs[0], outs[-1]
        lon, lat = lax.axis_index("lon"), lax.axis_index("lat")
        base = lat * lat_rows
        tab[...] = jnp.zeros(tab.shape, jnp.float32)
        tab[0:TAPS, :] = lat_step[...].astype(jnp.float32)
        tab[TAPS : 2 * TAPS, :] = lon_step[...].astype(jnp.float32)
        for k in range(TAPS):
            tab[2 * TAPS + k * BASIS : 2 * TAPS + (k + 1) * BASIS, :] = basis[k]
        table = tab[...].astype(jnp.bfloat16)
        source = lax.broadcasted_iota(jnp.int32, (tab.shape[1], cells), 0)
        lane = lax.broadcasted_iota(jnp.int32, (1, cells), 1)
        block, rest = lane // band, lane % band
        row_in, col_in = rest // lon_cols, rest % lon_cols
        column_home = (block ^ lon) * lon_cols + col_in
        piece = 64
        spot = lax.broadcasted_iota(jnp.int32, (piece, cells), 0)
        for i, (a, start) in enumerate(plan):
            row = row_in + (base + a)
            got = dot(table, (source == row).astype(jnp.bfloat16))
            step_lat = got[0:TAPS].astype(jnp.int32)
            step_lon = got[TAPS : 2 * TAPS].astype(jnp.int32)
            target = row + step_lat
            inside = (row >= 0) & (row < lat_total) & (target >= 0) & (target < lat_total)
            column = column_home + step_lon
            column = jnp.where(column < 0, column + ring, column)
            column = jnp.where(column >= ring, column - ring, column)
            local = target - (base + start)
            place = ((column // lon_cols) ^ lon) * win + local * lon_cols + column % lon_cols
            place = jnp.where(inside, place, -1)
            for p in range(0, blocks * win, piece):
                tables = [jnp.zeros((piece, cells), jnp.float32) for _ in range(BASIS)]
                for k in range(TAPS):
                    hit = spot == place[k : k + 1] - p
                    for b in range(BASIS):
                        at = 2 * TAPS + k * BASIS + b
                        tables[b] = tables[b] + jnp.where(hit, got[at : at + 1], 0.0)
                for b in range(BASIS):
                    span = slice(b * cells, (b + 1) * cells)
                    forward[i, span, p : p + piece] = tables[b].T.astype(jnp.bfloat16)
                    if len(outs) == 3:
                        outs[1][i, p : p + piece, span] = tables[b].astype(jnp.bfloat16)

    def put_spread(got, into, at):
        for b in range(BASIS):
            into[at : at + cells, b * channels : (b + 1) * channels] = got[b * cells : (b + 1) * cells]

    def spread(blk, forward, into):
        for m in range(members):
            for g, (a, start) in enumerate(first):
                o = (start + HALO) * lon_cols
                near = take(blk, m, state_parts, o, o + win)
                put_spread(dot(forward[g], near).astype(jnp.bfloat16), into, (m * nf + g) * cells)

    def first_section(blk, total, s1, again, mid, slope):
        for m in range(members):
            for g in range(nf):
                mixed = total[(m * nf + g) * cells : (m * nf + g + 1) * cells]
                sigma = 0.5 + 0.5 * jnp.tanh(0.5 * mixed)
                here = take(blk, m, state_parts, g * band, (g + 1) * band)
                value = (here.astype(jnp.float32) + mixed * sigma).astype(jnp.bfloat16)
                mid[m, :, g * band : (g + 1) * band, :] = value.reshape(blocks, band, channels)
                if slope is not None:
                    tilt = (sigma * (1.0 + mixed * (1.0 - sigma))).astype(slope.dtype).reshape(blocks, band, channels)
                    low, high = max(g * band, half_edge), min((g + 1) * band, 3 * half_edge + own)
                    slope[m, :, low - half_edge : high - half_edge, :] = tilt[:, low - g * band : high - g * band]
            for g in range(ns):
                near = mid[m, :, g * band : g * band + win, :].reshape(blocks * win, channels)
                put_spread(dot(again[g], near).astype(jnp.bfloat16), s1, (m * ns + g) * cells)

    def columns_of(lon):
        return pl.ds(pl.multiple_of(lon * (width // blocks), 128), width // blocks)

    def early(b0, b1, b2, b3, w_own, forward, again, s, left, slope, out, s0, mid):
        blk = (b0, b1, b2, b3)

        @pl.when(lax.axis_index("segment") == 0)
        def _():
            spread(blk, forward, s0)
            first_section(blk, dot(s0[...], w_own[...]), s, again, mid, slope)
            for m in range(members):
                size = (nf - 2) * cells
                left[m * size : (m + 1) * size, :] = s0[(m * nf + 1) * cells : (m * nf + nf - 1) * cells, columns_of(lax.axis_index("lon"))]
                out[m, :, :] = mid[m, 0, edge : edge + own, :]

        @pl.when(lax.axis_index("segment") == 1)
        def _():
            spread(blk, forward, s)

    def partial(s, near_half, far_half, w, part):
        rows = near_half.shape[0]
        here = lax.axis_index("lon") % 2 * (width // 2)
        for base, ref in ((here, near_half), (width // 2 - here, far_half)):
            w[pl.ds(pl.multiple_of(base, 32), rows), :] = ref[...]
        for i in range(2):
            late = slice(i * (width // 2) + rows, (i + 1) * (width // 2))
            w[late, :] = jnp.zeros((width // 2 - rows, channels), w.dtype)

        @pl.when(lax.axis_index("segment") == 1)
        def _():
            part[...] = dot(s[...], w[...])

    def own_part(g):
        return max(g * band, half_edge), min((g + 1) * band, half_edge + own)

    def apply_back(w, gates, feat):
        for b in range(BASIS):
            got = dot_nt(gates[...], w[b * channels : (b + 1) * channels, :]).astype(jnp.bfloat16)
            for i in range(members * ns):
                feat[(i * BASIS + b) * cells : (i * BASIS + b + 1) * cells, :] = got[i * cells : (i + 1) * cells]

    def chain(b0, b1, b2, b3, w_own, w_in, part, ends, again, backward, s, left0, slope, early_out, w,
              out_ref, next_ref, gate_ref, own_ref, p1, p2, p3, late, s1, mid, gates, feat, pull, grads):
        blk = (b0, b1, b2, b3)
        seg, lon, lat = lax.axis_index("segment"), lax.axis_index("lon"), lax.axis_index("lat")
        rest = ends.shape[0] // 2
        rows = width // 2 - rest
        aligned = rows // lanes * lanes
        span = width // 2 - aligned
        for i in range(2):
            piece = ends[i * rest : (i + 1) * rest, :]
            w[i * (width // 2) + rows : (i + 1) * (width // 2), :] = piece
            late[i * span : (i + 1) * span - rest, :] = jnp.zeros((span - rest, channels), late.dtype)
            late[(i + 1) * span - rest : (i + 1) * span, :] = piece

        def complete():
            total = part[...]
            for i in range(2):
                at = i * (width // 2) + aligned
                total = total + dot(s[:, at : at + span], late[i * span : (i + 1) * span, :])
            return total

        def coming_at(m, g):
            return take(blk, m, coming_parts, g * band, (g + 1) * band).astype(jnp.float32)

        def second_section(total, into, last):
            for m in range(members):
                for g in range(ns):
                    at = (m * ns + g) * cells
                    mixed = total[at : at + cells]
                    sigma = 0.5 + 0.5 * jnp.tanh(0.5 * mixed)
                    into[at : at + cells, :] = (coming_at(m, g) * sigma * (1.0 + mixed * (1.0 - sigma))).astype(jnp.bfloat16)
                    if last:
                        low, high = own_part(g)
                        base = mid[m, 0, half_edge + low : half_edge + high, :]
                        local = slice(low - g * band, high - g * band)
                        base = (base.astype(jnp.float32) + mixed[local] * sigma[local]).astype(jnp.bfloat16)
                        out_ref[m, low - half_edge : high - half_edge, :] = base

        def store_grads(left, right):
            got = dot_tn(left, jnp.concatenate(right, axis=0))
            for c in range(pieces):
                grads[pl.ds(c, width // blocks, stride=pieces), :] = got[:, c * lanes : (c + 1) * lanes]

        @pl.when(seg == 0)
        def _():
            second_section(dot(s[: members * ns * cells, :], w[...]), gates, False)
            out_ref[...] = early_out[...]
            apply_back(w, gates, feat)
            for m in range(members):
                for g in range(ns):
                    at = (m * ns + g) * cells * BASIS
                    low = max(g * band, half_edge)
                    high = min(g * band + win, 3 * half_edge + own)
                    local = range(0, blocks * win, win)
                    rows = [backward[g, q + low - g * band : q + high - g * band, :] for q in local]
                    got = dot(jnp.concatenate(rows, axis=0), feat[at : at + BASIS * cells, :])
                    got = got.reshape(blocks, high - low, channels)
                    turn = low if g == 0 else (g + 1) * band
                    if g > 0:
                        pull[m, :, low:turn, :] += got[:, : turn - low]
                    pull[m, :, turn:high, :] = got[:, turn - low :]
            right = []
            step = half_edge
            for m in range(members):
                for g in range(ns):
                    at = (m * ns + g) * cells
                    span = slice(half_edge + g * band, half_edge + (g + 1) * band)
                    value = (coming_at(m, g) + pull[m, :, span, :].reshape(cells, channels)).astype(jnp.bfloat16)
                    low, high = own_part(g)
                    next_ref[m, low - half_edge : high - half_edge, :] = value[low - g * band : high - g * band]
                    tilt = slope[m, :, g * band : (g + 1) * band, :].reshape(cells, channels)
                    gate_ref[at : at + cells, :] = (value.astype(jnp.float32) * tilt).astype(jnp.bfloat16)
                for g in range(1, nf - 1):
                    for q in range(blocks):
                        for o in range(0, band, step):
                            spot = half_edge + (g - 1) * band + o
                            turn, rest = spot // band, spot % band
                            at = (m * ns + turn) * cells + q * band + rest
                            right.append(gate_ref[at : at + step, :])
            store_grads(left0[...], right)

        @pl.when(seg == 1)
        def _():
            first_section(blk, complete(), s1, again, mid, None)
            second_section(dot(s1[...], w_own[...]), gate_ref, True)
            left, right = [], []
            for m in range(members):
                next_ref[m, :, :] = b0[m, own : 2 * own, :]
                for g in range(ns):
                    low, high = own_part(g)
                    for q in range(blocks):
                        at = (m * ns + g) * cells + q * band - g * band
                        left.append(s1[at + low : at + high, columns_of(lon)])
                        right.append(gate_ref[at + low : at + high, :])
            store_grads(jnp.concatenate(left, axis=0), right)

        share = width // blocks // lat_devices * pieces

        def rows_of(index):
            return grads[pl.ds(pl.multiple_of(index * share, share), share), :]

        own_ref[...] = rows_of(lat)
        for bit, ref in ((1, p1), (2, p2), (3, p3)):
            ref[...] = rows_of(lat ^ bit).astype(jnp.bfloat16)

    def finish(w_own, backward, gates, next_ref, last_ref, grad_ref, out_ref, feat, pull):
        apply_back(w_own, gates, feat)
        for m in range(members):
            for g in range(ns):
                at = (m * ns + g) * cells * BASIS
                got = dot(backward[g, 0:win, :], feat[at : at + BASIS * cells, :])
                if g == 0:
                    pull[m, :win, :] = got
                else:
                    pull[m, g * band : (g + 1) * band, :] += got[:band]
                    pull[m, (g + 1) * band : g * band + win, :] = got[band:]
            total = next_ref[m].astype(jnp.float32) + pull[m, edge : edge + own, :]
            grad_ref[m] = total.astype(jnp.bfloat16).reshape(lat_rows, lon_cols, channels)
            out_ref[m] = last_ref[m].reshape(lat_rows, lon_cols, channels)

    return prep, edges, maps, early, partial, chain, finish


def add_up(scale, mine, p1, p2, p3, out):
    out[...] = (mine[...] + p1[...].astype(jnp.float32) + p2[...].astype(jnp.float32) + p3[...].astype(jnp.float32)) * scale


def whole_ring(inputs, cotangent, weights, basis_values, lat_step, lon_step):
    members, lat_rows, lon_cols, channels = inputs.shape
    blocks = lax.axis_size("lon")
    lat_devices = lax.axis_size("lat")
    lat_total = lat_rows * lat_devices
    grad_scale = 1.0 / math.sqrt(members * lat_total * lon_cols * blocks)
    own = lat_rows * lon_cols
    edge = HALO * lon_cols
    half_edge = edge // 2
    halo = edge + half_edge
    width = BASIS * channels
    half_type, full_type = jnp.bfloat16, jnp.float32
    shape = jax.ShapeDtypeStruct
    first, second = window_plan(lat_rows)
    nf, ns = len(first), len(second)
    cells = blocks * BAND * lon_cols
    win = 16 * lon_cols
    vmem = pl.BlockSpec(memory_space=pltpu.VMEM)

    def call(body, name, outs, ins, mib, gflops, scratch=(), aliases={}):
        return pl.pallas_call(
            body,
            out_shape=outs,
            in_specs=[vmem] * len(ins),
            out_specs=(vmem,) * len(outs),
            scratch_shapes=list(scratch),
            input_output_aliases=aliases,
            compiler_params=pltpu.CompilerParams(vmem_limit_bytes=int(mib * 1024 * 1024)),
            cost_estimate=pl.CostEstimate(flops=int(gflops * 1e9), bytes_accessed=int(gflops * 1e6), transcendentals=0),
            name=name,
        )(*ins)

    prep, edges, maps, early, partial, chain, finish = make_steps(lat_rows, lon_cols, blocks, members, channels, lat_devices)
    kernel = weights.reshape(width, channels)
    rest = width // 2 // 12
    rows = width // 2 - rest
    half = lax.dynamic_slice_in_dim(kernel, lax.axis_index("lon") % 2 * (width // 2), rows, 0)
    ends = jnp.concatenate([kernel[rows : rows + rest], kernel[width - rest :]], axis=0)
    near_ends = lax.ppermute(ends, "segment", swap("segment", 1))
    near_half = lax.ppermute(half, "segment", swap("segment", 1))
    half, inputs, cotangent = lax.optimization_barrier((half, inputs, cotangent))
    loaded = jnp.concatenate([inputs, cotangent], axis=0)
    (both,) = call(prep, "prep", (shape((members, 2 * own, channels), half_type),), (loaded,), 4, 0.0)
    sides_type = shape((members, halo, channels), half_type)
    toward, away = call(edges, "edges", (sides_type, sides_type), (both,), 4, 0.0)
    both_y = lax.ppermute(both, "lon", swap("lon", 2))
    near_pairs = [(i, i ^ 1) for i in range(lat_devices)]
    far_pairs = [(i, j) for i in range(lat_devices) for j in [i + 1 if i % 2 else i - 1] if 0 <= j < lat_devices]
    from_near = lax.ppermute(toward, "lat", near_pairs)
    from_far = lax.ppermute(away, "lat", far_pairs)
    tables = (lat_step.T, lon_step.T, jnp.transpose(basis_values, (1, 2, 0)))
    _, _, *tables = lax.optimization_barrier((toward, away, *tables))
    (forward,) = call(
        functools.partial(maps, first),
        "maps_first",
        (shape((nf, BASIS * cells, blocks * win), half_type),),
        tables,
        4,
        0.0,
        (pltpu.VMEM((48, lat_total), full_type),),
    )
    from_near, from_far, forward = lax.optimization_barrier((from_near, from_far, forward))
    sides = jnp.concatenate([from_near, from_far], axis=1)
    sides, both_y = lax.optimization_barrier((sides, both_y))
    sides_y = lax.ppermute(sides, "lon", swap("lon", 2))
    b0 = jnp.concatenate([both, sides], axis=1)
    b1 = lax.ppermute(b0, "lon", swap("lon", 1))
    b0, *tables = lax.optimization_barrier((b0, *tables))
    again, backward = call(
        functools.partial(maps, second),
        "maps_again",
        (shape((ns, BASIS * cells, blocks * win), half_type), shape((ns, blocks * win, BASIS * cells), half_type)),
        tables,
        4,
        0.0,
        (pltpu.VMEM((48, lat_total), full_type),),
    )
    b2 = jnp.concatenate([both_y, sides_y], axis=1)
    b2, again, near_half = lax.optimization_barrier((b2, again, near_half))
    b3 = lax.ppermute(b2, "lon", swap("lon", 1))
    far_half = lax.ppermute(near_half, "lon", swap("lon", 1))
    s_type = (members * nf * cells, width)
    s, left, slope, early_out = call(
        early,
        "early",
        (
            shape(s_type, half_type),
            shape((members * (nf - 2) * cells, width // blocks), half_type),
            shape((members, blocks, own + edge, channels), half_type),
            shape((members, own, channels), half_type),
        ),
        (b0, b1, b2, b3, kernel, forward, again),
        12,
        3.0,
        (pltpu.VMEM(s_type, half_type), pltpu.VMEM((members, blocks, own + 2 * edge, channels), half_type)),
    )
    w_type = shape((width, channels), half_type)
    w, part = call(
        partial,
        "partial",
        (w_type, shape((s_type[0], channels), full_type)),
        (s, near_half, far_half),
        8,
        1.5,
    )
    near_ends, part = lax.optimization_barrier((near_ends, part))
    lines = (width // blocks // lat_devices * channels // 128, 128)
    _, out, follow, gates, mine, *parts = call(
        chain,
        "chain",
        (
            w_type,
            shape((members, own, channels), half_type),
            shape((members, own, channels), half_type),
            shape((members * ns * cells, channels), half_type),
            shape(lines, full_type),
        )
        + (shape(lines, half_type),) * 3,
        (b0, b1, b2, b3, kernel, w, part, near_ends, again, backward, s, left, slope, early_out),
        18,
        6.0,
        (
            pltpu.VMEM((2 * (width // 2 - (width // 2 - rest) // 128 * 128), channels), half_type),
            pltpu.VMEM((members * ns * cells, width), half_type),
            pltpu.VMEM((members, blocks, own + 2 * edge, channels), half_type),
            pltpu.VMEM((members * ns * cells, channels), half_type),
            pltpu.VMEM((members * ns * cells * BASIS, channels), half_type),
            pltpu.VMEM((members, blocks, own + 2 * edge, channels), full_type),
            pltpu.VMEM((width // blocks * channels // 128, 128), full_type),
        ),
        {5: 0},
    )
    got = [lax.ppermute(parts[bit - 1], "lat", swap("lat", bit)) for bit in (2, 1, 3)]
    block = (members, lat_rows, lon_cols, channels)
    grad, out = call(
        finish,
        "finish",
        (shape(block, half_type),) * 2,
        (kernel, backward, gates, follow, out),
        10,
        2.0,
        (
            pltpu.VMEM((members * ns * cells * BASIS, channels), half_type),
            pltpu.VMEM((members, own + 2 * edge, channels), full_type),
        ),
    )
    (total,) = call(functools.partial(add_up, grad_scale), "add_up", (shape(lines, full_type),), (mine, *got), 2, 0.1)
    return (out[None], grad[None], total.reshape(1, lines[0] * lines[1]))


def fits_ring(mesh, inputs):
    sizes = dict(mesh.shape)
    rows, cols = inputs.shape[1] // sizes["lat"], inputs.shape[2] // sizes["lon"]
    return sizes["segment"] == 2 and sizes["lon"] == 4 and sizes["lat"] == 4 and rows == 16 and cols == 4


def solution(mesh):
    def apply(*args):
        body = whole_ring if fits_ring(mesh, args[0]) else per_device
        return jax.shard_map(
            body,
            mesh=mesh,
            in_specs=(
                P(None, "lat", "lon", None),
                P(None, "lat", "lon", None),
                P("segment", None, None, None),
                P(),
                P(),
                P(),
            ),
            out_specs=(
                P("segment", None, "lat", "lon", None),
                P("segment", None, "lat", "lon", None),
                P("segment", ("lon", "lat")),
            ),
            check_vma=False,
        )(*args)

    return apply
```
